128 devices in a mesh: ctx: 16 (over y_lo, z, core), fsdp: 8 (over x, y_hi).
Axes of the slice: x: 4, y: 4 (y_hi: 2, y_lo: 2; y = y_hi * 2 + y_lo), z: 4, core: 2. Of those that a mesh axis runs over, the one named last changes fastest.
Arguments:
- tokens: bfloat16 [2, 8, 2048, 1024], P(None, 'fsdp', 'ctx')
- cotangent: bfloat16 [2, 8, 2048, 1024], P(None, 'fsdp', 'ctx')
- dest: int32 [2, 8, 2048], P(None, 'fsdp', 'ctx'), may hold values from 0 to 2047, as said below
- lengths: int32 [2, 8, 8], P(None, 'fsdp'), may hold values from 1 to 1024, as said below
- attn_weight: float32 [1024, 4096], P('fsdp')
- attn_first: float32 [1024, 4096], P('fsdp'), may hold values from -0.00048828125 to 0.00048828125
- attn_second: float32 [1024, 4096], P('fsdp'), may hold values from 7.9395324e-11 to 3.175813e-10
- ffn_weight: float32 [1024, 8192], P('fsdp')
- ffn_first: float32 [1024, 8192], P('fsdp'), may hold values from -0.00048828125 to 0.00048828125
- ffn_second: float32 [1024, 8192], P('fsdp'), may hold values from 7.9395324e-11 to 3.175813e-10
- vectors: float32 [12, 1024], P(None, 'fsdp')
- vec_first: float32 [12, 1024], P(None, 'fsdp'), may hold values from -0.0048828125 to 0.0048828125
- vec_second: float32 [12, 1024], P(None, 'fsdp'), may hold values from 2.3818598e-09 to 9.527439e-09
Outputs:
- layer_output: bfloat16 [2, 8, 2048, 1024], P(None, 'fsdp', 'ctx')
- input_grad: bfloat16 [2, 8, 2048, 1024], P(None, 'fsdp', 'ctx')
- grad_norm: float32 [], replicated
- attn_new: float32 [1024, 4096], P('fsdp')
- attn_first_new: float32 [1024, 4096], P('fsdp')
- attn_second_new: float32 [1024, 4096], P('fsdp')
- ffn_new: float32 [1024, 8192], P('fsdp')
- ffn_first_new: float32 [1024, 8192], P('fsdp')
- ffn_second_new: float32 [1024, 8192], P('fsdp')
- vec_new: float32 [12, 1024], P(None, 'fsdp')
- vec_first_new: float32 [12, 1024], P(None, 'fsdp')
- vec_second_new: float32 [12, 1024], P(None, 'fsdp')
- attn_copy: bfloat16 [1024, 4096], P('fsdp')
- ffn_copy: bfloat16 [1024, 8192], P('fsdp')
- output_bias_grad: float32 [1024], P('fsdp')
The draws below stay inside these ranges and needn't reach their ends.
Inputs may be any that keep to these rules, and one draw needn't show every extreme that they name: Within each micro-batch and fsdp index, dest is a permutation of the pack's slots; slot s lies on ctx device s // 128, and each ctx device's given tokens go exactly 8 to each ctx device. The lengths of a pack sum to at most 2048; one of them is exactly 1024; sequences fill the packed slots in order and the rest is padding.
All inputs are finite; a program needn't handle non-finite values.
Results may differ from the reference program's by a relative error of at most 0.03.
Values may be sent and summed in bfloat16 or wider, within the bound.
A program may use at most 320 MiB of HBM per device.

```python
import math
import jax
import jax.numpy as jnp
from jax import lax

D = 1024
HEADS = 16
HEAD = 64
FF = 4096
LONGEST = 1024
NSEQ = 8
MB = 2
STEP = 10
TOK_MB = 128
PACK = 2048
PARAMS = 12595200
N_CTX = 16
N_FSDP = 8


def random_perms(key, batch_count, length):
    keys_all = jax.random.split(key, batch_count)
    return jax.vmap(lambda one_key: jax.random.permutation(one_key, length))(keys_all)


def draw_dest(key, part):
    pack_count = MB * N_FSDP
    devices = N_CTX
    row_count = TOK_MB
    each_share = row_count // devices
    first_key, second_key = jax.random.split(jax.random.fold_in(key, 11))
    slot_perm = random_perms(first_key, pack_count * devices, row_count).reshape(pack_count, devices, row_count)
    slot_perm = slot_perm + (jnp.arange(devices) * row_count)[None, :, None]
    grouped = slot_perm.reshape(pack_count, devices, devices, each_share)
    by_source = jnp.transpose(grouped, (0, 2, 1, 3)).reshape(pack_count, devices, row_count)
    row_perm = random_perms(second_key, pack_count * devices, row_count).reshape(pack_count, devices, row_count)
    result = jnp.take_along_axis(by_source, row_perm, axis=2)
    return result.reshape(MB, N_FSDP, devices * row_count).astype(jnp.int32)


def draw_lengths(key, part):
    room = min(LONGEST, (TOK_MB * N_CTX - LONGEST) // (NSEQ - 1))
    first_key, second_key = jax.random.split(jax.random.fold_in(key, 23))
    others = jax.random.randint(first_key, (MB, N_FSDP, NSEQ), 1, room + 1)
    odd_first = 2 * jax.random.randint(second_key, (MB, N_FSDP, 1), 0, (room - 1) // 2 + 1) + 1
    slots = jnp.arange(NSEQ)[None, None, :]
    result = jnp.where(slots == 1, LONGEST, others)
    result = jnp.where(slots == 0, odd_first, result)
    return result.astype(jnp.int32)


def base_draw(key, shape):
    return jax.random.normal(key, shape, jnp.float32)


def column_ramp(width):
    spread_log = 1.3862944
    place = jnp.arange(width).astype(jnp.float32) / (width - 1) - 0.5
    ramp = jnp.exp(spread_log * place)
    return ramp / jnp.sqrt(jnp.mean(ramp * ramp))


def draw_tokens(key, part):
    base = base_draw(jax.random.fold_in(key, 29), (MB, N_FSDP, PACK, D))
    return (base * column_ramp(D)[None, None, None, :]).astype(jnp.bfloat16)


def draw_cotangent(key, part):
    first_key, second_key = jax.random.split(jax.random.fold_in(key, 43))
    base = base_draw(first_key, (MB, N_FSDP, PACK, D))
    offset = base_draw(second_key, (MB, N_FSDP, PACK, 1)) * 0.7
    return (base + offset).astype(jnp.bfloat16)


def draw_attn_weight(key, part):
    base = base_draw(jax.random.fold_in(key, 31), (D, 4 * D))
    columns = jnp.arange(4 * D)
    factor = jnp.where(columns < 3 * D, 1.0, 8.0) * D ** (-0.5)
    return base * factor[None, :]


def draw_ffn_weight(key, part):
    base = base_draw(jax.random.fold_in(key, 37), (D, 2 * FF))
    columns = jnp.arange(2 * FF)
    factor = jnp.where(columns < FF, D ** (-0.5), 2.0 * FF ** (-0.5))
    return base * factor[None, :]


def draw_vectors(key, part):
    first_key, second_key = jax.random.split(jax.random.fold_in(key, 41))
    shifts = base_draw(first_key, (12, D)) * 0.3
    gains = jax.random.uniform(second_key, (12, D), jnp.float32, 0.6, 1.4) * column_ramp(D)[None, :]
    row_ids = jnp.arange(12)[:, None]
    is_gain = (row_ids == 4) | (row_ids == 6)
    return jnp.where(is_gain, gains, shifts)


def block_scale(stream_key, dims, pieces, low, top_value):
    def one(axis_at, shards_of):
        heights = jax.random.uniform(jax.random.fold_in(jax.random.fold_in(stream_key, 6), axis_at), (shards_of,), jnp.float32, low / len(pieces), top_value / len(pieces))
        return jnp.repeat(jnp.exp(heights), dims[axis_at] // shards_of).reshape((-1,) + (1,) * (len(dims) - axis_at - 1))

    level = one(*pieces[0])
    for cut in pieces[1:]:
        level = level * one(*cut)
    return level


def gaussian(own_key, dims, deviation, reach, shards=(), kind=jnp.bfloat16):
    factor_of = block_scale(own_key, dims, shards, -0.22, 0.18) if shards else 1.0
    values = jax.random.normal(own_key, dims, jnp.float32) * deviation * factor_of
    return jnp.minimum(jnp.maximum(values, -reach), reach).astype(kind)


def setup_inputs(seed: int = 0) -> dict:
    splits = jax.random.split(jax.random.key(seed), 14)
    tokens = draw_tokens(jax.random.fold_in(splits[13], 71), 0)
    cotangent = draw_cotangent(jax.random.fold_in(splits[13], 71), 0)
    dest = draw_dest(jax.random.fold_in(splits[13], 71), 0)
    lengths = draw_lengths(jax.random.fold_in(splits[13], 71), 0)
    attn_weight = draw_attn_weight(jax.random.fold_in(splits[13], 71), 0)
    attn_first = gaussian(splits[5], (D, 4 * D), (0.11 * PARAMS ** -0.5), 0.00048828125, ((0, 8),), jnp.float32)
    attn_second = jnp.clip(jnp.exp(math.log(3.1758129459547035e-10) - 1.3862944 * jax.random.uniform(splits[6], (D, 4 * D), jnp.float32) ** block_scale(splits[6], (D, 4 * D), ((0, 8),), -0.2, 0.2)), 7.939532364886759e-11, 3.1758129459547035e-10)
    ffn_weight = draw_ffn_weight(jax.random.fold_in(splits[13], 71), 0)
    ffn_first = gaussian(splits[8], (D, 2 * FF), (0.11 * PARAMS ** -0.5), 0.00048828125, ((0, 8),), jnp.float32)
    ffn_second = jnp.clip(jnp.exp(math.log(3.1758129459547035e-10) - 1.3862944 * jax.random.uniform(splits[9], (D, 2 * FF), jnp.float32) ** block_scale(splits[9], (D, 2 * FF), ((0, 8),), -0.2, 0.2)), 7.939532364886759e-11, 3.1758129459547035e-10)
    vectors = draw_vectors(jax.random.fold_in(splits[13], 71), 0)
    vec_first = gaussian(splits[11], (12, D), (1.1 * PARAMS ** -0.5), 0.0048828125, ((1, 8),), jnp.float32)
    vec_second = jnp.clip(jnp.exp(math.log(9.52743928195332e-09) - 1.3862944 * jax.random.uniform(splits[12], (12, D), jnp.float32) ** block_scale(splits[12], (12, D), ((1, 8),), -0.2, 0.2)), 2.38185982048833e-09, 9.52743928195332e-09)
    return dict(tokens=tokens, cotangent=cotangent, dest=dest, lengths=lengths, attn_weight=attn_weight, attn_first=attn_first, attn_second=attn_second, ffn_weight=ffn_weight, ffn_first=ffn_first, ffn_second=ffn_second, vectors=vectors, vec_first=vec_first, vec_second=vec_second)


@jax.custom_vjp
def low(v):
    return lax.optimization_barrier(v.astype(jnp.bfloat16)).astype(jnp.float32)

@jax.custom_vjp
def low_back(v):
    return v

def low_keep(v):
    return (low(v), None)

def low_pass(kept, grad):
    return (grad,)

def back_keep(v):
    return (v, None)

def back_low(kept, grad):
    return (low(grad),)
low.defvjp(low_keep, low_pass)
low_back.defvjp(back_keep, back_low)
NORM_EPS = 1e-05
CLIP_NORM = 1.0
BETA_FIRST = 0.9
BETA_SECOND = 0.999
ADAM_EPS = 1e-08
WEIGHT_DECAY = 0.01
RATE_VECTOR = 0.3
ATTN_RATE_SCALE = 3.0
NEG_LARGE = -1e+30

def matmul_high(left, right):
    return jnp.dot(left, right, precision=lax.Precision.HIGHEST)

def layer_norm(values, gain_row, shift_row):
    center = values - lax.optimization_barrier(jnp.mean(values, axis=-1, keepdims=True))
    spread = lax.optimization_barrier(jnp.mean(center * center, axis=-1, keepdims=True))
    return center * lax.rsqrt(spread + NORM_EPS) * gain_row + shift_row

def segment_ids(lengths_row):
    ends = jnp.cumsum(lengths_row)
    slots = jnp.arange(PACK, dtype=jnp.int32)
    return lax.optimization_barrier(jnp.sum((slots[:, None] >= ends[None, :]).astype(jnp.int32), axis=1)).astype(jnp.int32)

def pack_forward(token_rows, cot_rows, seg_rows, attn_weight, ffn_weight, vectors):
    attn_low = low(attn_weight)
    ffn_low = low(ffn_weight)
    vec_low = low(vectors)
    queries = low(low_back(matmul_high(token_rows, attn_low[:, :D]) + vec_low[0]))
    key_rows = low(low_back(matmul_high(token_rows, attn_low[:, D:2 * D])))
    value_rows = low(low_back(matmul_high(token_rows, attn_low[:, 2 * D:3 * D]) + vec_low[1]))
    query_heads = queries.reshape(PACK, HEADS, HEAD)
    key_heads = key_rows.reshape(PACK, HEADS, HEAD)
    value_heads = value_rows.reshape(PACK, HEADS, HEAD)
    scores = jnp.einsum('qhd,khd->hqk', query_heads, key_heads, precision=lax.Precision.HIGHEST) * HEAD ** (-0.5)
    scores = low_back(scores)
    same_segment = seg_rows[:, None] == seg_rows[None, :]
    masked = jnp.where(same_segment[None], scores, NEG_LARGE)
    row_max = lax.optimization_barrier(jnp.max(masked, axis=-1, keepdims=True))
    exp_scores = jnp.exp(masked - row_max)
    attn_prob = low(exp_scores / lax.optimization_barrier(jnp.sum(exp_scores, axis=-1, keepdims=True)))
    mixed = jnp.einsum('hqk,khd->qhd', attn_prob, value_heads, precision=lax.Precision.HIGHEST).reshape(PACK, D)
    mixed = low(low_back(mixed))
    branch = low_back(matmul_high(mixed, attn_low[:, 3 * D:]) + vec_low[2])
    normed_one = layer_norm(token_rows + branch, vec_low[4], vec_low[5])
    hidden_pre = low_back(matmul_high(low(normed_one), ffn_low[:, :FF]) + vec_low[8:].reshape(FF))
    activ = low(jax.nn.gelu(hidden_pre, approximate=False))
    ffn_out = low_back(matmul_high(activ, ffn_low[:, FF:].T) + vec_low[3])
    output = layer_norm(normed_one + ffn_out, vec_low[6], vec_low[7])
    keep_rows = (seg_rows < NSEQ).astype(jnp.float32)[:, None]
    output = output * keep_rows
    return (jnp.sum(output * cot_rows), output)

def adamw(weight, grad_value, first, second, rate, decay):
    first_new = BETA_FIRST * first + (1.0 - BETA_FIRST) * grad_value
    second_new = BETA_SECOND * second + (1.0 - BETA_SECOND) * grad_value * grad_value
    first_hat = first_new / (1.0 - BETA_FIRST ** STEP)
    second_hat = second_new / (1.0 - BETA_SECOND ** STEP)
    weight_new = weight - rate * (first_hat / (jnp.sqrt(second_hat) + ADAM_EPS) + decay * weight)
    return (weight_new, first_new, second_new)

def reference(tokens, cotangent, dest, lengths, attn_weight, attn_first, attn_second, ffn_weight, ffn_first, ffn_second, vectors, vec_first, vec_second):
    pack_count = MB * N_FSDP
    flat_dest = dest.reshape(pack_count, PACK).astype(jnp.int32)
    inverse = jnp.argsort(flat_dest, axis=1).astype(jnp.int32)
    packed_tokens = jnp.take_along_axis(tokens.reshape(pack_count, PACK, D).astype(jnp.float32), inverse[:, :, None], axis=1)
    packed_cot = jnp.take_along_axis(cotangent.reshape(pack_count, PACK, D).astype(jnp.float32), inverse[:, :, None], axis=1)
    seg_all = jax.vmap(segment_ids)(lengths.reshape(pack_count, NSEQ))

    def total_loss(attn_value, ffn_value, vec_value, packed):

        def one_pack(running, pack_data):
            token_rows, cot_rows, seg_rows = pack_data
            loss_part, output = jax.checkpoint(pack_forward)(token_rows, cot_rows, seg_rows, attn_value, ffn_value, vec_value)
            return (running + loss_part, output)
        running, outputs = lax.scan(one_pack, jnp.zeros((), jnp.float32), (packed, packed_cot, seg_all))
        return (running, outputs)
    loss_value, pullback, outputs = jax.vjp(total_loss, attn_weight, ffn_weight, vectors, packed_tokens, has_aux=True)
    grad_attn, grad_ffn, grad_vec, grad_tokens = pullback(jnp.ones((), jnp.float32))
    layer_output = jnp.take_along_axis(outputs, flat_dest[:, :, None], axis=1).astype(jnp.bfloat16).reshape(MB, N_FSDP, PACK, D)
    input_grad = jnp.take_along_axis(grad_tokens, flat_dest[:, :, None], axis=1).astype(jnp.bfloat16).reshape(MB, N_FSDP, PACK, D)
    square_sum = jnp.sum(grad_attn * grad_attn) + jnp.sum(grad_ffn * grad_ffn) + jnp.sum(grad_vec * grad_vec)
    grad_norm = jnp.sqrt(square_sum)
    factor = jnp.minimum(1.0, CLIP_NORM / (grad_norm + 1e-06))
    rate_matrix = D ** (-0.5)
    attn_new, attn_first_new, attn_second_new = adamw(attn_weight, grad_attn * factor, attn_first, attn_second, ATTN_RATE_SCALE * rate_matrix, WEIGHT_DECAY)
    ffn_new, ffn_first_new, ffn_second_new = adamw(ffn_weight, grad_ffn * factor, ffn_first, ffn_second, rate_matrix, WEIGHT_DECAY)
    vec_new, vec_first_new, vec_second_new = adamw(vectors, grad_vec * factor, vec_first, vec_second, RATE_VECTOR, 0.0)
    output_bias_grad = grad_vec[2] * factor
    return (layer_output, input_grad, grad_norm, attn_new, attn_first_new, attn_second_new, ffn_new, ffn_first_new, ffn_second_new, vec_new, vec_first_new, vec_second_new, attn_new.astype(jnp.bfloat16), ffn_new.astype(jnp.bfloat16), output_bias_grad)
```

```python
from functools import partial
import math

import jax
import jax.numpy as jnp
from jax import lax
from jax.experimental import pallas as pl
from jax.experimental.pallas import tpu as pltpu
from jax.sharding import Mesh, PartitionSpec as P

HEADS = 16
HEAD = 64
STEP = 10
MB = 2
TOK = 128
ROWS = MB * TOK
D = 1024
FF = 4096
N_CTX = 16
N_FSDP = 8
PACK = 2048
SENT = 208

NORM_EPS = 1e-05
CLIP_NORM = 1.0
BETA_FIRST = 0.9
BETA_SECOND = 0.999
ADAM_EPS = 1e-08
WEIGHT_DECAY = 0.01
RATE_VECTOR = 0.3
ATTN_RATE_SCALE = 3.0
NEG_LARGE = -1e30
SCALE2 = HEAD ** (-0.5) * math.log2(math.e)
SCALE = HEAD ** (-0.5)
CONTRACT_ROWS = (((0,), (0,)), ((), ()))
CONTRACT_COLS = (((1,), (1,)), ((), ()))
CTX = ("yl", "z", "core")
FSDP = ("x", "yh")
ALL = ("x", "yh", "yl", "z", "core")
BLK = 256
NBLK = PACK // BLK
f32 = jnp.float32
bf16 = jnp.bfloat16


def dot(a, b):
    return jnp.dot(a, b, preferred_element_type=f32)


def dot_nt(a, b):
    return lax.dot_general(a, b, CONTRACT_COLS, preferred_element_type=f32)


def dot_tn(a, b):
    return lax.dot_general(a, b, CONTRACT_ROWS, preferred_element_type=f32)


def load_side(qkv_ref, keys, values, keys_t, values_t, seg_col):
    for s in range(N_CTX):
        at = slice(s * TOK, (s + 1) * TOK)
        key_t = qkv_ref[s, 0, HEAD : 2 * HEAD, :]
        value_t = qkv_ref[s, 0, 2 * HEAD : 3 * HEAD, :]
        keys[at, :] = key_t.T
        if values is not None:
            values[at, :] = value_t.T
        if keys_t is not None:
            keys_t[:, at] = key_t
        if values_t is not None:
            values_t[:, at] = value_t
        seg = qkv_ref[s, 0, 3 * HEAD : 3 * HEAD + 1, :].astype(f32)
        seg_col[at, :] = jnp.broadcast_to(seg, (TOK, TOK)).T


def pair(ref, j, rows):
    return jnp.concatenate([ref[2 * j, 0, rows, :], ref[2 * j + 1, 0, rows, :]], axis=1)


def attn_fwd_kernel(qkv_ref, out_ref, full_ref, lse_ref, keys, values_t, seg_col, scores):
    load_side(qkv_ref, keys, None, None, values_t, seg_col)

    def query_block(j, _):
        query_t = pair(qkv_ref, j, slice(0, HEAD))
        seg_row = pair(qkv_ref, j, slice(3 * HEAD, 3 * HEAD + 1)).astype(f32)
        top = jnp.full((1, BLK), NEG_LARGE, f32)
        for k in range(NBLK):
            at = slice(k * BLK, (k + 1) * BLK)
            s = dot(keys[at, :], query_t) * SCALE2
            col = seg_col[at, :]
            same = jnp.concatenate([col, col], axis=1) == seg_row
            s = jnp.where(same, s, NEG_LARGE)
            scores[at, :] = s
            top = jnp.maximum(top, jnp.max(s, axis=0, keepdims=True))
        total = jnp.zeros((1, BLK), f32)
        acc = jnp.zeros((HEAD, BLK), f32)
        for k in range(NBLK):
            at = slice(k * BLK, (k + 1) * BLK)
            p = jnp.exp2(scores[at, :] - top)
            total = total + jnp.sum(p, axis=0, keepdims=True)
            acc = acc + dot(values_t[:, at], p.astype(bf16))
        acc = acc / total
        out_ref[2 * j, 0] = acc[:, :TOK].astype(bf16)
        out_ref[2 * j + 1, 0] = acc[:, TOK:].astype(bf16)
        full_ref[2 * j, 0] = acc[:, :TOK]
        full_ref[2 * j + 1, 0] = acc[:, TOK:]
        lse = top + jnp.log2(total)
        lse_ref[2 * j, 0] = lse[:, :TOK]
        lse_ref[2 * j + 1, 0] = lse[:, TOK:]
        return 0

    lax.fori_loop(0, NBLK, query_block, 0)


def attn_fwd(qkv):
    spec = lambda rows: pl.BlockSpec((N_CTX, 1, rows, TOK), lambda m: (0, m, 0, 0))
    shape = lambda rows, dt: jax.ShapeDtypeStruct((N_CTX, MB, rows, TOK), dt)
    return pl.pallas_call(
        attn_fwd_kernel,
        grid=(MB,),
        in_specs=[spec(SENT)],
        out_specs=[spec(HEAD), spec(HEAD), spec(1)],
        out_shape=[shape(HEAD, bf16), shape(HEAD, f32), shape(1, f32)],
        scratch_shapes=[
            pltpu.VMEM((PACK, HEAD), bf16),
            pltpu.VMEM((HEAD, PACK), bf16),
            pltpu.VMEM((PACK, TOK), f32),
            pltpu.VMEM((PACK, BLK), f32),
        ],
        compiler_params=pltpu.CompilerParams(vmem_limit_bytes=40 * 2**20),
        cost_estimate=pl.CostEstimate(
            flops=4 * MB * PACK * PACK * HEAD, bytes_accessed=4 * 2**20, transcendentals=MB * PACK * PACK
        ),
        name="attn_fwd",
    )(qkv)


def attn_bwd_kernel(
    qkv_ref, grad_ref, full_ref, lse_ref, out_ref, keys, values, keys_t, seg_col, acc_k, acc_v
):
    load_side(qkv_ref, keys, values, keys_t, None, seg_col)
    acc_k[...] = jnp.zeros_like(acc_k)
    acc_v[...] = jnp.zeros_like(acc_v)

    def query_block(j, _):
        query_t = pair(qkv_ref, j, slice(0, HEAD))
        seg_row = pair(qkv_ref, j, slice(3 * HEAD, 3 * HEAD + 1)).astype(f32)
        grad_t = pair(grad_ref, j, slice(0, HEAD))
        lse = pair(lse_ref, j, slice(0, 1))
        delta = jnp.sum(
            grad_t.astype(f32) * pair(full_ref, j, slice(0, HEAD)), axis=0, keepdims=True
        )
        acc_q = jnp.zeros((HEAD, BLK), f32)
        for k in range(NBLK):
            at = slice(k * BLK, (k + 1) * BLK)
            s = dot(keys[at, :], query_t) * SCALE2 - lse
            col = seg_col[at, :]
            same = jnp.concatenate([col, col], axis=1) == seg_row
            p = jnp.exp2(jnp.where(same, s, NEG_LARGE))
            dp = dot(values[at, :], grad_t)
            ds = (p * (dp - delta)).astype(bf16)
            acc_q = acc_q + dot(keys_t[:, at], ds)
            acc_k[:, at] += dot_nt(query_t, ds)
            acc_v[:, at] += dot_nt(grad_t, p.astype(bf16))
        acc_q = (acc_q * SCALE).astype(bf16)
        out_ref[2 * j, 0, :HEAD, :] = acc_q[:, :TOK]
        out_ref[2 * j + 1, 0, :HEAD, :] = acc_q[:, TOK:]
        return 0

    lax.fori_loop(0, NBLK, query_block, 0)
    for s in range(N_CTX):
        at = slice(s * TOK, (s + 1) * TOK)
        out_ref[s, 0, HEAD : 2 * HEAD, :] = (acc_k[:, at] * SCALE).astype(bf16)
        out_ref[s, 0, 2 * HEAD :, :] = acc_v[:, at].astype(bf16)


def attn_bwd(qkv, grad, full, lse):
    spec = lambda rows: pl.BlockSpec((N_CTX, 1, rows, TOK), lambda m: (0, m, 0, 0))
    return pl.pallas_call(
        attn_bwd_kernel,
        grid=(MB,),
        in_specs=[spec(SENT), spec(HEAD), spec(HEAD), spec(1)],
        out_specs=spec(3 * HEAD),
        out_shape=jax.ShapeDtypeStruct((N_CTX, MB, 3 * HEAD, TOK), bf16),
        scratch_shapes=[
            pltpu.VMEM((PACK, HEAD), bf16),
            pltpu.VMEM((PACK, HEAD), bf16),
            pltpu.VMEM((HEAD, PACK), bf16),
            pltpu.VMEM((PACK, TOK), f32),
            pltpu.VMEM((HEAD, PACK), f32),
            pltpu.VMEM((HEAD, PACK), f32),
        ],
        compiler_params=pltpu.CompilerParams(vmem_limit_bytes=40 * 2**20),
        cost_estimate=pl.CostEstimate(
            flops=10 * MB * PACK * PACK * HEAD, bytes_accessed=8 * 2**20, transcendentals=MB * PACK * PACK
        ),
        name="attn_bwd",
    )(qkv, grad, full, lse)


MESH_ID = pl.DeviceIdType.MESH
COLS = 512
N_BLK = 4
VEC_AT = 2048
PART_COLS = (2048 + 128, 2048, 2048)
ORDERS = (("x", "z", "y"), ("z", "y", "x"), ("y", "x", "z"))
BLOCKS = tuple(
    tuple((b * COLS, COLS) for b in range(N_BLK)) + (((VEC_AT, 128),) if p == 0 else ()) for p in range(3)
)
HALF_Z = 3072


def coordinate(axis):
    if axis == "y":
        return lax.axis_index("yh") * 2 + lax.axis_index("yl")
    return lax.axis_index(axis)


def peer(axis, step):
    at = lax.rem(coordinate(axis) + step, 4)
    if axis == "y":
        return {"yh": at // 2, "yl": lax.rem(at, 2)}, at
    return {axis: at}, at


def pick(ref, axis, at, dims, cols):
    index = []
    for d in dims:
        if d == axis:
            index.append(at)
        elif axis == "y" and d == "yh":
            index.append(at // 2)
        elif axis == "y" and d == "yl":
            index.append(lax.rem(at, 2))
        else:
            index.append(slice(None))
    return ref.at[(*index, slice(None), cols)]


def dims_after(order, n):
    dims = ["x", "yh", "yl", "z"]
    for axis in order[:n]:
        for d in ("yh", "yl") if axis == "y" else (axis,):
            dims.remove(d)
    return dims


SIZES = {"x": 4, "yh": 2, "yl": 2, "z": 4}


def lead(order, n):
    return tuple(SIZES[d] for d in dims_after(order, n))


def send(src, dst, sems, index, to):
    return pltpu.make_async_remote_copy(
        src_ref=src, dst_ref=dst, send_sem=sems[0].at[index], recv_sem=sems[1].at[index],
        device_id=to, device_id_type=MESH_ID,
    )


def greet():
    barrier = pltpu.get_barrier_semaphore()
    others = [peer(axis, step)[0] for axis in ("x", "y", "z") for step in (1, 2, 3)]
    others.append({"core": 1 - lax.axis_index("core")})
    for other in others:
        pl.semaphore_signal(barrier, inc=1, device_id=other, device_id_type=MESH_ID)
    pl.semaphore_wait(barrier, len(others))


def grads_kernel(
    left_x, left_o, left_h, left_f, right_q, right_o, right_u, right_g, vec,
    out_attn, out_ffn, out_vec, out_sq,
    peer_left, peer_right, peer_vec,
    w_0, w_1, w_2, s1_0, s1_1, s1_2, s2_0, s2_1, s2_2,
    r1_0, r1_1, r1_2, r2_0, r2_1, r2_2, r3_0, r3_1, r3_2,
    gathered, sq_z, sq_y, sq_x, sq_c,
    swap_send, swap_recv, ring_send, ring_recv, gather_send, gather_recv, sq_send, sq_recv, out_sem,
):
    core = lax.axis_index("core")
    other = 1 - core
    place = lax.axis_index("yl") * 4 + lax.axis_index("z")
    lefts = (left_x, left_o, left_h, left_f)
    rights = (right_q, right_o, right_u, right_g)
    widths = (1536, 512, 2048, 2048)
    offsets = (0, 1536, 2048, 4096)
    works, firsts, seconds = (w_0, w_1, w_2), (s1_0, s1_1, s1_2), (s2_0, s2_1, s2_2)
    recvs = ((r1_0, r1_1, r1_2), (r2_0, r2_1, r2_2), (r3_0, r3_1, r3_2))
    greet()

    to_core = {"core": other}
    swaps = []
    for i in range(4):
        swaps.append(send(lefts[i], peer_left.at[i], (swap_send, swap_recv), 2 * i, to_core))
        from_cols = pl.ds(pl.multiple_of(other * widths[i], 512), widths[i])
        swaps.append(
            send(
                rights[i].at[:, from_cols], peer_right.at[:, offsets[i] : offsets[i] + widths[i]],
                (swap_send, swap_recv), 2 * i + 1, to_core,
            )
        )
    swaps.append(send(vec, peer_vec, (swap_send, swap_recv), 8, to_core))
    for copy in swaps:
        copy.start()
    for copy in swaps:
        copy.wait()

    def product_of(p, b):
        if p == 0:
            return (0, b * COLS) if b < 3 else (1, 0)
        return (p + 1, b * COLS)

    def copies(p, phase, b):
        order = ORDERS[p]
        axis = order[phase]
        at, width = BLOCKS[p][b]
        cols = slice(at, at + width)
        src = (works, firsts, seconds)[phase][p]
        out = []
        for step in (1, 2, 3):
            to, index = peer(axis, step)
            chunk = pick(src, axis, index, dims_after(order, phase), cols)
            land = recvs[phase][p].at[(step - 1, *(slice(None),) * (len(lead(order, phase + 1)) + 1), cols)]
            out.append(send(chunk, land, (ring_send, ring_recv), ((p * 3 + phase) * 5 + b) * 3 + step - 1, to))
        return out

    for b in range(5):
        for p in range(3):
            if b >= len(BLOCKS[p]):
                continue
            at, width = BLOCKS[p][b]
            work = works[p]
            if b == 4:
                work[:, :, :, :, :, VEC_AT:] = (vec[...].astype(f32) + peer_vec[...].astype(f32)).astype(bf16)
            else:
                i, col = product_of(p, b)
                mine = pl.ds(pl.multiple_of(core * widths[i] + col, 512), COLS)
                theirs = slice(offsets[i] + col, offsets[i] + col + COLS)

                def rows_block(x, _, i=i, mine=mine, theirs=theirs, work=work, at=at):
                    rows = pl.ds(pl.multiple_of(x * 256, 256), 256)
                    value = dot(lefts[i][rows, :], rights[i][:, mine])
                    value = value + dot(peer_left[i, rows, :], peer_right[:, theirs])
                    work[x, :, :, :, :, at : at + COLS] = value.astype(bf16).reshape(2, 2, 4, 16, COLS)
                    return 0

                lax.fori_loop(0, 4, rows_block, 0)
            for copy in copies(p, 0, b):
                copy.start()

    squares = jnp.zeros((8, 128), f32)
    for phase in range(3):
        for b in range(5):
            for p in range(3):
                if b >= len(BLOCKS[p]):
                    continue
                at, width = BLOCKS[p][b]
                cols = slice(at, at + width)
                order = ORDERS[p]
                axis = order[phase]
                src = (works, firsts, seconds)[phase][p]
                land = recvs[phase][p]
                for copy in copies(p, phase, b):
                    copy.wait()
                own = pick(src, axis, coordinate(axis), dims_after(order, phase), cols)
                rest = len(lead(order, phase + 1)) - 1
                if phase < 2:
                    dst = (firsts, seconds)[phase][p]

                    def add(n, _, own=own, land=land, dst=dst, rest=rest, cols=cols):
                        tail = (*(slice(None),) * (rest + 1), cols)
                        inner = (*(slice(None),) * (rest + 1), slice(None))
                        value = own[(n, *inner)].astype(f32)
                        for step in range(3):
                            value = value + land[(step, n, *tail)].astype(f32)
                        dst[(n, *tail)] = value.astype(bf16)
                        return 0

                    lax.fori_loop(0, lead(order, phase + 1)[0], add, 0)
                    for copy in copies(p, phase + 1, b):
                        copy.start()
                else:
                    value = own[...].astype(f32)
                    for step in range(3):
                        value = value + land[step, :, cols].astype(f32)
                    to = p * 2048 + at if width == COLS else 6144
                    gathered[core, place, :, to : to + width] = value.astype(bf16)
                    square = value * value
                    if width != COLS:
                        square = square * jnp.where(core == 0, 1.0, 0.0)
                    for c in range(0, width, 128):
                        squares = squares + square[:8, c : c + 128] + square[8:, c : c + 128]

    yl, z = lax.axis_index("yl"), lax.axis_index("z")
    z_first, y_first = slice(0, HALF_Z), slice(HALF_Z, 6272)
    to_y = {"yl": 1 - yl}
    gather_sems = (gather_send, gather_recv)
    sq_sems = (sq_send, sq_recv)

    def spread(buffer, axis, base):
        at = coordinate(axis)
        out = []
        for step in (1, 2, 3):
            out.append(send(buffer.at[at], buffer.at[at], sq_sems, base + step - 1, peer(axis, step)[0]))
        return out

    def total(buffer):
        return (buffer[0] + buffer[1]) + (buffer[2] + buffer[3])

    sq_z[z] = squares
    squares_z = spread(sq_z, "z", 0)
    first_z = [
        send(gathered.at[core, place, :, z_first], gathered.at[core, place, :, z_first], gather_sems, step - 1, peer("z", step)[0])
        for step in (1, 2, 3)
    ]
    first_y = send(gathered.at[core, place, :, y_first], gathered.at[core, place, :, y_first], gather_sems, 3, to_y)
    for copy in (*squares_z, *first_z, first_y):
        copy.start()
    for copy in squares_z:
        copy.wait()
    y_at = coordinate("y")
    sq_y[y_at] = total(sq_z)
    squares_y = spread(sq_y, "y", 3)
    for copy in squares_y:
        copy.start()
    for copy in (*first_z, first_y):
        copy.wait()
    quarter = pl.ds(yl * 4, 4)
    second_y = send(
        gathered.at[core, quarter, :, z_first], gathered.at[core, quarter, :, z_first], gather_sems, 4, to_y
    )
    second_y.start()
    second_z = []
    for step in (1, 2, 3):
        for half in range(2):
            view = gathered.at[core, half * 4 + z, :, y_first]
            second_z.append(send(view, view, gather_sems, 5 + (step - 1) * 2 + half, peer("z", step)[0]))
    for copy in second_z:
        copy.start()
    for copy in squares_y:
        copy.wait()
    x_at = coordinate("x")
    sq_x[x_at] = total(sq_y)
    squares_x = spread(sq_x, "x", 6)
    for copy in squares_x:
        copy.start()
    for copy in squares_x:
        copy.wait()
    sq_c[core] = total(sq_x)
    square_c = send(sq_c.at[core], sq_c.at[core], sq_sems, 9, to_core)
    square_c.start()
    square_c.wait()
    out_sq[...] = sq_c[0] + sq_c[1]
    second_y.wait()
    for copy in second_z:
        copy.wait()
    last = send(gathered.at[core], gathered.at[core], gather_sems, 11, to_core)
    last.start()
    last.wait()
    locals_ = []
    n = 0
    for c in range(2):
        for i in range(4):
            target, base = ((out_attn, c * 1536), (out_attn, 3072 + c * 512), (out_ffn, c * 2048), (out_ffn, 4096 + c * 2048))[i]
            locals_.append(
                pltpu.make_async_copy(
                    gathered.at[c, :, :, offsets[i] : offsets[i] + widths[i]],
                    target.at[:, :, base : base + widths[i]], out_sem.at[n],
                )
            )
            n += 1
    locals_.append(pltpu.make_async_copy(gathered.at[0, :, :, 6144:], out_vec, out_sem.at[n]))
    for copy in locals_:
        copy.start()
    for copy in locals_:
        copy.wait()


def grads(lefts, rights, vec):
    scratch = [
        pltpu.VMEM((4, D, ROWS), bf16),
        pltpu.VMEM((ROWS, 6144), bf16),
        pltpu.VMEM((4, 2, 2, 4, 16, 128), bf16),
    ]
    for n in range(3):
        scratch += [pltpu.VMEM((*lead(ORDERS[p], n), 16, PART_COLS[p]), bf16) for p in range(3)]
    for n in range(1, 4):
        scratch += [pltpu.VMEM((3, *lead(ORDERS[p], n), 16, PART_COLS[p]), bf16) for p in range(3)]
    scratch += [
        pltpu.VMEM((2, 8, 16, 6272), bf16),
        pltpu.VMEM((4, 8, 128), f32),
        pltpu.VMEM((4, 8, 128), f32),
        pltpu.VMEM((4, 8, 128), f32),
        pltpu.VMEM((2, 8, 128), f32),
    ]
    for count in (9, 9, 135, 135, 12, 12, 10, 10, 9):
        scratch.append(pltpu.SemaphoreType.DMA((count,)))
    vmem = pl.BlockSpec(memory_space=pltpu.VMEM)
    hbm = pl.BlockSpec(memory_space=pl.ANY)
    out = pl.pallas_call(
        grads_kernel,
        in_specs=[vmem] * 9,
        out_specs=[hbm, hbm, hbm, vmem],
        out_shape=[
            jax.ShapeDtypeStruct((8, 16, 4 * D), bf16),
            jax.ShapeDtypeStruct((8, 16, 2 * FF), bf16),
            jax.ShapeDtypeStruct((8, 16, 128), bf16),
            jax.ShapeDtypeStruct((8, 128), f32),
        ],
        scratch_shapes=scratch,
        compiler_params=pltpu.CompilerParams(
            collective_id=1, has_side_effects=True, vmem_limit_bytes=60 * 2**20
        ),
        cost_estimate=pl.CostEstimate(flops=2 * 512 * D * 6144, bytes_accessed=16 * 2**20, transcendentals=0),
        name="grads",
    )(*lefts, *rights, vec)
    return out[0].reshape(TOK, 4 * D), out[1].reshape(TOK, 2 * FF), out[2][0, :12], jnp.sum(out[3])


def layer_stats(values, gain_row, shift_row):
    center = values - jnp.mean(values, axis=-1, keepdims=True)
    inverse = lax.rsqrt(jnp.mean(center * center, axis=-1, keepdims=True) + NORM_EPS)
    normal = center * inverse
    return (normal * gain_row + shift_row, normal, inverse)


def layer_back(grad_value, normal, inverse, gain_row):
    scaled = grad_value * gain_row
    return inverse * (
        scaled
        - jnp.mean(scaled, axis=-1, keepdims=True)
        - normal * jnp.mean(scaled * normal, axis=-1, keepdims=True)
    )


def column_sum(values):
    return jnp.sum(values.astype(f32), axis=0)


def adamw(weight, grad_value, first, second, rate, decay):
    first_new = BETA_FIRST * first + (1.0 - BETA_FIRST) * grad_value
    second_new = BETA_SECOND * second + (1.0 - BETA_SECOND) * grad_value * grad_value
    first_hat = first_new / (1.0 - BETA_FIRST**STEP)
    second_hat = second_new / (1.0 - BETA_SECOND**STEP)
    weight_new = weight - rate * (first_hat / (jnp.sqrt(second_hat) + ADAM_EPS) + decay * weight)
    return (weight_new, first_new, second_new)


def to_heads(rows, parts):
    t = rows.T.reshape(parts, HEADS, HEAD, MB, TOK)
    return jnp.transpose(t, (1, 3, 0, 2, 4)).reshape(HEADS, MB, parts * HEAD, TOK)


def from_heads(blocks, parts):
    t = blocks.reshape(HEADS, MB, parts, HEAD, TOK)
    return jnp.transpose(t, (1, 4, 2, 0, 3)).reshape(ROWS, parts * D)


def swap(value):
    return lax.all_to_all(value, CTX, 0, 0, tiled=True)


def shards(
    tokens, cotangent, dest, lengths, attn_weight, attn_first, attn_second,
    ffn_weight, ffn_first, ffn_second, vectors, vec_first, vec_second,
):
    place = lax.axis_index(CTX)
    own_rows = D // N_FSDP // N_CTX
    both = jnp.concatenate(
        [
            lax.dynamic_slice_in_dim(attn_weight, place * own_rows, own_rows).astype(bf16),
            lax.dynamic_slice_in_dim(ffn_weight, place * own_rows, own_rows).astype(bf16),
            jnp.pad(vectors.reshape(8, 192).astype(bf16), ((0, 0), (0, 64))),
        ],
        axis=1,
    )
    full = lax.all_gather(both, ALL, axis=0, tiled=True)
    w_qkv = full[:, : 3 * D]
    w_out = full[:, 3 * D : 4 * D]
    w_one = full[:, 4 * D : 4 * D + FF]
    w_two = full[:, 4 * D + FF : 4 * D + 2 * FF]
    small = full[:, 4 * D + 2 * FF : 4 * D + 2 * FF + 192].reshape(N_FSDP, N_CTX, 8, 192)[:, 0]
    small = jnp.transpose(small.reshape(N_FSDP, 12, TOK), (1, 0, 2)).reshape(12, D).astype(f32)

    x = tokens.reshape(ROWS, D)
    cot = cotangent.reshape(ROWS, D).astype(f32)
    ends = jnp.cumsum(lengths[:, 0], axis=1)
    seg = jnp.sum((dest[:, 0, :, None] >= ends[:, None, :]).astype(jnp.int32), axis=2)
    keep = (seg.reshape(ROWS, 1) < 8).astype(f32)

    bias = jnp.concatenate([small[0], jnp.zeros((D,), f32), small[1]])
    qkv = (dot(x, w_qkv) + bias).astype(bf16)
    seg_rows = jnp.broadcast_to(seg.astype(bf16)[None, :, None, :], (HEADS, MB, 16, TOK))
    held = swap(jnp.concatenate([to_heads(qkv, 3), seg_rows], axis=2))
    mixed_t, mixed_full, lse = attn_fwd(held)
    mixed = from_heads(swap(mixed_t), 1)

    branch = dot(mixed, w_out) + small[2]
    normed_one, normal_one, inverse_one = layer_stats(x.astype(f32) + branch, small[4], small[5])
    normed_low = normed_one.astype(bf16)
    hidden_pre = dot(normed_low, w_one) + small[8:].reshape(FF)
    activ, gelu_back = jax.vjp(partial(jax.nn.gelu, approximate=False), hidden_pre)
    activ_low = activ.astype(bf16)
    ffn_out = dot_nt(activ_low, w_two) + small[3]
    output, normal_two, inverse_two = layer_stats(normed_one + ffn_out, small[6], small[7])
    output = output * keep
    grad_out = cot * keep
    grad_two = layer_back(grad_out, normal_two, inverse_two, small[6])
    ffn_grad_low = grad_two.astype(bf16)
    grad_hidden = gelu_back(dot(ffn_grad_low, w_two))[0].astype(bf16)
    grad_normed = dot_nt(grad_hidden, w_one) + grad_two
    grad_one = layer_back(grad_normed, normal_one, inverse_one, small[4])
    branch_grad_low = grad_one.astype(bf16)
    grad_mixed = dot_nt(branch_grad_low, w_out).astype(bf16)

    grad_held = attn_bwd(held, swap(to_heads(grad_mixed, 1)), mixed_full, lse)
    grad_qkv = from_heads(swap(grad_held), 3)
    grad_tokens = grad_one + dot_nt(grad_qkv, w_qkv)

    step_vec = jnp.concatenate(
        [
            jnp.stack(
                [
                    column_sum(grad_qkv[:, :D]),
                    column_sum(grad_qkv[:, 2 * D :]),
                    column_sum(branch_grad_low),
                    column_sum(ffn_grad_low),
                    jnp.sum(grad_normed * normal_one, axis=0),
                    jnp.sum(grad_normed, axis=0),
                    jnp.sum(grad_out * normal_two, axis=0),
                    jnp.sum(grad_out, axis=0),
                ]
            ),
            column_sum(grad_hidden).reshape(4, D),
        ],
        axis=0,
    )
    vec_rows = jnp.transpose(step_vec.reshape(12, N_FSDP, TOK), (1, 0, 2)).astype(bf16)
    vec_rows = jnp.pad(vec_rows.reshape(N_FSDP, 1, 12, TOK), ((0, 0), (0, 7), (0, 4), (0, 0)))
    total_attn, total_ffn, total_vec, square_sum = grads(
        (x.T, mixed.T, normed_low.T, ffn_grad_low.T),
        (grad_qkv, branch_grad_low, grad_hidden, activ_low),
        vec_rows.reshape(4, 2, 2, 4, 16, TOK),
    )
    total_attn, total_ffn, total_vec = total_attn.astype(f32), total_ffn.astype(f32), total_vec.astype(f32)
    grad_norm = jnp.sqrt(square_sum)
    factor = jnp.minimum(1.0, CLIP_NORM / (grad_norm + 1e-06))
    rate_matrix = D ** (-0.5)
    attn_new, attn_first_new, attn_second_new = adamw(
        attn_weight, total_attn * factor, attn_first, attn_second, ATTN_RATE_SCALE * rate_matrix, WEIGHT_DECAY
    )
    ffn_new, ffn_first_new, ffn_second_new = adamw(
        ffn_weight, total_ffn * factor, ffn_first, ffn_second, rate_matrix, WEIGHT_DECAY
    )
    vec_new, vec_first_new, vec_second_new = adamw(
        vectors, total_vec * factor, vec_first, vec_second, RATE_VECTOR, 0.0
    )
    return (
        output.astype(bf16).reshape(tokens.shape),
        grad_tokens.astype(bf16).reshape(tokens.shape),
        grad_norm,
        attn_new, attn_first_new, attn_second_new,
        ffn_new, ffn_first_new, ffn_second_new,
        vec_new, vec_first_new, vec_second_new,
        attn_new.astype(bf16),
        ffn_new.astype(bf16),
        total_vec[2] * factor,
    )


def solution(mesh):
    fine = Mesh(mesh.devices.reshape(2, 4, 2, 4, 2), ("yl", "z", "core", "x", "yh"))
    act = P(None, FSDP, CTX, None)
    row = P(FSDP, None)
    col = P(None, FSDP)
    return jax.shard_map(
        shards,
        mesh=fine,
        in_specs=(act, act, P(None, FSDP, CTX), P(None, FSDP, None), row, row, row, row, row, row, col, col, col),
        out_specs=(act, act, P(), row, row, row, row, row, row, col, col, col, row, row, P(FSDP)),
        check_vma=False,
    )
```

```python
from functools import partial
import math

import jax
import jax.numpy as jnp
from jax import lax
from jax.experimental import pallas as pl
from jax.experimental.pallas import tpu as pltpu
from jax.sharding import Mesh, PartitionSpec as P

HEADS = 16
HEAD = 64
STEP = 10
MB = 2
TOK = 128
ROWS = MB * TOK
D = 1024
FF = 4096
N_CTX = 16
N_FSDP = 8
PACK = 2048
SENT = 208

NORM_EPS = 1e-05
CLIP_NORM = 1.0
BETA_FIRST = 0.9
BETA_SECOND = 0.999
ADAM_EPS = 1e-08
WEIGHT_DECAY = 0.01
RATE_VECTOR = 0.3
ATTN_RATE_SCALE = 3.0
NEG_LARGE = -1e30
SCALE2 = HEAD ** (-0.5) * math.log2(math.e)
SCALE = HEAD ** (-0.5)
CONTRACT_ROWS = (((0,), (0,)), ((), ()))
CONTRACT_COLS = (((1,), (1,)), ((), ()))
CTX = ("yl", "z", "core")
FSDP = ("x", "yh")
ALL = ("x", "yh", "yl", "z", "core")
BLK = 256
NBLK = PACK // BLK
N_GROUPS = 3
STEPS = (1, 3, 6, 9, 12)
f32 = jnp.float32
bf16 = jnp.bfloat16


def dot(a, b):
    return jnp.dot(a, b, preferred_element_type=f32)


def dot_nt(a, b):
    return lax.dot_general(a, b, CONTRACT_COLS, preferred_element_type=f32)


def dot_tn(a, b):
    return lax.dot_general(a, b, CONTRACT_ROWS, preferred_element_type=f32)


MESH_ID = pl.DeviceIdType.MESH
COLS = 512
N_BLK = 4
ORDERS = (("x", "z", "y"), ("z", "y", "x"), ("y", "x", "z"))
EARLY = ((2, 0), (2, 512), (2, 1024), (2, 1536), (3, 0), (3, 512), (3, 1024), (3, 1536), (1, 0))
PRODUCT = tuple(
    tuple(EARLY[b * 3 + p] for b in range(3)) + ((0, p * COLS),) for p in range(3)
)
VEC_AT = 2048
PART_COLS = (2048 + 128, 2048, 2048)
WIDTHS = (1536, 512, 2048, 2048)
OFFSETS = (0, 1536, 2048, 4096)
HALF_Z = 3072
TASKS = {}
for _n, _at in enumerate((1, 2, 4, 5, 7, 8, 10, 11, 13)):
    TASKS.setdefault(_at, []).append((0, _n // 3, _n % 3))
for _n, _at in enumerate((6, 7, 9, 10, 12, 13, 15)):
    TASKS.setdefault(_at, []).append((1, _n // 3, _n % 3))


def coordinate(axis):
    if axis == "y":
        return lax.axis_index("yh") * 2 + lax.axis_index("yl")
    return lax.axis_index(axis)


def peer(axis, step):
    at = lax.rem(coordinate(axis) + step, 4)
    if axis == "y":
        return {"yh": at // 2, "yl": lax.rem(at, 2)}, at
    return {axis: at}, at


def pick(ref, axis, at, dims, cols):
    index = []
    for d in dims:
        if d == axis:
            index.append(at)
        elif axis == "y" and d == "yh":
            index.append(at // 2)
        elif axis == "y" and d == "yl":
            index.append(lax.rem(at, 2))
        else:
            index.append(slice(None))
    return ref.at[(*index, slice(None), cols)]


def dims_after(order, n):
    dims = ["x", "yh", "yl", "z"]
    for axis in order[:n]:
        for d in ("yh", "yl") if axis == "y" else (axis,):
            dims.remove(d)
    return dims


SIZES = {"x": 4, "yh": 2, "yl": 2, "z": 4}


def lead(order, n):
    return tuple(SIZES[d] for d in dims_after(order, n))


def send(src, dst, sems, index, to):
    return pltpu.make_async_remote_copy(
        src_ref=src, dst_ref=dst, send_sem=sems[0].at[index], recv_sem=sems[1].at[index],
        device_id=to, device_id_type=MESH_ID,
    )


def load_side(qkv_ref, m, keys, values, keys_t, values_t, seg_col):
    for s in range(N_CTX):
        at = slice(s * TOK, (s + 1) * TOK)
        key_t = qkv_ref[s, m, HEAD : 2 * HEAD, :]
        value_t = qkv_ref[s, m, 2 * HEAD : 3 * HEAD, :]
        keys[at, :] = key_t.T
        if values is not None:
            values[at, :] = value_t.T
        if keys_t is not None:
            keys_t[:, at] = key_t
        if values_t is not None:
            values_t[:, at] = value_t
        seg = qkv_ref[s, m, 3 * HEAD : 3 * HEAD + 1, :].astype(f32)
        seg_col[at, :] = jnp.broadcast_to(seg, (TOK, TOK)).T


def pair(ref, m, j, rows):
    return jnp.concatenate([ref[2 * j, m, rows, :], ref[2 * j + 1, m, rows, :]], axis=1)


def query_forward(held, m, j, out, full, lse_out, keys, values_t, seg_col, scores):
    query_t = pair(held, m, j, slice(0, HEAD))
    seg_row = pair(held, m, j, slice(3 * HEAD, 3 * HEAD + 1)).astype(f32)
    top = jnp.full((1, BLK), NEG_LARGE, f32)
    for k in range(NBLK):
        at = slice(k * BLK, (k + 1) * BLK)
        s = dot(keys[at, :], query_t) * SCALE2
        col = seg_col[at, :]
        same = jnp.concatenate([col, col], axis=1) == seg_row
        s = jnp.where(same, s, NEG_LARGE)
        scores[at, :] = s
        top = jnp.maximum(top, jnp.max(s, axis=0, keepdims=True))
    total = jnp.zeros((1, BLK), f32)
    acc = jnp.zeros((HEAD, BLK), f32)
    for k in range(NBLK):
        at = slice(k * BLK, (k + 1) * BLK)
        p = jnp.exp2(scores[at, :] - top)
        total = total + jnp.sum(p, axis=0, keepdims=True)
        acc = acc + dot(values_t[:, at], p.astype(bf16))
    acc = acc / total
    lse = top + jnp.log2(total)
    for half in range(2):
        cols = slice(half * TOK, (half + 1) * TOK)
        out[2 * j + half, m] = acc[:, cols].astype(bf16)
        full[2 * j + half, m] = acc[:, cols]
        lse_out[2 * j + half, m] = lse[:, cols]


X_COLS, Y_COLS, Z_COLS = slice(0, 512), slice(512, 1152), slice(1152, 2048)
GROUP = 2048
N_COPY = 31


def ctx_device(t):
    return {"yl": t // 8, "z": lax.rem(t // 2, 4), "core": lax.rem(t, 2)}


def rows_at(start, size):
    return pl.ds(pl.multiple_of(start, 16), size)


class Gather:
    def __init__(self, g, shard, dest, sems, base, local_sem):
        core = lax.axis_index("core")
        x, z = lax.axis_index("x"), lax.axis_index("z")
        yh, yl = lax.axis_index("yh"), lax.axis_index("yl")
        y = yh * 2 + yl
        every = slice(None)
        zq, half = rows_at(z * 32, 32), rows_at(yl * 64, 64)
        cross = {"yh": 1 - yh, "yl": 1 - yl}
        count = [0]

        def make(src, dst, to):
            copy = send(src, dst, sems, base + count[0], to)
            count[0] += 1
            return copy

        def own(rows, cols, to):
            return make(shard.at[g, rows, cols], dest(core, x, yh, rows, cols), to)

        def pass_on(xs, yhs, rows, cols, to):
            view = dest(core, xs, yhs, rows, cols)
            return make(view, view, to)

        x_to = {step: peer("x", step)[0] for step in (1, 2, 3)}
        y_to = {step: peer("y", step)[0] for step in (1, 3)}
        z_to = {step: peer("z", step)[0] for step in (1, 3)}
        self.x1 = own(every, X_COLS, cross)
        self.x2 = [own(every, X_COLS, x_to[s]) for s in (1, 3)]
        self.z1 = own(zq, Z_COLS, cross)
        self.z2 = [own(zq, Z_COLS, x_to[s]) for s in (1, 3, 2)]
        self.y1 = [own(half, Y_COLS, x_to[s]) for s in (1, 3, 2)]
        self.x3 = [pass_on(x, 1 - yh, every, X_COLS, x_to[s]) for s in (1, 3)]
        self.z3 = [pass_on(x, 1 - yh, zq, Z_COLS, x_to[s]) for s in (1, 3, 2)]
        self.y2 = [pass_on(every, yh, half, Y_COLS, y_to[s]) for s in (1, 3)]
        self.z4 = [pass_on(every, every, zq, Z_COLS, z_to[s]) for s in (1, 3)]
        before, after = lax.rem(x + 3, 4), lax.rem(x + 1, 4)
        self.x4 = [
            pass_on(before, yh, slice(0, 64), X_COLS, x_to[1]),
            pass_on(after, yh, slice(64, 128), X_COLS, x_to[3]),
        ]
        self.x5 = [
            pass_on(before, 1 - yh, slice(0, 64), X_COLS, x_to[1]),
            pass_on(after, 1 - yh, slice(64, 128), X_COLS, x_to[3]),
        ]
        before, after = lax.rem(y + 3, 4), lax.rem(y + 1, 4)
        self.y3 = [
            pass_on(every, before // 2, rows_at(lax.rem(before, 2) * 64, 32), Y_COLS, y_to[1]),
            pass_on(every, after // 2, rows_at(lax.rem(after, 2) * 64 + 32, 32), Y_COLS, y_to[3]),
        ]
        before, after = lax.rem(z + 3, 4), lax.rem(z + 1, 4)
        self.z5 = [
            pass_on(every, every, rows_at(before * 32, 16), Z_COLS, z_to[1]),
            pass_on(every, every, rows_at(after * 32 + 16, 16), Z_COLS, z_to[3]),
        ]
        self.swap = [
            pass_on(every, every, every, cols, {"core": 1 - core}) for cols in (X_COLS, Y_COLS, Z_COLS)
        ]
        self.place = [
            pltpu.make_async_copy(shard.at[g, rows, cols], dest(core, x, yh, rows, cols), local_sem.at[3 * g + n])
            for n, (rows, cols) in enumerate(((every, X_COLS), (half, Y_COLS), (zq, Z_COLS)))
        ]

    def start(self, copies):
        for copy in copies:
            copy.start()

    def arrive(self, copies):
        for copy in copies:
            copy.wait_recv()

    def stage(self, n):
        if n == 0:
            self.start([self.z1, self.x1, *self.z2, *self.y1, *self.x2, *self.place])
        elif n == 1:
            self.arrive([self.z1])
            self.start(self.z3)
            self.arrive([self.x1])
            self.start(self.x3)
            for copy in self.place:
                copy.wait()
        elif n == 2:
            self.arrive(self.y1)
            self.start(self.y2)
            self.arrive([*self.z2, *self.z3])
            self.start(self.z4)
        elif n == 3:
            self.arrive(self.x2)
            self.start(self.x4)
            self.arrive(self.y2)
            self.start(self.y3)
        elif n == 4:
            self.arrive(self.x3)
            self.start(self.x5)
            self.arrive(self.z4)
            self.start(self.z5)
        elif n == 5:
            self.arrive([*self.x4, *self.x5])
            self.start(self.swap[:1])
            self.arrive(self.y3)
            self.start(self.swap[1:2])
            self.arrive(self.z5)
            self.start(self.swap[2:])
        else:
            self.arrive(self.swap)
            for copy in (
                self.x1, self.z1, *self.x2, *self.z2, *self.y1, *self.x3, *self.z3, *self.y2, *self.z4,
                *self.x4, *self.x5, *self.y3, *self.z5, *self.swap,
            ):
                copy.wait_send()


def greet_all():
    barrier = pltpu.get_barrier_semaphore()
    place = lax.axis_index(CTX)
    others = [ctx_device(lax.rem(place + d, N_CTX)) for d in range(1, N_CTX)]
    others += [peer(axis, step)[0] for axis in ("x", "y") for step in (1, 2, 3)]
    for other in others:
        pl.semaphore_signal(barrier, inc=1, device_id=other, device_id_type=MESH_ID)
    pl.semaphore_wait(barrier, len(others))


def front_kernel(
    shard, vec_shard, x_ref, seg_ref,
    out_attn, out_ffn, out_vec, out_held, out_mixed, out_full, out_lse,
    wa, vecs, ready, held, mixed, out_t, keys, values_t, seg_col, scores,
    ag_send, ag_recv, vec_send, vec_recv, q_send, q_recv, o_send, o_recv, local_sem, out_sem,
):
    core = lax.axis_index("core")
    place = lax.axis_index(CTX)
    x, yh, yl = lax.axis_index("x"), lax.axis_index("yh"), lax.axis_index("yl")

    def dest(g):
        def view(c, xs, yhs, rows, cols):
            if g == 0:
                return wa.at[c, xs, yhs, rows, cols]
            start = (g - 1) * FF + c * GROUP + cols.start
            return out_ffn.at[xs, yhs, rows, pl.ds(pl.multiple_of(start, 128), cols.stop - cols.start)]

        return view

    gathers = [
        Gather(g, shard, dest(g), (ag_send, ag_recv), g * N_COPY, local_sem) for g in range(N_GROUPS)
    ]
    vec_sems = (vec_send, vec_recv)
    vec_cross = send(vec_shard, vecs.at[x, yh], vec_sems, 0, {"yh": 1 - yh, "yl": 1 - yl})
    vec_x = [send(vec_shard, vecs.at[x, yh], vec_sems, s, peer("x", s)[0]) for s in (1, 2, 3)]
    vec_x2 = [
        send(vecs.at[x, 1 - yh], vecs.at[x, 1 - yh], vec_sems, 3 + s, peer("x", s)[0]) for s in (1, 2, 3)
    ]
    greet_all()
    for copy in (vec_cross, *vec_x):
        copy.start()
    gathers[0].stage(0)
    vecs[x, yh] = vec_shard[...]
    for s in range(N_CTX):
        ready[s, :, 3 * HEAD :, :] = seg_ref[...]
    vec_cross.wait_recv()
    for copy in vec_x2:
        copy.start()
    for n in range(1, 7):
        gathers[0].stage(n)
    vec_cross.wait_send()
    for copy in (*vec_x, *vec_x2):
        copy.wait()

    for part in range(6):
        c, col = part // 3, (part % 3) * 512
        kind, first = part // 2, (part % 2) * 8
        value = jnp.zeros((ROWS, 512), f32)
        weight = wa[c, :, :, :, col : col + 512].reshape(D, 512)
        value = dot(x_ref[...], weight)
        if kind != 1:
            row = 0 if kind == 0 else 1
            value = value + jnp.concatenate(
                [vecs[f // 2, f % 2, row : row + 1, :].astype(f32) for f in range(first // 2, first // 2 + 4)], axis=1
            )
        value = value.T.astype(bf16)
        for h in range(8):
            for m in range(MB):
                ready[first + h, m, kind * HEAD : (kind + 1) * HEAD, :] = value[
                    h * HEAD : (h + 1) * HEAD, m * TOK : (m + 1) * TOK
                ]
    swaps = [[], []]
    for m in range(MB):
        for d in range(1, N_CTX):
            t = lax.rem(place + d, N_CTX)
            swaps[m].append(send(ready.at[t, m], held.at[place, m], (q_send, q_recv), m * N_CTX + d, ctx_device(t)))
            swaps[m][-1].start()
    held[place] = ready[place]
    returns = [[], []]
    for m in range(MB):
        for d in range(1, N_CTX):
            t = lax.rem(place + d, N_CTX)
            returns[m].append(
                send(out_t.at[t, m], mixed.at[place, m], (o_send, o_recv), m * N_CTX + d, ctx_device(t))
            )
    for gather in gathers[1:]:
        gather.stage(0)
    outs = []
    for c in range(2):
        outs.append((wa.at[c, :, :, :, 0:1536], out_attn.at[:, :, :, c * 1536 : (c + 1) * 1536]))
        outs.append((wa.at[c, :, :, :, 1536:2048], out_attn.at[:, :, :, 3072 + c * 512 : 3584 + c * 512]))
    outs = [pltpu.make_async_copy(src, dst, out_sem.at[n]) for n, (src, dst) in enumerate(outs)]
    for copy in outs:
        copy.start()
    for m in range(MB):
        for copy in swaps[m]:
            copy.wait_recv()
        load_side(held, m, keys, None, None, values_t, seg_col)

        def query_block(j, _, m=m):
            for n, at in enumerate(STEPS):
                if at // NBLK == m:

                    @pl.when(j == at % NBLK)
                    def _(n=n):
                        for gather in gathers[1:]:
                            gather.stage(n + 1)

            query_forward(held, m, j, out_t, out_full, out_lse, keys, values_t, seg_col, scores)
            return 0

        lax.fori_loop(0, NBLK, query_block, 0)
        for copy in returns[m]:
            copy.start()
        mixed[place, m] = out_t[place, m]
    last = [pltpu.make_async_copy(held, out_held, out_sem.at[4])]
    last[0].start()
    out_vec[...] = vecs[...]
    for n in range(len(STEPS) + 1, 7):
        for gather in gathers[1:]:
            gather.stage(n)
    for m in range(MB):
        for copy in swaps[m]:
            copy.wait_send()
        for copy in returns[m]:
            copy.wait()
    last.append(pltpu.make_async_copy(mixed, out_mixed, out_sem.at[5]))
    last[1].start()
    for copy in (*outs, *last):
        copy.wait()


def front(shard, vec_shard, x, seg_rows):
    vmem = pl.BlockSpec(memory_space=pltpu.VMEM)
    hbm = pl.BlockSpec(memory_space=pl.ANY)
    sem = lambda n: pltpu.SemaphoreType.DMA((n,))
    blocks = lambda rows, dt: (N_CTX, MB, rows, TOK)
    ffn_cols = 2 * FF if N_GROUPS > 1 else 128
    return pl.pallas_call(
        front_kernel,
        in_specs=[hbm, vmem, vmem, vmem],
        out_specs=[hbm, hbm, vmem, hbm, hbm, vmem, vmem],
        out_shape=[
            jax.ShapeDtypeStruct((4, 2, TOK, 4 * D), bf16),
            jax.ShapeDtypeStruct((4, 2, TOK, ffn_cols), bf16),
            jax.ShapeDtypeStruct((4, 2, 16, TOK), bf16),
            jax.ShapeDtypeStruct((N_CTX, MB, SENT, TOK), bf16),
            jax.ShapeDtypeStruct((N_CTX, MB, HEAD, TOK), bf16),
            jax.ShapeDtypeStruct((N_CTX, MB, HEAD, TOK), f32),
            jax.ShapeDtypeStruct((N_CTX, MB, 1, TOK), f32),
        ],
        scratch_shapes=[
            pltpu.VMEM((2, 4, 2, TOK, GROUP), bf16),
            pltpu.VMEM((4, 2, 16, TOK), bf16),
            pltpu.VMEM((N_CTX, MB, SENT, TOK), bf16),
            pltpu.VMEM((N_CTX, MB, SENT, TOK), bf16),
            pltpu.VMEM((N_CTX, MB, HEAD, TOK), bf16),
            pltpu.VMEM((N_CTX, MB, HEAD, TOK), bf16),
            pltpu.VMEM((PACK, HEAD), bf16),
            pltpu.VMEM((HEAD, PACK), bf16),
            pltpu.VMEM((PACK, TOK), f32),
            pltpu.VMEM((PACK, BLK), f32),
            sem(N_COPY * N_GROUPS), sem(N_COPY * N_GROUPS), sem(7), sem(7), sem(32), sem(32), sem(32), sem(32),
            sem(3 * N_GROUPS), sem(6),
        ],
        compiler_params=pltpu.CompilerParams(
            collective_id=2, has_side_effects=True, vmem_limit_bytes=48 * 2**20
        ),
        cost_estimate=pl.CostEstimate(
            flops=4 * MB * PACK * PACK * HEAD + 2 * ROWS * D * 3 * D, bytes_accessed=32 * 2**20,
            transcendentals=MB * PACK * PACK,
        ),
        name="front",
    )(shard, vec_shard, x, seg_rows)


def back_kernel(
    left_x, left_o, left_h, left_f, right_o, right_u, right_g, vec, grad_ready, held_in, full, lse,
    out_attn, out_ffn, out_vec, out_sq, out_q,
    peer_left, own_right, peer_right, own_vec, peer_vec,
    w_0, w_1, w_2, s1_0, s1_1, s1_2, s2_0, s2_1, s2_2,
    r1_0, r1_1, r1_2, r2_0, r2_1, r2_2, r3_0, r3_1, r3_2,
    gathered, sq_z, sq_y, sq_x, sq_c,
    held, grad_held, out_t, landed, right_q, keys, values, keys_t, seg_col, acc_k, acc_v, square_acc,
    swap_send, swap_recv, ring_send, ring_recv, gather_send, gather_recv, sq_send, sq_recv,
    o_send, o_recv, q_send, q_recv, local_sem, out_sem,
):
    core = lax.axis_index("core")
    other = 1 - core
    place = lax.axis_index(CTX)
    row_place = lax.axis_index("yl") * 4 + lax.axis_index("z")
    lefts = (left_x, left_o, left_h, left_f)
    rights = (None, right_o, right_u, right_g)
    works, firsts, seconds = (w_0, w_1, w_2), (s1_0, s1_1, s1_2), (s2_0, s2_1, s2_2)
    recvs = ((r1_0, r1_1, r1_2), (r2_0, r2_1, r2_2), (r3_0, r3_1, r3_2))
    to_core = {"core": other}

    fetch = pltpu.make_async_copy(held_in, held, local_sem.at[0])
    fetch.start()
    fetches = [fetch]
    for i in range(1, 4):
        cols = pl.ds(pl.multiple_of(core * WIDTHS[i], 512), WIDTHS[i])
        fetches.append(
            pltpu.make_async_copy(
                rights[i].at[:, cols], own_right.at[:, OFFSETS[i] : OFFSETS[i] + WIDTHS[i]], local_sem.at[i]
            )
        )
        fetches[-1].start()
    greet_all()

    pushes, returns = [[], []], [[], []]
    for m in range(MB):
        for d in range(1, N_CTX):
            t = lax.rem(place + d, N_CTX)
            to = ctx_device(t)
            pushes[m].append(
                send(grad_ready.at[t, m], grad_held.at[place, m], (o_send, o_recv), m * N_CTX + d, to)
            )
            returns[m].append(send(out_t.at[t, m], landed.at[place, m], (q_send, q_recv), m * N_CTX + d, to))
    swaps = []
    for i in (2, 3, 1, 0):
        swaps.append(send(lefts[i], peer_left.at[i], (swap_send, swap_recv), 2 * i, to_core))
        if i:
            from_cols = pl.ds(pl.multiple_of(other * WIDTHS[i], 512), WIDTHS[i])
            swaps.append(
                send(
                    rights[i].at[:, from_cols], peer_right.at[:, OFFSETS[i] : OFFSETS[i] + WIDTHS[i]],
                    (swap_send, swap_recv), 2 * i + 1, to_core,
                )
            )
    for m in range(MB):
        for copy in pushes[m]:
            copy.start()
    for copy in swaps:
        copy.start()
    grad_held[place] = grad_ready[place]
    for copy in fetches:
        copy.wait()

    def blocks(b):
        out = [(p, b * COLS, COLS) for p in range(3)]
        if b == 3:
            out.append((0, VEC_AT, 128))
        return out

    def copies(p, phase, at, width):
        order = ORDERS[p]
        axis = order[phase]
        cols = slice(at, at + width)
        src = (works, firsts, seconds)[phase][p]
        out = []
        for step in (1, 2, 3):
            to, index = peer(axis, step)
            chunk = pick(src, axis, index, dims_after(order, phase), cols)
            land = recvs[phase][p].at[(step - 1, *(slice(None),) * (len(lead(order, phase + 1)) + 1), cols)]
            out.append(
                send(chunk, land, (ring_send, ring_recv), ((p * 3 + phase) * 5 + at // COLS) * 3 + step - 1, to)
            )
        return out

    def multiply(p, b):
        i, col = PRODUCT[p][b]
        if i == 0:
            mine = right_q.at[:, pl.ds(pl.multiple_of(core * WIDTHS[0] + col, 512), COLS)]
        else:
            mine = own_right.at[:, OFFSETS[i] + col : OFFSETS[i] + col + COLS]
        theirs = peer_right.at[:, OFFSETS[i] + col : OFFSETS[i] + col + COLS]

        def rows_block(x, _):
            rows = pl.ds(pl.multiple_of(x * 256, 256), 256)
            value = dot(lefts[i][rows, :], mine[...]) + dot(peer_left[i, rows, :], theirs[...])
            works[p][x, :, :, :, :, b * COLS : (b + 1) * COLS] = value.astype(bf16).reshape(2, 2, 4, 16, COLS)
            return 0

        lax.fori_loop(0, 4, rows_block, 0)

    def reduce(phase, p, at, width):
        cols = slice(at, at + width)
        order = ORDERS[p]
        axis = order[phase]
        src = (works, firsts, seconds)[phase][p]
        land = recvs[phase][p]
        for copy in copies(p, phase, at, width):
            copy.wait()
        own = pick(src, axis, coordinate(axis), dims_after(order, phase), cols)
        rest = len(lead(order, phase + 1)) - 1
        if phase < 2:
            dst = (firsts, seconds)[phase][p]

            def add(n, _):
                tail = (*(slice(None),) * (rest + 1), cols)
                inner = (*(slice(None),) * (rest + 1), slice(None))
                value = own[(n, *inner)].astype(f32)
                for step in range(3):
                    value = value + land[(step, n, *tail)].astype(f32)
                dst[(n, *tail)] = value.astype(bf16)
                return 0

            lax.fori_loop(0, lead(order, phase + 1)[0], add, 0)
            for copy in copies(p, phase + 1, at, width):
                copy.start()
            return
        value = own[...].astype(f32)
        for step in range(3):
            value = value + land[step, :, cols].astype(f32)
        to = p * 2048 + at if width == COLS else 6144
        gathered[core, row_place, :, to : to + width] = value.astype(bf16)
        square = value * value
        if width != COLS:
            square = square * jnp.where(core == 0, 1.0, 0.0)
        squares = square_acc[...]
        for c in range(0, width, 128):
            squares = squares + square[:8, c : c + 128] + square[8:, c : c + 128]
        square_acc[...] = squares

    square_acc[...] = jnp.zeros_like(square_acc)
    for copy in swaps:
        copy.wait()
    for b in range(3):
        for p, at, width in blocks(b):
            multiply(p, b)
            for copy in copies(p, 0, at, width):
                copy.start()

    for m in range(MB):
        load_side(held, m, keys, values, keys_t, None, seg_col)
        acc_k[...] = jnp.zeros_like(acc_k)
        acc_v[...] = jnp.zeros_like(acc_v)
        for copy in pushes[m]:
            copy.wait_recv()

        def query_block(j, _, m=m):
            for at, tasks in TASKS.items():
                if at // NBLK == m:

                    @pl.when(j == at % NBLK)
                    def _(tasks=tasks):
                        for phase, b, p in tasks:
                            reduce(phase, p, b * COLS, COLS)

            query_t = pair(held, m, j, slice(0, HEAD))
            seg_row = pair(held, m, j, slice(3 * HEAD, 3 * HEAD + 1)).astype(f32)
            grad_t = pair(grad_held, m, j, slice(0, HEAD))
            row_lse = pair(lse, m, j, slice(0, 1))
            delta = jnp.sum(grad_t.astype(f32) * pair(full, m, j, slice(0, HEAD)), axis=0, keepdims=True)
            acc_q = jnp.zeros((HEAD, BLK), f32)
            for k in range(NBLK):
                at = slice(k * BLK, (k + 1) * BLK)
                s = dot(keys[at, :], query_t) * SCALE2 - row_lse
                col = seg_col[at, :]
                same = jnp.concatenate([col, col], axis=1) == seg_row
                p = jnp.exp2(jnp.where(same, s, NEG_LARGE))
                dp = dot(values[at, :], grad_t)
                ds = (p * (dp - delta)).astype(bf16)
                acc_q = acc_q + dot(keys_t[:, at], ds)
                acc_k[:, at] += dot_nt(query_t, ds)
                acc_v[:, at] += dot_nt(grad_t, p.astype(bf16))
            acc_q = (acc_q * SCALE).astype(bf16)
            out_t[2 * j, m, :HEAD, :] = acc_q[:, :TOK]
            out_t[2 * j + 1, m, :HEAD, :] = acc_q[:, TOK:]
            return 0

        lax.fori_loop(0, NBLK, query_block, 0)
        for s in range(N_CTX):
            at = slice(s * TOK, (s + 1) * TOK)
            out_t[s, m, HEAD : 2 * HEAD, :] = (acc_k[:, at] * SCALE).astype(bf16)
            out_t[s, m, 2 * HEAD :, :] = acc_v[:, at].astype(bf16)
        for copy in returns[m]:
            copy.start()
        landed[place, m] = out_t[place, m]

    done = [task for tasks in TASKS.values() for task in tasks]
    for phase in (0, 1):
        for b in range(3):
            for p in range(3):
                if (phase, b, p) not in done:
                    reduce(phase, p, b * COLS, COLS)
    for m in range(MB):
        for copy in pushes[m]:
            copy.wait_send()
        for copy in returns[m]:
            copy.wait()
        for i in range(HEADS // 2):
            for kind in range(3):
                rows = slice(kind * HEAD, (kind + 1) * HEAD)
                both = jnp.concatenate([landed[2 * i, m, rows, :], landed[2 * i + 1, m, rows, :]], axis=0)
                right_q[m * TOK : (m + 1) * TOK, kind * D + i * 128 : kind * D + (i + 1) * 128] = both.T
    give = send(
        right_q.at[:, pl.ds(pl.multiple_of(other * WIDTHS[0], 512), WIDTHS[0])], peer_right.at[:, 0 : WIDTHS[0]],
        (swap_send, swap_recv), 1, to_core,
    )
    give.start()
    sum_q = jnp.sum(right_q[:, :D].astype(f32), axis=0, keepdims=True)
    sum_v = jnp.sum(right_q[:, 2 * D :].astype(f32), axis=0, keepdims=True)
    row = lax.broadcasted_iota(jnp.int32, (16, TOK), 0)
    own_vec[...] = jnp.zeros_like(own_vec)
    for f in range(N_FSDP):
        cols = slice(f * TOK, (f + 1) * TOK)
        value = jnp.where(row == 0, sum_q[:, cols], jnp.where(row == 1, sum_v[:, cols], vec[f]))
        own_vec[f // 2, f % 2, 0, 0] = value.astype(bf16)
    give_vec = send(own_vec, peer_vec, (swap_send, swap_recv), 8, to_core)
    give_vec.start()
    keep_q = pltpu.make_async_copy(right_q, out_q, local_sem.at[4])
    keep_q.start()
    give.wait()
    for p, at, width in blocks(3):
        if width == COLS:
            multiply(p, 3)
        else:
            give_vec.wait()
            works[0][:, :, :, :, :, VEC_AT:] = (own_vec[...].astype(f32) + peer_vec[...].astype(f32)).astype(bf16)
        for copy in copies(p, 0, at, width):
            copy.start()
    for b in range(3):
        for p, at, width in blocks(b):
            reduce(2, p, at, width)
    for phase in range(3):
        for p, at, width in blocks(3):
            reduce(phase, p, at, width)
    squares = square_acc[...]
    yl, z = lax.axis_index("yl"), lax.axis_index("z")
    z_first, y_first = slice(0, HALF_Z), slice(HALF_Z, 6272)
    to_y = {"yl": 1 - yl}
    gather_sems = (gather_send, gather_recv)
    sq_sems = (sq_send, sq_recv)

    def spread(buffer, axis, base):
        at = coordinate(axis)
        out = []
        for step in (1, 2, 3):
            out.append(send(buffer.at[at], buffer.at[at], sq_sems, base + step - 1, peer(axis, step)[0]))
        return out

    def total(buffer):
        return (buffer[0] + buffer[1]) + (buffer[2] + buffer[3])

    sq_z[z] = squares
    squares_z = spread(sq_z, "z", 0)
    first_z = [
        send(gathered.at[core, row_place, :, z_first], gathered.at[core, row_place, :, z_first], gather_sems, step - 1, peer("z", step)[0])
        for step in (1, 2, 3)
    ]
    first_y = send(gathered.at[core, row_place, :, y_first], gathered.at[core, row_place, :, y_first], gather_sems, 3, to_y)
    for copy in (*squares_z, *first_z, first_y):
        copy.start()
    for copy in squares_z:
        copy.wait()
    y_at = coordinate("y")
    sq_y[y_at] = total(sq_z)
    squares_y = spread(sq_y, "y", 3)
    for copy in squares_y:
        copy.start()
    for copy in (*first_z, first_y):
        copy.wait()
    quarter = pl.ds(yl * 4, 4)
    second_y = send(
        gathered.at[core, quarter, :, z_first], gathered.at[core, quarter, :, z_first], gather_sems, 4, to_y
    )
    second_y.start()
    second_z = []
    for step in (1, 2, 3):
        for half in range(2):
            view = gathered.at[core, half * 4 + z, :, y_first]
            second_z.append(send(view, view, gather_sems, 5 + (step - 1) * 2 + half, peer("z", step)[0]))
    for copy in second_z:
        copy.start()
    for copy in squares_y:
        copy.wait()
    x_at = coordinate("x")
    sq_x[x_at] = total(sq_y)
    squares_x = spread(sq_x, "x", 6)
    for copy in squares_x:
        copy.start()
    for copy in squares_x:
        copy.wait()
    sq_c[core] = total(sq_x)
    square_c = send(sq_c.at[core], sq_c.at[core], sq_sems, 9, to_core)
    square_c.start()
    square_c.wait()
    out_sq[...] = sq_c[0] + sq_c[1]
    second_y.wait()
    for copy in second_z:
        copy.wait()
    last = send(gathered.at[core], gathered.at[core], gather_sems, 11, to_core)
    last.start()
    last.wait()
    locals_ = []
    for c in range(2):
        for p in range(3):
            for b in range(4):
                i, col = PRODUCT[p][b]
                target, base = ((out_attn, 0), (out_attn, 3072), (out_ffn, 0), (out_ffn, FF))[i]
                base = base + c * WIDTHS[i] + col
                at = p * 2048 + b * COLS
                locals_.append(
                    pltpu.make_async_copy(
                        gathered.at[c, :, :, at : at + COLS], target.at[:, :, base : base + COLS],
                        out_sem.at[len(locals_)],
                    )
                )
    locals_.append(pltpu.make_async_copy(gathered.at[0, :, :, 6144:], out_vec, out_sem.at[len(locals_)]))
    for copy in locals_:
        copy.start()
    for copy in locals_:
        copy.wait()
    keep_q.wait()


def back(lefts, rights, vec, grad_ready, held, full, lse):
    vmem = pl.BlockSpec(memory_space=pltpu.VMEM)
    hbm = pl.BlockSpec(memory_space=pl.ANY)
    scratch = [
        pltpu.VMEM((4, D, ROWS), bf16),
        pltpu.VMEM((ROWS, 6144), bf16),
        pltpu.VMEM((ROWS, 6144), bf16),
        pltpu.VMEM((4, 2, 2, 4, 16, 128), bf16),
        pltpu.VMEM((4, 2, 2, 4, 16, 128), bf16),
    ]
    for n in range(3):
        scratch += [pltpu.VMEM((*lead(ORDERS[p], n), 16, PART_COLS[p]), bf16) for p in range(3)]
    for n in range(1, 4):
        scratch += [pltpu.VMEM((3, *lead(ORDERS[p], n), 16, PART_COLS[p]), bf16) for p in range(3)]
    scratch += [
        pltpu.VMEM((2, 8, 16, 6272), bf16),
        pltpu.VMEM((4, 8, 128), f32),
        pltpu.VMEM((4, 8, 128), f32),
        pltpu.VMEM((4, 8, 128), f32),
        pltpu.VMEM((2, 8, 128), f32),
        pltpu.VMEM((N_CTX, MB, SENT, TOK), bf16),
        pltpu.VMEM((N_CTX, MB, HEAD, TOK), bf16),
        pltpu.VMEM((N_CTX, MB, 3 * HEAD, TOK), bf16),
        pltpu.VMEM((N_CTX, MB, 3 * HEAD, TOK), bf16),
        pltpu.VMEM((ROWS, 3 * D), bf16),
        pltpu.VMEM((PACK, HEAD), bf16),
        pltpu.VMEM((PACK, HEAD), bf16),
        pltpu.VMEM((HEAD, PACK), bf16),
        pltpu.VMEM((PACK, TOK), f32),
        pltpu.VMEM((HEAD, PACK), f32),
        pltpu.VMEM((HEAD, PACK), f32),
        pltpu.VMEM((8, 128), f32),
    ]
    for count in (9, 9, 135, 135, 12, 12, 10, 10, 32, 32, 32, 32, 5, 25):
        scratch.append(pltpu.SemaphoreType.DMA((count,)))
    out = pl.pallas_call(
        back_kernel,
        in_specs=[vmem] * 4 + [hbm] * 3 + [vmem, vmem, hbm, vmem, vmem],
        out_specs=[hbm, hbm, hbm, vmem, hbm],
        out_shape=[
            jax.ShapeDtypeStruct((8, 16, 4 * D), bf16),
            jax.ShapeDtypeStruct((8, 16, 2 * FF), bf16),
            jax.ShapeDtypeStruct((8, 16, 128), bf16),
            jax.ShapeDtypeStruct((8, 128), f32),
            jax.ShapeDtypeStruct((ROWS, 3 * D), bf16),
        ],
        scratch_shapes=scratch,
        compiler_params=pltpu.CompilerParams(
            collective_id=1, has_side_effects=True, vmem_limit_bytes=60 * 2**20
        ),
        cost_estimate=pl.CostEstimate(
            flops=2 * 512 * D * 6144 + 10 * MB * PACK * PACK * HEAD, bytes_accessed=16 * 2**20,
            transcendentals=MB * PACK * PACK,
        ),
        name="back",
    )(*lefts, *rights, vec, grad_ready, held, full, lse)
    return out[0].reshape(TOK, 4 * D), out[1].reshape(TOK, 2 * FF), out[2][0, :12], jnp.sum(out[3]), out[4]


def layer_stats(values, gain_row, shift_row):
    center = values - jnp.mean(values, axis=-1, keepdims=True)
    inverse = lax.rsqrt(jnp.mean(center * center, axis=-1, keepdims=True) + NORM_EPS)
    normal = center * inverse
    return (normal * gain_row + shift_row, normal, inverse)


def layer_back(grad_value, normal, inverse, gain_row):
    scaled = grad_value * gain_row
    return inverse * (
        scaled
        - jnp.mean(scaled, axis=-1, keepdims=True)
        - normal * jnp.mean(scaled * normal, axis=-1, keepdims=True)
    )


def column_sum(values):
    return jnp.sum(values.astype(f32), axis=0)


def adamw(weight, grad_value, first, second, rate, decay):
    first_new = BETA_FIRST * first + (1.0 - BETA_FIRST) * grad_value
    second_new = BETA_SECOND * second + (1.0 - BETA_SECOND) * grad_value * grad_value
    first_hat = first_new / (1.0 - BETA_FIRST**STEP)
    second_hat = second_new / (1.0 - BETA_SECOND**STEP)
    weight_new = weight - rate * (first_hat / (jnp.sqrt(second_hat) + ADAM_EPS) + decay * weight)
    return (weight_new, first_new, second_new)


def to_heads(rows, parts):
    t = rows.T.reshape(parts, HEADS, HEAD, MB, TOK)
    return jnp.transpose(t, (1, 3, 0, 2, 4)).reshape(HEADS, MB, parts * HEAD, TOK)


def from_heads(blocks, parts):
    t = blocks.reshape(HEADS, MB, parts, HEAD, TOK)
    return jnp.transpose(t, (1, 4, 2, 0, 3)).reshape(ROWS, parts * D)


def shards(
    tokens, cotangent, dest, lengths, attn_weight, attn_first, attn_second,
    ffn_weight, ffn_first, ffn_second, vectors, vec_first, vec_second,
):
    place, core = lax.axis_index(CTX), lax.axis_index("core")

    def half(weight, base, width):
        return lax.dynamic_slice_in_dim(weight, base + core * width, width, 1).astype(bf16)

    attn_half = jnp.concatenate([half(attn_weight, 0, 1536), half(attn_weight, 3 * D, 512)], axis=1)
    own_rows = D // N_FSDP // N_CTX
    if N_GROUPS == 1:
        shard = attn_half[None]
        w_ffn = lax.all_gather(
            lax.dynamic_slice_in_dim(ffn_weight, place * own_rows, own_rows).astype(bf16), ALL, axis=0, tiled=True
        )
    else:
        shard = jnp.stack([attn_half, half(ffn_weight, 0, GROUP), half(ffn_weight, FF, GROUP)])

    x = tokens.reshape(ROWS, D)
    cot = cotangent.reshape(ROWS, D).astype(f32)
    ends = jnp.cumsum(lengths[:, 0], axis=1)
    seg = jnp.sum((dest[:, 0, :, None] >= ends[:, None, :]).astype(jnp.int32), axis=2)
    keep = (seg.reshape(ROWS, 1) < 8).astype(f32)

    seg_rows = jnp.broadcast_to(seg.astype(bf16)[:, None, :], (MB, 16, TOK))
    vec_shard = jnp.pad(vectors.astype(bf16), ((0, 4), (0, 0)))
    w_attn, ffn_out, vecs, held, mixed_t, mixed_full, lse = front(shard, vec_shard, x, seg_rows)
    w_attn = w_attn.reshape(D, 4 * D)
    if N_GROUPS > 1:
        w_ffn = ffn_out.reshape(D, 2 * FF)
    small = jnp.transpose(vecs.reshape(N_FSDP, 16, TOK), (1, 0, 2)).reshape(16, D)[:12].astype(f32)
    w_qkv, w_out = w_attn[:, : 3 * D], w_attn[:, 3 * D :]
    w_one, w_two = w_ffn[:, :FF], w_ffn[:, FF:]
    mixed = from_heads(mixed_t, 1)

    branch = dot(mixed, w_out) + small[2]
    normed_one, normal_one, inverse_one = layer_stats(x.astype(f32) + branch, small[4], small[5])
    normed_low = normed_one.astype(bf16)
    hidden_pre = dot(normed_low, w_one) + small[8:].reshape(FF)
    activ, gelu_back = jax.vjp(partial(jax.nn.gelu, approximate=False), hidden_pre)
    activ_low = activ.astype(bf16)
    ffn_out = dot_nt(activ_low, w_two) + small[3]
    output, normal_two, inverse_two = layer_stats(normed_one + ffn_out, small[6], small[7])
    output = output * keep
    grad_out = cot * keep
    grad_two = layer_back(grad_out, normal_two, inverse_two, small[6])
    ffn_grad_low = grad_two.astype(bf16)
    grad_hidden = gelu_back(dot(ffn_grad_low, w_two))[0].astype(bf16)
    grad_normed = dot_nt(grad_hidden, w_one) + grad_two
    grad_one = layer_back(grad_normed, normal_one, inverse_one, small[4])
    branch_grad_low = grad_one.astype(bf16)
    grad_mixed = dot_nt(branch_grad_low, w_out).astype(bf16)

    step_vec = jnp.concatenate(
        [
            jnp.stack(
                [
                    jnp.zeros((D,), f32),
                    jnp.zeros((D,), f32),
                    column_sum(branch_grad_low),
                    column_sum(ffn_grad_low),
                    jnp.sum(grad_normed * normal_one, axis=0),
                    jnp.sum(grad_normed, axis=0),
                    jnp.sum(grad_out * normal_two, axis=0),
                    jnp.sum(grad_out, axis=0),
                ]
            ),
            column_sum(grad_hidden).reshape(4, D),
        ],
        axis=0,
    )
    vec_rows = jnp.transpose(step_vec.reshape(12, N_FSDP, TOK), (1, 0, 2))
    vec_rows = jnp.pad(vec_rows, ((0, 0), (0, 4), (0, 0)))
    total_attn, total_ffn, total_vec, square_sum, grad_qkv = back(
        (x.T, mixed.T, normed_low.T, ffn_grad_low.T),
        (branch_grad_low, grad_hidden, activ_low),
        vec_rows,
        to_heads(grad_mixed, 1),
        held,
        mixed_full,
        lse,
    )
    grad_tokens = grad_one + dot_nt(grad_qkv, w_qkv)
    total_attn, total_ffn, total_vec = total_attn.astype(f32), total_ffn.astype(f32), total_vec.astype(f32)
    grad_norm = jnp.sqrt(square_sum)
    factor = jnp.minimum(1.0, CLIP_NORM / (grad_norm + 1e-06))
    rate_matrix = D ** (-0.5)
    attn_new, attn_first_new, attn_second_new = adamw(
        attn_weight, total_attn * factor, attn_first, attn_second, ATTN_RATE_SCALE * rate_matrix, WEIGHT_DECAY
    )
    ffn_new, ffn_first_new, ffn_second_new = adamw(
        ffn_weight, total_ffn * factor, ffn_first, ffn_second, rate_matrix, WEIGHT_DECAY
    )
    vec_new, vec_first_new, vec_second_new = adamw(
        vectors, total_vec * factor, vec_first, vec_second, RATE_VECTOR, 0.0
    )
    return (
        output.astype(bf16).reshape(tokens.shape),
        grad_tokens.astype(bf16).reshape(tokens.shape),
        grad_norm,
        attn_new, attn_first_new, attn_second_new,
        ffn_new, ffn_first_new, ffn_second_new,
        vec_new, vec_first_new, vec_second_new,
        attn_new.astype(bf16),
        ffn_new.astype(bf16),
        total_vec[2] * factor,
    )


def solution(mesh):
    fine = Mesh(mesh.devices.reshape(2, 4, 2, 4, 2), ("yl", "z", "core", "x", "yh"))
    act = P(None, FSDP, CTX, None)
    row = P(FSDP, None)
    col = P(None, FSDP)
    return jax.shard_map(
        shards,
        mesh=fine,
        in_specs=(act, act, P(None, FSDP, CTX), P(None, FSDP, None), row, row, row, row, row, row, col, col, col),
        out_specs=(act, act, P(), row, row, row, row, row, row, col, col, col, row, row, P(FSDP)),
        check_vma=False,
    )
```

```python
import math

import jax
import jax.numpy as jnp
from jax import lax
from jax.experimental import pallas as pl
from jax.experimental.pallas import tpu as pltpu
from jax.sharding import Mesh, PartitionSpec as P

HEADS = 16
HEAD = 64
STEP = 10
MB = 2
TOK = 128
ROWS = MB * TOK
D = 1024
FF = 4096
N_CTX = 16
N_FSDP = 8
PACK = 2048
SENT = 208

NORM_EPS = 1e-05
CLIP_NORM = 1.0
BETA_FIRST = 0.9
BETA_SECOND = 0.999
ADAM_EPS = 1e-08
WEIGHT_DECAY = 0.01
RATE_VECTOR = 0.3
ATTN_RATE_SCALE = 3.0
NEG_LARGE = -1e30
SCALE2 = HEAD ** (-0.5) * math.log2(math.e)
SCALE = HEAD ** (-0.5)
CONTRACT_ROWS = (((0,), (0,)), ((), ()))
CONTRACT_COLS = (((1,), (1,)), ((), ()))
CTX = ("yl", "z", "core")
FSDP = ("x", "yh")
ALL = ("x", "yh", "yl", "z", "core")
BLK = 256
NBLK = PACK // BLK
f32 = jnp.float32
bf16 = jnp.bfloat16


def dot(a, b):
    return jnp.dot(a, b, preferred_element_type=f32)


def dot_nt(a, b):
    return lax.dot_general(a, b, CONTRACT_COLS, preferred_element_type=f32)


def dot_tn(a, b):
    return lax.dot_general(a, b, CONTRACT_ROWS, preferred_element_type=f32)


MESH_ID = pl.DeviceIdType.MESH
COLS = 512
N_BLK = 4
ORDERS = (("x", "z", "y"), ("z", "y", "x"), ("y", "x", "z"))
EARLY = ((2, 0), (2, 512), (2, 1024), (2, 1536), (3, 0), (3, 512), (3, 1024), (3, 1536), (1, 0))
PRODUCT = tuple(
    tuple(EARLY[b * 3 + p] for b in range(3)) + ((0, p * COLS),) for p in range(3)
)
VEC_AT = 2048
PART_COLS = (2048 + 128, 2048, 2048)
WIDTHS = (1536, 512, 2048, 2048)
OFFSETS = (0, 1536, 2048, 4096)
HALF_Z = 3072
TASKS = {}
for _n, _at in enumerate((7, 8, 9, 10, 11, 12, 13, 14, 15)):
    TASKS.setdefault(_at, []).append((0, _n // 3, _n % 3))
for _n, _at in enumerate(()):
    TASKS.setdefault(_at, []).append((1, _n // 3, _n % 3))


def coordinate(axis):
    if axis == "y":
        return lax.axis_index("yh") * 2 + lax.axis_index("yl")
    return lax.axis_index(axis)


def peer(axis, step):
    at = lax.rem(coordinate(axis) + step, 4)
    if axis == "y":
        return {"yh": at // 2, "yl": lax.rem(at, 2)}, at
    return {axis: at}, at


def pick(ref, axis, at, dims, cols):
    index = []
    for d in dims:
        if d == axis:
            index.append(at)
        elif axis == "y" and d == "yh":
            index.append(at // 2)
        elif axis == "y" and d == "yl":
            index.append(lax.rem(at, 2))
        else:
            index.append(slice(None))
    return ref.at[(*index, slice(None), cols)]


def dims_after(order, n):
    dims = ["x", "yh", "yl", "z"]
    for axis in order[:n]:
        for d in ("yh", "yl") if axis == "y" else (axis,):
            dims.remove(d)
    return dims


SIZES = {"x": 4, "yh": 2, "yl": 2, "z": 4}


def lead(order, n):
    return tuple(SIZES[d] for d in dims_after(order, n))


def send(src, dst, sems, index, to):
    return pltpu.make_async_remote_copy(
        src_ref=src, dst_ref=dst, send_sem=sems[0].at[index], recv_sem=sems[1].at[index],
        device_id=to, device_id_type=MESH_ID,
    )


def load_side(qkv_ref, m, keys, values, keys_t, values_t, seg_col):
    for s in range(N_CTX):
        at = slice(s * TOK, (s + 1) * TOK)
        key_t = qkv_ref[s, m, HEAD : 2 * HEAD, :]
        value_t = qkv_ref[s, m, 2 * HEAD : 3 * HEAD, :]
        keys[at, :] = key_t.T
        if values is not None:
            values[at, :] = value_t.T
        if keys_t is not None:
            keys_t[:, at] = key_t
        if values_t is not None:
            values_t[:, at] = value_t
        seg = qkv_ref[s, m, 3 * HEAD : 3 * HEAD + 1, :].astype(f32)
        seg_col[at, :] = jnp.broadcast_to(seg, (TOK, TOK)).T


def pair(ref, m, j, rows):
    return jnp.concatenate([ref[2 * j, m, rows, :], ref[2 * j + 1, m, rows, :]], axis=1)


def query_forward(held, m, j, out, full, lse_out, keys, values_t, seg_col, scores):
    query_t = pair(held, m, j, slice(0, HEAD))
    seg_row = pair(held, m, j, slice(3 * HEAD, 3 * HEAD + 1)).astype(f32)
    top = jnp.full((1, BLK), NEG_LARGE, f32)
    for k in range(NBLK):
        at = slice(k * BLK, (k + 1) * BLK)
        s = dot(keys[at, :], query_t) * SCALE2
        col = seg_col[at, :]
        same = jnp.concatenate([col, col], axis=1) == seg_row
        s = jnp.where(same, s, NEG_LARGE)
        scores[at, :] = s
        top = jnp.maximum(top, jnp.max(s, axis=0, keepdims=True))
    total = jnp.zeros((1, BLK), f32)
    acc = jnp.zeros((HEAD, BLK), f32)
    for k in range(NBLK):
        at = slice(k * BLK, (k + 1) * BLK)
        p = jnp.exp2(scores[at, :] - top)
        total = total + jnp.sum(p, axis=0, keepdims=True)
        acc = acc + dot(values_t[:, at], p.astype(bf16))
    acc = acc / total
    lse = top + jnp.log2(total)
    for half in range(2):
        cols = slice(half * TOK, (half + 1) * TOK)
        out[2 * j + half, m] = acc[:, cols].astype(bf16)
        full[2 * j + half, m] = acc[:, cols]
        lse_out[2 * j + half, m] = lse[:, cols]


GROUP_COLS = (1536, 2048, 2048, 512)
GROUP_AT = (0, 2048, 4096, 1536)
SPLITS = ((512, 1024), (1024, 1536), (1024, 1536), (128, 256))
N_COPY = 31
GROUPS = (1, 2, 3)
BEFORE = tuple((0, op) for op in ("z1", "x1", "z2", "y1", "z3", "x2", "x3", "y2", "z4", "x4", "x5"))
BEFORE += tuple((g, op) for op in ("z1", "z2", "y1") for g in GROUPS)
BEFORE += tuple((0, op) for op in ("y3", "z5", "sx", "sy", "sz", "end"))
PUSHED = tuple((g, op) for op in ("z3", "x1", "x2", "x3") for g in GROUPS)
STEPS = {
    0: tuple((g, "z4") for g in GROUPS),
    1: tuple((g, "y2") for g in GROUPS),
    3: tuple((g, "x4") for g in GROUPS),
    6: tuple((g, "x5") for g in GROUPS),
    9: tuple((g, "y3") for g in GROUPS),
    12: tuple((g, "z5") for g in GROUPS),
}
LAST = tuple((g, op) for op in ("sx", "sy", "sz", "end") for g in GROUPS)


def ctx_device(t):
    return {"yl": t // 8, "z": lax.rem(t // 2, 4), "core": lax.rem(t, 2)}


def rows_at(start, size):
    return pl.ds(pl.multiple_of(start, 16), size)


class Gather:
    def __init__(self, g, shard, dest, sems, base, local_sem):
        core = lax.axis_index("core")
        x, z = lax.axis_index("x"), lax.axis_index("z")
        yh, yl = lax.axis_index("yh"), lax.axis_index("yl")
        y = yh * 2 + yl
        every = slice(None)
        zq, half = rows_at(z * 32, 32), rows_at(yl * 64, 64)
        cross = {"yh": 1 - yh, "yl": 1 - yl}
        count = [0]
        x_end, y_end = SPLITS[g]
        x_cols, y_cols, z_cols = slice(0, x_end), slice(x_end, y_end), slice(y_end, GROUP_COLS[g])

        def given(rows, cols):
            return shard.at[rows, GROUP_AT[g] + cols.start : GROUP_AT[g] + cols.stop]

        def make(src, dst, to):
            copy = send(src, dst, sems, base + count[0], to)
            count[0] += 1
            return copy

        def own(rows, cols, to):
            return make(given(rows, cols), dest(core, x, yh, rows, cols), to)

        def pass_on(xs, yhs, rows, cols, to):
            view = dest(core, xs, yhs, rows, cols)
            return make(view, view, to)

        x_to = {step: peer("x", step)[0] for step in (1, 2, 3)}
        y_to = {step: peer("y", step)[0] for step in (1, 3)}
        z_to = {step: peer("z", step)[0] for step in (1, 3)}
        x_before, x_after = lax.rem(x + 3, 4), lax.rem(x + 1, 4)
        y_before, y_after = lax.rem(y + 3, 4), lax.rem(y + 1, 4)
        z_before, z_after = lax.rem(z + 3, 4), lax.rem(z + 1, 4)
        self.copies = {
            "x1": [own(every, x_cols, cross)],
            "x2": [own(every, x_cols, x_to[s]) for s in (1, 3)],
            "z1": [own(zq, z_cols, cross)],
            "z2": [own(zq, z_cols, x_to[s]) for s in (1, 3, 2)],
            "y1": [own(half, y_cols, x_to[s]) for s in (1, 3, 2)],
            "x3": [pass_on(x, 1 - yh, every, x_cols, x_to[s]) for s in (1, 3)],
            "z3": [pass_on(x, 1 - yh, zq, z_cols, x_to[s]) for s in (1, 3, 2)],
            "y2": [pass_on(every, yh, half, y_cols, y_to[s]) for s in (1, 3)],
            "z4": [pass_on(every, every, zq, z_cols, z_to[s]) for s in (1, 3)],
            "x4": [
                pass_on(x_before, yh, slice(0, 64), x_cols, x_to[1]),
                pass_on(x_after, yh, slice(64, 128), x_cols, x_to[3]),
            ],
            "x5": [
                pass_on(x_before, 1 - yh, slice(0, 64), x_cols, x_to[1]),
                pass_on(x_after, 1 - yh, slice(64, 128), x_cols, x_to[3]),
            ],
            "y3": [
                pass_on(every, y_before // 2, rows_at(lax.rem(y_before, 2) * 64, 32), y_cols, y_to[1]),
                pass_on(every, y_after // 2, rows_at(lax.rem(y_after, 2) * 64 + 32, 32), y_cols, y_to[3]),
            ],
            "z5": [
                pass_on(every, every, rows_at(z_before * 32, 16), z_cols, z_to[1]),
                pass_on(every, every, rows_at(z_after * 32 + 16, 16), z_cols, z_to[3]),
            ],
        }
        for name, cols in (("sx", x_cols), ("sy", y_cols), ("sz", z_cols)):
            self.copies[name] = [pass_on(every, every, every, cols, {"core": 1 - core})]
        self.places = [
            pltpu.make_async_copy(given(rows, cols), dest(core, x, yh, rows, cols), local_sem.at[3 * g + n])
            for n, (rows, cols) in enumerate(((every, x_cols), (half, y_cols), (zq, z_cols)))
        ]

    needs = {
        "x3": ("x1",), "z3": ("z1",), "y2": ("y1",), "z4": ("z2", "z3"), "x4": ("x2",), "x5": ("x3",), "y3": ("y2",),
        "z5": ("z4",), "sx": ("x4", "x5"), "sy": ("y3",), "sz": ("z5",),
    }

    def step(self, name):
        if name == "end":
            for copy in (*self.copies["sx"], *self.copies["sy"], *self.copies["sz"]):
                copy.wait_recv()
            for copies in self.copies.values():
                for copy in copies:
                    copy.wait_send()
            return
        for need in self.needs.get(name, ()):
            for copy in self.copies[need]:
                copy.wait_recv()
        if name == "z1":
            for copy in self.places:
                copy.start()
        if name == "z3":
            for copy in self.places:
                copy.wait()
        for copy in self.copies[name]:
            copy.start()


def greet_all():
    barrier = pltpu.get_barrier_semaphore()
    place = lax.axis_index(CTX)
    others = [ctx_device(lax.rem(place + d, N_CTX)) for d in range(1, N_CTX)]
    others += [peer(axis, step)[0] for axis in ("x", "y") for step in (1, 2, 3)]
    for other in others:
        pl.semaphore_signal(barrier, inc=1, device_id=other, device_id_type=MESH_ID)
    pl.semaphore_wait(barrier, len(others))


def front_kernel(
    shard, vec_shard, x_ref, seg_ref,
    out_attn, out_ffn, out_vec, out_held, out_mixed, out_full, out_lse,
    wa, vecs, ready, held, mixed, out_t, keys, values_t, seg_col, scores,
    ag_send, ag_recv, vec_send, vec_recv, q_send, q_recv, o_send, o_recv, local_sem, out_sem,
):
    core = lax.axis_index("core")
    place = lax.axis_index(CTX)
    x, yh, yl = lax.axis_index("x"), lax.axis_index("yh"), lax.axis_index("yl")

    def dest(g):
        def view(c, xs, yhs, rows, cols):
            if g == 0:
                return wa.at[c, xs, yhs, rows, cols]
            start = (0, 0, FF, 3 * D)[g] + c * GROUP_COLS[g] + cols.start
            target = out_attn if g == 3 else out_ffn
            return target.at[xs, yhs, rows, pl.ds(pl.multiple_of(start, 128), cols.stop - cols.start)]

        return view

    gathers = [
        Gather(g, shard, dest(g), (ag_send, ag_recv), g * N_COPY, local_sem) for g in range(4)
    ]
    vec_sems = (vec_send, vec_recv)
    vec_cross = send(vec_shard, vecs.at[x, yh], vec_sems, 0, {"yh": 1 - yh, "yl": 1 - yl})
    vec_x = [send(vec_shard, vecs.at[x, yh], vec_sems, s, peer("x", s)[0]) for s in (1, 2, 3)]
    vec_x2 = [
        send(vecs.at[x, 1 - yh], vecs.at[x, 1 - yh], vec_sems, 3 + s, peer("x", s)[0]) for s in (1, 2, 3)
    ]
    greet_all()
    for copy in (vec_cross, *vec_x):
        copy.start()
    done = set()

    def stages(todo):
        for g, n in todo:
            if (g, n) not in done:
                done.add((g, n))
                gathers[g].step(n)

    stages(BEFORE[:4])
    vecs[x, yh] = vec_shard[...]
    for s in range(N_CTX):
        ready[s, :, 3 * HEAD :, :] = seg_ref[...]
    vec_cross.wait_recv()
    for copy in vec_x2:
        copy.start()
    stages(BEFORE)
    vec_cross.wait_send()
    for copy in (*vec_x, *vec_x2):
        copy.wait()

    for part in range(6):
        c, col = part // 3, (part % 3) * 512
        kind, first = part // 2, (part % 2) * 8
        value = jnp.zeros((ROWS, 512), f32)
        weight = wa[c, :, :, :, col : col + 512].reshape(D, 512)
        value = dot(x_ref[...], weight)
        if kind != 1:
            row = 0 if kind == 0 else 1
            value = value + jnp.concatenate(
                [vecs[f // 2, f % 2, row : row + 1, :].astype(f32) for f in range(first // 2, first // 2 + 4)], axis=1
            )
        value = value.T.astype(bf16)
        for h in range(8):
            for m in range(MB):
                ready[first + h, m, kind * HEAD : (kind + 1) * HEAD, :] = value[
                    h * HEAD : (h + 1) * HEAD, m * TOK : (m + 1) * TOK
                ]
    swaps = [[], []]
    for m in range(MB):
        for d in range(1, N_CTX):
            t = lax.rem(place + d, N_CTX)
            swaps[m].append(send(ready.at[t, m], held.at[place, m], (q_send, q_recv), m * N_CTX + d, ctx_device(t)))
            swaps[m][-1].start()
    held[place] = ready[place]
    returns = [[], []]
    for m in range(MB):
        for d in range(1, N_CTX):
            t = lax.rem(place + d, N_CTX)
            returns[m].append(
                send(out_t.at[t, m], mixed.at[place, m], (o_send, o_recv), m * N_CTX + d, ctx_device(t))
            )
    stages(PUSHED)
    outs = [(wa.at[c], out_attn.at[:, :, :, c * 1536 : (c + 1) * 1536]) for c in range(2)]
    outs = [pltpu.make_async_copy(src, dst, out_sem.at[n]) for n, (src, dst) in enumerate(outs)]
    for copy in outs:
        copy.start()
    for m in range(MB):
        for copy in swaps[m]:
            copy.wait_recv()
        load_side(held, m, keys, None, None, values_t, seg_col)

        def query_block(j, _, m=m):
            for at, todo in STEPS.items():
                if at // NBLK == m:

                    @pl.when(j == at % NBLK)
                    def _(todo=todo):
                        stages(todo)

            query_forward(held, m, j, out_t, out_full, out_lse, keys, values_t, seg_col, scores)
            return 0

        lax.fori_loop(0, NBLK, query_block, 0)
        for copy in returns[m]:
            copy.start()
        mixed[place, m] = out_t[place, m]
    last = [pltpu.make_async_copy(held, out_held, out_sem.at[4])]
    last[0].start()
    out_vec[...] = vecs[...]
    stages(LAST)
    for m in range(MB):
        for copy in swaps[m]:
            copy.wait_send()
        for copy in returns[m]:
            copy.wait()
    last.append(pltpu.make_async_copy(mixed, out_mixed, out_sem.at[5]))
    last[1].start()
    for copy in (*outs, *last):
        copy.wait()


def front(shard, vec_shard, x, seg_rows):
    vmem = pl.BlockSpec(memory_space=pltpu.VMEM)
    hbm = pl.BlockSpec(memory_space=pl.ANY)
    sem = lambda n: pltpu.SemaphoreType.DMA((n,))
    blocks = lambda rows, dt: (N_CTX, MB, rows, TOK)
    return pl.pallas_call(
        front_kernel,
        in_specs=[hbm, vmem, vmem, vmem],
        out_specs=[hbm, hbm, vmem, hbm, hbm, vmem, vmem],
        out_shape=[
            jax.ShapeDtypeStruct((4, 2, TOK, 4 * D), bf16),
            jax.ShapeDtypeStruct((4, 2, TOK, 2 * FF), bf16),
            jax.ShapeDtypeStruct((4, 2, 16, TOK), bf16),
            jax.ShapeDtypeStruct((N_CTX, MB, SENT, TOK), bf16),
            jax.ShapeDtypeStruct((N_CTX, MB, HEAD, TOK), bf16),
            jax.ShapeDtypeStruct((N_CTX, MB, HEAD, TOK), f32),
            jax.ShapeDtypeStruct((N_CTX, MB, 1, TOK), f32),
        ],
        scratch_shapes=[
            pltpu.VMEM((2, 4, 2, TOK, 1536), bf16),
            pltpu.VMEM((4, 2, 16, TOK), bf16),
            pltpu.VMEM((N_CTX, MB, SENT, TOK), bf16),
            pltpu.VMEM((N_CTX, MB, SENT, TOK), bf16),
            pltpu.VMEM((N_CTX, MB, HEAD, TOK), bf16),
            pltpu.VMEM((N_CTX, MB, HEAD, TOK), bf16),
            pltpu.VMEM((PACK, HEAD), bf16),
            pltpu.VMEM((HEAD, PACK), bf16),
            pltpu.VMEM((PACK, TOK), f32),
            pltpu.VMEM((PACK, BLK), f32),
            sem(4 * N_COPY), sem(4 * N_COPY), sem(7), sem(7), sem(32), sem(32), sem(32), sem(32),
            sem(12), sem(6),
        ],
        compiler_params=pltpu.CompilerParams(
            collective_id=2, has_side_effects=True, vmem_limit_bytes=48 * 2**20
        ),
        cost_estimate=pl.CostEstimate(
            flops=4 * MB * PACK * PACK * HEAD + 2 * ROWS * D * 3 * D, bytes_accessed=32 * 2**20,
            transcendentals=MB * PACK * PACK,
        ),
        name="front",
    )(shard, vec_shard, x, seg_rows)


def back_kernel(
    left_x, left_o, left_h, left_f, right_o, right_u, right_g, vec, grad_ready, held_in, full, lse,
    out_attn, out_ffn, out_vec, out_sq, out_q,
    peer_left, own_right, peer_right, own_vec, peer_vec,
    w_0, w_1, w_2, s1_0, s1_1, s1_2, s2_0, s2_1, s2_2,
    r1_0, r1_1, r1_2, r2_0, r2_1, r2_2, r3_0, r3_1, r3_2,
    gathered, sq_z, sq_y, sq_x, sq_c,
    held, grad_held, out_t, landed, right_q, keys, values, keys_t, seg_col, acc_k, acc_v, square_acc,
    swap_send, swap_recv, ring_send, ring_recv, gather_send, gather_recv, sq_send, sq_recv,
    o_send, o_recv, q_send, q_recv, local_sem, out_sem,
):
    core = lax.axis_index("core")
    other = 1 - core
    place = lax.axis_index(CTX)
    row_place = lax.axis_index("yl") * 4 + lax.axis_index("z")
    lefts = (left_x, left_o, left_h, left_f)
    rights = (None, right_o, right_u, right_g)
    works, firsts, seconds = (w_0, w_1, w_2), (s1_0, s1_1, s1_2), (s2_0, s2_1, s2_2)
    recvs = ((r1_0, r1_1, r1_2), (r2_0, r2_1, r2_2), (r3_0, r3_1, r3_2))
    to_core = {"core": other}

    fetch = pltpu.make_async_copy(held_in, held, local_sem.at[0])
    fetch.start()
    fetches = [fetch]
    for i in range(1, 4):
        cols = pl.ds(pl.multiple_of(core * WIDTHS[i], 512), WIDTHS[i])
        fetches.append(
            pltpu.make_async_copy(
                rights[i].at[:, cols], own_right.at[:, OFFSETS[i] : OFFSETS[i] + WIDTHS[i]], local_sem.at[i]
            )
        )
        fetches[-1].start()
    greet_all()

    pushes, returns = [[], []], [[], []]
    for m in range(MB):
        for d in range(1, N_CTX):
            t = lax.rem(place + d, N_CTX)
            to = ctx_device(t)
            pushes[m].append(
                send(grad_ready.at[t, m], grad_held.at[place, m], (o_send, o_recv), m * N_CTX + d, to)
            )
            returns[m].append(send(out_t.at[t, m], landed.at[place, m], (q_send, q_recv), m * N_CTX + d, to))
    swaps = []
    for i in (2, 3, 1, 0):
        swaps.append(send(lefts[i], peer_left.at[i], (swap_send, swap_recv), 2 * i, to_core))
        if i:
            from_cols = pl.ds(pl.multiple_of(other * WIDTHS[i], 512), WIDTHS[i])
            swaps.append(
                send(
                    rights[i].at[:, from_cols], peer_right.at[:, OFFSETS[i] : OFFSETS[i] + WIDTHS[i]],
                    (swap_send, swap_recv), 2 * i + 1, to_core,
                )
            )
    for m in range(MB):
        for copy in pushes[m]:
            copy.start()
    for copy in swaps:
        copy.start()
    grad_held[place] = grad_ready[place]
    for copy in fetches:
        copy.wait()

    def blocks(b):
        out = [(p, b * COLS, COLS) for p in range(3)]
        if b == 3:
            out.append((0, VEC_AT, 128))
        return out

    def copies(p, phase, at, width):
        order = ORDERS[p]
        axis = order[phase]
        cols = slice(at, at + width)
        src = (works, firsts, seconds)[phase][p]
        out = []
        for step in (1, 2, 3):
            to, index = peer(axis, step)
            chunk = pick(src, axis, index, dims_after(order, phase), cols)
            land = recvs[phase][p].at[(step - 1, *(slice(None),) * (len(lead(order, phase + 1)) + 1), cols)]
            out.append(
                send(chunk, land, (ring_send, ring_recv), ((p * 3 + phase) * 5 + at // COLS) * 3 + step - 1, to)
            )
        return out

    def multiply(p, b):
        i, col = PRODUCT[p][b]
        if i == 0:
            mine = right_q.at[:, pl.ds(pl.multiple_of(core * WIDTHS[0] + col, 512), COLS)]
        else:
            mine = own_right.at[:, OFFSETS[i] + col : OFFSETS[i] + col + COLS]
        theirs = peer_right.at[:, OFFSETS[i] + col : OFFSETS[i] + col + COLS]

        def rows_block(x, _):
            rows = pl.ds(pl.multiple_of(x * 256, 256), 256)
            value = dot(lefts[i][rows, :], mine[...]) + dot(peer_left[i, rows, :], theirs[...])
            works[p][x, :, :, :, :, b * COLS : (b + 1) * COLS] = value.astype(bf16).reshape(2, 2, 4, 16, COLS)
            return 0

        lax.fori_loop(0, 4, rows_block, 0)

    def reduce(phase, p, at, width):
        cols = slice(at, at + width)
        order = ORDERS[p]
        axis = order[phase]
        src = (works, firsts, seconds)[phase][p]
        land = recvs[phase][p]
        for copy in copies(p, phase, at, width):
            copy.wait()
        own = pick(src, axis, coordinate(axis), dims_after(order, phase), cols)
        rest = len(lead(order, phase + 1)) - 1
        if phase < 2:
            dst = (firsts, seconds)[phase][p]

            def add(n, _):
                tail = (*(slice(None),) * (rest + 1), cols)
                inner = (*(slice(None),) * (rest + 1), slice(None))
                value = own[(n, *inner)].astype(f32)
                for step in range(3):
                    value = value + land[(step, n, *tail)].astype(f32)
                dst[(n, *tail)] = value.astype(bf16)
                return 0

            lax.fori_loop(0, lead(order, phase + 1)[0], add, 0)
            for copy in copies(p, phase + 1, at, width):
                copy.start()
            return
        value = own[...].astype(f32)
        for step in range(3):
            value = value + land[step, :, cols].astype(f32)
        to = p * 2048 + at if width == COLS else 6144
        gathered[core, row_place, :, to : to + width] = value.astype(bf16)
        square = value * value
        if width != COLS:
            square = square * jnp.where(core == 0, 1.0, 0.0)
        squares = square_acc[...]
        for c in range(0, width, 128):
            squares = squares + square[:8, c : c + 128] + square[8:, c : c + 128]
        square_acc[...] = squares

    square_acc[...] = jnp.zeros_like(square_acc)
    for copy in swaps:
        copy.wait()
    for b in range(3):
        for p, at, width in blocks(b):
            multiply(p, b)
            for copy in copies(p, 0, at, width):
                copy.start()

    for m in range(MB):
        load_side(held, m, keys, values, keys_t, None, seg_col)
        acc_k[...] = jnp.zeros_like(acc_k)
        acc_v[...] = jnp.zeros_like(acc_v)
        for copy in pushes[m]:
            copy.wait_recv()

        def query_block(j, _, m=m):
            for at, tasks in TASKS.items():
                if at // NBLK == m:

                    @pl.when(j == at % NBLK)
                    def _(tasks=tasks):
                        for phase, b, p in tasks:
                            reduce(phase, p, b * COLS, COLS)

            query_t = pair(held, m, j, slice(0, HEAD))
            seg_row = pair(held, m, j, slice(3 * HEAD, 3 * HEAD + 1)).astype(f32)
            grad_t = pair(grad_held, m, j, slice(0, HEAD))
            row_lse = pair(lse, m, j, slice(0, 1))
            delta = jnp.sum(grad_t.astype(f32) * pair(full, m, j, slice(0, HEAD)), axis=0, keepdims=True)
            acc_q = jnp.zeros((HEAD, BLK), f32)
            for k in range(NBLK):
                at = slice(k * BLK, (k + 1) * BLK)
                s = dot(keys[at, :], query_t) * SCALE2 - row_lse
                col = seg_col[at, :]
                same = jnp.concatenate([col, col], axis=1) == seg_row
                p = jnp.exp2(jnp.where(same, s, NEG_LARGE))
                dp = dot(values[at, :], grad_t)
                ds = (p * (dp - delta)).astype(bf16)
                acc_q = acc_q + dot(keys_t[:, at], ds)
                acc_k[:, at] += dot_nt(query_t, ds)
                acc_v[:, at] += dot_nt(grad_t, p.astype(bf16))
            acc_q = (acc_q * SCALE).astype(bf16)
            out_t[2 * j, m, :HEAD, :] = acc_q[:, :TOK]
            out_t[2 * j + 1, m, :HEAD, :] = acc_q[:, TOK:]
            return 0

        lax.fori_loop(0, NBLK, query_block, 0)
        for s in range(N_CTX):
            at = slice(s * TOK, (s + 1) * TOK)
            out_t[s, m, HEAD : 2 * HEAD, :] = (acc_k[:, at] * SCALE).astype(bf16)
            out_t[s, m, 2 * HEAD :, :] = acc_v[:, at].astype(bf16)
        for copy in returns[m]:
            copy.start()
        landed[place, m] = out_t[place, m]

    done = [task for tasks in TASKS.values() for task in tasks]
    for phase in (0, 1):
        for b in range(3):
            for p in range(3):
                if (phase, b, p) not in done:
                    reduce(phase, p, b * COLS, COLS)
    for m in range(MB):
        for copy in pushes[m]:
            copy.wait_send()
        for copy in returns[m]:
            copy.wait()
        for i in range(HEADS // 2):
            for kind in range(3):
                rows = slice(kind * HEAD, (kind + 1) * HEAD)
                both = jnp.concatenate([landed[2 * i, m, rows, :], landed[2 * i + 1, m, rows, :]], axis=0)
                right_q[m * TOK : (m + 1) * TOK, kind * D + i * 128 : kind * D + (i + 1) * 128] = both.T
    give = send(
        right_q.at[:, pl.ds(pl.multiple_of(other * WIDTHS[0], 512), WIDTHS[0])], peer_right.at[:, 0 : WIDTHS[0]],
        (swap_send, swap_recv), 1, to_core,
    )
    give.start()
    sum_q = jnp.sum(right_q[:, :D].astype(f32), axis=0, keepdims=True)
    sum_v = jnp.sum(right_q[:, 2 * D :].astype(f32), axis=0, keepdims=True)
    row = lax.broadcasted_iota(jnp.int32, (16, TOK), 0)
    own_vec[...] = jnp.zeros_like(own_vec)
    for f in range(N_FSDP):
        cols = slice(f * TOK, (f + 1) * TOK)
        value = jnp.where(row == 0, sum_q[:, cols], jnp.where(row == 1, sum_v[:, cols], vec[f]))
        own_vec[f // 2, f % 2, 0, 0] = value.astype(bf16)
    give_vec = send(own_vec, peer_vec, (swap_send, swap_recv), 8, to_core)
    give_vec.start()
    keep_q = pltpu.make_async_copy(right_q, out_q, local_sem.at[4])
    keep_q.start()
    give.wait()
    for p, at, width in blocks(3):
        if width == COLS:
            multiply(p, 3)
        else:
            give_vec.wait()
            works[0][:, :, :, :, :, VEC_AT:] = (own_vec[...].astype(f32) + peer_vec[...].astype(f32)).astype(bf16)
        for copy in copies(p, 0, at, width):
            copy.start()
    for b in range(3):
        for p, at, width in blocks(b):
            reduce(2, p, at, width)
    for phase in range(3):
        for p, at, width in blocks(3):
            reduce(phase, p, at, width)
    squares = square_acc[...]
    yl, z = lax.axis_index("yl"), lax.axis_index("z")
    z_first, y_first = slice(0, HALF_Z), slice(HALF_Z, 6272)
    to_y = {"yl": 1 - yl}
    gather_sems = (gather_send, gather_recv)
    sq_sems = (sq_send, sq_recv)

    def spread(buffer, axis, base):
        at = coordinate(axis)
        out = []
        for step in (1, 2, 3):
            out.append(send(buffer.at[at], buffer.at[at], sq_sems, base + step - 1, peer(axis, step)[0]))
        return out

    def total(buffer):
        return (buffer[0] + buffer[1]) + (buffer[2] + buffer[3])

    sq_z[z] = squares
    squares_z = spread(sq_z, "z", 0)
    first_z = [
        send(gathered.at[core, row_place, :, z_first], gathered.at[core, row_place, :, z_first], gather_sems, step - 1, peer("z", step)[0])
        for step in (1, 2, 3)
    ]
    first_y = send(gathered.at[core, row_place, :, y_first], gathered.at[core, row_place, :, y_first], gather_sems, 3, to_y)
    for copy in (*squares_z, *first_z, first_y):
        copy.start()
    for copy in squares_z:
        copy.wait()
    y_at = coordinate("y")
    sq_y[y_at] = total(sq_z)
    squares_y = spread(sq_y, "y", 3)
    for copy in squares_y:
        copy.start()
    for copy in (*first_z, first_y):
        copy.wait()
    quarter = pl.ds(yl * 4, 4)
    second_y = send(
        gathered.at[core, quarter, :, z_first], gathered.at[core, quarter, :, z_first], gather_sems, 4, to_y
    )
    second_y.start()
    second_z = []
    for step in (1, 2, 3):
        for half in range(2):
            view = gathered.at[core, half * 4 + z, :, y_first]
            second_z.append(send(view, view, gather_sems, 5 + (step - 1) * 2 + half, peer("z", step)[0]))
    for copy in second_z:
        copy.start()
    for copy in squares_y:
        copy.wait()
    x_at = coordinate("x")
    sq_x[x_at] = total(sq_y)
    squares_x = spread(sq_x, "x", 6)
    for copy in squares_x:
        copy.start()
    for copy in squares_x:
        copy.wait()
    sq_c[core] = total(sq_x)
    square_c = send(sq_c.at[core], sq_c.at[core], sq_sems, 9, to_core)
    square_c.start()
    square_c.wait()
    out_sq[...] = sq_c[0] + sq_c[1]
    second_y.wait()
    for copy in second_z:
        copy.wait()
    last = send(gathered.at[core], gathered.at[core], gather_sems, 11, to_core)
    last.start()
    last.wait()
    locals_ = []
    for c in range(2):
        for p in range(3):
            for b in range(4):
                i, col = PRODUCT[p][b]
                target, base = ((out_attn, 0), (out_attn, 3072), (out_ffn, 0), (out_ffn, FF))[i]
                base = base + c * WIDTHS[i] + col
                at = p * 2048 + b * COLS
                locals_.append(
                    pltpu.make_async_copy(
                        gathered.at[c, :, :, at : at + COLS], target.at[:, :, base : base + COLS],
                        out_sem.at[len(locals_)],
                    )
                )
    locals_.append(pltpu.make_async_copy(gathered.at[0, :, :, 6144:], out_vec, out_sem.at[len(locals_)]))
    for copy in locals_:
        copy.start()
    for copy in locals_:
        copy.wait()
    keep_q.wait()


def back(lefts, rights, vec, grad_ready, held, full, lse):
    vmem = pl.BlockSpec(memory_space=pltpu.VMEM)
    hbm = pl.BlockSpec(memory_space=pl.ANY)
    scratch = [
        pltpu.VMEM((4, D, ROWS), bf16),
        pltpu.VMEM((ROWS, 6144), bf16),
        pltpu.VMEM((ROWS, 6144), bf16),
        pltpu.VMEM((4, 2, 2, 4, 16, 128), bf16),
        pltpu.VMEM((4, 2, 2, 4, 16, 128), bf16),
    ]
    for n in range(3):
        scratch += [pltpu.VMEM((*lead(ORDERS[p], n), 16, PART_COLS[p]), bf16) for p in range(3)]
    for n in range(1, 4):
        scratch += [pltpu.VMEM((3, *lead(ORDERS[p], n), 16, PART_COLS[p]), bf16) for p in range(3)]
    scratch += [
        pltpu.VMEM((2, 8, 16, 6272), bf16),
        pltpu.VMEM((4, 8, 128), f32),
        pltpu.VMEM((4, 8, 128), f32),
        pltpu.VMEM((4, 8, 128), f32),
        pltpu.VMEM((2, 8, 128), f32),
        pltpu.VMEM((N_CTX, MB, SENT, TOK), bf16),
        pltpu.VMEM((N_CTX, MB, HEAD, TOK), bf16),
        pltpu.VMEM((N_CTX, MB, 3 * HEAD, TOK), bf16),
        pltpu.VMEM((N_CTX, MB, 3 * HEAD, TOK), bf16),
        pltpu.VMEM((ROWS, 3 * D), bf16),
        pltpu.VMEM((PACK, HEAD), bf16),
        pltpu.VMEM((PACK, HEAD), bf16),
        pltpu.VMEM((HEAD, PACK), bf16),
        pltpu.VMEM((PACK, TOK), f32),
        pltpu.VMEM((HEAD, PACK), f32),
        pltpu.VMEM((HEAD, PACK), f32),
        pltpu.VMEM((8, 128), f32),
    ]
    for count in (9, 9, 135, 135, 12, 12, 10, 10, 32, 32, 32, 32, 5, 25):
        scratch.append(pltpu.SemaphoreType.DMA((count,)))
    out = pl.pallas_call(
        back_kernel,
        in_specs=[vmem] * 4 + [hbm] * 3 + [vmem, vmem, hbm, vmem, vmem],
        out_specs=[hbm, hbm, hbm, vmem, hbm],
        out_shape=[
            jax.ShapeDtypeStruct((8, 16, 4 * D), bf16),
            jax.ShapeDtypeStruct((8, 16, 2 * FF), bf16),
            jax.ShapeDtypeStruct((8, 16, 128), bf16),
            jax.ShapeDtypeStruct((8, 128), f32),
            jax.ShapeDtypeStruct((ROWS, 3 * D), bf16),
        ],
        scratch_shapes=scratch,
        compiler_params=pltpu.CompilerParams(
            collective_id=1, has_side_effects=True, vmem_limit_bytes=60 * 2**20
        ),
        cost_estimate=pl.CostEstimate(
            flops=2 * 512 * D * 6144 + 10 * MB * PACK * PACK * HEAD, bytes_accessed=16 * 2**20,
            transcendentals=MB * PACK * PACK,
        ),
        name="back",
    )(*lefts, *rights, vec, grad_ready, held, full, lse)
    return out[0].reshape(TOK, 4 * D), out[1].reshape(TOK, 2 * FF), out[2][0, :12], jnp.sum(out[3]), out[4]


def layer_stats(values, gain_row, shift_row):
    center = values - jnp.mean(values, axis=-1, keepdims=True)
    inverse = lax.rsqrt(jnp.mean(center * center, axis=-1, keepdims=True) + NORM_EPS)
    normal = center * inverse
    return (normal * gain_row + shift_row, normal, inverse)


def layer_back(grad_value, normal, inverse, gain_row):
    scaled = grad_value * gain_row
    return inverse * (
        scaled
        - jnp.mean(scaled, axis=-1, keepdims=True)
        - normal * jnp.mean(scaled * normal, axis=-1, keepdims=True)
    )


N_CHUNK = 8
CHUNK = FF // N_CHUNK
ERF_TOP = (
    -2.72614225801306e-10, 2.77068142495902e-08, -2.10102402082508e-06, -5.69250639462346e-05,
    -7.34990630326855e-04, -2.95459980854025e-03, -1.60960333262415e-02,
)
ERF_LOW = (
    -1.45660718464996e-05, -2.13374055278905e-04, -1.68282697438203e-03, -7.37332916720468e-03,
    -1.42647390514189e-02,
)


def erf(value):
    value = jnp.clip(value, -4.0, 4.0)
    square = value * value
    top, low = jnp.full_like(square, ERF_TOP[0]), jnp.full_like(square, ERF_LOW[0])
    for c in ERF_TOP[1:]:
        top = top * square + c
    for c in ERF_LOW[1:]:
        low = low * square + c
    return value * top / low


def dense_kernel(
    mixed_ref, x_ref, cot_ref, keep_ref, small_ref, w_attn, w_ffn,
    out_ref, one_ref, x_t, o_t, h_t, f_t, a_low_ref, du_ref, g_ref, vec_ref, ready_ref,
    w_out, w_one, w_two, mixed, normal_one_ref, slope, total, sem,
):
    fetch_out = pltpu.make_async_copy(w_attn.at[:, 3 * D :], w_out, sem.at[0])
    fetch_out.start()
    fetch_one, fetch_two = [], []
    for n in range(N_CHUNK):
        at = n * CHUNK
        fetch_one.append(pltpu.make_async_copy(w_ffn.at[:, at : at + CHUNK], w_one.at[n], sem.at[1 + n]))
        fetch_two.append(
            pltpu.make_async_copy(w_ffn.at[:, FF + at : FF + at + CHUNK], w_two.at[n], sem.at[1 + N_CHUNK + n])
        )
        fetch_one[n].start()
        fetch_two[n].start()

    def row(i):
        return small_ref[i : i + 1, :]

    def put(i, value):
        for f in range(N_FSDP):
            vec_ref[f, i : i + 1, :] = value[:, f * TOK : (f + 1) * TOK]

    def sums(value):
        return jnp.sum(value, axis=0, keepdims=True)

    vec_ref[...] = jnp.zeros_like(vec_ref)
    for m in range(MB):
        tok = slice(m * TOK, (m + 1) * TOK)
        for i in range(HEADS // 2):
            both = jnp.concatenate([mixed_ref[2 * i, m], mixed_ref[2 * i + 1, m]], axis=0)
            o_t[i * 128 : (i + 1) * 128, tok] = both
            mixed[tok, i * 128 : (i + 1) * 128] = both.T
    x_t[...] = x_ref[...].T
    fetch_out.wait()
    normed_one, normal_one, inverse_one = layer_stats(
        x_ref[...].astype(f32) + dot(mixed[...], w_out[...]) + row(2), row(4), row(5)
    )
    normal_one_ref[...] = normal_one
    normed_low = normed_one.astype(bf16)
    h_t[...] = normed_low.T
    total[...] = normed_one + row(3)
    for n in range(N_CHUNK):
        cols = slice(n * CHUNK, (n + 1) * CHUNK)
        fetch_one[n].wait()
        bias = small_ref[8 + n // 2 : 9 + n // 2, (n % 2) * CHUNK : (n % 2 + 1) * CHUNK]
        u = dot(normed_low, w_one[n]) + bias
        share = 0.5 + 0.5 * erf(u * math.sqrt(0.5))
        g = (u * share).astype(bf16)
        g_ref[:, cols] = g
        slope[:, cols] = share + u * (jnp.exp(-0.5 * u * u) * (1.0 / math.sqrt(2.0 * math.pi)))
        fetch_two[n].wait()
        total[...] += dot_nt(g, w_two[n])
    output, normal_two, inverse_two = layer_stats(total[...], row(6), row(7))
    keep = keep_ref[...]
    out_ref[...] = (output * keep).astype(bf16)
    grad_out = cot_ref[...].astype(f32) * keep
    put(6, sums(grad_out * normal_two))
    put(7, sums(grad_out))
    grad_two = layer_back(grad_out, normal_two, inverse_two, row(6))
    f_low = grad_two.astype(bf16)
    f_t[...] = f_low.T
    put(3, sums(f_low.astype(f32)))
    total[...] = grad_two
    for n in range(N_CHUNK):
        cols = slice(n * CHUNK, (n + 1) * CHUNK)
        du = (dot(f_low, w_two[n]) * slope[:, cols]).astype(bf16)
        du_ref[:, cols] = du
        part = sums(du.astype(f32))
        for i in range(CHUNK // TOK):
            f = (n % 2) * (CHUNK // TOK) + i
            vec_ref[f, 8 + n // 2 : 9 + n // 2, :] = part[:, i * TOK : (i + 1) * TOK]
        total[...] += dot_nt(du, w_one[n])
    grad_normed = total[...]
    normal_one = normal_one_ref[...]
    put(4, sums(grad_normed * normal_one))
    put(5, sums(grad_normed))
    grad_one = layer_back(grad_normed, normal_one, inverse_one, row(4))
    one_ref[...] = grad_one
    a_low = grad_one.astype(bf16)
    a_low_ref[...] = a_low
    put(2, sums(a_low.astype(f32)))
    grad_mixed = dot_nt(a_low, w_out[...]).T.astype(bf16)
    for h in range(HEADS):
        for m in range(MB):
            ready_ref[h, m] = grad_mixed[h * HEAD : (h + 1) * HEAD, m * TOK : (m + 1) * TOK]


def dense(mixed_t, x, cot, keep, small, w_attn, w_ffn):
    vmem = pl.BlockSpec(memory_space=pltpu.VMEM)
    hbm = pl.BlockSpec(memory_space=pl.ANY)
    turned = jax.ShapeDtypeStruct((D, ROWS), bf16)
    return pl.pallas_call(
        dense_kernel,
        in_specs=[vmem] * 5 + [hbm, hbm],
        out_specs=[vmem] * 11,
        out_shape=[
            jax.ShapeDtypeStruct((ROWS, D), bf16),
            jax.ShapeDtypeStruct((ROWS, D), f32),
            turned, turned, turned, turned,
            jax.ShapeDtypeStruct((ROWS, D), bf16),
            jax.ShapeDtypeStruct((ROWS, FF), bf16),
            jax.ShapeDtypeStruct((ROWS, FF), bf16),
            jax.ShapeDtypeStruct((N_FSDP, 16, TOK), f32),
            jax.ShapeDtypeStruct((HEADS, MB, HEAD, TOK), bf16),
        ],
        scratch_shapes=[
            pltpu.VMEM((D, D), bf16),
            pltpu.VMEM((N_CHUNK, D, CHUNK), bf16),
            pltpu.VMEM((N_CHUNK, D, CHUNK), bf16),
            pltpu.VMEM((ROWS, D), bf16),
            pltpu.VMEM((ROWS, D), f32),
            pltpu.VMEM((ROWS, FF), f32),
            pltpu.VMEM((ROWS, D), f32),
            pltpu.SemaphoreType.DMA((1 + 2 * N_CHUNK,)),
        ],
        compiler_params=pltpu.CompilerParams(vmem_limit_bytes=56 * 2**20),
        cost_estimate=pl.CostEstimate(
            flops=2 * ROWS * D * (2 * D + 4 * FF), bytes_accessed=32 * 2**20, transcendentals=ROWS * FF
        ),
        name="dense",
    )(mixed_t, x, cot, keep, small, w_attn, w_ffn)


def adamw(weight, grad_value, first, second, rate, decay):
    first_new = BETA_FIRST * first + (1.0 - BETA_FIRST) * grad_value
    second_new = BETA_SECOND * second + (1.0 - BETA_SECOND) * grad_value * grad_value
    first_hat = first_new / (1.0 - BETA_FIRST**STEP)
    second_hat = second_new / (1.0 - BETA_SECOND**STEP)
    weight_new = weight - rate * (first_hat / (jnp.sqrt(second_hat) + ADAM_EPS) + decay * weight)
    return (weight_new, first_new, second_new)


def shards(
    tokens, cotangent, dest, lengths, attn_weight, attn_first, attn_second,
    ffn_weight, ffn_first, ffn_second, vectors, vec_first, vec_second,
):
    core = lax.axis_index("core")

    def half(weight, base, width):
        return lax.dynamic_slice_in_dim(weight, base + core * width, width, 1).astype(bf16)

    shard = jnp.concatenate(
        [half(attn_weight, 0, 1536), half(attn_weight, 3 * D, 512), half(ffn_weight, 0, 2048), half(ffn_weight, FF, 2048)],
        axis=1,
    )
    x = tokens.reshape(ROWS, D)
    cot = cotangent.reshape(ROWS, D)
    ends = jnp.cumsum(lengths[:, 0], axis=1)
    seg = jnp.sum((dest[:, 0, :, None] >= ends[:, None, :]).astype(jnp.int32), axis=2)
    keep = (seg.reshape(ROWS, 1) < 8).astype(f32)

    seg_rows = jnp.broadcast_to(seg.astype(bf16)[:, None, :], (MB, 16, TOK))
    vec_shard = jnp.pad(vectors.astype(bf16), ((0, 4), (0, 0)))
    w_attn, ffn_out, vecs, held, mixed_t, mixed_full, lse = front(shard, vec_shard, x, seg_rows)
    w_attn = w_attn.reshape(D, 4 * D)
    w_ffn = ffn_out.reshape(D, 2 * FF)
    small = jnp.transpose(vecs.reshape(N_FSDP, 16, TOK), (1, 0, 2)).reshape(16, D).astype(f32)
    output, grad_one, x_t, o_t, h_t, f_t, a_low, du, g, vec_rows, grad_ready = dense(
        mixed_t, x, cot, keep, small, w_attn, w_ffn
    )
    total_attn, total_ffn, total_vec, square_sum, grad_qkv = back(
        (x_t, o_t, h_t, f_t),
        (a_low, du, g),
        vec_rows,
        grad_ready,
        held,
        mixed_full,
        lse,
    )
    grad_tokens = grad_one + dot_nt(grad_qkv, w_attn[:, : 3 * D])
    total_attn, total_ffn, total_vec = total_attn.astype(f32), total_ffn.astype(f32), total_vec.astype(f32)
    grad_norm = jnp.sqrt(square_sum)
    factor = jnp.minimum(1.0, CLIP_NORM / (grad_norm + 1e-06))
    rate_matrix = D ** (-0.5)
    attn_new, attn_first_new, attn_second_new = adamw(
        attn_weight, total_attn * factor, attn_first, attn_second, ATTN_RATE_SCALE * rate_matrix, WEIGHT_DECAY
    )
    ffn_new, ffn_first_new, ffn_second_new = adamw(
        ffn_weight, total_ffn * factor, ffn_first, ffn_second, rate_matrix, WEIGHT_DECAY
    )
    vec_new, vec_first_new, vec_second_new = adamw(
        vectors, total_vec * factor, vec_first, vec_second, RATE_VECTOR, 0.0
    )
    return (
        output.reshape(tokens.shape),
        grad_tokens.astype(bf16).reshape(tokens.shape),
        grad_norm,
        attn_new, attn_first_new, attn_second_new,
        ffn_new, ffn_first_new, ffn_second_new,
        vec_new, vec_first_new, vec_second_new,
        attn_new.astype(bf16),
        ffn_new.astype(bf16),
        total_vec[2] * factor,
    )


def solution(mesh):
    fine = Mesh(mesh.devices.reshape(2, 4, 2, 4, 2), ("yl", "z", "core", "x", "yh"))
    act = P(None, FSDP, CTX, None)
    row = P(FSDP, None)
    col = P(None, FSDP)
    return jax.shard_map(
        shards,
        mesh=fine,
        in_specs=(act, act, P(None, FSDP, CTX), P(None, FSDP, None), row, row, row, row, row, row, col, col, col),
        out_specs=(act, act, P(), row, row, row, row, row, row, col, col, col, row, row, P(FSDP)),
        check_vma=False,
    )
```

```python
import math

import jax
import jax.numpy as jnp
from jax import lax
from jax.experimental import pallas as pl
from jax.experimental.pallas import tpu as pltpu
from jax.sharding import Mesh, PartitionSpec as P

HEADS = 16
HEAD = 64
STEP = 10
MB = 2
TOK = 128
ROWS = MB * TOK
D = 1024
FF = 4096
N_CTX = 16
N_FSDP = 8
PACK = 2048
SENT = 208

NORM_EPS = 1e-05
CLIP_NORM = 1.0
BETA_FIRST = 0.9
BETA_SECOND = 0.999
ADAM_EPS = 1e-08
WEIGHT_DECAY = 0.01
RATE_VECTOR = 0.3
ATTN_RATE_SCALE = 3.0
NEG_LARGE = -1e30
SCALE2 = HEAD ** (-0.5) * math.log2(math.e)
SCALE = HEAD ** (-0.5)
CONTRACT_ROWS = (((0,), (0,)), ((), ()))
CONTRACT_COLS = (((1,), (1,)), ((), ()))
CTX = ("yl", "z", "core")
FSDP = ("x", "yh")
ALL = ("x", "yh", "yl", "z", "core")
BLK = 256
NBLK = PACK // BLK
f32 = jnp.float32
bf16 = jnp.bfloat16


def dot(a, b):
    return jnp.dot(a, b, preferred_element_type=f32)


def dot_nt(a, b):
    return lax.dot_general(a, b, CONTRACT_COLS, preferred_element_type=f32)


def dot_tn(a, b):
    return lax.dot_general(a, b, CONTRACT_ROWS, preferred_element_type=f32)


MESH_ID = pl.DeviceIdType.MESH
COLS = 512
N_BLK = 4
ORDERS = (("x", "z", "y"), ("z", "y", "x"), ("y", "x", "z"))
EARLY = ((2, 0), (2, 512), (2, 1024), (2, 1536), (3, 0), (3, 512), (3, 1024), (3, 1536), (1, 0))
PRODUCT = tuple(
    tuple(EARLY[b * 3 + p] for b in range(3)) + ((0, p * COLS),) for p in range(3)
)
VEC_AT = 2048
PART_COLS = (2048 + 128, 2048, 2048)
WIDTHS = (1536, 512, 2048, 2048)
OFFSETS = (0, 1536, 2048, 4096)
HALF_Z = 3072
TASKS = {}
for _n, _at in enumerate((7, 8, 9, 10, 11, 12, 13, 14, 15)):
    TASKS.setdefault(_at, []).append((0, _n // 3, _n % 3))
for _n, _at in enumerate(()):
    TASKS.setdefault(_at, []).append((1, _n // 3, _n % 3))


def coordinate(axis):
    if axis == "y":
        return lax.axis_index("yh") * 2 + lax.axis_index("yl")
    return lax.axis_index(axis)


def peer(axis, step):
    at = lax.rem(coordinate(axis) + step, 4)
    if axis == "y":
        return {"yh": at // 2, "yl": lax.rem(at, 2)}, at
    return {axis: at}, at


def pick(ref, axis, at, dims, cols):
    index = []
    for d in dims:
        if d == axis:
            index.append(at)
        elif axis == "y" and d == "yh":
            index.append(at // 2)
        elif axis == "y" and d == "yl":
            index.append(lax.rem(at, 2))
        else:
            index.append(slice(None))
    return ref.at[(*index, slice(None), cols)]


def dims_after(order, n):
    dims = ["x", "yh", "yl", "z"]
    for axis in order[:n]:
        for d in ("yh", "yl") if axis == "y" else (axis,):
            dims.remove(d)
    return dims


SIZES = {"x": 4, "yh": 2, "yl": 2, "z": 4}


def lead(order, n):
    return tuple(SIZES[d] for d in dims_after(order, n))


def send(src, dst, sems, index, to):
    return pltpu.make_async_remote_copy(
        src_ref=src, dst_ref=dst, send_sem=sems[0].at[index], recv_sem=sems[1].at[index],
        device_id=to, device_id_type=MESH_ID,
    )


def load_side(qkv_ref, m, keys, values, keys_t, values_t, seg_col):
    for s in range(N_CTX):
        at = slice(s * TOK, (s + 1) * TOK)
        key_t = qkv_ref[s, m, HEAD : 2 * HEAD, :]
        value_t = qkv_ref[s, m, 2 * HEAD : 3 * HEAD, :]
        keys[at, :] = key_t.T
        if values is not None:
            values[at, :] = value_t.T
        if keys_t is not None:
            keys_t[:, at] = key_t
        if values_t is not None:
            values_t[:, at] = value_t
        seg = qkv_ref[s, m, 3 * HEAD : 3 * HEAD + 1, :].astype(f32)
        seg_col[at, :] = jnp.broadcast_to(seg, (TOK, TOK)).T


def pair(ref, m, j, rows):
    return jnp.concatenate([ref[2 * j, m, rows, :], ref[2 * j + 1, m, rows, :]], axis=1)


def query_forward(held, m, j, out, full, lse_out, keys, values_t, seg_col, scores):
    query_t = pair(held, m, j, slice(0, HEAD))
    seg_row = pair(held, m, j, slice(3 * HEAD, 3 * HEAD + 1)).astype(f32)
    top = jnp.full((1, BLK), NEG_LARGE, f32)
    for k in range(NBLK):
        at = slice(k * BLK, (k + 1) * BLK)
        s = dot(keys[at, :], query_t) * SCALE2
        col = seg_col[at, :]
        same = jnp.concatenate([col, col], axis=1) == seg_row
        s = jnp.where(same, s, NEG_LARGE)
        scores[at, :] = s
        top = jnp.maximum(top, jnp.max(s, axis=0, keepdims=True))
    total = jnp.zeros((1, BLK), f32)
    acc = jnp.zeros((HEAD, BLK), f32)
    for k in range(NBLK):
        at = slice(k * BLK, (k + 1) * BLK)
        p = jnp.exp2(scores[at, :] - top)
        total = total + jnp.sum(p, axis=0, keepdims=True)
        acc = acc + dot(values_t[:, at], p.astype(bf16))
    acc = acc / total
    lse = top + jnp.log2(total)
    for half in range(2):
        cols = slice(half * TOK, (half + 1) * TOK)
        out[2 * j + half, m] = acc[:, cols].astype(bf16)
        full[2 * j + half, m] = acc[:, cols]
        lse_out[2 * j + half, m] = lse[:, cols]


GROUP_COLS = (1536, 2048, 2048, 512)
GROUP_AT = (0, 2048, 4096, 1536)
SPLITS = ((512, 1024), (1024, 1536), (1024, 1536), (128, 256))
N_COPY = 31
GROUPS = (3, 1, 2)
BEFORE = tuple((0, op) for op in ("z1", "x1", "z2", "y1", "z3", "x2", "x3", "y2", "z4", "x4", "x5"))
BEFORE += tuple((g, op) for op in ("z1", "z2", "y1") for g in GROUPS)
BEFORE += tuple((0, op) for op in ("y3", "z5", "sx", "sy", "sz", "got"))
PUSHED = tuple((g, op) for op in ("z3", "x1", "x2", "x3") for g in GROUPS)
STEPS = {
    0: tuple((g, "z4") for g in GROUPS),
    1: tuple((g, "y2") for g in GROUPS),
    3: tuple((g, "x4") for g in GROUPS),
    6: tuple((g, "x5") for g in GROUPS),
    9: tuple((g, "y3") for g in GROUPS),
    12: tuple((g, "z5") for g in GROUPS),
}
LAST = (
    tuple((g, op) for g in (3, 1) for op in ("sx", "sy", "sz")) + ((3, "got"),),
    tuple((2, op) for op in ("sx", "sy", "sz")) + ((1, "got"),),
    ((2, "got"),),
)


def ctx_device(t):
    return {"yl": t // 8, "z": lax.rem(t // 2, 4), "core": lax.rem(t, 2)}


def rows_at(start, size):
    return pl.ds(pl.multiple_of(start, 16), size)


class Gather:
    def __init__(self, g, shard, dest, sems, base, local_sem):
        core = lax.axis_index("core")
        x, z = lax.axis_index("x"), lax.axis_index("z")
        yh, yl = lax.axis_index("yh"), lax.axis_index("yl")
        y = yh * 2 + yl
        every = slice(None)
        zq, half = rows_at(z * 32, 32), rows_at(yl * 64, 64)
        cross = {"yh": 1 - yh, "yl": 1 - yl}
        count = [0]
        x_end, y_end = SPLITS[g]
        x_cols, y_cols, z_cols = slice(0, x_end), slice(x_end, y_end), slice(y_end, GROUP_COLS[g])

        def given(rows, cols):
            return shard.at[rows, GROUP_AT[g] + cols.start : GROUP_AT[g] + cols.stop]

        def make(src, dst, to):
            copy = send(src, dst, sems, base + count[0], to)
            count[0] += 1
            return copy

        def own(rows, cols, to):
            return make(given(rows, cols), dest(core, x, yh, rows, cols), to)

        def pass_on(xs, yhs, rows, cols, to):
            view = dest(core, xs, yhs, rows, cols)
            return make(view, view, to)

        x_to = {step: peer("x", step)[0] for step in (1, 2, 3)}
        y_to = {step: peer("y", step)[0] for step in (1, 3)}
        z_to = {step: peer("z", step)[0] for step in (1, 3)}
        x_before, x_after = lax.rem(x + 3, 4), lax.rem(x + 1, 4)
        y_before, y_after = lax.rem(y + 3, 4), lax.rem(y + 1, 4)
        z_before, z_after = lax.rem(z + 3, 4), lax.rem(z + 1, 4)
        self.copies = {
            "x1": [own(every, x_cols, cross)],
            "x2": [own(every, x_cols, x_to[s]) for s in (1, 3)],
            "z1": [own(zq, z_cols, cross)],
            "z2": [own(zq, z_cols, x_to[s]) for s in (1, 3, 2)],
            "y1": [own(half, y_cols, x_to[s]) for s in (1, 3, 2)],
            "x3": [pass_on(x, 1 - yh, every, x_cols, x_to[s]) for s in (1, 3)],
            "z3": [pass_on(x, 1 - yh, zq, z_cols, x_to[s]) for s in (1, 3, 2)],
            "y2": [pass_on(every, yh, half, y_cols, y_to[s]) for s in (1, 3)],
            "z4": [pass_on(every, every, zq, z_cols, z_to[s]) for s in (1, 3)],
            "x4": [
                pass_on(x_before, yh, slice(0, 64), x_cols, x_to[1]),
                pass_on(x_after, yh, slice(64, 128), x_cols, x_to[3]),
            ],
            "x5": [
                pass_on(x_before, 1 - yh, slice(0, 64), x_cols, x_to[1]),
                pass_on(x_after, 1 - yh, slice(64, 128), x_cols, x_to[3]),
            ],
            "y3": [
                pass_on(every, y_before // 2, rows_at(lax.rem(y_before, 2) * 64, 32), y_cols, y_to[1]),
                pass_on(every, y_after // 2, rows_at(lax.rem(y_after, 2) * 64 + 32, 32), y_cols, y_to[3]),
            ],
            "z5": [
                pass_on(every, every, rows_at(z_before * 32, 16), z_cols, z_to[1]),
                pass_on(every, every, rows_at(z_after * 32 + 16, 16), z_cols, z_to[3]),
            ],
        }
        for name, cols in (("sx", x_cols), ("sy", y_cols), ("sz", z_cols)):
            self.copies[name] = [pass_on(every, every, every, cols, {"core": 1 - core})]
        self.places = [
            pltpu.make_async_copy(given(rows, cols), dest(core, x, yh, rows, cols), local_sem.at[3 * g + n])
            for n, (rows, cols) in enumerate(((every, x_cols), (half, y_cols), (zq, z_cols)))
        ]

    needs = {
        "x3": ("x1",), "z3": ("z1",), "y2": ("y1",), "z4": ("z2", "z3"), "x4": ("x2",), "x5": ("x3",), "y3": ("y2",),
        "z5": ("z4",), "sx": ("x4", "x5"), "sy": ("y3",), "sz": ("z5",),
    }

    def step(self, name):
        if name == "got":
            for copy in (*self.copies["sx"], *self.copies["sy"], *self.copies["sz"]):
                copy.wait_recv()
            return
        if name == "end":
            for copies in self.copies.values():
                for copy in copies:
                    copy.wait_send()
            return
        for need in self.needs.get(name, ()):
            for copy in self.copies[need]:
                copy.wait_recv()
        if name == "z1":
            for copy in self.places:
                copy.start()
        if name == "z3":
            for copy in self.places:
                copy.wait()
        for copy in self.copies[name]:
            copy.start()


def greet_all():
    barrier = pltpu.get_barrier_semaphore()
    place = lax.axis_index(CTX)
    others = [ctx_device(lax.rem(place + d, N_CTX)) for d in range(1, N_CTX)]
    others += [peer(axis, step)[0] for axis in ("x", "y") for step in (1, 2, 3)]
    for other in others:
        pl.semaphore_signal(barrier, inc=1, device_id=other, device_id_type=MESH_ID)
    pl.semaphore_wait(barrier, len(others))


def front_kernel(
    shard, vec_shard, x_ref, seg_ref, cot_ref, keep_ref,
    out_attn, out_held, out_full, out_lse,
    out_ref, one_ref, x_t, o_t, h_t, f_t, a_low_ref, du_ref, g_ref, vec_ref, ready_ref,
    wa, w_one, w_two, w_out, vecs, small, ready, held, mixed, out_t, keys, values_t, seg_col, scores,
    mixed_rows, normal_one, slope, total,
    ag_send, ag_recv, vec_send, vec_recv, q_send, q_recv, o_send, o_recv, local_sem, out_sem,
):
    core = lax.axis_index("core")
    place = lax.axis_index(CTX)
    x, yh, yl = lax.axis_index("x"), lax.axis_index("yh"), lax.axis_index("yl")

    weights = (wa, w_one, w_two, w_out)

    def dest(g):
        def view(c, xs, yhs, rows, cols):
            return weights[g].at[c, xs, yhs, rows, cols]

        return view

    gathers = [
        Gather(g, shard, dest(g), (ag_send, ag_recv), g * N_COPY, local_sem) for g in range(4)
    ]
    vec_sems = (vec_send, vec_recv)
    vec_cross = send(vec_shard, vecs.at[x, yh], vec_sems, 0, {"yh": 1 - yh, "yl": 1 - yl})
    vec_x = [send(vec_shard, vecs.at[x, yh], vec_sems, s, peer("x", s)[0]) for s in (1, 2, 3)]
    vec_x2 = [
        send(vecs.at[x, 1 - yh], vecs.at[x, 1 - yh], vec_sems, 3 + s, peer("x", s)[0]) for s in (1, 2, 3)
    ]
    greet_all()
    for copy in (vec_cross, *vec_x):
        copy.start()
    done = set()

    def stages(todo):
        for g, n in todo:
            if (g, n) not in done:
                done.add((g, n))
                gathers[g].step(n)

    stages(BEFORE[:4])
    vecs[x, yh] = vec_shard[...]
    for s in range(N_CTX):
        ready[s, :, 3 * HEAD :, :] = seg_ref[...]
    vec_cross.wait_recv()
    for copy in vec_x2:
        copy.start()
    stages(BEFORE)
    vec_cross.wait_send()
    for copy in (*vec_x, *vec_x2):
        copy.wait()
    for f in range(N_FSDP):
        small[:, f * TOK : (f + 1) * TOK] = vecs[f // 2, f % 2].astype(f32)

    for part in range(6):
        c, col = part // 3, (part % 3) * 512
        kind, first = part // 2, (part % 2) * 8
        value = jnp.zeros((ROWS, 512), f32)
        weight = wa[c, :, :, :, col : col + 512].reshape(D, 512)
        value = dot(x_ref[...], weight)
        if kind != 1:
            row = 0 if kind == 0 else 1
            value = value + small[row : row + 1, first * HEAD : first * HEAD + 512]
        value = value.T.astype(bf16)
        for h in range(8):
            for m in range(MB):
                ready[first + h, m, kind * HEAD : (kind + 1) * HEAD, :] = value[
                    h * HEAD : (h + 1) * HEAD, m * TOK : (m + 1) * TOK
                ]
    swaps = [[], []]
    for m in range(MB):
        for d in range(1, N_CTX):
            t = lax.rem(place + d, N_CTX)
            swaps[m].append(send(ready.at[t, m], held.at[place, m], (q_send, q_recv), m * N_CTX + d, ctx_device(t)))
            swaps[m][-1].start()
    held[place] = ready[place]
    returns = [[], []]
    for m in range(MB):
        for d in range(1, N_CTX):
            t = lax.rem(place + d, N_CTX)
            returns[m].append(
                send(out_t.at[t, m], mixed.at[place, m], (o_send, o_recv), m * N_CTX + d, ctx_device(t))
            )
    stages(PUSHED)
    outs = [(wa.at[c], out_attn.at[:, :, :, c * 1536 : (c + 1) * 1536]) for c in range(2)]
    outs = [pltpu.make_async_copy(src, dst, out_sem.at[n]) for n, (src, dst) in enumerate(outs)]
    for copy in outs:
        copy.start()
    for m in range(MB):
        for copy in swaps[m]:
            copy.wait_recv()
        load_side(held, m, keys, None, None, values_t, seg_col)

        def query_block(j, _, m=m):
            for at, todo in STEPS.items():
                if at // NBLK == m:

                    @pl.when(j == at % NBLK)
                    def _(todo=todo):
                        stages(todo)

            query_forward(held, m, j, out_t, out_full, out_lse, keys, values_t, seg_col, scores)
            return 0

        lax.fori_loop(0, NBLK, query_block, 0)
        for copy in returns[m]:
            copy.start()
        mixed[place, m] = out_t[place, m]
    outs.append(pltpu.make_async_copy(held, out_held, out_sem.at[4]))
    outs[-1].start()

    def before(n):
        stages(LAST[n])

    for m in range(MB):
        for copy in returns[m]:
            copy.wait_recv()
    dense_part(
        mixed, x_ref, cot_ref, keep_ref, small, w_out, w_one, w_two, before,
        out_ref, one_ref, x_t, o_t, h_t, f_t, a_low_ref, du_ref, g_ref, vec_ref, ready_ref,
        mixed_rows, normal_one, slope, total,
    )
    for m in range(MB):
        for copy in (*swaps[m], *returns[m]):
            copy.wait_send()
    stages([(g, "end") for g in (0, *GROUPS)])
    for copy in outs:
        copy.wait()


def front(shard, vec_shard, x, seg_rows, cot, keep):
    vmem = pl.BlockSpec(memory_space=pltpu.VMEM)
    hbm = pl.BlockSpec(memory_space=pl.ANY)
    sem = lambda n: pltpu.SemaphoreType.DMA((n,))
    turned = jax.ShapeDtypeStruct((D, ROWS), bf16)
    return pl.pallas_call(
        front_kernel,
        in_specs=[hbm, vmem, vmem, vmem, vmem, vmem],
        out_specs=[hbm, hbm] + [vmem] * 13,
        out_shape=[
            jax.ShapeDtypeStruct((4, 2, TOK, 3 * D), bf16),
            jax.ShapeDtypeStruct((N_CTX, MB, SENT, TOK), bf16),
            jax.ShapeDtypeStruct((N_CTX, MB, HEAD, TOK), f32),
            jax.ShapeDtypeStruct((N_CTX, MB, 1, TOK), f32),
            jax.ShapeDtypeStruct((ROWS, D), bf16),
            jax.ShapeDtypeStruct((ROWS, D), f32),
            turned, turned, turned, turned,
            jax.ShapeDtypeStruct((ROWS, D), bf16),
            jax.ShapeDtypeStruct((ROWS, FF), bf16),
            jax.ShapeDtypeStruct((ROWS, FF), bf16),
            jax.ShapeDtypeStruct((N_FSDP, 16, TOK), f32),
            jax.ShapeDtypeStruct((HEADS, MB, HEAD, TOK), bf16),
        ],
        scratch_shapes=[
            *(pltpu.VMEM((2, 4, 2, TOK, GROUP_COLS[g]), bf16) for g in range(4)),
            pltpu.VMEM((4, 2, 16, TOK), bf16),
            pltpu.VMEM((16, D), f32),
            pltpu.VMEM((N_CTX, MB, SENT, TOK), bf16),
            pltpu.VMEM((N_CTX, MB, SENT, TOK), bf16),
            pltpu.VMEM((N_CTX, MB, HEAD, TOK), bf16),
            pltpu.VMEM((N_CTX, MB, HEAD, TOK), bf16),
            pltpu.VMEM((PACK, HEAD), bf16),
            pltpu.VMEM((HEAD, PACK), bf16),
            pltpu.VMEM((PACK, TOK), f32),
            pltpu.VMEM((PACK, BLK), f32),
            pltpu.VMEM((ROWS, D), bf16),
            pltpu.VMEM((ROWS, D), f32),
            pltpu.VMEM((ROWS, FF), f32),
            pltpu.VMEM((ROWS, D), f32),
            sem(4 * N_COPY), sem(4 * N_COPY), sem(7), sem(7), sem(32), sem(32), sem(32), sem(32),
            sem(12), sem(6),
        ],
        compiler_params=pltpu.CompilerParams(
            collective_id=2, has_side_effects=True, vmem_limit_bytes=60 * 2**20
        ),
        cost_estimate=pl.CostEstimate(
            flops=4 * MB * PACK * PACK * HEAD + 2 * ROWS * D * (5 * D + 4 * FF), bytes_accessed=32 * 2**20,
            transcendentals=MB * PACK * PACK,
        ),
        name="front",
    )(shard, vec_shard, x, seg_rows, cot, keep)


def back_kernel(
    left_x, left_o, left_h, left_f, right_o, right_u, right_g, vec, grad_ready, held_in, full, lse, w_qkv,
    out_attn, out_ffn, out_vec, out_sq, out_x,
    peer_left, own_right, peer_right, own_vec, peer_vec,
    w_0, w_1, w_2, s1_0, s1_1, s1_2, s2_0, s2_1, s2_2,
    r1_0, r1_1, r1_2, r2_0, r2_1, r2_2, r3_0, r3_1, r3_2,
    gathered, sq_z, sq_y, sq_x, sq_c,
    held, grad_held, out_t, landed, right_q, keys, values, keys_t, seg_col, acc_kv, square_acc, w_part,
    swap_send, swap_recv, ring_send, ring_recv, gather_send, gather_recv, sq_send, sq_recv,
    o_send, o_recv, q_send, q_recv, local_sem, out_sem,
):
    core = lax.axis_index("core")
    other = 1 - core
    place = lax.axis_index(CTX)
    row_place = lax.axis_index("yl") * 4 + lax.axis_index("z")
    lefts = (left_x, left_o, left_h, left_f)
    rights = (None, right_o, right_u, right_g)
    works, firsts, seconds = (w_0, w_1, w_2), (s1_0, s1_1, s1_2), (s2_0, s2_1, s2_2)
    recvs = ((r1_0, r1_1, r1_2), (r2_0, r2_1, r2_2), (r3_0, r3_1, r3_2))
    to_core = {"core": other}

    fetch = pltpu.make_async_copy(held_in, held, local_sem.at[0])
    fetch.start()
    fetches = [fetch]
    for i in range(1, 4):
        cols = pl.ds(pl.multiple_of(core * WIDTHS[i], 512), WIDTHS[i])
        fetches.append(
            pltpu.make_async_copy(
                rights[i].at[:, cols], own_right.at[:, OFFSETS[i] : OFFSETS[i] + WIDTHS[i]], local_sem.at[i]
            )
        )
        fetches[-1].start()
    greet_all()

    pushes, returns = [[], []], [[], []]
    for m in range(MB):
        for d in range(1, N_CTX):
            t = lax.rem(place + d, N_CTX)
            to = ctx_device(t)
            pushes[m].append(
                send(grad_ready.at[t, m], grad_held.at[place, m], (o_send, o_recv), m * N_CTX + d, to)
            )
            returns[m].append(send(out_t.at[t, m], landed.at[place, m], (q_send, q_recv), m * N_CTX + d, to))
    swaps = []
    for i in (2, 3, 1, 0):
        swaps.append(send(lefts[i], peer_left.at[i], (swap_send, swap_recv), 2 * i, to_core))
        if i:
            from_cols = pl.ds(pl.multiple_of(other * WIDTHS[i], 512), WIDTHS[i])
            swaps.append(
                send(
                    rights[i].at[:, from_cols], peer_right.at[:, OFFSETS[i] : OFFSETS[i] + WIDTHS[i]],
                    (swap_send, swap_recv), 2 * i + 1, to_core,
                )
            )
    for m in range(MB):
        for copy in pushes[m]:
            copy.start()
    for copy in swaps:
        copy.start()
    grad_held[place] = grad_ready[place]
    for copy in fetches:
        copy.wait()

    def blocks(b):
        out = [(p, b * COLS, COLS) for p in range(3)]
        if b == 3:
            out.append((0, VEC_AT, 128))
        return out

    def copies(p, phase, at, width):
        order = ORDERS[p]
        axis = order[phase]
        cols = slice(at, at + width)
        src = (works, firsts, seconds)[phase][p]
        out = []
        for step in (1, 2, 3):
            to, index = peer(axis, step)
            chunk = pick(src, axis, index, dims_after(order, phase), cols)
            land = recvs[phase][p].at[(step - 1, *(slice(None),) * (len(lead(order, phase + 1)) + 1), cols)]
            out.append(
                send(chunk, land, (ring_send, ring_recv), ((p * 3 + phase) * 5 + at // COLS) * 3 + step - 1, to)
            )
        return out

    def multiply(p, b):
        i, col = PRODUCT[p][b]
        if i == 0:
            mine = right_q.at[:, pl.ds(pl.multiple_of(core * WIDTHS[0] + col, 512), COLS)]
        else:
            mine = own_right.at[:, OFFSETS[i] + col : OFFSETS[i] + col + COLS]
        theirs = peer_right.at[:, OFFSETS[i] + col : OFFSETS[i] + col + COLS]

        def rows_block(x, _):
            rows = pl.ds(pl.multiple_of(x * 256, 256), 256)
            value = dot(lefts[i][rows, :], mine[...]) + dot(peer_left[i, rows, :], theirs[...])
            works[p][x, :, :, :, :, b * COLS : (b + 1) * COLS] = value.astype(bf16).reshape(2, 2, 4, 16, COLS)
            return 0

        lax.fori_loop(0, 4, rows_block, 0)

    def reduce(phase, p, at, width):
        cols = slice(at, at + width)
        order = ORDERS[p]
        axis = order[phase]
        src = (works, firsts, seconds)[phase][p]
        land = recvs[phase][p]
        for copy in copies(p, phase, at, width):
            copy.wait()
        own = pick(src, axis, coordinate(axis), dims_after(order, phase), cols)
        rest = len(lead(order, phase + 1)) - 1
        if phase < 2:
            dst = (firsts, seconds)[phase][p]

            def add(n, _):
                tail = (*(slice(None),) * (rest + 1), cols)
                inner = (*(slice(None),) * (rest + 1), slice(None))
                value = own[(n, *inner)].astype(f32)
                for step in range(3):
                    value = value + land[(step, n, *tail)].astype(f32)
                dst[(n, *tail)] = value.astype(bf16)
                return 0

            lax.fori_loop(0, lead(order, phase + 1)[0], add, 0)
            for copy in copies(p, phase + 1, at, width):
                copy.start()
            return
        value = own[...].astype(f32)
        for step in range(3):
            value = value + land[step, :, cols].astype(f32)
        to = p * 2048 + at if width == COLS else 6144
        gathered[core, row_place, :, to : to + width] = value.astype(bf16)
        square = value * value
        if width != COLS:
            square = square * jnp.where(core == 0, 1.0, 0.0)
        squares = square_acc[...]
        for c in range(0, width, 128):
            squares = squares + square[:8, c : c + 128] + square[8:, c : c + 128]
        square_acc[...] = squares

    square_acc[...] = jnp.zeros_like(square_acc)
    for copy in swaps:
        copy.wait()
    for b in range(3):
        for p, at, width in blocks(b):
            multiply(p, b)
            for copy in copies(p, 0, at, width):
                copy.start()

    for m in range(MB):
        load_side(held, m, keys, values, keys_t, None, seg_col)
        acc_kv[...] = jnp.zeros_like(acc_kv)
        for copy in pushes[m]:
            copy.wait_recv()

        def query_block(j, _, m=m):
            for at, tasks in TASKS.items():
                if at // NBLK == m:

                    @pl.when(j == at % NBLK)
                    def _(tasks=tasks):
                        for phase, b, p in tasks:
                            reduce(phase, p, b * COLS, COLS)

            query_t = pair(held, m, j, slice(0, HEAD))
            seg_row = pair(held, m, j, slice(3 * HEAD, 3 * HEAD + 1)).astype(f32)
            grad_t = pair(grad_held, m, j, slice(0, HEAD))
            row_lse = pair(lse, m, j, slice(0, 1))
            delta = jnp.sum(grad_t.astype(f32) * pair(full, m, j, slice(0, HEAD)), axis=0, keepdims=True)
            acc_q = jnp.zeros((HEAD, BLK), f32)
            none = jnp.zeros((BLK, HEAD), bf16)
            sides = jnp.concatenate(
                [jnp.concatenate([query_t.T, none], axis=1), jnp.concatenate([none, grad_t.T], axis=1)], axis=0
            )
            for k in range(NBLK):
                at = slice(k * BLK, (k + 1) * BLK)
                s = dot(keys[at, :], query_t) * SCALE2 - row_lse
                col = seg_col[at, :]
                same = jnp.concatenate([col, col], axis=1) == seg_row
                p = jnp.exp2(jnp.where(same, s, NEG_LARGE))
                dp = dot(values[at, :], grad_t)
                ds = (p * (dp - delta)).astype(bf16)
                acc_q = acc_q + dot(keys_t[:, at], ds)
                acc_kv[at, :] += dot(jnp.concatenate([ds, p.astype(bf16)], axis=1), sides)
            acc_q = (acc_q * SCALE).astype(bf16)
            out_t[2 * j, m, :HEAD, :] = acc_q[:, :TOK]
            out_t[2 * j + 1, m, :HEAD, :] = acc_q[:, TOK:]
            return 0

        lax.fori_loop(0, NBLK, query_block, 0)
        for s in range(N_CTX):
            at = slice(s * TOK, (s + 1) * TOK)
            both = acc_kv[at, :].T
            out_t[s, m, HEAD : 2 * HEAD, :] = (both[:HEAD] * SCALE).astype(bf16)
            out_t[s, m, 2 * HEAD :, :] = both[HEAD:].astype(bf16)
        for copy in returns[m]:
            copy.start()
        landed[place, m] = out_t[place, m]

    fetch_w = [
        pltpu.make_async_copy(w_qkv.at[:, n * COLS : (n + 1) * COLS], w_part.at[n % 2], local_sem.at[4 + n])
        for n in range(6)
    ]
    done = [task for tasks in TASKS.values() for task in tasks]
    for phase in (0, 1):
        for b in range(3):
            for p in range(3):
                if (phase, b, p) not in done:
                    reduce(phase, p, b * COLS, COLS)
    gives = []
    for m in range(MB):
        for copy in pushes[m]:
            copy.wait_send()
        for copy in returns[m]:
            copy.wait()
        if m == 0:
            fetch_w[0].start()
            fetch_w[1].start()
        for i in range(HEADS // 2):
            for kind in range(3):
                rows = slice(kind * HEAD, (kind + 1) * HEAD)
                both = jnp.concatenate([landed[2 * i, m, rows, :], landed[2 * i + 1, m, rows, :]], axis=0)
                right_q[m * TOK : (m + 1) * TOK, kind * D + i * 128 : kind * D + (i + 1) * 128] = both.T
        rows = slice(m * TOK, (m + 1) * TOK)
        gives.append(
            send(
                right_q.at[rows, pl.ds(pl.multiple_of(other * WIDTHS[0], 512), WIDTHS[0])],
                peer_right.at[rows, 0 : WIDTHS[0]], (swap_send, swap_recv), (1, 9)[m], to_core,
            )
        )
        gives[m].start()
    sum_q = jnp.sum(right_q[:, :D].astype(f32), axis=0, keepdims=True)
    sum_v = jnp.sum(right_q[:, 2 * D :].astype(f32), axis=0, keepdims=True)
    row = lax.broadcasted_iota(jnp.int32, (16, TOK), 0)
    own_vec[...] = jnp.zeros_like(own_vec)
    for f in range(N_FSDP):
        cols = slice(f * TOK, (f + 1) * TOK)
        value = jnp.where(row == 0, sum_q[:, cols], jnp.where(row == 1, sum_v[:, cols], vec[f]))
        own_vec[f // 2, f % 2, 0, 0] = value.astype(bf16)
    give_vec = send(own_vec, peer_vec, (swap_send, swap_recv), 8, to_core)
    give_vec.start()
    for copy in gives:
        copy.wait()
    for p, at, width in blocks(3):
        if width == COLS:
            multiply(p, 3)
        else:
            give_vec.wait()
            works[0][:, :, :, :, :, VEC_AT:] = (own_vec[...].astype(f32) + peer_vec[...].astype(f32)).astype(bf16)
        for copy in copies(p, 0, at, width):
            copy.start()
    for n in range(6):
        fetch_w[n].wait()
        part = dot_nt(right_q[:, n * COLS : (n + 1) * COLS], w_part[n % 2])
        if n == 0:
            out_x[...] = part
        else:
            out_x[...] += part
        if n < 4:
            fetch_w[n + 2].start()
    for b in range(3):
        for p, at, width in blocks(b):
            reduce(2, p, at, width)
    for phase in range(3):
        for p, at, width in blocks(3):
            reduce(phase, p, at, width)
    squares = square_acc[...]
    yl, z = lax.axis_index("yl"), lax.axis_index("z")
    z_first, y_first = slice(0, HALF_Z), slice(HALF_Z, 6272)
    to_y = {"yl": 1 - yl}
    gather_sems = (gather_send, gather_recv)
    sq_sems = (sq_send, sq_recv)

    def spread(buffer, axis, base):
        at = coordinate(axis)
        out = []
        for step in (1, 2, 3):
            out.append(send(buffer.at[at], buffer.at[at], sq_sems, base + step - 1, peer(axis, step)[0]))
        return out

    def total(buffer):
        return (buffer[0] + buffer[1]) + (buffer[2] + buffer[3])

    sq_z[z] = squares
    squares_z = spread(sq_z, "z", 0)
    first_z = [
        send(gathered.at[core, row_place, :, z_first], gathered.at[core, row_place, :, z_first], gather_sems, step - 1, peer("z", step)[0])
        for step in (1, 2, 3)
    ]
    first_y = send(gathered.at[core, row_place, :, y_first], gathered.at[core, row_place, :, y_first], gather_sems, 3, to_y)
    for copy in (*squares_z, *first_z, first_y):
        copy.start()
    for copy in squares_z:
        copy.wait()
    y_at = coordinate("y")
    sq_y[y_at] = total(sq_z)
    squares_y = spread(sq_y, "y", 3)
    for copy in squares_y:
        copy.start()
    for copy in (*first_z, first_y):
        copy.wait()
    quarter = pl.ds(yl * 4, 4)
    second_y = send(
        gathered.at[core, quarter, :, z_first], gathered.at[core, quarter, :, z_first], gather_sems, 4, to_y
    )
    second_y.start()
    second_z = []
    for step in (1, 2, 3):
        for half in range(2):
            view = gathered.at[core, half * 4 + z, :, y_first]
            second_z.append(send(view, view, gather_sems, 5 + (step - 1) * 2 + half, peer("z", step)[0]))
    for copy in second_z:
        copy.start()
    for copy in squares_y:
        copy.wait()
    x_at = coordinate("x")
    sq_x[x_at] = total(sq_y)
    squares_x = spread(sq_x, "x", 6)
    for copy in squares_x:
        copy.start()
    for copy in squares_x:
        copy.wait()
    sq_c[core] = total(sq_x)
    square_c = send(sq_c.at[core], sq_c.at[core], sq_sems, 9, to_core)
    square_c.start()
    square_c.wait()
    out_sq[...] = sq_c[0] + sq_c[1]
    second_y.wait()
    for copy in second_z:
        copy.wait()
    last = send(gathered.at[core], gathered.at[core], gather_sems, 11, to_core)
    last.start()
    last.wait()
    locals_ = []
    for c in range(2):
        for p in range(3):
            for b in range(4):
                i, col = PRODUCT[p][b]
                target, base = ((out_attn, 0), (out_attn, 3072), (out_ffn, 0), (out_ffn, FF))[i]
                base = base + c * WIDTHS[i] + col
                at = p * 2048 + b * COLS
                locals_.append(
                    pltpu.make_async_copy(
                        gathered.at[c, :, :, at : at + COLS], target.at[:, :, base : base + COLS],
                        out_sem.at[len(locals_)],
                    )
                )
    locals_.append(pltpu.make_async_copy(gathered.at[0, :, :, 6144:], out_vec, out_sem.at[len(locals_)]))
    for copy in locals_:
        copy.start()
    for copy in locals_:
        copy.wait()


def back(lefts, rights, vec, grad_ready, held, full, lse, w_qkv):
    vmem = pl.BlockSpec(memory_space=pltpu.VMEM)
    hbm = pl.BlockSpec(memory_space=pl.ANY)
    scratch = [
        pltpu.VMEM((4, D, ROWS), bf16),
        pltpu.VMEM((ROWS, 6144), bf16),
        pltpu.VMEM((ROWS, 6144), bf16),
        pltpu.VMEM((4, 2, 2, 4, 16, 128), bf16),
        pltpu.VMEM((4, 2, 2, 4, 16, 128), bf16),
    ]
    for n in range(3):
        scratch += [pltpu.VMEM((*lead(ORDERS[p], n), 16, PART_COLS[p]), bf16) for p in range(3)]
    for n in range(1, 4):
        scratch += [pltpu.VMEM((3, *lead(ORDERS[p], n), 16, PART_COLS[p]), bf16) for p in range(3)]
    scratch += [
        pltpu.VMEM((2, 8, 16, 6272), bf16),
        pltpu.VMEM((4, 8, 128), f32),
        pltpu.VMEM((4, 8, 128), f32),
        pltpu.VMEM((4, 8, 128), f32),
        pltpu.VMEM((2, 8, 128), f32),
        pltpu.VMEM((N_CTX, MB, SENT, TOK), bf16),
        pltpu.VMEM((N_CTX, MB, HEAD, TOK), bf16),
        pltpu.VMEM((N_CTX, MB, 3 * HEAD, TOK), bf16),
        pltpu.VMEM((N_CTX, MB, 3 * HEAD, TOK), bf16),
        pltpu.VMEM((ROWS, 3 * D), bf16),
        pltpu.VMEM((PACK, HEAD), bf16),
        pltpu.VMEM((PACK, HEAD), bf16),
        pltpu.VMEM((HEAD, PACK), bf16),
        pltpu.VMEM((PACK, TOK), f32),
        pltpu.VMEM((PACK, 2 * HEAD), f32),
        pltpu.VMEM((8, 128), f32),
        pltpu.VMEM((2, D, COLS), bf16),
    ]
    for count in (10, 10, 135, 135, 12, 12, 10, 10, 32, 32, 32, 32, 10, 25):
        scratch.append(pltpu.SemaphoreType.DMA((count,)))
    out = pl.pallas_call(
        back_kernel,
        in_specs=[vmem] * 4 + [hbm] * 3 + [vmem, vmem, hbm, vmem, vmem, hbm],
        out_specs=[hbm, hbm, hbm, vmem, vmem],
        out_shape=[
            jax.ShapeDtypeStruct((8, 16, 4 * D), bf16),
            jax.ShapeDtypeStruct((8, 16, 2 * FF), bf16),
            jax.ShapeDtypeStruct((8, 16, 128), bf16),
            jax.ShapeDtypeStruct((8, 128), f32),
            jax.ShapeDtypeStruct((ROWS, D), f32),
        ],
        scratch_shapes=scratch,
        compiler_params=pltpu.CompilerParams(
            collective_id=1, has_side_effects=True, vmem_limit_bytes=60 * 2**20
        ),
        cost_estimate=pl.CostEstimate(
            flops=2 * 512 * D * 6144 + 10 * MB * PACK * PACK * HEAD, bytes_accessed=16 * 2**20,
            transcendentals=MB * PACK * PACK,
        ),
        name="back",
    )(*lefts, *rights, vec, grad_ready, held, full, lse, w_qkv)
    return out[0].reshape(TOK, 4 * D), out[1].reshape(TOK, 2 * FF), out[2][0, :12], jnp.sum(out[3]), out[4]


def layer_stats(values, gain_row, shift_row):
    center = values - jnp.mean(values, axis=-1, keepdims=True)
    inverse = lax.rsqrt(jnp.mean(center * center, axis=-1, keepdims=True) + NORM_EPS)
    normal = center * inverse
    return (normal * gain_row + shift_row, normal, inverse)


def layer_back(grad_value, normal, inverse, gain_row):
    scaled = grad_value * gain_row
    return inverse * (
        scaled
        - jnp.mean(scaled, axis=-1, keepdims=True)
        - normal * jnp.mean(scaled * normal, axis=-1, keepdims=True)
    )


N_CHUNK = 8
CHUNK = FF // N_CHUNK
ERF_TOP = (
    -2.72614225801306e-10, 2.77068142495902e-08, -2.10102402082508e-06, -5.69250639462346e-05,
    -7.34990630326855e-04, -2.95459980854025e-03, -1.60960333262415e-02,
)
ERF_LOW = (
    -1.45660718464996e-05, -2.13374055278905e-04, -1.68282697438203e-03, -7.37332916720468e-03,
    -1.42647390514189e-02,
)


def erf(value):
    value = jnp.clip(value, -4.0, 4.0)
    square = value * value
    top, low = jnp.full_like(square, ERF_TOP[0]), jnp.full_like(square, ERF_LOW[0])
    for c in ERF_TOP[1:]:
        top = top * square + c
    for c in ERF_LOW[1:]:
        low = low * square + c
    return value * top / low


def w_block(ref, n):
    per = ref.shape[-1] // CHUNK
    at = (n % per) * CHUNK
    return ref[n // per, :, :, :, at : at + CHUNK].reshape(D, CHUNK)


def dense_part(
    mixed_ref, x_ref, cot_ref, keep_ref, small_ref, w_out, w_one, w_two, before,
    out_ref, one_ref, x_t, o_t, h_t, f_t, a_low_ref, du_ref, g_ref, vec_ref, ready_ref,
    mixed, normal_one_ref, slope, total,
):
    def row(i):
        return small_ref[i : i + 1, :]

    def put(i, value):
        for f in range(N_FSDP):
            vec_ref[f, i : i + 1, :] = value[:, f * TOK : (f + 1) * TOK]

    def sums(value):
        return jnp.sum(value, axis=0, keepdims=True)

    vec_ref[...] = jnp.zeros_like(vec_ref)
    for m in range(MB):
        tok = slice(m * TOK, (m + 1) * TOK)
        for i in range(HEADS // 2):
            both = jnp.concatenate([mixed_ref[2 * i, m], mixed_ref[2 * i + 1, m]], axis=0)
            o_t[i * 128 : (i + 1) * 128, tok] = both
            mixed[tok, i * 128 : (i + 1) * 128] = both.T
    before(0)
    branch = jnp.concatenate([dot(mixed[...], w_block(w_out, n)) for n in range(2)], axis=1)
    normed_one, normal_one, inverse_one = layer_stats(x_ref[...].astype(f32) + branch + row(2), row(4), row(5))
    normal_one_ref[...] = normal_one
    normed_low = normed_one.astype(bf16)
    h_t[...] = normed_low.T
    total[...] = normed_one + row(3)
    before(1)
    for n in range(N_CHUNK):
        cols = slice(n * CHUNK, (n + 1) * CHUNK)
        bias = small_ref[8 + n // 2 : 9 + n // 2, (n % 2) * CHUNK : (n % 2 + 1) * CHUNK]
        u = dot(normed_low, w_block(w_one, n)) + bias
        share = 0.5 + 0.5 * erf(u * math.sqrt(0.5))
        g_ref[:, cols] = (u * share).astype(bf16)
        slope[:, cols] = share + u * (jnp.exp(-0.5 * u * u) * (1.0 / math.sqrt(2.0 * math.pi)))
    before(2)
    for n in range(N_CHUNK):
        total[...] += dot_nt(g_ref[:, n * CHUNK : (n + 1) * CHUNK], w_block(w_two, n))
    output, normal_two, inverse_two = layer_stats(total[...], row(6), row(7))
    keep = keep_ref[...]
    out_ref[...] = (output * keep).astype(bf16)
    grad_out = cot_ref[...].astype(f32) * keep
    put(6, sums(grad_out * normal_two))
    put(7, sums(grad_out))
    grad_two = layer_back(grad_out, normal_two, inverse_two, row(6))
    f_low = grad_two.astype(bf16)
    f_t[...] = f_low.T
    put(3, sums(f_low.astype(f32)))
    total[...] = grad_two
    for n in range(N_CHUNK):
        cols = slice(n * CHUNK, (n + 1) * CHUNK)
        du = (dot(f_low, w_block(w_two, n)) * slope[:, cols]).astype(bf16)
        du_ref[:, cols] = du
        part = sums(du.astype(f32))
        for i in range(CHUNK // TOK):
            f = (n % 2) * (CHUNK // TOK) + i
            vec_ref[f, 8 + n // 2 : 9 + n // 2, :] = part[:, i * TOK : (i + 1) * TOK]
        total[...] += dot_nt(du, w_block(w_one, n))
    grad_normed = total[...]
    normal_one = normal_one_ref[...]
    put(4, sums(grad_normed * normal_one))
    put(5, sums(grad_normed))
    grad_one = layer_back(grad_normed, normal_one, inverse_one, row(4))
    one_ref[...] = grad_one
    a_low = grad_one.astype(bf16)
    a_low_ref[...] = a_low
    put(2, sums(a_low.astype(f32)))
    for n in range(2):
        part = a_low[:, n * CHUNK : (n + 1) * CHUNK]
        part = dot_nt(part, w_block(w_out, n))
        grad_mixed = part if n == 0 else grad_mixed + part
    grad_mixed = grad_mixed.T.astype(bf16)
    for h in range(HEADS):
        for m in range(MB):
            ready_ref[h, m] = grad_mixed[h * HEAD : (h + 1) * HEAD, m * TOK : (m + 1) * TOK]
    x_t[...] = x_ref[...].T


def adamw(weight, grad_value, first, second, rate, decay):
    first_new = BETA_FIRST * first + (1.0 - BETA_FIRST) * grad_value
    second_new = BETA_SECOND * second + (1.0 - BETA_SECOND) * grad_value * grad_value
    first_hat = first_new / (1.0 - BETA_FIRST**STEP)
    second_hat = second_new / (1.0 - BETA_SECOND**STEP)
    weight_new = weight - rate * (first_hat / (jnp.sqrt(second_hat) + ADAM_EPS) + decay * weight)
    return (weight_new, first_new, second_new)


def shards(
    tokens, cotangent, dest, lengths, attn_weight, attn_first, attn_second,
    ffn_weight, ffn_first, ffn_second, vectors, vec_first, vec_second,
):
    core = lax.axis_index("core")

    def half(weight, base, width):
        return lax.dynamic_slice_in_dim(weight, base + core * width, width, 1).astype(bf16)

    shard = jnp.concatenate(
        [half(attn_weight, 0, 1536), half(attn_weight, 3 * D, 512), half(ffn_weight, 0, 2048), half(ffn_weight, FF, 2048)],
        axis=1,
    )
    x = tokens.reshape(ROWS, D)
    cot = cotangent.reshape(ROWS, D)
    ends = jnp.cumsum(lengths[:, 0], axis=1)
    seg = jnp.sum((dest[:, 0, :, None] >= ends[:, None, :]).astype(jnp.int32), axis=2)
    keep = (seg.reshape(ROWS, 1) < 8).astype(f32)

    seg_rows = jnp.broadcast_to(seg.astype(bf16)[:, None, :], (MB, 16, TOK))
    vec_shard = jnp.pad(vectors.astype(bf16), ((0, 4), (0, 0)))
    (
        w_qkv, held, mixed_full, lse, output, grad_one, x_t, o_t, h_t, f_t, a_low, du, g, vec_rows, grad_ready,
    ) = front(shard, vec_shard, x, seg_rows, cot, keep)
    total_attn, total_ffn, total_vec, square_sum, grad_x = back(
        (x_t, o_t, h_t, f_t),
        (a_low, du, g),
        vec_rows,
        grad_ready,
        held,
        mixed_full,
        lse,
        w_qkv.reshape(D, 3 * D),
    )
    grad_tokens = grad_one + grad_x
    total_attn, total_ffn, total_vec = total_attn.astype(f32), total_ffn.astype(f32), total_vec.astype(f32)
    grad_norm = jnp.sqrt(square_sum)
    factor = jnp.minimum(1.0, CLIP_NORM / (grad_norm + 1e-06))
    rate_matrix = D ** (-0.5)
    attn_new, attn_first_new, attn_second_new = adamw(
        attn_weight, total_attn * factor, attn_first, attn_second, ATTN_RATE_SCALE * rate_matrix, WEIGHT_DECAY
    )
    ffn_new, ffn_first_new, ffn_second_new = adamw(
        ffn_weight, total_ffn * factor, ffn_first, ffn_second, rate_matrix, WEIGHT_DECAY
    )
    vec_new, vec_first_new, vec_second_new = adamw(
        vectors, total_vec * factor, vec_first, vec_second, RATE_VECTOR, 0.0
    )
    return (
        output.reshape(tokens.shape),
        grad_tokens.astype(bf16).reshape(tokens.shape),
        grad_norm,
        attn_new, attn_first_new, attn_second_new,
        ffn_new, ffn_first_new, ffn_second_new,
        vec_new, vec_first_new, vec_second_new,
        attn_new.astype(bf16),
        ffn_new.astype(bf16),
        total_vec[2] * factor,
    )


def solution(mesh):
    fine = Mesh(mesh.devices.reshape(2, 4, 2, 4, 2), ("yl", "z", "core", "x", "yh"))
    act = P(None, FSDP, CTX, None)
    row = P(FSDP, None)
    col = P(None, FSDP)
    return jax.shard_map(
        shards,
        mesh=fine,
        in_specs=(act, act, P(None, FSDP, CTX), P(None, FSDP, None), row, row, row, row, row, row, col, col, col),
        out_specs=(act, act, P(), row, row, row, row, row, row, col, col, col, row, row, P(FSDP)),
        check_vma=False,
    )
```

```python
import math

import jax
import jax.numpy as jnp
from jax import lax
from jax.experimental import pallas as pl
from jax.experimental.pallas import tpu as pltpu
from jax.sharding import Mesh, PartitionSpec as P

HEADS = 16
HEAD = 64
STEP = 10
MB = 2
TOK = 128
ROWS = MB * TOK
D = 1024
FF = 4096
N_CTX = 16
N_FSDP = 8
PACK = 2048
SENT = 208

NORM_EPS = 1e-05
CLIP_NORM = 1.0
BETA_FIRST = 0.9
BETA_SECOND = 0.999
ADAM_EPS = 1e-08
WEIGHT_DECAY = 0.01
RATE_VECTOR = 0.3
ATTN_RATE_SCALE = 3.0
NEG_LARGE = -1e30
SCALE2 = HEAD ** (-0.5) * math.log2(math.e)
SCALE = HEAD ** (-0.5)
CONTRACT_ROWS = (((0,), (0,)), ((), ()))
CONTRACT_COLS = (((1,), (1,)), ((), ()))
CTX = ("yl", "z", "core")
FSDP = ("x", "yh")
ALL = ("x", "yh", "yl", "z", "core")
BLK = 256
NBLK = PACK // BLK
f32 = jnp.float32
bf16 = jnp.bfloat16


def dot(a, b):
    return jnp.dot(a, b, preferred_element_type=f32)


def dot_nt(a, b):
    return lax.dot_general(a, b, CONTRACT_COLS, preferred_element_type=f32)


def dot_tn(a, b):
    return lax.dot_general(a, b, CONTRACT_ROWS, preferred_element_type=f32)


MESH_ID = pl.DeviceIdType.MESH
COLS = 512
N_BLK = 4
ORDERS = (("x", "z", "y"), ("z", "y", "x"), ("y", "x", "z"))
EARLY = ((0, 0), (1, 0), (2, 0), (0, 1), (1, 1), (2, 1), (0, 2), (1, 2), (2, 2))
N_EARLY = (3, 3, 3)
EARLY_PRODUCT = ((2, 0), (2, 512), (2, 1024), (2, 1536), (3, 0), (3, 512), (3, 1024), (3, 1536), (1, 0))
PRODUCT = {part_block: product for part_block, product in zip(EARLY, EARLY_PRODUCT)}
PRODUCT.update({(p, N_EARLY[p]): (0, p * COLS) for p in range(3)})
PART_AT = (0, 2048, 4096, 6144)
VEC_AT = 3072
WIDTHS = (1536, 512, 2048, 2048)
OFFSETS = (0, 1536, 2048, 4096)
HALF_Z = 3072
TASKS = {}
for _n, _at in enumerate((2, 2, 2, 5, 5, 5, 8, 8, 8)):
    TASKS.setdefault(_at, []).append(("relay", *EARLY[_n]))
for _n, _at in enumerate((7, 7, 7, 10, 10, 10, 13, 13, 13)):
    TASKS.setdefault(_at, []).append((0, *EARLY[_n]))


def coordinate(axis):
    if axis == "y":
        return lax.axis_index("yh") * 2 + lax.axis_index("yl")
    return lax.axis_index(axis)


def peer(axis, step):
    at = lax.rem(coordinate(axis) + step, 4)
    if axis == "y":
        return {"yh": at // 2, "yl": lax.rem(at, 2)}, at
    return {axis: at}, at


def pick(ref, axis, at, dims):
    index = []
    for d in dims:
        if d == axis:
            index.append(at)
        elif axis == "y" and d == "yh":
            index.append(at // 2)
        elif axis == "y" and d == "yl":
            index.append(lax.rem(at, 2))
        else:
            index.append(slice(None))
    return ref.at[tuple(index)]


def dims_after(order, n):
    dims = ["x", "yh", "yl", "z"]
    for axis in order[:n]:
        for d in ("yh", "yl") if axis == "y" else (axis,):
            dims.remove(d)
    return dims


SIZES = {"x": 4, "yh": 2, "yl": 2, "z": 4}


def lead(order, n):
    return tuple(SIZES[d] for d in dims_after(order, n))


def send(src, dst, sems, index, to):
    return pltpu.make_async_remote_copy(
        src_ref=src, dst_ref=dst, send_sem=sems[0].at[index], recv_sem=sems[1].at[index],
        device_id=to, device_id_type=MESH_ID,
    )


def load_side(qkv_ref, m, keys, values, keys_t, values_t, seg_col):
    for s in range(N_CTX):
        at = slice(s * TOK, (s + 1) * TOK)
        key_t = qkv_ref[s, m, HEAD : 2 * HEAD, :]
        value_t = qkv_ref[s, m, 2 * HEAD : 3 * HEAD, :]
        keys[at, :] = key_t.T
        if values is not None:
            values[at, :] = value_t.T
        if keys_t is not None:
            keys_t[:, at] = key_t
        if values_t is not None:
            values_t[:, at] = value_t
        seg = qkv_ref[s, m, 3 * HEAD : 3 * HEAD + 1, :].astype(f32)
        seg_col[at, :] = jnp.broadcast_to(seg, (TOK, TOK)).T


def pair(ref, m, j, rows):
    return jnp.concatenate([ref[2 * j, m, rows, :], ref[2 * j + 1, m, rows, :]], axis=1)


def query_forward(held, m, j, out, full, lse_out, keys, values_t, seg_col, scores):
    query_t = pair(held, m, j, slice(0, HEAD))
    seg_row = pair(held, m, j, slice(3 * HEAD, 3 * HEAD + 1)).astype(f32)
    top = jnp.full((1, BLK), NEG_LARGE, f32)
    for k in range(NBLK):
        at = slice(k * BLK, (k + 1) * BLK)
        s = dot(keys[at, :], query_t) * SCALE2
        col = seg_col[at, :]
        same = jnp.concatenate([col, col], axis=1) == seg_row
        s = jnp.where(same, s, NEG_LARGE)
        scores[at, :] = s
        top = jnp.maximum(top, jnp.max(s, axis=0, keepdims=True))
    total = jnp.zeros((1, BLK), f32)
    acc = jnp.zeros((HEAD, BLK), f32)
    for k in range(NBLK):
        at = slice(k * BLK, (k + 1) * BLK)
        p = jnp.exp2(scores[at, :] - top)
        total = total + jnp.sum(p, axis=0, keepdims=True)
        acc = acc + dot(values_t[:, at], p.astype(bf16))
    acc = acc / total
    lse = top + jnp.log2(total)
    for half in range(2):
        cols = slice(half * TOK, (half + 1) * TOK)
        out[2 * j + half, m] = acc[:, cols].astype(bf16)
        full[2 * j + half, m] = acc[:, cols]
        lse_out[2 * j + half, m] = lse[:, cols]


GROUP_COLS = (1536, 2048, 2048, 512)
GROUP_AT = (0, 2048, 4096, 1536)
SPLITS = ((512, 1024), (1024, 1536), (1024, 1536), (128, 256))
N_COPY = 31
GROUPS = (3, 1, 2)
BEFORE = tuple((0, op) for op in ("z1", "x1", "z2", "y1", "z3", "x2", "x3", "y2", "z4", "x4", "x5"))
BEFORE += tuple((g, op) for op in ("z1", "z2", "y1") for g in GROUPS)
BEFORE += tuple((0, op) for op in ("y3", "z5", "sx", "sy", "sz", "got"))
PUSHED = tuple((g, op) for op in ("z3", "x1", "x2", "x3") for g in GROUPS)
STEPS = {
    0: tuple((g, "z4") for g in GROUPS),
    1: tuple((g, "y2") for g in GROUPS),
    3: tuple((g, "x4") for g in GROUPS),
    6: tuple((g, "x5") for g in GROUPS),
    9: tuple((g, "y3") for g in GROUPS),
    12: tuple((g, "z5") for g in GROUPS),
}
LAST = (
    tuple((g, op) for g in (3, 1) for op in ("sx", "sy", "sz")) + ((3, "got"),),
    tuple((2, op) for op in ("sx", "sy", "sz")) + ((1, "got"),),
    ((2, "got"),),
)


def ctx_device(t):
    return {"yl": t // 8, "z": lax.rem(t // 2, 4), "core": lax.rem(t, 2)}


def rows_at(start, size):
    return pl.ds(pl.multiple_of(start, 16), size)


class Gather:
    def __init__(self, g, shard, dest, sems, base, local_sem):
        core = lax.axis_index("core")
        x, z = lax.axis_index("x"), lax.axis_index("z")
        yh, yl = lax.axis_index("yh"), lax.axis_index("yl")
        y = yh * 2 + yl
        every = slice(None)
        zq, half = rows_at(z * 32, 32), rows_at(yl * 64, 64)
        cross = {"yh": 1 - yh, "yl": 1 - yl}
        count = [0]
        x_end, y_end = SPLITS[g]
        x_cols, y_cols, z_cols = slice(0, x_end), slice(x_end, y_end), slice(y_end, GROUP_COLS[g])

        def given(rows, cols):
            return shard.at[rows, GROUP_AT[g] + cols.start : GROUP_AT[g] + cols.stop]

        def make(src, dst, to):
            copy = send(src, dst, sems, base + count[0], to)
            count[0] += 1
            return copy

        def own(rows, cols, to):
            return make(given(rows, cols), dest(core, x, yh, rows, cols), to)

        def pass_on(xs, yhs, rows, cols, to):
            view = dest(core, xs, yhs, rows, cols)
            return make(view, view, to)

        x_to = {step: peer("x", step)[0] for step in (1, 2, 3)}
        y_to = {step: peer("y", step)[0] for step in (1, 3)}
        z_to = {step: peer("z", step)[0] for step in (1, 3)}
        x_before, x_after = lax.rem(x + 3, 4), lax.rem(x + 1, 4)
        y_before, y_after = lax.rem(y + 3, 4), lax.rem(y + 1, 4)
        z_before, z_after = lax.rem(z + 3, 4), lax.rem(z + 1, 4)
        self.copies = {
            "x1": [own(every, x_cols, cross)],
            "x2": [own(every, x_cols, x_to[s]) for s in (1, 3)],
            "z1": [own(zq, z_cols, cross)],
            "z2": [own(zq, z_cols, x_to[s]) for s in (1, 3, 2)],
            "y1": [own(half, y_cols, x_to[s]) for s in (1, 3, 2)],
            "x3": [pass_on(x, 1 - yh, every, x_cols, x_to[s]) for s in (1, 3)],
            "z3": [pass_on(x, 1 - yh, zq, z_cols, x_to[s]) for s in (1, 3, 2)],
            "y2": [pass_on(every, yh, half, y_cols, y_to[s]) for s in (1, 3)],
            "z4": [pass_on(every, every, zq, z_cols, z_to[s]) for s in (1, 3)],
            "x4": [
                pass_on(x_before, yh, slice(0, 64), x_cols, x_to[1]),
                pass_on(x_after, yh, slice(64, 128), x_cols, x_to[3]),
            ],
            "x5": [
                pass_on(x_before, 1 - yh, slice(0, 64), x_cols, x_to[1]),
                pass_on(x_after, 1 - yh, slice(64, 128), x_cols, x_to[3]),
            ],
            "y3": [
                pass_on(every, y_before // 2, rows_at(lax.rem(y_before, 2) * 64, 32), y_cols, y_to[1]),
                pass_on(every, y_after // 2, rows_at(lax.rem(y_after, 2) * 64 + 32, 32), y_cols, y_to[3]),
            ],
            "z5": [
                pass_on(every, every, rows_at(z_before * 32, 16), z_cols, z_to[1]),
                pass_on(every, every, rows_at(z_after * 32 + 16, 16), z_cols, z_to[3]),
            ],
        }
        for name, cols in (("sx", x_cols), ("sy", y_cols), ("sz", z_cols)):
            self.copies[name] = [pass_on(every, every, every, cols, {"core": 1 - core})]
        self.places = [
            pltpu.make_async_copy(given(rows, cols), dest(core, x, yh, rows, cols), local_sem.at[3 * g + n])
            for n, (rows, cols) in enumerate(((every, x_cols), (half, y_cols), (zq, z_cols)))
        ]

    needs = {
        "x3": ("x1",), "z3": ("z1",), "y2": ("y1",), "z4": ("z2", "z3"), "x4": ("x2",), "x5": ("x3",), "y3": ("y2",),
        "z5": ("z4",), "sx": ("x4", "x5"), "sy": ("y3",), "sz": ("z5",),
    }

    def step(self, name):
        if name == "got":
            for copy in (*self.copies["sx"], *self.copies["sy"], *self.copies["sz"]):
                copy.wait_recv()
            return
        if name == "end":
            for copies in self.copies.values():
                for copy in copies:
                    copy.wait_send()
            return
        for need in self.needs.get(name, ()):
            for copy in self.copies[need]:
                copy.wait_recv()
        if name == "z1":
            for copy in self.places:
                copy.start()
        if name == "z3":
            for copy in self.places:
                copy.wait()
        for copy in self.copies[name]:
            copy.start()


def greet_all():
    barrier = pltpu.get_barrier_semaphore()
    place = lax.axis_index(CTX)
    others = [ctx_device(lax.rem(place + d, N_CTX)) for d in range(1, N_CTX)]
    others += [peer(axis, step)[0] for axis in ("x", "y") for step in (1, 2, 3)]
    for other in others:
        pl.semaphore_signal(barrier, inc=1, device_id=other, device_id_type=MESH_ID)
    pl.semaphore_wait(barrier, len(others))


def front_kernel(
    shard, vec_shard, x_ref, seg_ref, cot_ref, keep_ref,
    out_attn, out_held, out_full, out_lse,
    out_ref, one_ref, x_t, o_t, h_t, f_t, a_low_ref, du_ref, g_ref, vec_ref, ready_ref,
    wa, w_one, w_two, w_out, vecs, small, ready, held, mixed, out_t, keys, values_t, seg_col, scores,
    mixed_rows, normal_one, slope, total,
    ag_send, ag_recv, vec_send, vec_recv, q_send, q_recv, o_send, o_recv, local_sem, out_sem,
):
    core = lax.axis_index("core")
    place = lax.axis_index(CTX)
    x, yh, yl = lax.axis_index("x"), lax.axis_index("yh"), lax.axis_index("yl")

    weights = (wa, w_one, w_two, w_out)

    def dest(g):
        def view(c, xs, yhs, rows, cols):
            return weights[g].at[c, xs, yhs, rows, cols]

        return view

    gathers = [
        Gather(g, shard, dest(g), (ag_send, ag_recv), g * N_COPY, local_sem) for g in range(4)
    ]
    vec_sems = (vec_send, vec_recv)
    vec_cross = send(vec_shard, vecs.at[x, yh], vec_sems, 0, {"yh": 1 - yh, "yl": 1 - yl})
    vec_x = [send(vec_shard, vecs.at[x, yh], vec_sems, s, peer("x", s)[0]) for s in (1, 2, 3)]
    vec_x2 = [
        send(vecs.at[x, 1 - yh], vecs.at[x, 1 - yh], vec_sems, 3 + s, peer("x", s)[0]) for s in (1, 2, 3)
    ]
    greet_all()
    for copy in (vec_cross, *vec_x):
        copy.start()
    done = set()

    def stages(todo):
        for g, n in todo:
            if (g, n) not in done:
                done.add((g, n))
                gathers[g].step(n)

    stages(BEFORE[:4])
    vecs[x, yh] = vec_shard[...]
    for s in range(N_CTX):
        ready[s, :, 3 * HEAD :, :] = seg_ref[...]
    vec_cross.wait_recv()
    for copy in vec_x2:
        copy.start()
    stages(BEFORE)
    vec_cross.wait_send()
    for copy in (*vec_x, *vec_x2):
        copy.wait()
    for f in range(N_FSDP):
        small[:, f * TOK : (f + 1) * TOK] = vecs[f // 2, f % 2].astype(f32)

    for part in range(6):
        c, col = part // 3, (part % 3) * 512
        kind, first = part // 2, (part % 2) * 8
        value = jnp.zeros((ROWS, 512), f32)
        weight = wa[c, :, :, :, col : col + 512].reshape(D, 512)
        value = dot(x_ref[...], weight)
        if kind != 1:
            row = 0 if kind == 0 else 1
            value = value + small[row : row + 1, first * HEAD : first * HEAD + 512]
        value = value.T.astype(bf16)
        for h in range(8):
            for m in range(MB):
                ready[first + h, m, kind * HEAD : (kind + 1) * HEAD, :] = value[
                    h * HEAD : (h + 1) * HEAD, m * TOK : (m + 1) * TOK
                ]
    swaps = [[], []]
    for m in range(MB):
        for d in range(1, N_CTX):
            t = lax.rem(place + d, N_CTX)
            swaps[m].append(send(ready.at[t, m], held.at[place, m], (q_send, q_recv), m * N_CTX + d, ctx_device(t)))
            swaps[m][-1].start()
    held[place] = ready[place]
    returns = [[], []]
    for m in range(MB):
        for d in range(1, N_CTX):
            t = lax.rem(place + d, N_CTX)
            returns[m].append(
                send(out_t.at[t, m], mixed.at[place, m], (o_send, o_recv), m * N_CTX + d, ctx_device(t))
            )
    stages(PUSHED)
    outs = [(wa.at[c], out_attn.at[:, :, :, c * 1536 : (c + 1) * 1536]) for c in range(2)]
    outs = [pltpu.make_async_copy(src, dst, out_sem.at[n]) for n, (src, dst) in enumerate(outs)]
    for copy in outs:
        copy.start()
    for m in range(MB):
        for copy in swaps[m]:
            copy.wait_recv()
        load_side(held, m, keys, None, None, values_t, seg_col)

        def query_block(j, _, m=m):
            for at, todo in STEPS.items():
                if at // NBLK == m:

                    @pl.when(j == at % NBLK)
                    def _(todo=todo):
                        stages(todo)

            query_forward(held, m, j, out_t, out_full, out_lse, keys, values_t, seg_col, scores)
            return 0

        lax.fori_loop(0, NBLK, query_block, 0)
        for copy in returns[m]:
            copy.start()
        mixed[place, m] = out_t[place, m]
    outs.append(pltpu.make_async_copy(held, out_held, out_sem.at[4]))
    outs[-1].start()

    def before(n):
        stages(LAST[n])

    for m in range(MB):
        for copy in returns[m]:
            copy.wait_recv()
    dense_part(
        mixed, x_ref, cot_ref, keep_ref, small, w_out, w_one, w_two, before,
        out_ref, one_ref, x_t, o_t, h_t, f_t, a_low_ref, du_ref, g_ref, vec_ref, ready_ref,
        mixed_rows, normal_one, slope, total,
    )
    for m in range(MB):
        for copy in (*swaps[m], *returns[m]):
            copy.wait_send()
    stages([(g, "end") for g in (0, *GROUPS)])
    for copy in outs:
        copy.wait()


def front(shard, vec_shard, x, seg_rows, cot, keep):
    vmem = pl.BlockSpec(memory_space=pltpu.VMEM)
    hbm = pl.BlockSpec(memory_space=pl.ANY)
    sem = lambda n: pltpu.SemaphoreType.DMA((n,))
    turned = jax.ShapeDtypeStruct((D, ROWS), bf16)
    return pl.pallas_call(
        front_kernel,
        in_specs=[hbm, vmem, vmem, vmem, vmem, vmem],
        out_specs=[hbm, hbm] + [vmem] * 13,
        out_shape=[
            jax.ShapeDtypeStruct((4, 2, TOK, 3 * D), bf16),
            jax.ShapeDtypeStruct((N_CTX, MB, SENT, TOK), bf16),
            jax.ShapeDtypeStruct((N_CTX, MB, HEAD, TOK), f32),
            jax.ShapeDtypeStruct((N_CTX, MB, 1, TOK), f32),
            jax.ShapeDtypeStruct((ROWS, D), bf16),
            jax.ShapeDtypeStruct((ROWS, D), f32),
            turned, turned, turned, turned,
            jax.ShapeDtypeStruct((ROWS, D), bf16),
            jax.ShapeDtypeStruct((ROWS, FF), bf16),
            jax.ShapeDtypeStruct((ROWS, FF), bf16),
            jax.ShapeDtypeStruct((N_FSDP, 16, TOK), f32),
            jax.ShapeDtypeStruct((HEADS, MB, HEAD, TOK), bf16),
        ],
        scratch_shapes=[
            *(pltpu.VMEM((2, 4, 2, TOK, GROUP_COLS[g]), bf16) for g in range(4)),
            pltpu.VMEM((4, 2, 16, TOK), bf16),
            pltpu.VMEM((16, D), f32),
            pltpu.VMEM((N_CTX, MB, SENT, TOK), bf16),
            pltpu.VMEM((N_CTX, MB, SENT, TOK), bf16),
            pltpu.VMEM((N_CTX, MB, HEAD, TOK), bf16),
            pltpu.VMEM((N_CTX, MB, HEAD, TOK), bf16),
            pltpu.VMEM((PACK, HEAD), bf16),
            pltpu.VMEM((HEAD, PACK), bf16),
            pltpu.VMEM((PACK, TOK), f32),
            pltpu.VMEM((PACK, BLK), f32),
            pltpu.VMEM((ROWS, D), bf16),
            pltpu.VMEM((ROWS, D), f32),
            pltpu.VMEM((ROWS, FF), f32),
            pltpu.VMEM((ROWS, D), f32),
            sem(4 * N_COPY), sem(4 * N_COPY), sem(7), sem(7), sem(32), sem(32), sem(32), sem(32),
            sem(12), sem(6),
        ],
        compiler_params=pltpu.CompilerParams(
            collective_id=2, has_side_effects=True, vmem_limit_bytes=60 * 2**20
        ),
        cost_estimate=pl.CostEstimate(
            flops=4 * MB * PACK * PACK * HEAD + 2 * ROWS * D * (5 * D + 4 * FF), bytes_accessed=32 * 2**20,
            transcendentals=MB * PACK * PACK,
        ),
        name="front",
    )(shard, vec_shard, x, seg_rows, cot, keep)


def back_kernel(
    left_x, left_o, left_h, left_f, right_o, right_u, right_g, vec, grad_ready, held_in, full, lse, w_qkv,
    out_attn, out_ffn, out_vec, out_sq, out_x,
    peer_left, own_right, peer_right, own_vec, peer_vec,
    *rest_refs,
):
    stores, rest_refs = rest_refs[:24], rest_refs[24:]
    (
    gathered, sq_z, sq_y, sq_x, sq_c,
    held, grad_held, out_t, landed, right_q, keys, values, keys_t, seg_col, acc_kv, square_acc, w_part,
    swap_send, swap_recv, ring_send, ring_recv, gather_send, gather_recv, sq_send, sq_recv,
    o_send, o_recv, q_send, q_recv, local_sem, out_sem,
    ) = rest_refs
    core = lax.axis_index("core")
    other = 1 - core
    place = lax.axis_index(CTX)
    row_place = lax.axis_index("yl") * 4 + lax.axis_index("z")
    lefts = (left_x, left_o, left_h, left_f)
    rights = (None, right_o, right_u, right_g)
    to_core = {"core": other}

    fetch = pltpu.make_async_copy(held_in, held, local_sem.at[0])
    fetch.start()
    fetches = [fetch]
    for i in range(1, 4):
        cols = pl.ds(pl.multiple_of(core * WIDTHS[i], 512), WIDTHS[i])
        fetches.append(
            pltpu.make_async_copy(
                rights[i].at[:, cols], own_right.at[:, OFFSETS[i] : OFFSETS[i] + WIDTHS[i]], local_sem.at[i]
            )
        )
        fetches[-1].start()
    greet_all()

    pushes, returns = [[], []], [[], []]
    for m in range(MB):
        for d in range(1, N_CTX):
            t = lax.rem(place + d, N_CTX)
            to = ctx_device(t)
            pushes[m].append(
                send(grad_ready.at[t, m], grad_held.at[place, m], (o_send, o_recv), m * N_CTX + d, to)
            )
            returns[m].append(send(out_t.at[t, m], landed.at[place, m], (q_send, q_recv), m * N_CTX + d, to))
    swaps = []
    for i in (2, 3, 1, 0):
        swaps.append(send(lefts[i], peer_left.at[i], (swap_send, swap_recv), 2 * i, to_core))
        if i:
            from_cols = pl.ds(pl.multiple_of(other * WIDTHS[i], 512), WIDTHS[i])
            swaps.append(
                send(
                    rights[i].at[:, from_cols], peer_right.at[:, OFFSETS[i] : OFFSETS[i] + WIDTHS[i]],
                    (swap_send, swap_recv), 2 * i + 1, to_core,
                )
            )
    for m in range(MB):
        for copy in pushes[m]:
            copy.start()
    for copy in swaps:
        copy.start()
    grad_held[place] = grad_ready[place]
    for copy in fetches:
        copy.wait()

    late = [(p, N_EARLY[p] * COLS, COLS) for p in range(3)] + [(0, VEC_AT, 128)]
    early = [(p, b * COLS, COLS) for p, b in EARLY]

    def number(p, at, width):
        return 12 if width != COLS else PART_AT[p] // COLS + at // COLS

    def store(kind, p, at, width):
        return stores[4 * kind + 3].at[0] if width != COLS else stores[4 * kind + p].at[at // COLS]

    def copies(p, phase, at, width):
        order = ORDERS[p]
        axis = order[phase]
        out = []
        for step in (1, 2, 3):
            to, index = peer(axis, step)
            chunk = pick(store(phase, p, at, width), axis, index, dims_after(order, phase))
            land = store(3 + phase, p, at, width).at[step - 1]
            out.append(
                send(
                    chunk, land, (ring_send, ring_recv), 39 + 39 * phase + number(p, at, width) * 3 + step - 1, to
                )
            )
        return out

    def first_copies(p, at, width):
        order = ORDERS[p]
        axis = order[0]
        n = lead(order, 1)[0]
        halves = (slice(0, n // 2), slice(n // 2, n))
        (up, up_at), (_, far_at), (down, down_at) = (peer(axis, step) for step in (1, 2, 3))
        out = []
        for k, (index, half, slot, to) in enumerate(
            (
                (far_at, 0, 2, up), (far_at, 1, 2, down), (up_at, 1, 0, up), (down_at, 0, 1, down),
                (up_at, 0, 0, up), (down_at, 1, 1, down),
            )
        ):
            chunk = pick(store(0, p, at, width), axis, index, dims_after(order, 0)).at[halves[half]]
            land = store(3, p, at, width).at[slot, halves[half]]
            out.append(send(chunk, land, (ring_send, ring_recv), number(p, at, width) * 6 + k, to))
        return out

    def begin(p, at, width):
        for copy in first_copies(p, at, width)[:4]:
            copy.start()

    def relay(p, at, width):
        order = ORDERS[p]
        axis = order[0]
        n = lead(order, 1)[0]
        all_copies = first_copies(p, at, width)
        land = store(3, p, at, width)
        for half, step in ((0, 1), (1, 3)):
            all_copies[half].wait_recv()
            own = pick(store(0, p, at, width), axis, peer(axis, step)[1], dims_after(order, 0))

            def add(i, _, own=own):
                own[i] = (own[i].astype(f32) + land[2, i].astype(f32)).astype(bf16)
                return 0

            lax.fori_loop(half * (n // 2), (half + 1) * (n // 2), add, 0)
            all_copies[4 + half].start()

    def multiply(p, b):
        i, col = PRODUCT[(p, b)]
        if i == 0:
            mine = right_q.at[:, pl.ds(pl.multiple_of(core * WIDTHS[0] + col, 512), COLS)]
        else:
            mine = own_right.at[:, OFFSETS[i] + col : OFFSETS[i] + col + COLS]
        theirs = peer_right.at[:, OFFSETS[i] + col : OFFSETS[i] + col + COLS]

        def rows_block(x, _):
            rows = pl.ds(pl.multiple_of(x * 256, 256), 256)
            value = dot(lefts[i][rows, :], mine[...]) + dot(peer_left[i, rows, :], theirs[...])
            stores[p][b, x] = value.astype(bf16).reshape(2, 2, 4, 16, COLS)
            return 0

        lax.fori_loop(0, 4, rows_block, 0)

    def reduce(phase, p, at, width):
        order = ORDERS[p]
        axis = order[phase]
        land = store(3 + phase, p, at, width)
        if phase == 0:
            all_copies = first_copies(p, at, width)
            for copy in all_copies[:2]:
                copy.wait_send()
            for copy in all_copies[2:]:
                copy.wait()
        else:
            for copy in copies(p, phase, at, width):
                copy.wait()
        own = pick(store(phase, p, at, width), axis, coordinate(axis), dims_after(order, phase))
        if phase < 2:
            dst = store(phase + 1, p, at, width)

            def add(n, _):
                value = own[n].astype(f32)
                for step in range(3 if phase else 2):
                    value = value + land[step, n].astype(f32)
                dst[n] = value.astype(bf16)
                return 0

            lax.fori_loop(0, lead(order, phase + 1)[0], add, 0)
            for copy in copies(p, phase + 1, at, width):
                copy.start()
            return
        value = own[...].astype(f32)
        for step in range(3):
            value = value + land[step].astype(f32)
        to = PART_AT[p] + at if width == COLS else 6144
        gathered[core, row_place, :, to : to + width] = value.astype(bf16)
        square = value * value
        if width != COLS:
            square = square * jnp.where(core == 0, 1.0, 0.0)
        squares = square_acc[...]
        for c in range(0, width, 128):
            squares = squares + square[:8, c : c + 128] + square[8:, c : c + 128]
        square_acc[...] = squares

    def run_task(phase, p, b):
        if phase == "relay":
            relay(p, b * COLS, COLS)
        else:
            reduce(phase, p, b * COLS, COLS)

    square_acc[...] = jnp.zeros_like(square_acc)
    for copy in swaps:
        copy.wait()
    for p, at, width in early:
        multiply(p, at // COLS)
        begin(p, at, width)

    for m in range(MB):
        load_side(held, m, keys, values, keys_t, None, seg_col)
        acc_kv[...] = jnp.zeros_like(acc_kv)
        for copy in pushes[m]:
            copy.wait_recv()

        def query_block(j, _, m=m):
            for at, tasks in TASKS.items():
                if at // NBLK == m:

                    @pl.when(j == at % NBLK)
                    def _(tasks=tasks):
                        for phase, p, b in tasks:
                            run_task(phase, p, b)

            query_t = pair(held, m, j, slice(0, HEAD))
            seg_row = pair(held, m, j, slice(3 * HEAD, 3 * HEAD + 1)).astype(f32)
            grad_t = pair(grad_held, m, j, slice(0, HEAD))
            row_lse = pair(lse, m, j, slice(0, 1))
            delta = jnp.sum(grad_t.astype(f32) * pair(full, m, j, slice(0, HEAD)), axis=0, keepdims=True)
            acc_q = jnp.zeros((HEAD, BLK), f32)
            none = jnp.zeros((BLK, HEAD), bf16)
            sides = jnp.concatenate(
                [jnp.concatenate([query_t.T, none], axis=1), jnp.concatenate([none, grad_t.T], axis=1)], axis=0
            )
            block = lambda k: slice(k * BLK, (k + 1) * BLK)
            ahead = (dot(keys[block(0), :], query_t), dot(values[block(0), :], grad_t))
            behind = None
            for k in range(NBLK + 1):
                if k < NBLK:
                    at = block(k)
                    s, dp = ahead
                    if k + 1 < NBLK:
                        ahead = (dot(keys[block(k + 1), :], query_t), dot(values[block(k + 1), :], grad_t))
                if behind is not None:
                    to, ds, pb = behind
                    acc_q = acc_q + dot(keys_t[:, to], ds)
                    acc_kv[to, :] += dot(jnp.concatenate([ds, pb], axis=1), sides)
                if k < NBLK:
                    col = seg_col[at, :]
                    same = jnp.concatenate([col, col], axis=1) == seg_row
                    p = jnp.exp2(jnp.where(same, s * SCALE2 - row_lse, NEG_LARGE))
                    behind = (at, (p * (dp - delta)).astype(bf16), p.astype(bf16))
            acc_q = (acc_q * SCALE).astype(bf16)
            out_t[2 * j, m, :HEAD, :] = acc_q[:, :TOK]
            out_t[2 * j + 1, m, :HEAD, :] = acc_q[:, TOK:]
            return 0

        lax.fori_loop(0, NBLK, query_block, 0)
        for s in range(N_CTX):
            at = slice(s * TOK, (s + 1) * TOK)
            both = acc_kv[at, :].T
            out_t[s, m, HEAD : 2 * HEAD, :] = (both[:HEAD] * SCALE).astype(bf16)
            out_t[s, m, 2 * HEAD :, :] = both[HEAD:].astype(bf16)
        for copy in returns[m]:
            copy.start()
        landed[place, m] = out_t[place, m]

    fetch_w = [
        pltpu.make_async_copy(w_qkv.at[:, n * COLS : (n + 1) * COLS], w_part.at[n % 2], local_sem.at[4 + n])
        for n in range(6)
    ]
    done = [task for tasks in TASKS.values() for task in tasks]
    for phase in ("relay", 0, 1):
        for p, b in EARLY:
            if (phase, p, b) not in done:
                run_task(phase, p, b)
    gives = []
    for m in range(MB):
        for copy in pushes[m]:
            copy.wait_send()
        for copy in returns[m]:
            copy.wait()
        if m == 0:
            fetch_w[0].start()
            fetch_w[1].start()
        for i in range(HEADS // 2):
            for kind in range(3):
                rows = slice(kind * HEAD, (kind + 1) * HEAD)
                both = jnp.concatenate([landed[2 * i, m, rows, :], landed[2 * i + 1, m, rows, :]], axis=0)
                right_q[m * TOK : (m + 1) * TOK, kind * D + i * 128 : kind * D + (i + 1) * 128] = both.T
        rows = slice(m * TOK, (m + 1) * TOK)
        gives.append(
            send(
                right_q.at[rows, pl.ds(pl.multiple_of(other * WIDTHS[0], 512), WIDTHS[0])],
                peer_right.at[rows, 0 : WIDTHS[0]], (swap_send, swap_recv), (1, 9)[m], to_core,
            )
        )
        gives[m].start()
    sum_q = jnp.sum(right_q[:, :D].astype(f32), axis=0, keepdims=True)
    sum_v = jnp.sum(right_q[:, 2 * D :].astype(f32), axis=0, keepdims=True)
    row = lax.broadcasted_iota(jnp.int32, (16, TOK), 0)
    own_vec[...] = jnp.zeros_like(own_vec)
    for f in range(N_FSDP):
        cols = slice(f * TOK, (f + 1) * TOK)
        value = jnp.where(row == 0, sum_q[:, cols], jnp.where(row == 1, sum_v[:, cols], vec[f]))
        own_vec[f // 2, f % 2, 0, 0] = value.astype(bf16)
    give_vec = send(own_vec, peer_vec, (swap_send, swap_recv), 8, to_core)
    give_vec.start()
    for copy in gives:
        copy.wait()
    for p, at, width in late:
        if width == COLS:
            multiply(p, at // COLS)
        else:
            give_vec.wait()
            stores[3][0] = (own_vec[...].astype(f32) + peer_vec[...].astype(f32)).astype(bf16)
        begin(p, at, width)
    for n in range(6):
        fetch_w[n].wait()
        part = dot_nt(right_q[:, n * COLS : (n + 1) * COLS], w_part[n % 2])
        if n == 0:
            out_x[...] = part
        else:
            out_x[...] += part
        if n < 4:
            fetch_w[n + 2].start()
    for piece in late:
        relay(*piece)
    for piece in early:
        reduce(2, *piece)
    for phase in range(3):
        for piece in late:
            reduce(phase, *piece)
    squares = square_acc[...]
    yl, z = lax.axis_index("yl"), lax.axis_index("z")
    z_first, y_first = slice(0, HALF_Z), slice(HALF_Z, 6272)
    to_y = {"yl": 1 - yl}
    gather_sems = (gather_send, gather_recv)
    sq_sems = (sq_send, sq_recv)

    def spread(buffer, axis, base):
        at = coordinate(axis)
        out = []
        for step in (1, 2, 3):
            out.append(send(buffer.at[at], buffer.at[at], sq_sems, base + step - 1, peer(axis, step)[0]))
        return out

    def total(buffer):
        return (buffer[0] + buffer[1]) + (buffer[2] + buffer[3])

    sq_z[z] = squares
    squares_z = spread(sq_z, "z", 0)
    first_z = [
        send(gathered.at[core, row_place, :, z_first], gathered.at[core, row_place, :, z_first], gather_sems, step - 1, peer("z", step)[0])
        for step in (1, 2, 3)
    ]
    first_y = send(gathered.at[core, row_place, :, y_first], gathered.at[core, row_place, :, y_first], gather_sems, 3, to_y)
    for copy in (*squares_z, *first_z, first_y):
        copy.start()
    for copy in squares_z:
        copy.wait()
    y_at = coordinate("y")
    sq_y[y_at] = total(sq_z)
    squares_y = spread(sq_y, "y", 3)
    for copy in squares_y:
        copy.start()
    for copy in (*first_z, first_y):
        copy.wait()
    quarter = pl.ds(yl * 4, 4)
    second_y = send(
        gathered.at[core, quarter, :, z_first], gathered.at[core, quarter, :, z_first], gather_sems, 4, to_y
    )
    second_y.start()
    second_z = []
    for step in (1, 2, 3):
        for half in range(2):
            view = gathered.at[core, half * 4 + z, :, y_first]
            second_z.append(send(view, view, gather_sems, 5 + (step - 1) * 2 + half, peer("z", step)[0]))
    for copy in second_z:
        copy.start()
    for copy in squares_y:
        copy.wait()
    x_at = coordinate("x")
    sq_x[x_at] = total(sq_y)
    squares_x = spread(sq_x, "x", 6)
    for copy in squares_x:
        copy.start()
    for copy in squares_x:
        copy.wait()
    sq_c[core] = total(sq_x)
    square_c = send(sq_c.at[core], sq_c.at[core], sq_sems, 9, to_core)
    square_c.start()
    square_c.wait()
    out_sq[...] = sq_c[0] + sq_c[1]
    second_y.wait()
    for copy in second_z:
        copy.wait()
    last = send(gathered.at[core], gathered.at[core], gather_sems, 11, to_core)
    last.start()
    last.wait()
    locals_ = []
    for c in range(2):
        for p in range(3):
            for b in range(N_EARLY[p] + 1):
                i, col = PRODUCT[(p, b)]
                target, base = ((out_attn, 0), (out_attn, 3072), (out_ffn, 0), (out_ffn, FF))[i]
                base = base + c * WIDTHS[i] + col
                at = PART_AT[p] + b * COLS
                locals_.append(
                    pltpu.make_async_copy(
                        gathered.at[c, :, :, at : at + COLS], target.at[:, :, base : base + COLS],
                        out_sem.at[len(locals_)],
                    )
                )
    locals_.append(pltpu.make_async_copy(gathered.at[0, :, :, 6144:], out_vec, out_sem.at[len(locals_)]))
    for copy in locals_:
        copy.start()
    for copy in locals_:
        copy.wait()


def back(lefts, rights, vec, grad_ready, held, full, lse, w_qkv):
    vmem = pl.BlockSpec(memory_space=pltpu.VMEM)
    hbm = pl.BlockSpec(memory_space=pl.ANY)
    scratch = [
        pltpu.VMEM((4, D, ROWS), bf16),
        pltpu.VMEM((ROWS, 6144), bf16),
        pltpu.VMEM((ROWS, 6144), bf16),
        pltpu.VMEM((4, 2, 2, 4, 16, 128), bf16),
        pltpu.VMEM((4, 2, 2, 4, 16, 128), bf16),
    ]
    for kind in range(6):
        n = kind if kind < 3 else kind - 2
        for p, count, width in (*((p, N_EARLY[p] + 1, COLS) for p in range(3)), (0, 1, 128)):
            landing = (3,) if kind >= 3 else ()
            scratch.append(pltpu.VMEM((count, *landing, *lead(ORDERS[p], n), 16, width), bf16))
    scratch += [
        pltpu.VMEM((2, 8, 16, 6272), bf16),
        pltpu.VMEM((4, 8, 128), f32),
        pltpu.VMEM((4, 8, 128), f32),
        pltpu.VMEM((4, 8, 128), f32),
        pltpu.VMEM((2, 8, 128), f32),
        pltpu.VMEM((N_CTX, MB, SENT, TOK), bf16),
        pltpu.VMEM((N_CTX, MB, HEAD, TOK), bf16),
        pltpu.VMEM((N_CTX, MB, 3 * HEAD, TOK), bf16),
        pltpu.VMEM((N_CTX, MB, 3 * HEAD, TOK), bf16),
        pltpu.VMEM((ROWS, 3 * D), bf16),
        pltpu.VMEM((PACK, HEAD), bf16),
        pltpu.VMEM((PACK, HEAD), bf16),
        pltpu.VMEM((HEAD, PACK), bf16),
        pltpu.VMEM((PACK, TOK), f32),
        pltpu.VMEM((PACK, 2 * HEAD), f32),
        pltpu.VMEM((8, 128), f32),
        pltpu.VMEM((2, D, COLS), bf16),
    ]
    for count in (10, 10, 156, 156, 12, 12, 10, 10, 32, 32, 32, 32, 10, 25):
        scratch.append(pltpu.SemaphoreType.DMA((count,)))
    out = pl.pallas_call(
        back_kernel,
        in_specs=[vmem] * 4 + [hbm] * 3 + [vmem, vmem, hbm, vmem, vmem, hbm],
        out_specs=[hbm, hbm, hbm, vmem, vmem],
        out_shape=[
            jax.ShapeDtypeStruct((8, 16, 4 * D), bf16),
            jax.ShapeDtypeStruct((8, 16, 2 * FF), bf16),
            jax.ShapeDtypeStruct((8, 16, 128), bf16),
            jax.ShapeDtypeStruct((8, 128), f32),
            jax.ShapeDtypeStruct((ROWS, D), f32),
        ],
        scratch_shapes=scratch,
        compiler_params=pltpu.CompilerParams(
            collective_id=1, has_side_effects=True, vmem_limit_bytes=60 * 2**20
        ),
        cost_estimate=pl.CostEstimate(
            flops=2 * 512 * D * 6144 + 10 * MB * PACK * PACK * HEAD, bytes_accessed=16 * 2**20,
            transcendentals=MB * PACK * PACK,
        ),
        name="back",
    )(*lefts, *rights, vec, grad_ready, held, full, lse, w_qkv)
    return out[0].reshape(TOK, 4 * D), out[1].reshape(TOK, 2 * FF), out[2][0, :12], jnp.sum(out[3]), out[4]


def layer_stats(values, gain_row, shift_row):
    center = values - jnp.mean(values, axis=-1, keepdims=True)
    inverse = lax.rsqrt(jnp.mean(center * center, axis=-1, keepdims=True) + NORM_EPS)
    normal = center * inverse
    return (normal * gain_row + shift_row, normal, inverse)


def layer_back(grad_value, normal, inverse, gain_row):
    scaled = grad_value * gain_row
    return inverse * (
        scaled
        - jnp.mean(scaled, axis=-1, keepdims=True)
        - normal * jnp.mean(scaled * normal, axis=-1, keepdims=True)
    )


N_CHUNK = 8
CHUNK = FF // N_CHUNK
ERF_TOP = (
    -2.72614225801306e-10, 2.77068142495902e-08, -2.10102402082508e-06, -5.69250639462346e-05,
    -7.34990630326855e-04, -2.95459980854025e-03, -1.60960333262415e-02,
)
ERF_LOW = (
    -1.45660718464996e-05, -2.13374055278905e-04, -1.68282697438203e-03, -7.37332916720468e-03,
    -1.42647390514189e-02,
)


def erf(value):
    value = jnp.clip(value, -4.0, 4.0)
    square = value * value
    top, low = jnp.full_like(square, ERF_TOP[0]), jnp.full_like(square, ERF_LOW[0])
    for c in ERF_TOP[1:]:
        top = top * square + c
    for c in ERF_LOW[1:]:
        low = low * square + c
    return value * top / low


def w_block(ref, n):
    per = ref.shape[-1] // CHUNK
    at = (n % per) * CHUNK
    return ref[n // per, :, :, :, at : at + CHUNK].reshape(D, CHUNK)


def dense_part(
    mixed_ref, x_ref, cot_ref, keep_ref, small_ref, w_out, w_one, w_two, before,
    out_ref, one_ref, x_t, o_t, h_t, f_t, a_low_ref, du_ref, g_ref, vec_ref, ready_ref,
    mixed, normal_one_ref, slope, total,
):
    def row(i):
        return small_ref[i : i + 1, :]

    def put(i, value):
        for f in range(N_FSDP):
            vec_ref[f, i : i + 1, :] = value[:, f * TOK : (f + 1) * TOK]

    def sums(value):
        return jnp.sum(value, axis=0, keepdims=True)

    vec_ref[...] = jnp.zeros_like(vec_ref)
    for m in range(MB):
        tok = slice(m * TOK, (m + 1) * TOK)
        for i in range(HEADS // 2):
            both = jnp.concatenate([mixed_ref[2 * i, m], mixed_ref[2 * i + 1, m]], axis=0)
            o_t[i * 128 : (i + 1) * 128, tok] = both
            mixed[tok, i * 128 : (i + 1) * 128] = both.T
    before(0)
    branch = jnp.concatenate([dot(mixed[...], w_block(w_out, n)) for n in range(2)], axis=1)
    normed_one, normal_one, inverse_one = layer_stats(x_ref[...].astype(f32) + branch + row(2), row(4), row(5))
    normal_one_ref[...] = normal_one
    normed_low = normed_one.astype(bf16)
    h_t[...] = normed_low.T
    total[...] = normed_one + row(3)
    before(1)
    for n in range(N_CHUNK):
        cols = slice(n * CHUNK, (n + 1) * CHUNK)
        bias = small_ref[8 + n // 2 : 9 + n // 2, (n % 2) * CHUNK : (n % 2 + 1) * CHUNK]
        u = dot(normed_low, w_block(w_one, n)) + bias
        share = 0.5 + 0.5 * erf(u * math.sqrt(0.5))
        g_ref[:, cols] = (u * share).astype(bf16)
        slope[:, cols] = share + u * (jnp.exp(-0.5 * u * u) * (1.0 / math.sqrt(2.0 * math.pi)))
    before(2)
    for n in range(N_CHUNK):
        total[...] += dot_nt(g_ref[:, n * CHUNK : (n + 1) * CHUNK], w_block(w_two, n))
    output, normal_two, inverse_two = layer_stats(total[...], row(6), row(7))
    keep = keep_ref[...]
    out_ref[...] = (output * keep).astype(bf16)
    grad_out = cot_ref[...].astype(f32) * keep
    put(6, sums(grad_out * normal_two))
    put(7, sums(grad_out))
    grad_two = layer_back(grad_out, normal_two, inverse_two, row(6))
    f_low = grad_two.astype(bf16)
    f_t[...] = f_low.T
    put(3, sums(f_low.astype(f32)))
    total[...] = grad_two
    for n in range(N_CHUNK):
        cols = slice(n * CHUNK, (n + 1) * CHUNK)
        du = (dot(f_low, w_block(w_two, n)) * slope[:, cols]).astype(bf16)
        du_ref[:, cols] = du
        part = sums(du.astype(f32))
        for i in range(CHUNK // TOK):
            f = (n % 2) * (CHUNK // TOK) + i
            vec_ref[f, 8 + n // 2 : 9 + n // 2, :] = part[:, i * TOK : (i + 1) * TOK]
        total[...] += dot_nt(du, w_block(w_one, n))
    grad_normed = total[...]
    normal_one = normal_one_ref[...]
    put(4, sums(grad_normed * normal_one))
    put(5, sums(grad_normed))
    grad_one = layer_back(grad_normed, normal_one, inverse_one, row(4))
    one_ref[...] = grad_one
    a_low = grad_one.astype(bf16)
    a_low_ref[...] = a_low
    put(2, sums(a_low.astype(f32)))
    for n in range(2):
        part = a_low[:, n * CHUNK : (n + 1) * CHUNK]
        part = dot_nt(part, w_block(w_out, n))
        grad_mixed = part if n == 0 else grad_mixed + part
    grad_mixed = grad_mixed.T.astype(bf16)
    for h in range(HEADS):
        for m in range(MB):
            ready_ref[h, m] = grad_mixed[h * HEAD : (h + 1) * HEAD, m * TOK : (m + 1) * TOK]
    x_t[...] = x_ref[...].T


def adamw(weight, grad_value, first, second, rate, decay):
    first_new = BETA_FIRST * first + (1.0 - BETA_FIRST) * grad_value
    second_new = BETA_SECOND * second + (1.0 - BETA_SECOND) * grad_value * grad_value
    first_hat = first_new / (1.0 - BETA_FIRST**STEP)
    second_hat = second_new / (1.0 - BETA_SECOND**STEP)
    weight_new = weight - rate * (first_hat / (jnp.sqrt(second_hat) + ADAM_EPS) + decay * weight)
    return (weight_new, first_new, second_new)


def shards(
    tokens, cotangent, dest, lengths, attn_weight, attn_first, attn_second,
    ffn_weight, ffn_first, ffn_second, vectors, vec_first, vec_second,
):
    core = lax.axis_index("core")

    def half(weight, base, width):
        return lax.dynamic_slice_in_dim(weight, base + core * width, width, 1).astype(bf16)

    shard = jnp.concatenate(
        [half(attn_weight, 0, 1536), half(attn_weight, 3 * D, 512), half(ffn_weight, 0, 2048), half(ffn_weight, FF, 2048)],
        axis=1,
    )
    x = tokens.reshape(ROWS, D)
    cot = cotangent.reshape(ROWS, D)
    ends = jnp.cumsum(lengths[:, 0], axis=1)
    seg = jnp.sum((dest[:, 0, :, None] >= ends[:, None, :]).astype(jnp.int32), axis=2)
    keep = (seg.reshape(ROWS, 1) < 8).astype(f32)

    seg_rows = jnp.broadcast_to(seg.astype(bf16)[:, None, :], (MB, 16, TOK))
    vec_shard = jnp.pad(vectors.astype(bf16), ((0, 4), (0, 0)))
    (
        w_qkv, held, mixed_full, lse, output, grad_one, x_t, o_t, h_t, f_t, a_low, du, g, vec_rows, grad_ready,
    ) = front(shard, vec_shard, x, seg_rows, cot, keep)
    total_attn, total_ffn, total_vec, square_sum, grad_x = back(
        (x_t, o_t, h_t, f_t),
        (a_low, du, g),
        vec_rows,
        grad_ready,
        held,
        mixed_full,
        lse,
        w_qkv.reshape(D, 3 * D),
    )
    grad_tokens = grad_one + grad_x
    total_attn, total_ffn, total_vec = total_attn.astype(f32), total_ffn.astype(f32), total_vec.astype(f32)
    grad_norm = jnp.sqrt(square_sum)
    factor = jnp.minimum(1.0, CLIP_NORM / (grad_norm + 1e-06))
    rate_matrix = D ** (-0.5)
    attn_new, attn_first_new, attn_second_new = adamw(
        attn_weight, total_attn * factor, attn_first, attn_second, ATTN_RATE_SCALE * rate_matrix, WEIGHT_DECAY
    )
    ffn_new, ffn_first_new, ffn_second_new = adamw(
        ffn_weight, total_ffn * factor, ffn_first, ffn_second, rate_matrix, WEIGHT_DECAY
    )
    vec_new, vec_first_new, vec_second_new = adamw(
        vectors, total_vec * factor, vec_first, vec_second, RATE_VECTOR, 0.0
    )
    return (
        output.reshape(tokens.shape),
        grad_tokens.astype(bf16).reshape(tokens.shape),
        grad_norm,
        attn_new, attn_first_new, attn_second_new,
        ffn_new, ffn_first_new, ffn_second_new,
        vec_new, vec_first_new, vec_second_new,
        attn_new.astype(bf16),
        ffn_new.astype(bf16),
        total_vec[2] * factor,
    )


def solution(mesh):
    fine = Mesh(mesh.devices.reshape(2, 4, 2, 4, 2), ("yl", "z", "core", "x", "yh"))
    act = P(None, FSDP, CTX, None)
    row = P(FSDP, None)
    col = P(None, FSDP)
    return jax.shard_map(
        shards,
        mesh=fine,
        in_specs=(act, act, P(None, FSDP, CTX), P(None, FSDP, None), row, row, row, row, row, row, col, col, col),
        out_specs=(act, act, P(), row, row, row, row, row, row, col, col, col, row, row, P(FSDP)),
        check_vma=False,
    )
```

```python
import math

import jax
import jax.numpy as jnp
from jax import lax
from jax.experimental import pallas as pl
from jax.experimental.pallas import tpu as pltpu
from jax.sharding import Mesh, PartitionSpec as P

HEADS = 16
HEAD = 64
STEP = 10
MB = 2
TOK = 128
ROWS = MB * TOK
D = 1024
FF = 4096
N_CTX = 16
N_FSDP = 8
PACK = 2048
SENT = 208

NORM_EPS = 1e-05
CLIP_NORM = 1.0
BETA_FIRST = 0.9
BETA_SECOND = 0.999
ADAM_EPS = 1e-08
WEIGHT_DECAY = 0.01
RATE_VECTOR = 0.3
ATTN_RATE_SCALE = 3.0
NEG_LARGE = -1e30
SCALE2 = HEAD ** (-0.5) * math.log2(math.e)
SCALE = HEAD ** (-0.5)
CONTRACT_ROWS = (((0,), (0,)), ((), ()))
CONTRACT_COLS = (((1,), (1,)), ((), ()))
CTX = ("yl", "z", "core")
FSDP = ("x", "yh")
ALL = ("x", "yh", "yl", "z", "core")
BLK = 256
NBLK = PACK // BLK
f32 = jnp.float32
bf16 = jnp.bfloat16


def dot(a, b):
    return jnp.dot(a, b, preferred_element_type=f32)


def dot_nt(a, b):
    return lax.dot_general(a, b, CONTRACT_COLS, preferred_element_type=f32)


def dot_tn(a, b):
    return lax.dot_general(a, b, CONTRACT_ROWS, preferred_element_type=f32)


MESH_ID = pl.DeviceIdType.MESH
COLS = 512
N_BLK = 4
ORDERS = (("x", "z", "y"), ("z", "y", "x"), ("y", "x", "z"))
EARLY = ((0, 0), (1, 0), (2, 0), (0, 1), (1, 1), (2, 1), (0, 2), (1, 2), (2, 2))
N_EARLY = (3, 3, 3)
EARLY_PRODUCT = ((2, 0), (2, 512), (2, 1024), (2, 1536), (3, 0), (3, 512), (3, 1024), (3, 1536), (1, 0))
PRODUCT = {part_block: product for part_block, product in zip(EARLY, EARLY_PRODUCT)}
PRODUCT.update({(p, N_EARLY[p]): (0, p * COLS) for p in range(3)})
PART_AT = (0, 2048, 4096, 6144)
VEC_AT = 3072
WIDTHS = (1536, 512, 2048, 2048)
OFFSETS = (0, 1536, 2048, 4096)
HALF_Z = 3072
TASKS = {}
for _n, _at in enumerate((2, 2, 2, 5, 5, 5, 8, 8, 8)):
    TASKS.setdefault(_at, []).append(("relay", *EARLY[_n]))
for _n, _at in enumerate((7, 7, 7, 10, 10, 10, 13, 13, 13)):
    TASKS.setdefault(_at, []).append((0, *EARLY[_n]))


def coordinate(axis):
    if axis == "y":
        return lax.axis_index("yh") * 2 + lax.axis_index("yl")
    return lax.axis_index(axis)


def peer(axis, step):
    at = lax.rem(coordinate(axis) + step, 4)
    if axis == "y":
        return {"yh": at // 2, "yl": lax.rem(at, 2)}, at
    return {axis: at}, at


def pick(ref, axis, at, dims):
    index = []
    for d in dims:
        if d == axis:
            index.append(at)
        elif axis == "y" and d == "yh":
            index.append(at // 2)
        elif axis == "y" and d == "yl":
            index.append(lax.rem(at, 2))
        else:
            index.append(slice(None))
    return ref.at[tuple(index)]


def dims_after(order, n):
    dims = ["x", "yh", "yl", "z"]
    for axis in order[:n]:
        for d in ("yh", "yl") if axis == "y" else (axis,):
            dims.remove(d)
    return dims


SIZES = {"x": 4, "yh": 2, "yl": 2, "z": 4}


def lead(order, n):
    return tuple(SIZES[d] for d in dims_after(order, n))


def send(src, dst, sems, index, to):
    return pltpu.make_async_remote_copy(
        src_ref=src, dst_ref=dst, send_sem=sems[0].at[index], recv_sem=sems[1].at[index],
        device_id=to, device_id_type=MESH_ID,
    )


def load_side(qkv_ref, m, keys, values, keys_t, values_t, seg_col):
    for s in range(N_CTX):
        at = slice(s * TOK, (s + 1) * TOK)
        key_t = qkv_ref[s, m, HEAD : 2 * HEAD, :]
        value_t = qkv_ref[s, m, 2 * HEAD : 3 * HEAD, :]
        keys[at, :] = key_t.T
        if values is not None:
            values[at, :] = value_t.T
        if keys_t is not None:
            keys_t[:, at] = key_t
        if values_t is not None:
            values_t[:, at] = value_t
        seg = qkv_ref[s, m, 3 * HEAD : 3 * HEAD + 1, :].astype(f32)
        seg_col[at, :] = jnp.broadcast_to(seg, (TOK, TOK)).T


def pair(ref, m, j, rows):
    return jnp.concatenate([ref[2 * j, m, rows, :], ref[2 * j + 1, m, rows, :]], axis=1)


def query_forward(held, m, j, out, full, lse_out, keys, values_t, seg_col, scores):
    query_t = pair(held, m, j, slice(0, HEAD))
    seg_row = pair(held, m, j, slice(3 * HEAD, 3 * HEAD + 1)).astype(f32)
    top = jnp.full((1, BLK), NEG_LARGE, f32)
    for k in range(NBLK):
        at = slice(k * BLK, (k + 1) * BLK)
        s = dot(keys[at, :], query_t) * SCALE2
        col = seg_col[at, :]
        same = jnp.concatenate([col, col], axis=1) == seg_row
        s = jnp.where(same, s, NEG_LARGE)
        scores[at, :] = s
        top = jnp.maximum(top, jnp.max(s, axis=0, keepdims=True))
    total = jnp.zeros((1, BLK), f32)
    acc = jnp.zeros((HEAD, BLK), f32)
    for k in range(NBLK):
        at = slice(k * BLK, (k + 1) * BLK)
        p = jnp.exp2(scores[at, :] - top)
        total = total + jnp.sum(p, axis=0, keepdims=True)
        acc = acc + dot(values_t[:, at], p.astype(bf16))
    acc = acc / total
    lse = top + jnp.log2(total)
    for half in range(2):
        cols = slice(half * TOK, (half + 1) * TOK)
        out[2 * j + half, m] = acc[:, cols].astype(bf16)
        full[2 * j + half, m] = acc[:, cols]
        lse_out[2 * j + half, m] = lse[:, cols]


GROUP_COLS = (1536, 2048, 2048, 512)
GROUP_AT = (0, 2048, 4096, 1536)
SPLITS = ((512, 1024), (1024, 1536), (1024, 1536), (128, 256))
N_COPY = 31
GROUPS = (3, 1, 2)
BEFORE = tuple((0, op) for op in ("z1", "x1", "z2", "y1", "z3", "x2", "x3", "y2", "z4", "x4", "x5"))
BEFORE += tuple((g, op) for op in ("z1", "z2", "y1") for g in GROUPS)
BEFORE += tuple((0, op) for op in ("y3", "z5", "sx", "sy", "sz", "got"))
PUSHED = tuple((g, op) for op in ("z3", "x1", "x2", "x3") for g in GROUPS)
STEPS = {
    0: tuple((g, "z4") for g in GROUPS),
    1: tuple((g, "y2") for g in GROUPS),
    3: tuple((g, "x4") for g in GROUPS),
    6: tuple((g, "x5") for g in GROUPS),
    9: tuple((g, "y3") for g in GROUPS),
    12: tuple((g, "z5") for g in GROUPS),
}
LAST = (
    tuple((g, op) for g in (3, 1) for op in ("sx", "sy", "sz")) + ((3, "got"),),
    tuple((2, op) for op in ("sx", "sy", "sz")) + ((1, "got"),),
    ((2, "got"),),
)


def ctx_device(t):
    return {"yl": t // 8, "z": lax.rem(t // 2, 4), "core": lax.rem(t, 2)}


def rows_at(start, size):
    return pl.ds(pl.multiple_of(start, 16), size)


class Gather:
    def __init__(self, g, shard, dest, sems, base, local_sem):
        core = lax.axis_index("core")
        x, z = lax.axis_index("x"), lax.axis_index("z")
        yh, yl = lax.axis_index("yh"), lax.axis_index("yl")
        y = yh * 2 + yl
        every = slice(None)
        zq, half = rows_at(z * 32, 32), rows_at(yl * 64, 64)
        cross = {"yh": 1 - yh, "yl": 1 - yl}
        count = [0]
        x_end, y_end = SPLITS[g]
        x_cols, y_cols, z_cols = slice(0, x_end), slice(x_end, y_end), slice(y_end, GROUP_COLS[g])

        def given(rows, cols):
            return shard.at[rows, GROUP_AT[g] + cols.start : GROUP_AT[g] + cols.stop]

        def make(src, dst, to):
            copy = send(src, dst, sems, base + count[0], to)
            count[0] += 1
            return copy

        def own(rows, cols, to):
            return make(given(rows, cols), dest(core, x, yh, rows, cols), to)

        def pass_on(xs, yhs, rows, cols, to):
            view = dest(core, xs, yhs, rows, cols)
            return make(view, view, to)

        x_to = {step: peer("x", step)[0] for step in (1, 2, 3)}
        y_to = {step: peer("y", step)[0] for step in (1, 3)}
        z_to = {step: peer("z", step)[0] for step in (1, 3)}
        x_before, x_after = lax.rem(x + 3, 4), lax.rem(x + 1, 4)
        y_before, y_after = lax.rem(y + 3, 4), lax.rem(y + 1, 4)
        z_before, z_after = lax.rem(z + 3, 4), lax.rem(z + 1, 4)
        self.copies = {
            "x1": [own(every, x_cols, cross)],
            "x2": [own(every, x_cols, x_to[s]) for s in (1, 3)],
            "z1": [own(zq, z_cols, cross)],
            "z2": [own(zq, z_cols, x_to[s]) for s in (1, 3, 2)],
            "y1": [own(half, y_cols, x_to[s]) for s in (1, 3, 2)],
            "x3": [pass_on(x, 1 - yh, every, x_cols, x_to[s]) for s in (1, 3)],
            "z3": [pass_on(x, 1 - yh, zq, z_cols, x_to[s]) for s in (1, 3, 2)],
            "y2": [pass_on(every, yh, half, y_cols, y_to[s]) for s in (1, 3)],
            "z4": [pass_on(every, every, zq, z_cols, z_to[s]) for s in (1, 3)],
            "x4": [
                pass_on(x_before, yh, slice(0, 64), x_cols, x_to[1]),
                pass_on(x_after, yh, slice(64, 128), x_cols, x_to[3]),
            ],
            "x5": [
                pass_on(x_before, 1 - yh, slice(0, 64), x_cols, x_to[1]),
                pass_on(x_after, 1 - yh, slice(64, 128), x_cols, x_to[3]),
            ],
            "y3": [
                pass_on(every, y_before // 2, rows_at(lax.rem(y_before, 2) * 64, 32), y_cols, y_to[1]),
                pass_on(every, y_after // 2, rows_at(lax.rem(y_after, 2) * 64 + 32, 32), y_cols, y_to[3]),
            ],
            "z5": [
                pass_on(every, every, rows_at(z_before * 32, 16), z_cols, z_to[1]),
                pass_on(every, every, rows_at(z_after * 32 + 16, 16), z_cols, z_to[3]),
            ],
        }
        for name, cols in (("sx", x_cols), ("sy", y_cols), ("sz", z_cols)):
            self.copies[name] = [pass_on(every, every, every, cols, {"core": 1 - core})]
        self.places = [
            pltpu.make_async_copy(given(rows, cols), dest(core, x, yh, rows, cols), local_sem.at[3 * g + n])
            for n, (rows, cols) in enumerate(((every, x_cols), (half, y_cols), (zq, z_cols)))
        ]

    needs = {
        "x3": ("x1",), "z3": ("z1",), "y2": ("y1",), "z4": ("z2", "z3"), "x4": ("x2",), "x5": ("x3",), "y3": ("y2",),
        "z5": ("z4",), "sx": ("x4", "x5"), "sy": ("y3",), "sz": ("z5",),
    }

    def step(self, name):
        if name == "got":
            for copy in (*self.copies["sx"], *self.copies["sy"], *self.copies["sz"]):
                copy.wait_recv()
            return
        if name == "end":
            for copies in self.copies.values():
                for copy in copies:
                    copy.wait_send()
            return
        for need in self.needs.get(name, ()):
            for copy in self.copies[need]:
                copy.wait_recv()
        if name == "z1":
            for copy in self.places:
                copy.start()
        if name == "z3":
            for copy in self.places:
                copy.wait()
        for copy in self.copies[name]:
            copy.start()


def greet_all():
    barrier = pltpu.get_barrier_semaphore()
    place = lax.axis_index(CTX)
    others = [ctx_device(lax.rem(place + d, N_CTX)) for d in range(1, N_CTX)]
    others += [peer(axis, step)[0] for axis in ("x", "y") for step in (1, 2, 3)]
    for other in others:
        pl.semaphore_signal(barrier, inc=1, device_id=other, device_id_type=MESH_ID)
    pl.semaphore_wait(barrier, len(others))


def front_kernel(
    shard, vec_shard, x_ref, seg_ref, cot_ref,
    out_attn, out_held, out_full, out_lse,
    out_ref, one_ref, x_t, o_t, h_t, f_t, a_low_ref, du_ref, g_ref, vec_ref, ready_ref,
    wa, w_one, w_two, w_out, vecs, small, ready, held, mixed, out_t, keys, values_t, seg_col, scores,
    mixed_rows, normal_one, slope, total,
    ag_send, ag_recv, vec_send, vec_recv, q_send, q_recv, o_send, o_recv, local_sem, out_sem,
):
    core = lax.axis_index("core")
    place = lax.axis_index(CTX)
    x, yh, yl = lax.axis_index("x"), lax.axis_index("yh"), lax.axis_index("yl")

    weights = (wa, w_one, w_two, w_out)

    def dest(g):
        def view(c, xs, yhs, rows, cols):
            return weights[g].at[c, xs, yhs, rows, cols]

        return view

    gathers = [
        Gather(g, shard, dest(g), (ag_send, ag_recv), g * N_COPY, local_sem) for g in range(4)
    ]
    vec_sems = (vec_send, vec_recv)
    vec_cross = send(vec_shard, vecs.at[x, yh], vec_sems, 0, {"yh": 1 - yh, "yl": 1 - yl})
    vec_x = [send(vec_shard, vecs.at[x, yh], vec_sems, s, peer("x", s)[0]) for s in (1, 2, 3)]
    vec_x2 = [
        send(vecs.at[x, 1 - yh], vecs.at[x, 1 - yh], vec_sems, 3 + s, peer("x", s)[0]) for s in (1, 2, 3)
    ]
    greet_all()
    for copy in (vec_cross, *vec_x):
        copy.start()
    done = set()

    def stages(todo):
        for g, n in todo:
            if (g, n) not in done:
                done.add((g, n))
                gathers[g].step(n)

    stages(BEFORE[:4])
    vecs[x, yh] = vec_shard[...]
    for s in range(N_CTX):
        ready[s, :, 3 * HEAD :, :] = seg_ref[...]
    vec_cross.wait_recv()
    for copy in vec_x2:
        copy.start()
    stages(BEFORE)
    vec_cross.wait_send()
    for copy in (*vec_x, *vec_x2):
        copy.wait()
    for f in range(N_FSDP):
        small[:, f * TOK : (f + 1) * TOK] = vecs[f // 2, f % 2].astype(f32)

    for part in range(6):
        c, col = part // 3, (part % 3) * 512
        kind, first = part // 2, (part % 2) * 8
        value = jnp.zeros((ROWS, 512), f32)
        weight = wa[c, :, :, :, col : col + 512].reshape(D, 512)
        value = dot(x_ref[...], weight)
        if kind != 1:
            row = 0 if kind == 0 else 1
            value = value + small[row : row + 1, first * HEAD : first * HEAD + 512]
        value = value.T.astype(bf16)
        for h in range(8):
            for m in range(MB):
                ready[first + h, m, kind * HEAD : (kind + 1) * HEAD, :] = value[
                    h * HEAD : (h + 1) * HEAD, m * TOK : (m + 1) * TOK
                ]
    swaps = [[], []]
    for m in range(MB):
        for d in range(1, N_CTX):
            t = lax.rem(place + d, N_CTX)
            swaps[m].append(send(ready.at[t, m], held.at[place, m], (q_send, q_recv), m * N_CTX + d, ctx_device(t)))
            swaps[m][-1].start()
    held[place] = ready[place]
    returns = [[], []]
    for m in range(MB):
        for d in range(1, N_CTX):
            t = lax.rem(place + d, N_CTX)
            returns[m].append(
                send(out_t.at[t, m], mixed.at[place, m], (o_send, o_recv), m * N_CTX + d, ctx_device(t))
            )
    stages(PUSHED)
    outs = [(wa.at[c], out_attn.at[:, :, :, c * 1536 : (c + 1) * 1536]) for c in range(2)]
    outs = [pltpu.make_async_copy(src, dst, out_sem.at[n]) for n, (src, dst) in enumerate(outs)]
    for copy in outs:
        copy.start()
    for m in range(MB):
        for copy in swaps[m]:
            copy.wait_recv()
        load_side(held, m, keys, None, None, values_t, seg_col)

        def query_block(j, _, m=m):
            for at, todo in STEPS.items():
                if at // NBLK == m:

                    @pl.when(j == at % NBLK)
                    def _(todo=todo):
                        stages(todo)

            query_forward(held, m, j, out_t, out_full, out_lse, keys, values_t, seg_col, scores)
            return 0

        lax.fori_loop(0, NBLK, query_block, 0)
        for copy in returns[m]:
            copy.start()
        mixed[place, m] = out_t[place, m]
    outs.append(pltpu.make_async_copy(held, out_held, out_sem.at[4]))
    outs[-1].start()

    def before(n):
        stages(LAST[n])

    for m in range(MB):
        for copy in returns[m]:
            copy.wait_recv()
    dense_part(
        mixed, x_ref, cot_ref, seg_ref, small, w_out, w_one, w_two, before,
        out_ref, one_ref, x_t, o_t, h_t, f_t, a_low_ref, du_ref, g_ref, vec_ref, ready_ref,
        mixed_rows, normal_one, slope, total,
    )
    for m in range(MB):
        for copy in (*swaps[m], *returns[m]):
            copy.wait_send()
    stages([(g, "end") for g in (0, *GROUPS)])
    for copy in outs:
        copy.wait()


def front(shard, vec_shard, x, seg_rows, cot):
    vmem = pl.BlockSpec(memory_space=pltpu.VMEM)
    hbm = pl.BlockSpec(memory_space=pl.ANY)
    sem = lambda n: pltpu.SemaphoreType.DMA((n,))
    turned = jax.ShapeDtypeStruct((D, ROWS), bf16)
    return pl.pallas_call(
        front_kernel,
        in_specs=[hbm, vmem, vmem, vmem, vmem],
        out_specs=[hbm, hbm] + [vmem] * 13,
        out_shape=[
            jax.ShapeDtypeStruct((4, 2, TOK, 3 * D), bf16),
            jax.ShapeDtypeStruct((N_CTX, MB, SENT, TOK), bf16),
            jax.ShapeDtypeStruct((N_CTX, MB, HEAD, TOK), f32),
            jax.ShapeDtypeStruct((N_CTX, MB, 1, TOK), f32),
            jax.ShapeDtypeStruct((ROWS, D), bf16),
            jax.ShapeDtypeStruct((ROWS, D), f32),
            turned, turned, turned, turned,
            jax.ShapeDtypeStruct((ROWS, D), bf16),
            jax.ShapeDtypeStruct((ROWS, FF), bf16),
            jax.ShapeDtypeStruct((ROWS, FF), bf16),
            jax.ShapeDtypeStruct((N_FSDP, 16, TOK), f32),
            jax.ShapeDtypeStruct((HEADS, MB, HEAD, TOK), bf16),
        ],
        scratch_shapes=[
            *(pltpu.VMEM((2, 4, 2, TOK, GROUP_COLS[g]), bf16) for g in range(4)),
            pltpu.VMEM((4, 2, 16, TOK), bf16),
            pltpu.VMEM((16, D), f32),
            pltpu.VMEM((N_CTX, MB, SENT, TOK), bf16),
            pltpu.VMEM((N_CTX, MB, SENT, TOK), bf16),
            pltpu.VMEM((N_CTX, MB, HEAD, TOK), bf16),
            pltpu.VMEM((N_CTX, MB, HEAD, TOK), bf16),
            pltpu.VMEM((PACK, HEAD), bf16),
            pltpu.VMEM((HEAD, PACK), bf16),
            pltpu.VMEM((PACK, TOK), f32),
            pltpu.VMEM((PACK, BLK), f32),
            pltpu.VMEM((ROWS, D), bf16),
            pltpu.VMEM((ROWS, D), f32),
            pltpu.VMEM((ROWS, FF), f32),
            pltpu.VMEM((ROWS, D), f32),
            sem(4 * N_COPY), sem(4 * N_COPY), sem(7), sem(7), sem(32), sem(32), sem(32), sem(32),
            sem(12), sem(6),
        ],
        compiler_params=pltpu.CompilerParams(
            collective_id=2, has_side_effects=True, vmem_limit_bytes=60 * 2**20
        ),
        cost_estimate=pl.CostEstimate(
            flops=4 * MB * PACK * PACK * HEAD + 2 * ROWS * D * (5 * D + 4 * FF), bytes_accessed=32 * 2**20,
            transcendentals=MB * PACK * PACK,
        ),
        name="front",
    )(shard, vec_shard, x, seg_rows, cot)


def back_kernel(
    left_x, left_o, left_h, left_f, right_o, right_u, right_g, vec, grad_ready, held_in, full, lse, w_qkv,
    out_attn, out_ffn, out_vec, out_sq, out_x,
    peer_left, own_right, peer_right, own_vec, peer_vec,
    *rest_refs,
):
    stores, rest_refs = rest_refs[:24], rest_refs[24:]
    (
    gathered, sq_z, sq_y, sq_x, sq_c,
    held, grad_held, out_t, landed, right_q, keys, values, keys_t, seg_col, acc_kv, square_acc, w_part,
    swap_send, swap_recv, ring_send, ring_recv, gather_send, gather_recv, sq_send, sq_recv,
    o_send, o_recv, q_send, q_recv, local_sem, out_sem,
    ) = rest_refs
    core = lax.axis_index("core")
    other = 1 - core
    place = lax.axis_index(CTX)
    row_place = lax.axis_index("yl") * 4 + lax.axis_index("z")
    lefts = (left_x, left_o, left_h, left_f)
    rights = (None, right_o, right_u, right_g)
    to_core = {"core": other}

    fetch = pltpu.make_async_copy(held_in, held, local_sem.at[0])
    fetch.start()
    fetches = [fetch]
    for i in range(1, 4):
        cols = pl.ds(pl.multiple_of(core * WIDTHS[i], 512), WIDTHS[i])
        fetches.append(
            pltpu.make_async_copy(
                rights[i].at[:, cols], own_right.at[:, OFFSETS[i] : OFFSETS[i] + WIDTHS[i]], local_sem.at[i]
            )
        )
        fetches[-1].start()
    greet_all()

    pushes, returns = [[], []], [[], []]
    for m in range(MB):
        for d in range(1, N_CTX):
            t = lax.rem(place + d, N_CTX)
            to = ctx_device(t)
            pushes[m].append(
                send(grad_ready.at[t, m], grad_held.at[place, m], (o_send, o_recv), m * N_CTX + d, to)
            )
            returns[m].append(send(out_t.at[t, m], landed.at[place, m], (q_send, q_recv), m * N_CTX + d, to))
    swaps = []
    for i in (2, 3, 1, 0):
        swaps.append(send(lefts[i], peer_left.at[i], (swap_send, swap_recv), 2 * i, to_core))
        if i:
            from_cols = pl.ds(pl.multiple_of(other * WIDTHS[i], 512), WIDTHS[i])
            swaps.append(
                send(
                    rights[i].at[:, from_cols], peer_right.at[:, OFFSETS[i] : OFFSETS[i] + WIDTHS[i]],
                    (swap_send, swap_recv), 2 * i + 1, to_core,
                )
            )
    for m in range(MB):
        for copy in pushes[m]:
            copy.start()
    for copy in swaps:
        copy.start()
    grad_held[place] = grad_ready[place]
    for copy in fetches:
        copy.wait()

    late = [(p, N_EARLY[p] * COLS, COLS) for p in range(3)] + [(0, VEC_AT, 128)]
    early = [(p, b * COLS, COLS) for p, b in EARLY]

    def number(p, at, width):
        return 12 if width != COLS else PART_AT[p] // COLS + at // COLS

    def store(kind, p, at, width):
        return stores[4 * kind + 3].at[0] if width != COLS else stores[4 * kind + p].at[at // COLS]

    def copies(p, phase, at, width):
        order = ORDERS[p]
        axis = order[phase]
        out = []
        for step in (1, 2, 3):
            to, index = peer(axis, step)
            chunk = pick(store(phase, p, at, width), axis, index, dims_after(order, phase))
            land = store(3 + phase, p, at, width).at[step - 1]
            out.append(
                send(
                    chunk, land, (ring_send, ring_recv), 39 + 39 * phase + number(p, at, width) * 3 + step - 1, to
                )
            )
        return out

    def first_copies(p, at, width):
        order = ORDERS[p]
        axis = order[0]
        n = lead(order, 1)[0]
        halves = (slice(0, n // 2), slice(n // 2, n))
        (up, up_at), (_, far_at), (down, down_at) = (peer(axis, step) for step in (1, 2, 3))
        out = []
        for k, (index, half, slot, to) in enumerate(
            (
                (far_at, 0, 2, up), (far_at, 1, 2, down), (up_at, 1, 0, up), (down_at, 0, 1, down),
                (up_at, 0, 0, up), (down_at, 1, 1, down),
            )
        ):
            chunk = pick(store(0, p, at, width), axis, index, dims_after(order, 0)).at[halves[half]]
            land = store(3, p, at, width).at[slot, halves[half]]
            out.append(send(chunk, land, (ring_send, ring_recv), number(p, at, width) * 6 + k, to))
        return out

    def begin(p, at, width):
        for copy in first_copies(p, at, width)[:4]:
            copy.start()

    def relay(p, at, width):
        order = ORDERS[p]
        axis = order[0]
        n = lead(order, 1)[0]
        all_copies = first_copies(p, at, width)
        land = store(3, p, at, width)
        for half, step in ((0, 1), (1, 3)):
            all_copies[half].wait_recv()
            own = pick(store(0, p, at, width), axis, peer(axis, step)[1], dims_after(order, 0))

            def add(i, _, own=own):
                own[i] = (own[i].astype(f32) + land[2, i].astype(f32)).astype(bf16)
                return 0

            lax.fori_loop(half * (n // 2), (half + 1) * (n // 2), add, 0)
            all_copies[4 + half].start()

    def multiply(p, b):
        i, col = PRODUCT[(p, b)]
        if i == 0:
            mine = right_q.at[:, pl.ds(pl.multiple_of(core * WIDTHS[0] + col, 512), COLS)]
        else:
            mine = own_right.at[:, OFFSETS[i] + col : OFFSETS[i] + col + COLS]
        theirs = peer_right.at[:, OFFSETS[i] + col : OFFSETS[i] + col + COLS]

        def rows_block(x, _):
            rows = pl.ds(pl.multiple_of(x * 256, 256), 256)
            value = dot(lefts[i][rows, :], mine[...]) + dot(peer_left[i, rows, :], theirs[...])
            stores[p][b, x] = value.astype(bf16).reshape(2, 2, 4, 16, COLS)
            return 0

        lax.fori_loop(0, 4, rows_block, 0)

    def reduce(phase, p, at, width):
        order = ORDERS[p]
        axis = order[phase]
        land = store(3 + phase, p, at, width)
        if phase == 0:
            all_copies = first_copies(p, at, width)
            for copy in all_copies[:2]:
                copy.wait_send()
            for copy in all_copies[2:]:
                copy.wait()
        else:
            for copy in copies(p, phase, at, width):
                copy.wait()
        own = pick(store(phase, p, at, width), axis, coordinate(axis), dims_after(order, phase))
        if phase < 2:
            dst = store(phase + 1, p, at, width)

            def add(n, _):
                value = own[n].astype(f32)
                for step in range(3 if phase else 2):
                    value = value + land[step, n].astype(f32)
                dst[n] = value.astype(bf16)
                return 0

            lax.fori_loop(0, lead(order, phase + 1)[0], add, 0)
            for copy in copies(p, phase + 1, at, width):
                copy.start()
            return
        value = own[...].astype(f32)
        for step in range(3):
            value = value + land[step].astype(f32)
        to = PART_AT[p] + at if width == COLS else 6144
        gathered[core, row_place, :, to : to + width] = value.astype(bf16)
        square = value * value
        if width != COLS:
            square = square * jnp.where(core == 0, 1.0, 0.0)
        squares = square_acc[...]
        for c in range(0, width, 128):
            squares = squares + square[:8, c : c + 128] + square[8:, c : c + 128]
        square_acc[...] = squares

    def run_task(phase, p, b):
        if phase == "relay":
            relay(p, b * COLS, COLS)
        else:
            reduce(phase, p, b * COLS, COLS)

    square_acc[...] = jnp.zeros_like(square_acc)
    for copy in swaps:
        copy.wait()
    for p, at, width in early:
        multiply(p, at // COLS)
        begin(p, at, width)

    for m in range(MB):
        load_side(held, m, keys, values, keys_t, None, seg_col)
        acc_kv[...] = jnp.zeros_like(acc_kv)
        for copy in pushes[m]:
            copy.wait_recv()

        def query_block(j, _, m=m):
            for at, tasks in TASKS.items():
                if at // NBLK == m:

                    @pl.when(j == at % NBLK)
                    def _(tasks=tasks):
                        for phase, p, b in tasks:
                            run_task(phase, p, b)

            query_t = pair(held, m, j, slice(0, HEAD))
            seg_row = pair(held, m, j, slice(3 * HEAD, 3 * HEAD + 1)).astype(f32)
            grad_t = pair(grad_held, m, j, slice(0, HEAD))
            row_lse = pair(lse, m, j, slice(0, 1))
            delta = jnp.sum(grad_t.astype(f32) * pair(full, m, j, slice(0, HEAD)), axis=0, keepdims=True)
            acc_q = jnp.zeros((HEAD, BLK), f32)
            none = jnp.zeros((BLK, HEAD), bf16)
            sides = jnp.concatenate(
                [jnp.concatenate([query_t.T, none], axis=1), jnp.concatenate([none, grad_t.T], axis=1)], axis=0
            )
            block = lambda k: slice(k * BLK, (k + 1) * BLK)
            ahead = (dot(keys[block(0), :], query_t), dot(values[block(0), :], grad_t))
            behind = None
            for k in range(NBLK + 1):
                if k < NBLK:
                    at = block(k)
                    s, dp = ahead
                    if k + 1 < NBLK:
                        ahead = (dot(keys[block(k + 1), :], query_t), dot(values[block(k + 1), :], grad_t))
                if behind is not None:
                    to, ds, pb = behind
                    acc_q = acc_q + dot(keys_t[:, to], ds)
                    acc_kv[to, :] += dot(jnp.concatenate([ds, pb], axis=1), sides)
                if k < NBLK:
                    col = seg_col[at, :]
                    same = jnp.concatenate([col, col], axis=1) == seg_row
                    p = jnp.exp2(jnp.where(same, s * SCALE2 - row_lse, NEG_LARGE))
                    behind = (at, (p * (dp - delta)).astype(bf16), p.astype(bf16))
            acc_q = (acc_q * SCALE).astype(bf16)
            out_t[2 * j, m, :HEAD, :] = acc_q[:, :TOK]
            out_t[2 * j + 1, m, :HEAD, :] = acc_q[:, TOK:]
            return 0

        lax.fori_loop(0, NBLK, query_block, 0)
        for s in range(N_CTX):
            at = slice(s * TOK, (s + 1) * TOK)
            both = acc_kv[at, :].T
            out_t[s, m, HEAD : 2 * HEAD, :] = (both[:HEAD] * SCALE).astype(bf16)
            out_t[s, m, 2 * HEAD :, :] = both[HEAD:].astype(bf16)
        for copy in returns[m]:
            copy.start()
        landed[place, m] = out_t[place, m]

    fetch_w = [
        pltpu.make_async_copy(w_qkv.at[:, n * COLS : (n + 1) * COLS], w_part.at[n % 2], local_sem.at[4 + n])
        for n in range(6)
    ]
    done = [task for tasks in TASKS.values() for task in tasks]
    for phase in ("relay", 0, 1):
        for p, b in EARLY:
            if (phase, p, b) not in done:
                run_task(phase, p, b)
    gives = []
    for m in range(MB):
        for copy in pushes[m]:
            copy.wait_send()
        for copy in returns[m]:
            copy.wait()
        if m == 0:
            fetch_w[0].start()
            fetch_w[1].start()
        for i in range(HEADS // 2):
            for kind in range(3):
                rows = slice(kind * HEAD, (kind + 1) * HEAD)
                both = jnp.concatenate([landed[2 * i, m, rows, :], landed[2 * i + 1, m, rows, :]], axis=0)
                right_q[m * TOK : (m + 1) * TOK, kind * D + i * 128 : kind * D + (i + 1) * 128] = both.T
        rows = slice(m * TOK, (m + 1) * TOK)
        gives.append(
            send(
                right_q.at[rows, pl.ds(pl.multiple_of(other * WIDTHS[0], 512), WIDTHS[0])],
                peer_right.at[rows, 0 : WIDTHS[0]], (swap_send, swap_recv), (1, 9)[m], to_core,
            )
        )
        gives[m].start()
    sum_q = jnp.sum(right_q[:, :D].astype(f32), axis=0, keepdims=True)
    sum_v = jnp.sum(right_q[:, 2 * D :].astype(f32), axis=0, keepdims=True)
    row = lax.broadcasted_iota(jnp.int32, (16, TOK), 0)
    own_vec[...] = jnp.zeros_like(own_vec)
    for f in range(N_FSDP):
        cols = slice(f * TOK, (f + 1) * TOK)
        value = jnp.where(row == 0, sum_q[:, cols], jnp.where(row == 1, sum_v[:, cols], vec[f]))
        own_vec[f // 2, f % 2, 0, 0] = value.astype(bf16)
    give_vec = send(own_vec, peer_vec, (swap_send, swap_recv), 8, to_core)
    give_vec.start()
    for copy in gives:
        copy.wait()
    for p, at, width in late:
        if width == COLS:
            multiply(p, at // COLS)
        else:
            give_vec.wait()
            stores[3][0] = (own_vec[...].astype(f32) + peer_vec[...].astype(f32)).astype(bf16)
        begin(p, at, width)
    for n in range(6):
        fetch_w[n].wait()
        part = dot_nt(right_q[:, n * COLS : (n + 1) * COLS], w_part[n % 2])
        if n == 0:
            out_x[...] = part
        else:
            out_x[...] += part
        if n < 4:
            fetch_w[n + 2].start()
    for piece in late:
        relay(*piece)
    for piece in early:
        reduce(2, *piece)
    for phase in range(3):
        for piece in late:
            reduce(phase, *piece)
    squares = square_acc[...]
    yl, z = lax.axis_index("yl"), lax.axis_index("z")
    z_first, y_first = slice(0, HALF_Z), slice(HALF_Z, 6272)
    to_y = {"yl": 1 - yl}
    gather_sems = (gather_send, gather_recv)
    sq_sems = (sq_send, sq_recv)

    def spread(buffer, axis, base):
        at = coordinate(axis)
        out = []
        for step in (1, 2, 3):
            out.append(send(buffer.at[at], buffer.at[at], sq_sems, base + step - 1, peer(axis, step)[0]))
        return out

    def total(buffer):
        return (buffer[0] + buffer[1]) + (buffer[2] + buffer[3])

    sq_z[z] = squares
    squares_z = spread(sq_z, "z", 0)
    first_z = [
        send(gathered.at[core, row_place, :, z_first], gathered.at[core, row_place, :, z_first], gather_sems, step - 1, peer("z", step)[0])
        for step in (1, 2, 3)
    ]
    first_y = send(gathered.at[core, row_place, :, y_first], gathered.at[core, row_place, :, y_first], gather_sems, 3, to_y)
    for copy in (*squares_z, *first_z, first_y):
        copy.start()
    for copy in squares_z:
        copy.wait()
    y_at = coordinate("y")
    sq_y[y_at] = total(sq_z)
    squares_y = spread(sq_y, "y", 3)
    for copy in squares_y:
        copy.start()
    for copy in (*first_z, first_y):
        copy.wait()
    quarter = pl.ds(yl * 4, 4)
    second_y = send(
        gathered.at[core, quarter, :, z_first], gathered.at[core, quarter, :, z_first], gather_sems, 4, to_y
    )
    second_y.start()
    second_z = []
    for step in (1, 2, 3):
        for half in range(2):
            view = gathered.at[core, half * 4 + z, :, y_first]
            second_z.append(send(view, view, gather_sems, 5 + (step - 1) * 2 + half, peer("z", step)[0]))
    for copy in second_z:
        copy.start()
    for copy in squares_y:
        copy.wait()
    x_at = coordinate("x")
    sq_x[x_at] = total(sq_y)
    squares_x = spread(sq_x, "x", 6)
    for copy in squares_x:
        copy.start()
    for copy in squares_x:
        copy.wait()
    sq_c[core] = total(sq_x)
    square_c = send(sq_c.at[core], sq_c.at[core], sq_sems, 9, to_core)
    square_c.start()
    square_c.wait()
    out_sq[...] = sq_c[0] + sq_c[1]
    second_y.wait()
    for copy in second_z:
        copy.wait()
    last = send(gathered.at[core], gathered.at[core], gather_sems, 11, to_core)
    last.start()
    last.wait()
    locals_ = []
    for c in range(2):
        for p in range(3):
            for b in range(N_EARLY[p] + 1):
                i, col = PRODUCT[(p, b)]
                target, base = ((out_attn, 0), (out_attn, 3072), (out_ffn, 0), (out_ffn, FF))[i]
                base = base + c * WIDTHS[i] + col
                at = PART_AT[p] + b * COLS
                locals_.append(
                    pltpu.make_async_copy(
                        gathered.at[c, :, :, at : at + COLS], target.at[:, :, base : base + COLS],
                        out_sem.at[len(locals_)],
                    )
                )
    locals_.append(pltpu.make_async_copy(gathered.at[0, :, :, 6144:], out_vec, out_sem.at[len(locals_)]))
    for copy in locals_:
        copy.start()
    for copy in locals_:
        copy.wait()


def back(lefts, rights, vec, grad_ready, held, full, lse, w_qkv):
    vmem = pl.BlockSpec(memory_space=pltpu.VMEM)
    hbm = pl.BlockSpec(memory_space=pl.ANY)
    scratch = [
        pltpu.VMEM((4, D, ROWS), bf16),
        pltpu.VMEM((ROWS, 6144), bf16),
        pltpu.VMEM((ROWS, 6144), bf16),
        pltpu.VMEM((4, 2, 2, 4, 16, 128), bf16),
        pltpu.VMEM((4, 2, 2, 4, 16, 128), bf16),
    ]
    for kind in range(6):
        n = kind if kind < 3 else kind - 2
        for p, count, width in (*((p, N_EARLY[p] + 1, COLS) for p in range(3)), (0, 1, 128)):
            landing = (3,) if kind >= 3 else ()
            scratch.append(pltpu.VMEM((count, *landing, *lead(ORDERS[p], n), 16, width), bf16))
    scratch += [
        pltpu.VMEM((2, 8, 16, 6272), bf16),
        pltpu.VMEM((4, 8, 128), f32),
        pltpu.VMEM((4, 8, 128), f32),
        pltpu.VMEM((4, 8, 128), f32),
        pltpu.VMEM((2, 8, 128), f32),
        pltpu.VMEM((N_CTX, MB, SENT, TOK), bf16),
        pltpu.VMEM((N_CTX, MB, HEAD, TOK), bf16),
        pltpu.VMEM((N_CTX, MB, 3 * HEAD, TOK), bf16),
        pltpu.VMEM((N_CTX, MB, 3 * HEAD, TOK), bf16),
        pltpu.VMEM((ROWS, 3 * D), bf16),
        pltpu.VMEM((PACK, HEAD), bf16),
        pltpu.VMEM((PACK, HEAD), bf16),
        pltpu.VMEM((HEAD, PACK), bf16),
        pltpu.VMEM((PACK, TOK), f32),
        pltpu.VMEM((PACK, 2 * HEAD), f32),
        pltpu.VMEM((8, 128), f32),
        pltpu.VMEM((2, D, COLS), bf16),
    ]
    for count in (10, 10, 156, 156, 12, 12, 10, 10, 32, 32, 32, 32, 10, 25):
        scratch.append(pltpu.SemaphoreType.DMA((count,)))
    out = pl.pallas_call(
        back_kernel,
        in_specs=[vmem] * 4 + [hbm] * 3 + [vmem, vmem, hbm, vmem, vmem, hbm],
        out_specs=[hbm, hbm, hbm, vmem, vmem],
        out_shape=[
            jax.ShapeDtypeStruct((8, 16, 4 * D), bf16),
            jax.ShapeDtypeStruct((8, 16, 2 * FF), bf16),
            jax.ShapeDtypeStruct((8, 16, 128), bf16),
            jax.ShapeDtypeStruct((8, 128), f32),
            jax.ShapeDtypeStruct((ROWS, D), f32),
        ],
        scratch_shapes=scratch,
        compiler_params=pltpu.CompilerParams(
            collective_id=1, has_side_effects=True, vmem_limit_bytes=60 * 2**20
        ),
        cost_estimate=pl.CostEstimate(
            flops=2 * 512 * D * 6144 + 10 * MB * PACK * PACK * HEAD, bytes_accessed=16 * 2**20,
            transcendentals=MB * PACK * PACK,
        ),
        name="back",
    )(*lefts, *rights, vec, grad_ready, held, full, lse, w_qkv)
    return out[0].reshape(TOK, 4 * D), out[1].reshape(TOK, 2 * FF), out[2], out[3], out[4]


def layer_stats(values, gain_row, shift_row):
    center = values - jnp.mean(values, axis=-1, keepdims=True)
    inverse = lax.rsqrt(jnp.mean(center * center, axis=-1, keepdims=True) + NORM_EPS)
    normal = center * inverse
    return (normal * gain_row + shift_row, normal, inverse)


def layer_back(grad_value, normal, inverse, gain_row):
    scaled = grad_value * gain_row
    return inverse * (
        scaled
        - jnp.mean(scaled, axis=-1, keepdims=True)
        - normal * jnp.mean(scaled * normal, axis=-1, keepdims=True)
    )


N_CHUNK = 8
CHUNK = FF // N_CHUNK
ERF_TOP = (
    -2.72614225801306e-10, 2.77068142495902e-08, -2.10102402082508e-06, -5.69250639462346e-05,
    -7.34990630326855e-04, -2.95459980854025e-03, -1.60960333262415e-02,
)
ERF_LOW = (
    -1.45660718464996e-05, -2.13374055278905e-04, -1.68282697438203e-03, -7.37332916720468e-03,
    -1.42647390514189e-02,
)


def erf(value):
    value = jnp.clip(value, -4.0, 4.0)
    square = value * value
    top, low = jnp.full_like(square, ERF_TOP[0]), jnp.full_like(square, ERF_LOW[0])
    for c in ERF_TOP[1:]:
        top = top * square + c
    for c in ERF_LOW[1:]:
        low = low * square + c
    return value * top / low


def w_block(ref, n):
    per = ref.shape[-1] // CHUNK
    at = (n % per) * CHUNK
    return ref[n // per, :, :, :, at : at + CHUNK].reshape(D, CHUNK)


def dense_part(
    mixed_ref, x_ref, cot_ref, seg_ref, small_ref, w_out, w_one, w_two, before,
    out_ref, one_ref, x_t, o_t, h_t, f_t, a_low_ref, du_ref, g_ref, vec_ref, ready_ref,
    mixed, normal_one_ref, slope, total,
):
    def row(i):
        return small_ref[i : i + 1, :]

    def put(i, value):
        for f in range(N_FSDP):
            vec_ref[f, i : i + 1, :] = value[:, f * TOK : (f + 1) * TOK]

    def sums(value):
        return jnp.sum(value, axis=0, keepdims=True)

    vec_ref[...] = jnp.zeros_like(vec_ref)
    for m in range(MB):
        tok = slice(m * TOK, (m + 1) * TOK)
        for i in range(HEADS // 2):
            both = jnp.concatenate([mixed_ref[2 * i, m], mixed_ref[2 * i + 1, m]], axis=0)
            o_t[i * 128 : (i + 1) * 128, tok] = both
            mixed[tok, i * 128 : (i + 1) * 128] = both.T
    before(0)
    branch = jnp.concatenate([dot(mixed[...], w_block(w_out, n)) for n in range(2)], axis=1)
    normed_one, normal_one, inverse_one = layer_stats(x_ref[...].astype(f32) + branch + row(2), row(4), row(5))
    normal_one_ref[...] = normal_one
    normed_low = normed_one.astype(bf16)
    h_t[...] = normed_low.T
    total[...] = normed_one + row(3)
    before(1)
    for n in range(N_CHUNK):
        cols = slice(n * CHUNK, (n + 1) * CHUNK)
        bias = small_ref[8 + n // 2 : 9 + n // 2, (n % 2) * CHUNK : (n % 2 + 1) * CHUNK]
        u = dot(normed_low, w_block(w_one, n)) + bias
        share = 0.5 + 0.5 * erf(u * math.sqrt(0.5))
        g_ref[:, cols] = (u * share).astype(bf16)
        slope[:, cols] = share + u * (jnp.exp(-0.5 * u * u) * (1.0 / math.sqrt(2.0 * math.pi)))
    before(2)
    for n in range(N_CHUNK):
        total[...] += dot_nt(g_ref[:, n * CHUNK : (n + 1) * CHUNK], w_block(w_two, n))
    output, normal_two, inverse_two = layer_stats(total[...], row(6), row(7))
    keep = []
    for m in range(MB):
        inside = jnp.where(seg_ref[m, 0:1, :].astype(f32) < 8.0, 1.0, 0.0)
        keep.append(jnp.broadcast_to(inside, (TOK, TOK)).T[:, 0:1])
    keep = jnp.concatenate(keep, axis=0)
    out_ref[...] = (output * keep).astype(bf16)
    grad_out = cot_ref[...].astype(f32) * keep
    put(6, sums(grad_out * normal_two))
    put(7, sums(grad_out))
    grad_two = layer_back(grad_out, normal_two, inverse_two, row(6))
    f_low = grad_two.astype(bf16)
    f_t[...] = f_low.T
    put(3, sums(f_low.astype(f32)))
    total[...] = grad_two
    for n in range(N_CHUNK):
        cols = slice(n * CHUNK, (n + 1) * CHUNK)
        du = (dot(f_low, w_block(w_two, n)) * slope[:, cols]).astype(bf16)
        du_ref[:, cols] = du
        part = sums(du.astype(f32))
        for i in range(CHUNK // TOK):
            f = (n % 2) * (CHUNK // TOK) + i
            vec_ref[f, 8 + n // 2 : 9 + n // 2, :] = part[:, i * TOK : (i + 1) * TOK]
        total[...] += dot_nt(du, w_block(w_one, n))
    grad_normed = total[...]
    normal_one = normal_one_ref[...]
    put(4, sums(grad_normed * normal_one))
    put(5, sums(grad_normed))
    grad_one = layer_back(grad_normed, normal_one, inverse_one, row(4))
    one_ref[...] = grad_one
    a_low = grad_one.astype(bf16)
    a_low_ref[...] = a_low
    put(2, sums(a_low.astype(f32)))
    for n in range(2):
        part = a_low[:, n * CHUNK : (n + 1) * CHUNK]
        part = dot_nt(part, w_block(w_out, n))
        grad_mixed = part if n == 0 else grad_mixed + part
    grad_mixed = grad_mixed.T.astype(bf16)
    for h in range(HEADS):
        for m in range(MB):
            ready_ref[h, m] = grad_mixed[h * HEAD : (h + 1) * HEAD, m * TOK : (m + 1) * TOK]
    x_t[...] = x_ref[...].T


def adamw(weight, grad_value, first, second, rate, decay):
    first_new = BETA_FIRST * first + (1.0 - BETA_FIRST) * grad_value
    second_new = BETA_SECOND * second + (1.0 - BETA_SECOND) * grad_value * grad_value
    first_hat = first_new * (1.0 / (1.0 - BETA_FIRST**STEP))
    second_hat = second_new * (1.0 / (1.0 - BETA_SECOND**STEP))
    weight_new = weight - rate * (first_hat / (jnp.sqrt(second_hat) + ADAM_EPS) + decay * weight)
    return (weight_new, first_new, second_new)


def finish_kernel(
    squares, grad_vec, grad_attn, grad_ffn, aw, am, av, fw, fm, fv, vw, vm, vv, one, grad_x, y,
    norm, aw_new, am_new, av_new, fw_new, fm_new, fv_new, vw_new, vm_new, vv_new, a_copy, f_copy, bias, dx, y_out,
):
    total = jnp.sum(jnp.sum(squares[...], axis=0, keepdims=True), axis=1, keepdims=True)
    root = jnp.sqrt(total)
    norm[...] = root
    factor = jnp.minimum(1.0, CLIP_NORM / (root + 1e-06))
    rate = D ** (-0.5)
    for grad, ins, outs, low, scale in (
        (grad_attn, (aw, am, av), (aw_new, am_new, av_new), a_copy, ATTN_RATE_SCALE * rate),
        (grad_ffn, (fw, fm, fv), (fw_new, fm_new, fv_new), f_copy, rate),
    ):
        for at in range(0, grad.shape[1], 1024):
            cols = slice(at, at + 1024)
            weight, first, second = adamw(
                ins[0][:, cols], grad[:, cols].astype(f32) * factor, ins[1][:, cols], ins[2][:, cols], scale,
                WEIGHT_DECAY,
            )
            outs[0][:, cols] = weight
            outs[1][:, cols] = first
            outs[2][:, cols] = second
            low[:, cols] = weight.astype(bf16)
    clipped = grad_vec[0].astype(f32) * factor
    vw_new[...], vm_new[...], vv_new[...] = adamw(
        vw[...], clipped[:12], vm[...], vv[...], RATE_VECTOR, 0.0
    )
    bias[...] = clipped[2:3]
    dx[...] = (one[...] + grad_x[...]).astype(bf16)
    y_out[...] = y[...]


def finish(squares, grad_vec, grad_attn, grad_ffn, attn, ffn, vec, one, grad_x, y):
    steps = 8
    rows = TOK // steps
    whole = lambda a: pl.BlockSpec(a.shape, lambda i: (0,) * len(a.shape))
    part = lambda a: pl.BlockSpec((a.shape[0] // steps, a.shape[1]), lambda i: (i, 0))
    shape = lambda a, dt=f32: jax.ShapeDtypeStruct(a.shape, dt)
    ins = [squares, grad_vec, grad_attn, grad_ffn, *attn, *ffn, *vec, one, grad_x, y]
    specs = [whole(squares), pl.BlockSpec((1, 16, TOK), lambda i: (0, 0, 0)), part(grad_attn), part(grad_ffn)]
    specs += [part(a) for a in (*attn, *ffn)] + [whole(a) for a in vec] + [part(a) for a in (one, grad_x, y)]
    outs = [jax.ShapeDtypeStruct((1, 1), f32), *(shape(a) for a in (*attn, *ffn, *vec))]
    outs += [shape(attn[0], bf16), shape(ffn[0], bf16), jax.ShapeDtypeStruct((1, TOK), f32), shape(one, bf16), shape(y, bf16)]
    out_specs = [whole(outs[0]), *(part(a) for a in outs[1:7]), *(whole(a) for a in outs[7:10])]
    out_specs += [part(outs[10]), part(outs[11]), whole(outs[12]), part(outs[13]), part(outs[14])]
    return pl.pallas_call(
        finish_kernel,
        grid=(steps,),
        in_specs=specs,
        out_specs=out_specs,
        out_shape=outs,
        compiler_params=pltpu.CompilerParams(vmem_limit_bytes=40 * 2**20),
        cost_estimate=pl.CostEstimate(flops=40 * 12 * D * TOK, bytes_accessed=44 * 2**20, transcendentals=24 * D * TOK),
        name="finish",
    )(*ins)


def shards(
    tokens, cotangent, dest, lengths, attn_weight, attn_first, attn_second,
    ffn_weight, ffn_first, ffn_second, vectors, vec_first, vec_second,
):
    core = lax.axis_index("core")

    def half(weight, base, width):
        return lax.dynamic_slice_in_dim(weight, base + core * width, width, 1).astype(bf16)

    shard = jnp.concatenate(
        [half(attn_weight, 0, 1536), half(attn_weight, 3 * D, 512), half(ffn_weight, 0, 2048), half(ffn_weight, FF, 2048)],
        axis=1,
    )
    x = tokens.reshape(ROWS, D)
    cot = cotangent.reshape(ROWS, D)
    ends = jnp.cumsum(lengths[:, 0], axis=1)
    seg = jnp.sum((dest[:, 0, :, None] >= ends[:, None, :]).astype(jnp.int32), axis=2)
    seg_rows = jnp.broadcast_to(seg.astype(bf16)[:, None, :], (MB, 16, TOK))
    vec_shard = jnp.pad(vectors.astype(bf16), ((0, 4), (0, 0)))
    (
        w_qkv, held, mixed_full, lse, output, grad_one, x_t, o_t, h_t, f_t, a_low, du, g, vec_rows, grad_ready,
    ) = front(shard, vec_shard, x, seg_rows, cot)
    grad_attn, grad_ffn, grad_vec, squares, grad_x = back(
        (x_t, o_t, h_t, f_t),
        (a_low, du, g),
        vec_rows,
        grad_ready,
        held,
        mixed_full,
        lse,
        w_qkv.reshape(D, 3 * D),
    )
    (
        norm, aw, am, av, fw, fm, fv, vw, vm, vv, a_copy, f_copy, bias, input_grad, output,
    ) = finish(
        squares, grad_vec, grad_attn, grad_ffn,
        (attn_weight, attn_first, attn_second), (ffn_weight, ffn_first, ffn_second),
        (vectors, vec_first, vec_second), grad_one, grad_x, output,
    )
    return (
        output.reshape(tokens.shape), input_grad.reshape(tokens.shape), norm.reshape(()),
        aw, am, av, fw, fm, fv, vw, vm, vv, a_copy, f_copy, bias.reshape(TOK),
    )


def solution(mesh):
    fine = Mesh(mesh.devices.reshape(2, 4, 2, 4, 2), ("yl", "z", "core", "x", "yh"))
    act = P(None, FSDP, CTX, None)
    row = P(FSDP, None)
    col = P(None, FSDP)
    return jax.shard_map(
        shards,
        mesh=fine,
        in_specs=(act, act, P(None, FSDP, CTX), P(None, FSDP, None), row, row, row, row, row, row, col, col, col),
        out_specs=(act, act, P(), row, row, row, row, row, row, col, col, col, row, row, P(FSDP)),
        check_vma=False,
    )
```

```python
import math

import jax
import jax.numpy as jnp
from jax import lax
from jax.experimental import pallas as pl
from jax.experimental.pallas import tpu as pltpu
from jax.sharding import Mesh, PartitionSpec as P

HEADS = 16
HEAD = 64
STEP = 10
MB = 2
TOK = 128
ROWS = MB * TOK
D = 1024
FF = 4096
N_CTX = 16
N_FSDP = 8
PACK = 2048
SENT = 208

NORM_EPS = 1e-05
CLIP_NORM = 1.0
BETA_FIRST = 0.9
BETA_SECOND = 0.999
ADAM_EPS = 1e-08
WEIGHT_DECAY = 0.01
RATE_VECTOR = 0.3
ATTN_RATE_SCALE = 3.0
NEG_LARGE = -1e30
SCALE2 = HEAD ** (-0.5) * math.log2(math.e)
SCALE = HEAD ** (-0.5)
CONTRACT_ROWS = (((0,), (0,)), ((), ()))
CONTRACT_COLS = (((1,), (1,)), ((), ()))
CTX = ("yl", "z", "core")
FSDP = ("x", "yh")
ALL = ("x", "yh", "yl", "z", "core")
BLK = 256
NBLK = PACK // BLK
f32 = jnp.float32
bf16 = jnp.bfloat16


def dot(a, b):
    return jnp.dot(a, b, preferred_element_type=f32)


def dot_nt(a, b):
    return lax.dot_general(a, b, CONTRACT_COLS, preferred_element_type=f32)


def dot_tn(a, b):
    return lax.dot_general(a, b, CONTRACT_ROWS, preferred_element_type=f32)


MESH_ID = pl.DeviceIdType.MESH
COLS = 512
N_BLK = 4
ORDERS = (("x", "z", "y"), ("z", "y", "x"), ("y", "x", "z"))
EARLY = ((0, 0), (1, 0), (2, 0), (0, 1), (1, 1), (2, 1), (0, 2), (1, 2), (2, 2))
N_EARLY = (3, 3, 3)
EARLY_PRODUCT = ((2, 0), (2, 512), (2, 1024), (2, 1536), (3, 0), (3, 512), (3, 1024), (3, 1536), (1, 0))
PRODUCT = {part_block: product for part_block, product in zip(EARLY, EARLY_PRODUCT)}
PRODUCT.update({(p, N_EARLY[p]): (0, p * COLS) for p in range(3)})
PART_AT = (0, 2048, 4096, 6144)
VEC_AT = 3072
WIDTHS = (1536, 512, 2048, 2048)
OFFSETS = (0, 1536, 2048, 4096)
HALF_Z = 3072
TASKS = {}
for _n, _at in enumerate((2, 2, 2, 5, 5, 5, 8, 8, 8)):
    TASKS.setdefault(_at, []).append(("relay", *EARLY[_n]))
for _n, _at in enumerate((7, 7, 7, 10, 10, 10, 13, 13, 13)):
    TASKS.setdefault(_at, []).append((0, *EARLY[_n]))


def coordinate(axis):
    if axis == "y":
        return lax.axis_index("yh") * 2 + lax.axis_index("yl")
    return lax.axis_index(axis)


def peer(axis, step):
    at = lax.rem(coordinate(axis) + step, 4)
    if axis == "y":
        return {"yh": at // 2, "yl": lax.rem(at, 2)}, at
    return {axis: at}, at


def pick(ref, axis, at, dims):
    index = []
    for d in dims:
        if d == axis:
            index.append(at)
        elif axis == "y" and d == "yh":
            index.append(at // 2)
        elif axis == "y" and d == "yl":
            index.append(lax.rem(at, 2))
        else:
            index.append(slice(None))
    return ref.at[tuple(index)]


def dims_after(order, n):
    dims = ["x", "yh", "yl", "z"]
    for axis in order[:n]:
        for d in ("yh", "yl") if axis == "y" else (axis,):
            dims.remove(d)
    return dims


SIZES = {"x": 4, "yh": 2, "yl": 2, "z": 4}


def lead(order, n):
    return tuple(SIZES[d] for d in dims_after(order, n))


def send(src, dst, sems, index, to):
    return pltpu.make_async_remote_copy(
        src_ref=src, dst_ref=dst, send_sem=sems[0].at[index], recv_sem=sems[1].at[index],
        device_id=to, device_id_type=MESH_ID,
    )


def load_side(qkv_ref, m, keys, values, keys_t, values_t, seg_col):
    for s in range(N_CTX):
        at = slice(s * TOK, (s + 1) * TOK)
        key_t = qkv_ref[s, m, HEAD : 2 * HEAD, :]
        value_t = qkv_ref[s, m, 2 * HEAD : 3 * HEAD, :]
        keys[at, :] = key_t.T
        if values is not None:
            values[at, :] = value_t.T
        if keys_t is not None:
            keys_t[:, at] = key_t
        if values_t is not None:
            values_t[:, at] = value_t
        seg = qkv_ref[s, m, 3 * HEAD : 3 * HEAD + 1, :].astype(f32)
        seg_col[at, :] = jnp.broadcast_to(seg, (TOK, TOK)).T


def pair(ref, m, j, rows):
    return jnp.concatenate([ref[2 * j, m, rows, :], ref[2 * j + 1, m, rows, :]], axis=1)


def query_forward(held, m, j, out, full, lse_out, keys, values_t, seg_col, scores):
    query_t = pair(held, m, j, slice(0, HEAD))
    seg_row = pair(held, m, j, slice(3 * HEAD, 3 * HEAD + 1)).astype(f32)
    top = jnp.full((1, BLK), NEG_LARGE, f32)
    for k in range(NBLK):
        at = slice(k * BLK, (k + 1) * BLK)
        s = dot(keys[at, :], query_t) * SCALE2
        col = seg_col[at, :]
        same = jnp.concatenate([col, col], axis=1) == seg_row
        s = jnp.where(same, s, NEG_LARGE)
        scores[at, :] = s
        top = jnp.maximum(top, jnp.max(s, axis=0, keepdims=True))
    total = jnp.zeros((1, BLK), f32)
    acc = jnp.zeros((HEAD, BLK), f32)
    for k in range(NBLK):
        at = slice(k * BLK, (k + 1) * BLK)
        p = jnp.exp2(scores[at, :] - top)
        total = total + jnp.sum(p, axis=0, keepdims=True)
        acc = acc + dot(values_t[:, at], p.astype(bf16))
    acc = acc / total
    lse = top + jnp.log2(total)
    for half in range(2):
        cols = slice(half * TOK, (half + 1) * TOK)
        out[2 * j + half, m] = acc[:, cols].astype(bf16)
        full[2 * j + half, m] = acc[:, cols]
        lse_out[2 * j + half, m] = lse[:, cols]


GROUP_COLS = (1536, 2048, 2048, 512)
GROUP_AT = (0, 2048, 4096, 1536)
SPLITS = ((512, 1024), (1024, 1536), (1024, 1536), (128, 256))
N_COPY = 31
GROUPS = (3, 1, 2)
BEFORE = tuple((0, op) for op in ("z1", "x1", "z2", "y1", "z3", "x2", "x3", "y2", "z4", "x4", "x5"))
BEFORE += tuple((g, op) for op in ("z1", "z2", "y1") for g in GROUPS)
BEFORE += tuple((0, op) for op in ("y3", "z5", "sx", "sy", "sz", "got"))
PUSHED = tuple((g, op) for op in ("z3", "x1", "x2", "x3") for g in GROUPS)
STEPS = {
    0: tuple((g, "z4") for g in GROUPS),
    1: tuple((g, "y2") for g in GROUPS),
    3: tuple((g, "x4") for g in GROUPS),
    6: tuple((g, "x5") for g in GROUPS),
    9: tuple((g, "y3") for g in GROUPS),
    12: tuple((g, "z5") for g in GROUPS),
}
LAST = (
    tuple((g, op) for g in (3, 1) for op in ("sx", "sy", "sz")) + ((3, "got"),),
    tuple((2, op) for op in ("sx", "sy", "sz")) + ((1, "got"),),
    ((2, "got"),),
)


def ctx_device(t):
    return {"yl": t // 8, "z": lax.rem(t // 2, 4), "core": lax.rem(t, 2)}


def rows_at(start, size):
    return pl.ds(pl.multiple_of(start, 16), size)


class Gather:
    def __init__(self, g, shard, dest, sems, base, local_sem):
        core = lax.axis_index("core")
        x, z = lax.axis_index("x"), lax.axis_index("z")
        yh, yl = lax.axis_index("yh"), lax.axis_index("yl")
        y = yh * 2 + yl
        every = slice(None)
        zq, half = rows_at(z * 32, 32), rows_at(yl * 64, 64)
        cross = {"yh": 1 - yh, "yl": 1 - yl}
        count = [0]
        x_end, y_end = SPLITS[g]
        x_cols, y_cols, z_cols = slice(0, x_end), slice(x_end, y_end), slice(y_end, GROUP_COLS[g])

        def given(rows, cols):
            return shard.at[rows, GROUP_AT[g] + cols.start : GROUP_AT[g] + cols.stop]

        def make(src, dst, to):
            copy = send(src, dst, sems, base + count[0], to)
            count[0] += 1
            return copy

        def own(rows, cols, to):
            return make(given(rows, cols), dest(core, x, yh, rows, cols), to)

        def pass_on(xs, yhs, rows, cols, to):
            view = dest(core, xs, yhs, rows, cols)
            return make(view, view, to)

        x_to = {step: peer("x", step)[0] for step in (1, 2, 3)}
        y_to = {step: peer("y", step)[0] for step in (1, 3)}
        z_to = {step: peer("z", step)[0] for step in (1, 3)}
        x_before, x_after = lax.rem(x + 3, 4), lax.rem(x + 1, 4)
        y_before, y_after = lax.rem(y + 3, 4), lax.rem(y + 1, 4)
        z_before, z_after = lax.rem(z + 3, 4), lax.rem(z + 1, 4)
        self.copies = {
            "x1": [own(every, x_cols, cross)],
            "x2": [own(every, x_cols, x_to[s]) for s in (1, 3)],
            "z1": [own(zq, z_cols, cross)],
            "z2": [own(zq, z_cols, x_to[s]) for s in (1, 3, 2)],
            "y1": [own(half, y_cols, x_to[s]) for s in (1, 3, 2)],
            "x3": [pass_on(x, 1 - yh, every, x_cols, x_to[s]) for s in (1, 3)],
            "z3": [pass_on(x, 1 - yh, zq, z_cols, x_to[s]) for s in (1, 3, 2)],
            "y2": [pass_on(every, yh, half, y_cols, y_to[s]) for s in (1, 3)],
            "z4": [pass_on(every, every, zq, z_cols, z_to[s]) for s in (1, 3)],
            "x4": [
                pass_on(x_before, yh, slice(0, 64), x_cols, x_to[1]),
                pass_on(x_after, yh, slice(64, 128), x_cols, x_to[3]),
            ],
            "x5": [
                pass_on(x_before, 1 - yh, slice(0, 64), x_cols, x_to[1]),
                pass_on(x_after, 1 - yh, slice(64, 128), x_cols, x_to[3]),
            ],
            "y3": [
                pass_on(every, y_before // 2, rows_at(lax.rem(y_before, 2) * 64, 32), y_cols, y_to[1]),
                pass_on(every, y_after // 2, rows_at(lax.rem(y_after, 2) * 64 + 32, 32), y_cols, y_to[3]),
            ],
            "z5": [
                pass_on(every, every, rows_at(z_before * 32, 16), z_cols, z_to[1]),
                pass_on(every, every, rows_at(z_after * 32 + 16, 16), z_cols, z_to[3]),
            ],
        }
        for name, cols in (("sx", x_cols), ("sy", y_cols), ("sz", z_cols)):
            self.copies[name] = [pass_on(every, every, every, cols, {"core": 1 - core})]
        self.places = [
            pltpu.make_async_copy(given(rows, cols), dest(core, x, yh, rows, cols), local_sem.at[3 * g + n])
            for n, (rows, cols) in enumerate(((every, x_cols), (half, y_cols), (zq, z_cols)))
        ]

    needs = {
        "x3": ("x1",), "z3": ("z1",), "y2": ("y1",), "z4": ("z2", "z3"), "x4": ("x2",), "x5": ("x3",), "y3": ("y2",),
        "z5": ("z4",), "sx": ("x4", "x5"), "sy": ("y3",), "sz": ("z5",),
    }

    def step(self, name):
        if name == "got":
            for copy in (*self.copies["sx"], *self.copies["sy"], *self.copies["sz"]):
                copy.wait_recv()
            return
        if name == "end":
            for copies in self.copies.values():
                for copy in copies:
                    copy.wait_send()
            return
        for need in self.needs.get(name, ()):
            for copy in self.copies[need]:
                copy.wait_recv()
        if name == "z1":
            for copy in self.places:
                copy.start()
        if name == "z3":
            for copy in self.places:
                copy.wait()
        for copy in self.copies[name]:
            copy.start()


def greet_all():
    barrier = pltpu.get_barrier_semaphore()
    place = lax.axis_index(CTX)
    others = [ctx_device(lax.rem(place + d, N_CTX)) for d in range(1, N_CTX)]
    others += [peer(axis, step)[0] for axis in ("x", "y") for step in (1, 2, 3)]
    for other in others:
        pl.semaphore_signal(barrier, inc=1, device_id=other, device_id_type=MESH_ID)
    pl.semaphore_wait(barrier, len(others))


def front_kernel(
    w_attn, w_ffn, vectors, dest_ref, lengths, x_ref, cot_ref,
    out_attn, out_held, out_full, out_lse,
    out_ref, one_ref, x_t, o_t, h_t, f_t, a_low_ref, du_ref, g_ref, vec_ref, ready_ref,
    wa, w_one, w_two, w_out, vecs, small, ready, held, mixed, out_t, keys, values_t, seg_col, scores,
    mixed_rows, normal_one, slope, total, stage, shard, vec_shard, seg_ref,
    ag_send, ag_recv, vec_send, vec_recv, q_send, q_recv, o_send, o_recv, local_sem, out_sem, in_sem,
):
    core = lax.axis_index("core")
    place = lax.axis_index(CTX)
    x, yh, yl = lax.axis_index("x"), lax.axis_index("yh"), lax.axis_index("yl")

    weights = (wa, w_one, w_two, w_out)

    def dest(g):
        def view(c, xs, yhs, rows, cols):
            return weights[g].at[c, xs, yhs, rows, cols]

        return view

    gathers = [
        Gather(g, shard, dest(g), (ag_send, ag_recv), g * N_COPY, local_sem) for g in range(4)
    ]
    vec_sems = (vec_send, vec_recv)
    vec_cross = send(vec_shard, vecs.at[x, yh], vec_sems, 0, {"yh": 1 - yh, "yl": 1 - yl})
    vec_x = [send(vec_shard, vecs.at[x, yh], vec_sems, s, peer("x", s)[0]) for s in (1, 2, 3)]
    vec_x2 = [
        send(vecs.at[x, 1 - yh], vecs.at[x, 1 - yh], vec_sems, 3 + s, peer("x", s)[0]) for s in (1, 2, 3)
    ]
    fetches = []
    for g in range(4):
        start = (0, 0, FF, 3 * D)[g] + core * GROUP_COLS[g]
        source = w_ffn if g in (1, 2) else w_attn
        fetches.append(
            pltpu.make_async_copy(
                source.at[:, pl.ds(pl.multiple_of(start, 512), GROUP_COLS[g])],
                stage.at[:, GROUP_AT[g] : GROUP_AT[g] + GROUP_COLS[g]], in_sem.at[g],
            )
        )
        fetches[g].start()
    vec_shard[...] = jnp.concatenate([vectors[...], jnp.zeros((4, TOK), f32)], axis=0).astype(bf16)
    for m in range(MB):
        end = jnp.zeros((1, 1), jnp.int32)
        seg = jnp.zeros((1, TOK), jnp.int32)
        for j in range(8):
            end = end + lengths[m : m + 1, j : j + 1]
            seg = seg + jnp.where(dest_ref[m : m + 1, :] >= end, 1, 0)
        seg_ref[m] = jnp.broadcast_to(seg.astype(f32), (16, TOK)).astype(bf16)
    greet_all()
    for g in range(4):
        fetches[g].wait()
    shard[...] = stage[...].astype(bf16)
    for copy in (vec_cross, *vec_x):
        copy.start()
    done = set()

    def stages(todo):
        for g, n in todo:
            if (g, n) not in done:
                done.add((g, n))
                gathers[g].step(n)

    stages(BEFORE[:4])
    vecs[x, yh] = vec_shard[...]
    for s in range(N_CTX):
        ready[s, :, 3 * HEAD :, :] = seg_ref[...]
    vec_cross.wait_recv()
    for copy in vec_x2:
        copy.start()
    stages(BEFORE)
    vec_cross.wait_send()
    for copy in (*vec_x, *vec_x2):
        copy.wait()
    for f in range(N_FSDP):
        small[:, f * TOK : (f + 1) * TOK] = vecs[f // 2, f % 2].astype(f32)

    for part in range(6):
        c, col = part // 3, (part % 3) * 512
        kind, first = part // 2, (part % 2) * 8
        value = jnp.zeros((ROWS, 512), f32)
        weight = wa[c, :, :, :, col : col + 512].reshape(D, 512)
        value = dot(x_ref[...], weight)
        if kind != 1:
            row = 0 if kind == 0 else 1
            value = value + small[row : row + 1, first * HEAD : first * HEAD + 512]
        value = value.T.astype(bf16)
        for h in range(8):
            for m in range(MB):
                ready[first + h, m, kind * HEAD : (kind + 1) * HEAD, :] = value[
                    h * HEAD : (h + 1) * HEAD, m * TOK : (m + 1) * TOK
                ]
    swaps = [[], []]
    for m in range(MB):
        for d in range(1, N_CTX):
            t = lax.rem(place + d, N_CTX)
            swaps[m].append(send(ready.at[t, m], held.at[place, m], (q_send, q_recv), m * N_CTX + d, ctx_device(t)))
            swaps[m][-1].start()
    held[place] = ready[place]
    returns = [[], []]
    for m in range(MB):
        for d in range(1, N_CTX):
            t = lax.rem(place + d, N_CTX)
            returns[m].append(
                send(out_t.at[t, m], mixed.at[place, m], (o_send, o_recv), m * N_CTX + d, ctx_device(t))
            )
    stages(PUSHED)
    outs = [(wa.at[c], out_attn.at[:, :, :, c * 1536 : (c + 1) * 1536]) for c in range(2)]
    outs = [pltpu.make_async_copy(src, dst, out_sem.at[n]) for n, (src, dst) in enumerate(outs)]
    for copy in outs:
        copy.start()
    for m in range(MB):
        for copy in swaps[m]:
            copy.wait_recv()
        load_side(held, m, keys, None, None, values_t, seg_col)

        def query_block(j, _, m=m):
            for at, todo in STEPS.items():
                if at // NBLK == m:

                    @pl.when(j == at % NBLK)
                    def _(todo=todo):
                        stages(todo)

            query_forward(held, m, j, out_t, out_full, out_lse, keys, values_t, seg_col, scores)
            return 0

        lax.fori_loop(0, NBLK, query_block, 0)
        for copy in returns[m]:
            copy.start()
        mixed[place, m] = out_t[place, m]
    outs.append(pltpu.make_async_copy(held, out_held, out_sem.at[4]))
    outs[-1].start()

    def before(n):
        stages(LAST[n])

    for m in range(MB):
        for copy in returns[m]:
            copy.wait_recv()
    dense_part(
        mixed, x_ref, cot_ref, seg_ref, small, w_out, w_one, w_two, before,
        out_ref, one_ref, x_t, o_t, h_t, f_t, a_low_ref, du_ref, g_ref, vec_ref, ready_ref,
        mixed_rows, normal_one, slope, total,
    )
    for m in range(MB):
        for copy in (*swaps[m], *returns[m]):
            copy.wait_send()
    stages([(g, "end") for g in (0, *GROUPS)])
    for copy in outs:
        copy.wait()


def front(w_attn, w_ffn, vectors, dest, lengths, x, cot):
    vmem = pl.BlockSpec(memory_space=pltpu.VMEM)
    hbm = pl.BlockSpec(memory_space=pl.ANY)
    sem = lambda n: pltpu.SemaphoreType.DMA((n,))
    turned = jax.ShapeDtypeStruct((D, ROWS), bf16)
    return pl.pallas_call(
        front_kernel,
        in_specs=[hbm, hbm, vmem, vmem, vmem, vmem, vmem],
        out_specs=[hbm, hbm] + [vmem] * 13,
        out_shape=[
            jax.ShapeDtypeStruct((4, 2, TOK, 3 * D), bf16),
            jax.ShapeDtypeStruct((N_CTX, MB, SENT, TOK), bf16),
            jax.ShapeDtypeStruct((N_CTX, MB, HEAD, TOK), f32),
            jax.ShapeDtypeStruct((N_CTX, MB, 1, TOK), f32),
            jax.ShapeDtypeStruct((ROWS, D), bf16),
            jax.ShapeDtypeStruct((ROWS, D), f32),
            turned, turned, turned, turned,
            jax.ShapeDtypeStruct((ROWS, D), bf16),
            jax.ShapeDtypeStruct((ROWS, FF), bf16),
            jax.ShapeDtypeStruct((ROWS, FF), bf16),
            jax.ShapeDtypeStruct((N_FSDP, 16, TOK), f32),
            jax.ShapeDtypeStruct((HEADS, MB, HEAD, TOK), bf16),
        ],
        scratch_shapes=[
            *(pltpu.VMEM((2, 4, 2, TOK, GROUP_COLS[g]), bf16) for g in range(4)),
            pltpu.VMEM((4, 2, 16, TOK), bf16),
            pltpu.VMEM((16, D), f32),
            pltpu.VMEM((N_CTX, MB, SENT, TOK), bf16),
            pltpu.VMEM((N_CTX, MB, SENT, TOK), bf16),
            pltpu.VMEM((N_CTX, MB, HEAD, TOK), bf16),
            pltpu.VMEM((N_CTX, MB, HEAD, TOK), bf16),
            pltpu.VMEM((PACK, HEAD), bf16),
            pltpu.VMEM((HEAD, PACK), bf16),
            pltpu.VMEM((PACK, TOK), f32),
            pltpu.VMEM((PACK, BLK), f32),
            pltpu.VMEM((ROWS, D), bf16),
            pltpu.VMEM((ROWS, D), f32),
            pltpu.VMEM((ROWS, FF), f32),
            pltpu.VMEM((ROWS, D), f32),
            pltpu.VMEM((TOK, 6144), f32),
            pltpu.VMEM((TOK, 6144), bf16),
            pltpu.VMEM((16, TOK), bf16),
            pltpu.VMEM((MB, 16, TOK), bf16),
            sem(4 * N_COPY), sem(4 * N_COPY), sem(7), sem(7), sem(32), sem(32), sem(32), sem(32),
            sem(12), sem(6), sem(4),
        ],
        compiler_params=pltpu.CompilerParams(
            collective_id=2, has_side_effects=True, vmem_limit_bytes=60 * 2**20
        ),
        cost_estimate=pl.CostEstimate(
            flops=4 * MB * PACK * PACK * HEAD + 2 * ROWS * D * (5 * D + 4 * FF), bytes_accessed=32 * 2**20,
            transcendentals=MB * PACK * PACK,
        ),
        name="front",
    )(w_attn, w_ffn, vectors, dest, lengths, x, cot)


def back_kernel(
    left_x, left_o, left_h, left_f, right_o, right_u, right_g, vec, grad_ready, held_in, full, lse, w_qkv,
    out_attn, out_ffn, out_vec, out_sq, out_x,
    peer_left, own_right, peer_right, own_vec, peer_vec,
    *rest_refs,
):
    stores, rest_refs = rest_refs[:24], rest_refs[24:]
    (
    gathered, sq_z, sq_y, sq_x, sq_c,
    held, grad_held, out_t, landed, right_q, keys, values, keys_t, seg_col, acc_kv, square_acc, w_part,
    swap_send, swap_recv, ring_send, ring_recv, gather_send, gather_recv, sq_send, sq_recv,
    o_send, o_recv, q_send, q_recv, local_sem, out_sem,
    ) = rest_refs
    core = lax.axis_index("core")
    other = 1 - core
    place = lax.axis_index(CTX)
    row_place = lax.axis_index("yl") * 4 + lax.axis_index("z")
    lefts = (left_x, left_o, left_h, left_f)
    rights = (None, right_o, right_u, right_g)
    to_core = {"core": other}

    fetch = pltpu.make_async_copy(held_in, held, local_sem.at[0])
    fetch.start()
    fetches = [fetch]
    for i in range(1, 4):
        cols = pl.ds(pl.multiple_of(core * WIDTHS[i], 512), WIDTHS[i])
        fetches.append(
            pltpu.make_async_copy(
                rights[i].at[:, cols], own_right.at[:, OFFSETS[i] : OFFSETS[i] + WIDTHS[i]], local_sem.at[i]
            )
        )
        fetches[-1].start()
    greet_all()

    pushes, returns = [[], []], [[], []]
    for m in range(MB):
        for d in range(1, N_CTX):
            t = lax.rem(place + d, N_CTX)
            to = ctx_device(t)
            pushes[m].append(
                send(grad_ready.at[t, m], grad_held.at[place, m], (o_send, o_recv), m * N_CTX + d, to)
            )
            returns[m].append(send(out_t.at[t, m], landed.at[place, m], (q_send, q_recv), m * N_CTX + d, to))
    swaps = []
    for i in (2, 3, 1, 0):
        swaps.append(send(lefts[i], peer_left.at[i], (swap_send, swap_recv), 2 * i, to_core))
        if i:
            from_cols = pl.ds(pl.multiple_of(other * WIDTHS[i], 512), WIDTHS[i])
            swaps.append(
                send(
                    rights[i].at[:, from_cols], peer_right.at[:, OFFSETS[i] : OFFSETS[i] + WIDTHS[i]],
                    (swap_send, swap_recv), 2 * i + 1, to_core,
                )
            )
    for m in range(MB):
        for copy in pushes[m]:
            copy.start()
    for copy in swaps:
        copy.start()
    grad_held[place] = grad_ready[place]
    for copy in fetches:
        copy.wait()

    late = [(p, N_EARLY[p] * COLS, COLS) for p in range(3)] + [(0, VEC_AT, 128)]
    early = [(p, b * COLS, COLS) for p, b in EARLY]

    def number(p, at, width):
        return 12 if width != COLS else PART_AT[p] // COLS + at // COLS

    def store(kind, p, at, width):
        return stores[4 * kind + 3].at[0] if width != COLS else stores[4 * kind + p].at[at // COLS]

    def copies(p, phase, at, width):
        order = ORDERS[p]
        axis = order[phase]
        out = []
        for step in (1, 2, 3):
            to, index = peer(axis, step)
            chunk = pick(store(phase, p, at, width), axis, index, dims_after(order, phase))
            land = store(3 + phase, p, at, width).at[step - 1]
            out.append(
                send(
                    chunk, land, (ring_send, ring_recv), 39 + 39 * phase + number(p, at, width) * 3 + step - 1, to
                )
            )
        return out

    def first_copies(p, at, width):
        order = ORDERS[p]
        axis = order[0]
        n = lead(order, 1)[0]
        halves = (slice(0, n // 2), slice(n // 2, n))
        (up, up_at), (_, far_at), (down, down_at) = (peer(axis, step) for step in (1, 2, 3))
        out = []
        for k, (index, half, slot, to) in enumerate(
            (
                (far_at, 0, 2, up), (far_at, 1, 2, down), (up_at, 1, 0, up), (down_at, 0, 1, down),
                (up_at, 0, 0, up), (down_at, 1, 1, down),
            )
        ):
            chunk = pick(store(0, p, at, width), axis, index, dims_after(order, 0)).at[halves[half]]
            land = store(3, p, at, width).at[slot, halves[half]]
            out.append(send(chunk, land, (ring_send, ring_recv), number(p, at, width) * 6 + k, to))
        return out

    def begin(p, at, width):
        for copy in first_copies(p, at, width)[:4]:
            copy.start()

    def relay(p, at, width):
        order = ORDERS[p]
        axis = order[0]
        n = lead(order, 1)[0]
        all_copies = first_copies(p, at, width)
        land = store(3, p, at, width)
        for half, step in ((0, 1), (1, 3)):
            all_copies[half].wait_recv()
            own = pick(store(0, p, at, width), axis, peer(axis, step)[1], dims_after(order, 0))

            def add(i, _, own=own):
                own[i] = (own[i].astype(f32) + land[2, i].astype(f32)).astype(bf16)
                return 0

            lax.fori_loop(half * (n // 2), (half + 1) * (n // 2), add, 0)
            all_copies[4 + half].start()

    def multiply(p, b):
        i, col = PRODUCT[(p, b)]
        if i == 0:
            mine = right_q.at[:, pl.ds(pl.multiple_of(core * WIDTHS[0] + col, 512), COLS)]
        else:
            mine = own_right.at[:, OFFSETS[i] + col : OFFSETS[i] + col + COLS]
        theirs = peer_right.at[:, OFFSETS[i] + col : OFFSETS[i] + col + COLS]

        def rows_block(x, _):
            rows = pl.ds(pl.multiple_of(x * 256, 256), 256)
            value = dot(lefts[i][rows, :], mine[...]) + dot(peer_left[i, rows, :], theirs[...])
            stores[p][b, x] = value.astype(bf16).reshape(2, 2, 4, 16, COLS)
            return 0

        lax.fori_loop(0, 4, rows_block, 0)

    def reduce(phase, p, at, width):
        order = ORDERS[p]
        axis = order[phase]
        land = store(3 + phase, p, at, width)
        if phase == 0:
            all_copies = first_copies(p, at, width)
            for copy in all_copies[:2]:
                copy.wait_send()
            for copy in all_copies[2:]:
                copy.wait()
        else:
            for copy in copies(p, phase, at, width):
                copy.wait()
        own = pick(store(phase, p, at, width), axis, coordinate(axis), dims_after(order, phase))
        if phase < 2:
            dst = store(phase + 1, p, at, width)

            def add(n, _):
                value = own[n].astype(f32)
                for step in range(3 if phase else 2):
                    value = value + land[step, n].astype(f32)
                dst[n] = value.astype(bf16)
                return 0

            lax.fori_loop(0, lead(order, phase + 1)[0], add, 0)
            for copy in copies(p, phase + 1, at, width):
                copy.start()
            return
        value = own[...].astype(f32)
        for step in range(3):
            value = value + land[step].astype(f32)
        to = PART_AT[p] + at if width == COLS else 6144
        gathered[core, row_place, :, to : to + width] = value.astype(bf16)
        square = value * value
        if width != COLS:
            square = square * jnp.where(core == 0, 1.0, 0.0)
        squares = square_acc[...]
        for c in range(0, width, 128):
            squares = squares + square[:8, c : c + 128] + square[8:, c : c + 128]
        square_acc[...] = squares

    def run_task(phase, p, b):
        if phase == "relay":
            relay(p, b * COLS, COLS)
        else:
            reduce(phase, p, b * COLS, COLS)

    square_acc[...] = jnp.zeros_like(square_acc)
    for copy in swaps:
        copy.wait()
    for p, at, width in early:
        multiply(p, at // COLS)
        begin(p, at, width)

    for m in range(MB):
        load_side(held, m, keys, values, keys_t, None, seg_col)
        acc_kv[...] = jnp.zeros_like(acc_kv)
        for copy in pushes[m]:
            copy.wait_recv()

        def query_block(j, _, m=m):
            for at, tasks in TASKS.items():
                if at // NBLK == m:

                    @pl.when(j == at % NBLK)
                    def _(tasks=tasks):
                        for phase, p, b in tasks:
                            run_task(phase, p, b)

            query_t = pair(held, m, j, slice(0, HEAD))
            seg_row = pair(held, m, j, slice(3 * HEAD, 3 * HEAD + 1)).astype(f32)
            grad_t = pair(grad_held, m, j, slice(0, HEAD))
            row_lse = pair(lse, m, j, slice(0, 1))
            delta = jnp.sum(grad_t.astype(f32) * pair(full, m, j, slice(0, HEAD)), axis=0, keepdims=True)
            acc_q = jnp.zeros((HEAD, BLK), f32)
            none = jnp.zeros((BLK, HEAD), bf16)
            sides = jnp.concatenate(
                [jnp.concatenate([query_t.T, none], axis=1), jnp.concatenate([none, grad_t.T], axis=1)], axis=0
            )
            block = lambda k: slice(k * BLK, (k + 1) * BLK)
            ahead = (dot(keys[block(0), :], query_t), dot(values[block(0), :], grad_t))
            behind = None
            for k in range(NBLK + 1):
                if k < NBLK:
                    at = block(k)
                    s, dp = ahead
                    if k + 1 < NBLK:
                        ahead = (dot(keys[block(k + 1), :], query_t), dot(values[block(k + 1), :], grad_t))
                if behind is not None:
                    to, ds, pb = behind
                    acc_q = acc_q + dot(keys_t[:, to], ds)
                    acc_kv[to, :] += dot(jnp.concatenate([ds, pb], axis=1), sides)
                if k < NBLK:
                    col = seg_col[at, :]
                    same = jnp.concatenate([col, col], axis=1) == seg_row
                    p = jnp.exp2(jnp.where(same, s * SCALE2 - row_lse, NEG_LARGE))
                    behind = (at, (p * (dp - delta)).astype(bf16), p.astype(bf16))
            acc_q = (acc_q * SCALE).astype(bf16)
            out_t[2 * j, m, :HEAD, :] = acc_q[:, :TOK]
            out_t[2 * j + 1, m, :HEAD, :] = acc_q[:, TOK:]
            return 0

        lax.fori_loop(0, NBLK, query_block, 0)
        for s in range(N_CTX):
            at = slice(s * TOK, (s + 1) * TOK)
            both = acc_kv[at, :].T
            out_t[s, m, HEAD : 2 * HEAD, :] = (both[:HEAD] * SCALE).astype(bf16)
            out_t[s, m, 2 * HEAD :, :] = both[HEAD:].astype(bf16)
        for copy in returns[m]:
            copy.start()
        landed[place, m] = out_t[place, m]

    fetch_w = [
        pltpu.make_async_copy(w_qkv.at[:, n * COLS : (n + 1) * COLS], w_part.at[n % 2], local_sem.at[4 + n])
        for n in range(6)
    ]
    done = [task for tasks in TASKS.values() for task in tasks]
    for phase in ("relay", 0, 1):
        for p, b in EARLY:
            if (phase, p, b) not in done:
                run_task(phase, p, b)
    gives = []
    for m in range(MB):
        for copy in pushes[m]:
            copy.wait_send()
        for copy in returns[m]:
            copy.wait()
        if m == 0:
            fetch_w[0].start()
            fetch_w[1].start()
        for i in range(HEADS // 2):
            for kind in range(3):
                rows = slice(kind * HEAD, (kind + 1) * HEAD)
                both = jnp.concatenate([landed[2 * i, m, rows, :], landed[2 * i + 1, m, rows, :]], axis=0)
                right_q[m * TOK : (m + 1) * TOK, kind * D + i * 128 : kind * D + (i + 1) * 128] = both.T
        rows = slice(m * TOK, (m + 1) * TOK)
        gives.append(
            send(
                right_q.at[rows, pl.ds(pl.multiple_of(other * WIDTHS[0], 512), WIDTHS[0])],
                peer_right.at[rows, 0 : WIDTHS[0]], (swap_send, swap_recv), (1, 9)[m], to_core,
            )
        )
        gives[m].start()
    sum_q = jnp.sum(right_q[:, :D].astype(f32), axis=0, keepdims=True)
    sum_v = jnp.sum(right_q[:, 2 * D :].astype(f32), axis=0, keepdims=True)
    row = lax.broadcasted_iota(jnp.int32, (16, TOK), 0)
    own_vec[...] = jnp.zeros_like(own_vec)
    for f in range(N_FSDP):
        cols = slice(f * TOK, (f + 1) * TOK)
        value = jnp.where(row == 0, sum_q[:, cols], jnp.where(row == 1, sum_v[:, cols], vec[f]))
        own_vec[f // 2, f % 2, 0, 0] = value.astype(bf16)
    give_vec = send(own_vec, peer_vec, (swap_send, swap_recv), 8, to_core)
    give_vec.start()
    for copy in gives:
        copy.wait()
    for p, at, width in late:
        if width == COLS:
            multiply(p, at // COLS)
        else:
            give_vec.wait()
            stores[3][0] = (own_vec[...].astype(f32) + peer_vec[...].astype(f32)).astype(bf16)
        begin(p, at, width)
    for n in range(6):
        fetch_w[n].wait()
        part = dot_nt(right_q[:, n * COLS : (n + 1) * COLS], w_part[n % 2])
        if n == 0:
            out_x[...] = part
        else:
            out_x[...] += part
        if n < 4:
            fetch_w[n + 2].start()
    for piece in late:
        relay(*piece)
    for piece in early:
        reduce(2, *piece)
    for phase in range(3):
        for piece in late:
            reduce(phase, *piece)
    squares = square_acc[...]
    yl, z = lax.axis_index("yl"), lax.axis_index("z")
    z_first, y_first = slice(0, HALF_Z), slice(HALF_Z, 6272)
    to_y = {"yl": 1 - yl}
    gather_sems = (gather_send, gather_recv)
    sq_sems = (sq_send, sq_recv)

    def spread(buffer, axis, base):
        at = coordinate(axis)
        out = []
        for step in (1, 2, 3):
            out.append(send(buffer.at[at], buffer.at[at], sq_sems, base + step - 1, peer(axis, step)[0]))
        return out

    def total(buffer):
        return (buffer[0] + buffer[1]) + (buffer[2] + buffer[3])

    sq_z[z] = squares
    squares_z = spread(sq_z, "z", 0)
    first_z = [
        send(gathered.at[core, row_place, :, z_first], gathered.at[core, row_place, :, z_first], gather_sems, step - 1, peer("z", step)[0])
        for step in (1, 2, 3)
    ]
    first_y = send(gathered.at[core, row_place, :, y_first], gathered.at[core, row_place, :, y_first], gather_sems, 3, to_y)
    for copy in (*squares_z, *first_z, first_y):
        copy.start()
    for copy in squares_z:
        copy.wait()
    y_at = coordinate("y")
    sq_y[y_at] = total(sq_z)
    squares_y = spread(sq_y, "y", 3)
    for copy in squares_y:
        copy.start()
    for copy in (*first_z, first_y):
        copy.wait()
    quarter = pl.ds(yl * 4, 4)
    second_y = send(
        gathered.at[core, quarter, :, z_first], gathered.at[core, quarter, :, z_first], gather_sems, 4, to_y
    )
    second_y.start()
    second_z = []
    for step in (1, 2, 3):
        for half in range(2):
            view = gathered.at[core, half * 4 + z, :, y_first]
            second_z.append(send(view, view, gather_sems, 5 + (step - 1) * 2 + half, peer("z", step)[0]))
    for copy in second_z:
        copy.start()
    for copy in squares_y:
        copy.wait()
    x_at = coordinate("x")
    sq_x[x_at] = total(sq_y)
    squares_x = spread(sq_x, "x", 6)
    for copy in squares_x:
        copy.start()
    for copy in squares_x:
        copy.wait()
    sq_c[core] = total(sq_x)
    square_c = send(sq_c.at[core], sq_c.at[core], sq_sems, 9, to_core)
    square_c.start()
    square_c.wait()
    out_sq[...] = sq_c[0] + sq_c[1]
    second_y.wait()
    for copy in second_z:
        copy.wait()
    last = send(gathered.at[core], gathered.at[core], gather_sems, 11, to_core)
    last.start()
    last.wait()
    locals_ = []
    for c in range(2):
        for p in range(3):
            for b in range(N_EARLY[p] + 1):
                i, col = PRODUCT[(p, b)]
                target, base = ((out_attn, 0), (out_attn, 3072), (out_ffn, 0), (out_ffn, FF))[i]
                base = base + c * WIDTHS[i] + col
                at = PART_AT[p] + b * COLS
                locals_.append(
                    pltpu.make_async_copy(
                        gathered.at[c, :, :, at : at + COLS], target.at[:, :, base : base + COLS],
                        out_sem.at[len(locals_)],
                    )
                )
    locals_.append(pltpu.make_async_copy(gathered.at[0, :, :, 6144:], out_vec, out_sem.at[len(locals_)]))
    for copy in locals_:
        copy.start()
    for copy in locals_:
        copy.wait()


def back(lefts, rights, vec, grad_ready, held, full, lse, w_qkv):
    vmem = pl.BlockSpec(memory_space=pltpu.VMEM)
    hbm = pl.BlockSpec(memory_space=pl.ANY)
    scratch = [
        pltpu.VMEM((4, D, ROWS), bf16),
        pltpu.VMEM((ROWS, 6144), bf16),
        pltpu.VMEM((ROWS, 6144), bf16),
        pltpu.VMEM((4, 2, 2, 4, 16, 128), bf16),
        pltpu.VMEM((4, 2, 2, 4, 16, 128), bf16),
    ]
    for kind in range(6):
        n = kind if kind < 3 else kind - 2
        for p, count, width in (*((p, N_EARLY[p] + 1, COLS) for p in range(3)), (0, 1, 128)):
            landing = (3,) if kind >= 3 else ()
            scratch.append(pltpu.VMEM((count, *landing, *lead(ORDERS[p], n), 16, width), bf16))
    scratch += [
        pltpu.VMEM((2, 8, 16, 6272), bf16),
        pltpu.VMEM((4, 8, 128), f32),
        pltpu.VMEM((4, 8, 128), f32),
        pltpu.VMEM((4, 8, 128), f32),
        pltpu.VMEM((2, 8, 128), f32),
        pltpu.VMEM((N_CTX, MB, SENT, TOK), bf16),
        pltpu.VMEM((N_CTX, MB, HEAD, TOK), bf16),
        pltpu.VMEM((N_CTX, MB, 3 * HEAD, TOK), bf16),
        pltpu.VMEM((N_CTX, MB, 3 * HEAD, TOK), bf16),
        pltpu.VMEM((ROWS, 3 * D), bf16),
        pltpu.VMEM((PACK, HEAD), bf16),
        pltpu.VMEM((PACK, HEAD), bf16),
        pltpu.VMEM((HEAD, PACK), bf16),
        pltpu.VMEM((PACK, TOK), f32),
        pltpu.VMEM((PACK, 2 * HEAD), f32),
        pltpu.VMEM((8, 128), f32),
        pltpu.VMEM((2, D, COLS), bf16),
    ]
    for count in (10, 10, 156, 156, 12, 12, 10, 10, 32, 32, 32, 32, 10, 25):
        scratch.append(pltpu.SemaphoreType.DMA((count,)))
    out = pl.pallas_call(
        back_kernel,
        in_specs=[vmem] * 4 + [hbm] * 3 + [vmem, vmem, hbm, vmem, vmem, hbm],
        out_specs=[hbm, hbm, hbm, vmem, vmem],
        out_shape=[
            jax.ShapeDtypeStruct((8, 16, 4 * D), bf16),
            jax.ShapeDtypeStruct((8, 16, 2 * FF), bf16),
            jax.ShapeDtypeStruct((8, 16, 128), bf16),
            jax.ShapeDtypeStruct((8, 128), f32),
            jax.ShapeDtypeStruct((ROWS, D), f32),
        ],
        scratch_shapes=scratch,
        compiler_params=pltpu.CompilerParams(
            collective_id=1, has_side_effects=True, vmem_limit_bytes=60 * 2**20
        ),
        cost_estimate=pl.CostEstimate(
            flops=2 * 512 * D * 6144 + 10 * MB * PACK * PACK * HEAD, bytes_accessed=16 * 2**20,
            transcendentals=MB * PACK * PACK,
        ),
        name="back",
    )(*lefts, *rights, vec, grad_ready, held, full, lse, w_qkv)
    return out[0].reshape(TOK, 4 * D), out[1].reshape(TOK, 2 * FF), out[2], out[3], out[4]


def layer_stats(values, gain_row, shift_row):
    center = values - jnp.mean(values, axis=-1, keepdims=True)
    inverse = lax.rsqrt(jnp.mean(center * center, axis=-1, keepdims=True) + NORM_EPS)
    normal = center * inverse
    return (normal * gain_row + shift_row, normal, inverse)


def layer_back(grad_value, normal, inverse, gain_row):
    scaled = grad_value * gain_row
    return inverse * (
        scaled
        - jnp.mean(scaled, axis=-1, keepdims=True)
        - normal * jnp.mean(scaled * normal, axis=-1, keepdims=True)
    )


N_CHUNK = 8
CHUNK = FF // N_CHUNK
ERF_TOP = (
    -2.72614225801306e-10, 2.77068142495902e-08, -2.10102402082508e-06, -5.69250639462346e-05,
    -7.34990630326855e-04, -2.95459980854025e-03, -1.60960333262415e-02,
)
ERF_LOW = (
    -1.45660718464996e-05, -2.13374055278905e-04, -1.68282697438203e-03, -7.37332916720468e-03,
    -1.42647390514189e-02,
)


def erf(value):
    value = jnp.clip(value, -4.0, 4.0)
    square = value * value
    top, low = jnp.full_like(square, ERF_TOP[0]), jnp.full_like(square, ERF_LOW[0])
    for c in ERF_TOP[1:]:
        top = top * square + c
    for c in ERF_LOW[1:]:
        low = low * square + c
    return value * top / low


def w_block(ref, n):
    per = ref.shape[-1] // CHUNK
    at = (n % per) * CHUNK
    return ref[n // per, :, :, :, at : at + CHUNK].reshape(D, CHUNK)


def dense_part(
    mixed_ref, x_ref, cot_ref, seg_ref, small_ref, w_out, w_one, w_two, before,
    out_ref, one_ref, x_t, o_t, h_t, f_t, a_low_ref, du_ref, g_ref, vec_ref, ready_ref,
    mixed, normal_one_ref, slope, total,
):
    def row(i):
        return small_ref[i : i + 1, :]

    def put(i, value):
        for f in range(N_FSDP):
            vec_ref[f, i : i + 1, :] = value[:, f * TOK : (f + 1) * TOK]

    def sums(value):
        return jnp.sum(value, axis=0, keepdims=True)

    vec_ref[...] = jnp.zeros_like(vec_ref)
    for m in range(MB):
        tok = slice(m * TOK, (m + 1) * TOK)
        for i in range(HEADS // 2):
            both = jnp.concatenate([mixed_ref[2 * i, m], mixed_ref[2 * i + 1, m]], axis=0)
            o_t[i * 128 : (i + 1) * 128, tok] = both
            mixed[tok, i * 128 : (i + 1) * 128] = both.T
    before(0)
    branch = jnp.concatenate([dot(mixed[...], w_block(w_out, n)) for n in range(2)], axis=1)
    normed_one, normal_one, inverse_one = layer_stats(x_ref[...].astype(f32) + branch + row(2), row(4), row(5))
    normal_one_ref[...] = normal_one
    normed_low = normed_one.astype(bf16)
    h_t[...] = normed_low.T
    total[...] = normed_one + row(3)
    before(1)
    for n in range(N_CHUNK):
        cols = slice(n * CHUNK, (n + 1) * CHUNK)
        bias = small_ref[8 + n // 2 : 9 + n // 2, (n % 2) * CHUNK : (n % 2 + 1) * CHUNK]
        u = dot(normed_low, w_block(w_one, n)) + bias
        share = 0.5 + 0.5 * erf(u * math.sqrt(0.5))
        g_ref[:, cols] = (u * share).astype(bf16)
        slope[:, cols] = share + u * (jnp.exp(-0.5 * u * u) * (1.0 / math.sqrt(2.0 * math.pi)))
    before(2)
    for n in range(N_CHUNK):
        total[...] += dot_nt(g_ref[:, n * CHUNK : (n + 1) * CHUNK], w_block(w_two, n))
    output, normal_two, inverse_two = layer_stats(total[...], row(6), row(7))
    keep = []
    for m in range(MB):
        inside = jnp.where(seg_ref[m, 0:1, :].astype(f32) < 8.0, 1.0, 0.0)
        keep.append(jnp.broadcast_to(inside, (TOK, TOK)).T[:, 0:1])
    keep = jnp.concatenate(keep, axis=0)
    out_ref[...] = (output * keep).astype(bf16)
    grad_out = cot_ref[...].astype(f32) * keep
    put(6, sums(grad_out * normal_two))
    put(7, sums(grad_out))
    grad_two = layer_back(grad_out, normal_two, inverse_two, row(6))
    f_low = grad_two.astype(bf16)
    f_t[...] = f_low.T
    put(3, sums(f_low.astype(f32)))
    total[...] = grad_two
    for n in range(N_CHUNK):
        cols = slice(n * CHUNK, (n + 1) * CHUNK)
        du = (dot(f_low, w_block(w_two, n)) * slope[:, cols]).astype(bf16)
        du_ref[:, cols] = du
        part = sums(du.astype(f32))
        for i in range(CHUNK // TOK):
            f = (n % 2) * (CHUNK // TOK) + i
            vec_ref[f, 8 + n // 2 : 9 + n // 2, :] = part[:, i * TOK : (i + 1) * TOK]
        total[...] += dot_nt(du, w_block(w_one, n))
    grad_normed = total[...]
    normal_one = normal_one_ref[...]
    put(4, sums(grad_normed * normal_one))
    put(5, sums(grad_normed))
    grad_one = layer_back(grad_normed, normal_one, inverse_one, row(4))
    one_ref[...] = grad_one
    a_low = grad_one.astype(bf16)
    a_low_ref[...] = a_low
    put(2, sums(a_low.astype(f32)))
    for n in range(2):
        part = a_low[:, n * CHUNK : (n + 1) * CHUNK]
        part = dot_nt(part, w_block(w_out, n))
        grad_mixed = part if n == 0 else grad_mixed + part
    grad_mixed = grad_mixed.T.astype(bf16)
    for h in range(HEADS):
        for m in range(MB):
            ready_ref[h, m] = grad_mixed[h * HEAD : (h + 1) * HEAD, m * TOK : (m + 1) * TOK]
    x_t[...] = x_ref[...].T


def adamw(weight, grad_value, first, second, rate, decay):
    first_new = BETA_FIRST * first + (1.0 - BETA_FIRST) * grad_value
    second_new = BETA_SECOND * second + (1.0 - BETA_SECOND) * grad_value * grad_value
    first_hat = first_new * (1.0 / (1.0 - BETA_FIRST**STEP))
    second_hat = second_new * (1.0 / (1.0 - BETA_SECOND**STEP))
    weight_new = weight - rate * (first_hat / (jnp.sqrt(second_hat) + ADAM_EPS) + decay * weight)
    return (weight_new, first_new, second_new)


def finish_kernel(
    squares, grad_vec, grad_attn, grad_ffn, aw, am, av, fw, fm, fv, vw, vm, vv, one, grad_x, y,
    norm, aw_new, am_new, av_new, fw_new, fm_new, fv_new, vw_new, vm_new, vv_new, a_copy, f_copy, bias, dx, y_out,
):
    total = jnp.sum(jnp.sum(squares[...], axis=0, keepdims=True), axis=1, keepdims=True)
    root = jnp.sqrt(total)
    norm[...] = root
    factor = jnp.minimum(1.0, CLIP_NORM / (root + 1e-06))
    rate = D ** (-0.5)
    for grad, ins, outs, low, scale in (
        (grad_attn, (aw, am, av), (aw_new, am_new, av_new), a_copy, ATTN_RATE_SCALE * rate),
        (grad_ffn, (fw, fm, fv), (fw_new, fm_new, fv_new), f_copy, rate),
    ):
        for at in range(0, grad.shape[1], 1024):
            cols = slice(at, at + 1024)
            weight, first, second = adamw(
                ins[0][:, cols], grad[:, cols].astype(f32) * factor, ins[1][:, cols], ins[2][:, cols], scale,
                WEIGHT_DECAY,
            )
            outs[0][:, cols] = weight
            outs[1][:, cols] = first
            outs[2][:, cols] = second
            low[:, cols] = weight.astype(bf16)
    clipped = grad_vec[0].astype(f32) * factor
    vw_new[...], vm_new[...], vv_new[...] = adamw(
        vw[...], clipped[:12], vm[...], vv[...], RATE_VECTOR, 0.0
    )
    bias[...] = clipped[2:3]
    dx[...] = (one[...] + grad_x[...]).astype(bf16)
    y_out[...] = y[...]


def finish(squares, grad_vec, grad_attn, grad_ffn, attn, ffn, vec, one, grad_x, y):
    steps = 8
    rows = TOK // steps
    whole = lambda a: pl.BlockSpec(a.shape, lambda i: (0,) * len(a.shape))
    part = lambda a: pl.BlockSpec((a.shape[0] // steps, a.shape[1]), lambda i: (i, 0))
    shape = lambda a, dt=f32: jax.ShapeDtypeStruct(a.shape, dt)
    ins = [squares, grad_vec, grad_attn, grad_ffn, *attn, *ffn, *vec, one, grad_x, y]
    specs = [whole(squares), pl.BlockSpec((1, 16, TOK), lambda i: (0, 0, 0)), part(grad_attn), part(grad_ffn)]
    specs += [part(a) for a in (*attn, *ffn)] + [whole(a) for a in vec] + [part(a) for a in (one, grad_x, y)]
    outs = [jax.ShapeDtypeStruct((1, 1), f32), *(shape(a) for a in (*attn, *ffn, *vec))]
    outs += [shape(attn[0], bf16), shape(ffn[0], bf16), jax.ShapeDtypeStruct((1, TOK), f32), shape(one, bf16), shape(y, bf16)]
    out_specs = [whole(outs[0]), *(part(a) for a in outs[1:7]), *(whole(a) for a in outs[7:10])]
    out_specs += [part(outs[10]), part(outs[11]), whole(outs[12]), part(outs[13]), part(outs[14])]
    return pl.pallas_call(
        finish_kernel,
        grid=(steps,),
        in_specs=specs,
        out_specs=out_specs,
        out_shape=outs,
        compiler_params=pltpu.CompilerParams(vmem_limit_bytes=60 * 2**20),
        cost_estimate=pl.CostEstimate(flops=40 * 12 * D * TOK, bytes_accessed=44 * 2**20, transcendentals=24 * D * TOK),
        name="finish",
    )(*ins)


def shards(
    tokens, cotangent, dest, lengths, attn_weight, attn_first, attn_second,
    ffn_weight, ffn_first, ffn_second, vectors, vec_first, vec_second,
):
    x = tokens.reshape(ROWS, D)
    cot = cotangent.reshape(ROWS, D)
    (
        w_qkv, held, mixed_full, lse, output, grad_one, x_t, o_t, h_t, f_t, a_low, du, g, vec_rows, grad_ready,
    ) = front(attn_weight, ffn_weight, vectors, dest[:, 0], lengths[:, 0], x, cot)
    grad_attn, grad_ffn, grad_vec, squares, grad_x = back(
        (x_t, o_t, h_t, f_t),
        (a_low, du, g),
        vec_rows,
        grad_ready,
        held,
        mixed_full,
        lse,
        w_qkv.reshape(D, 3 * D),
    )
    (
        norm, aw, am, av, fw, fm, fv, vw, vm, vv, a_copy, f_copy, bias, input_grad, output,
    ) = finish(
        squares, grad_vec, grad_attn, grad_ffn,
        (attn_weight, attn_first, attn_second), (ffn_weight, ffn_first, ffn_second),
        (vectors, vec_first, vec_second), grad_one, grad_x, output,
    )
    return (
        output.reshape(tokens.shape), input_grad.reshape(tokens.shape), norm.reshape(()),
        aw, am, av, fw, fm, fv, vw, vm, vv, a_copy, f_copy, bias.reshape(TOK),
    )


def solution(mesh):
    fine = Mesh(mesh.devices.reshape(2, 4, 2, 4, 2), ("yl", "z", "core", "x", "yh"))
    act = P(None, FSDP, CTX, None)
    row = P(FSDP, None)
    col = P(None, FSDP)
    return jax.shard_map(
        shards,
        mesh=fine,
        in_specs=(act, act, P(None, FSDP, CTX), P(None, FSDP, None), row, row, row, row, row, row, col, col, col),
        out_specs=(act, act, P(), row, row, row, row, row, row, col, col, col, row, row, P(FSDP)),
        check_vma=False,
    )
```

```python
import math

import jax
import jax.numpy as jnp
from jax import lax
from jax.experimental import pallas as pl
from jax.experimental.pallas import tpu as pltpu
from jax.sharding import Mesh, PartitionSpec as P

HEADS = 16
HEAD = 64
STEP = 10
MB = 2
TOK = 128
ROWS = MB * TOK
D = 1024
FF = 4096
N_CTX = 16
N_FSDP = 8
PACK = 2048
SENT = 208

NORM_EPS = 1e-05
CLIP_NORM = 1.0
BETA_FIRST = 0.9
BETA_SECOND = 0.999
ADAM_EPS = 1e-08
WEIGHT_DECAY = 0.01
RATE_VECTOR = 0.3
ATTN_RATE_SCALE = 3.0
NEG_LARGE = -1e30
SCALE2 = HEAD ** (-0.5) * math.log2(math.e)
SCALE = HEAD ** (-0.5)
CONTRACT_ROWS = (((0,), (0,)), ((), ()))
CONTRACT_COLS = (((1,), (1,)), ((), ()))
CTX = ("yl", "z", "core")
FSDP = ("x", "yh")
ALL = ("x", "yh", "yl", "z", "core")
BLK = 256
NBLK = PACK // BLK
f32 = jnp.float32
bf16 = jnp.bfloat16


def dot(a, b):
    return jnp.dot(a, b, preferred_element_type=f32)


def dot_nt(a, b):
    return lax.dot_general(a, b, CONTRACT_COLS, preferred_element_type=f32)


def dot_tn(a, b):
    return lax.dot_general(a, b, CONTRACT_ROWS, preferred_element_type=f32)


MESH_ID = pl.DeviceIdType.MESH
COLS = 512
N_BLK = 4
ORDERS = (("x", "z", "y"), ("z", "y", "x"), ("y", "x", "z"))
EARLY = ((0, 0), (1, 0), (2, 0), (0, 1), (1, 1), (2, 1), (0, 2), (1, 2), (2, 2))
N_EARLY = (3, 3, 3)
EARLY_PRODUCT = ((2, 0), (2, 512), (2, 1024), (2, 1536), (3, 0), (3, 512), (3, 1024), (3, 1536), (1, 0))
PRODUCT = {part_block: product for part_block, product in zip(EARLY, EARLY_PRODUCT)}
PRODUCT.update({(p, N_EARLY[p]): (0, p * COLS) for p in range(3)})
PART_AT = (0, 2048, 4096, 6144)
VEC_AT = 3072
WIDTHS = (1536, 512, 2048, 2048)
OFFSETS = (0, 1536, 2048, 4096)
HALF_Z = 3072
TASKS = {}
for _n, _at in enumerate((2, 2, 2, 5, 5, 5, 8, 8, 8)):
    TASKS.setdefault(_at, []).append(("relay", *EARLY[_n]))
for _n, _at in enumerate((7, 7, 7, 10, 10, 10, 13, 13, 13)):
    TASKS.setdefault(_at, []).append((0, *EARLY[_n]))


def coordinate(axis):
    if axis == "y":
        return lax.axis_index("yh") * 2 + lax.axis_index("yl")
    return lax.axis_index(axis)


def peer(axis, step):
    at = lax.rem(coordinate(axis) + step, 4)
    if axis == "y":
        return {"yh": at // 2, "yl": lax.rem(at, 2)}, at
    return {axis: at}, at


def pick(ref, axis, at, dims):
    index = []
    for d in dims:
        if d == axis:
            index.append(at)
        elif axis == "y" and d == "yh":
            index.append(at // 2)
        elif axis == "y" and d == "yl":
            index.append(lax.rem(at, 2))
        else:
            index.append(slice(None))
    return ref.at[tuple(index)]


def dims_after(order, n):
    dims = ["x", "yh", "yl", "z"]
    for axis in order[:n]:
        for d in ("yh", "yl") if axis == "y" else (axis,):
            dims.remove(d)
    return dims


SIZES = {"x": 4, "yh": 2, "yl": 2, "z": 4}


def lead(order, n):
    return tuple(SIZES[d] for d in dims_after(order, n))


def send(src, dst, sems, index, to):
    return pltpu.make_async_remote_copy(
        src_ref=src, dst_ref=dst, send_sem=sems[0].at[index], recv_sem=sems[1].at[index],
        device_id=to, device_id_type=MESH_ID,
    )


def load_side(qkv_ref, m, keys, values, keys_t, values_t, seg_col):
    for s in range(N_CTX):
        at = slice(s * TOK, (s + 1) * TOK)
        key_t = qkv_ref[s, m, HEAD : 2 * HEAD, :]
        value_t = qkv_ref[s, m, 2 * HEAD : 3 * HEAD, :]
        keys[at, :] = key_t.T
        if values is not None:
            values[at, :] = value_t.T
        if keys_t is not None:
            keys_t[:, at] = key_t
        if values_t is not None:
            values_t[:, at] = value_t
        seg = qkv_ref[s, m, 3 * HEAD : 3 * HEAD + 1, :].astype(f32)
        seg_col[at, :] = jnp.broadcast_to(seg, (TOK, TOK)).T


def pair(ref, m, j, rows):
    return jnp.concatenate([ref[2 * j, m, rows, :], ref[2 * j + 1, m, rows, :]], axis=1)


def query_forward(held, m, j, out, full, lse_out, keys, values_t, seg_col, scores):
    query_t = pair(held, m, j, slice(0, HEAD))
    seg_row = pair(held, m, j, slice(3 * HEAD, 3 * HEAD + 1)).astype(f32)
    top = jnp.full((1, BLK), NEG_LARGE, f32)
    for k in range(NBLK):
        at = slice(k * BLK, (k + 1) * BLK)
        s = dot(keys[at, :], query_t) * SCALE2
        col = seg_col[at, :]
        same = jnp.concatenate([col, col], axis=1) == seg_row
        s = jnp.where(same, s, NEG_LARGE)
        scores[at, :] = s
        top = jnp.maximum(top, jnp.max(s, axis=0, keepdims=True))
    total = jnp.zeros((1, BLK), f32)
    acc = jnp.zeros((HEAD, BLK), f32)
    for k in range(NBLK):
        at = slice(k * BLK, (k + 1) * BLK)
        p = jnp.exp2(scores[at, :] - top)
        total = total + jnp.sum(p, axis=0, keepdims=True)
        acc = acc + dot(values_t[:, at], p.astype(bf16))
    acc = acc / total
    lse = top + jnp.log2(total)
    for half in range(2):
        cols = slice(half * TOK, (half + 1) * TOK)
        out[2 * j + half, m] = acc[:, cols].astype(bf16)
        full[2 * j + half, m] = acc[:, cols]
        lse_out[2 * j + half, m] = lse[:, cols]


GROUP_COLS = (1536, 2048, 2048, 512)
GROUP_AT = (0, 2048, 4096, 1536)
SPLITS = ((512, 1024), (1024, 1536), (1024, 1536), (128, 256))
N_COPY = 31
GROUPS = (3, 1, 2)
BEFORE = tuple((0, op) for op in ("z1", "x1", "z2", "y1", "z3", "x2", "x3", "y2", "z4", "x4", "x5"))
BEFORE += tuple((g, op) for op in ("z1", "z2", "y1") for g in GROUPS)
BEFORE += tuple((0, op) for op in ("y3", "z5", "sx", "sy", "sz", "got"))
PUSHED = tuple((g, op) for op in ("z3", "x1", "x2", "x3") for g in GROUPS)
STEPS = {
    0: tuple((g, "z4") for g in GROUPS),
    1: tuple((g, "y2") for g in GROUPS),
    3: tuple((g, "x4") for g in GROUPS),
    6: tuple((g, "x5") for g in GROUPS),
    9: tuple((g, "y3") for g in GROUPS),
    12: tuple((g, "z5") for g in GROUPS),
}
LAST = (
    tuple((g, op) for g in (3, 1) for op in ("sx", "sy", "sz")) + ((3, "got"),),
    tuple((2, op) for op in ("sx", "sy", "sz")) + ((1, "got"),),
    ((2, "got"),),
)


def ctx_device(t):
    return {"yl": t // 8, "z": lax.rem(t // 2, 4), "core": lax.rem(t, 2)}


def rows_at(start, size):
    return pl.ds(pl.multiple_of(start, 16), size)


class Gather:
    def __init__(self, g, shard, dest, sems, base, local_sem):
        core = lax.axis_index("core")
        x, z = lax.axis_index("x"), lax.axis_index("z")
        yh, yl = lax.axis_index("yh"), lax.axis_index("yl")
        y = yh * 2 + yl
        every = slice(None)
        zq, half = rows_at(z * 32, 32), rows_at(yl * 64, 64)
        cross = {"yh": 1 - yh, "yl": 1 - yl}
        count = [0]
        x_end, y_end = SPLITS[g]
        x_cols, y_cols, z_cols = slice(0, x_end), slice(x_end, y_end), slice(y_end, GROUP_COLS[g])

        def given(rows, cols):
            return shard.at[rows, GROUP_AT[g] + cols.start : GROUP_AT[g] + cols.stop]

        def make(src, dst, to):
            copy = send(src, dst, sems, base + count[0], to)
            count[0] += 1
            return copy

        def own(rows, cols, to):
            return make(given(rows, cols), dest(core, x, yh, rows, cols), to)

        def pass_on(xs, yhs, rows, cols, to):
            view = dest(core, xs, yhs, rows, cols)
            return make(view, view, to)

        x_to = {step: peer("x", step)[0] for step in (1, 2, 3)}
        y_to = {step: peer("y", step)[0] for step in (1, 3)}
        z_to = {step: peer("z", step)[0] for step in (1, 3)}
        x_before, x_after = lax.rem(x + 3, 4), lax.rem(x + 1, 4)
        y_before, y_after = lax.rem(y + 3, 4), lax.rem(y + 1, 4)
        z_before, z_after = lax.rem(z + 3, 4), lax.rem(z + 1, 4)
        self.copies = {
            "x1": [own(every, x_cols, cross)],
            "x2": [own(every, x_cols, x_to[s]) for s in (1, 3)],
            "z1": [own(zq, z_cols, cross)],
            "z2": [own(zq, z_cols, x_to[s]) for s in (1, 3, 2)],
            "y1": [own(half, y_cols, x_to[s]) for s in (1, 3, 2)],
            "x3": [pass_on(x, 1 - yh, every, x_cols, x_to[s]) for s in (1, 3)],
            "z3": [pass_on(x, 1 - yh, zq, z_cols, x_to[s]) for s in (1, 3, 2)],
            "y2": [pass_on(every, yh, half, y_cols, y_to[s]) for s in (1, 3)],
            "z4": [pass_on(every, every, zq, z_cols, z_to[s]) for s in (1, 3)],
            "x4": [
                pass_on(x_before, yh, slice(0, 64), x_cols, x_to[1]),
                pass_on(x_after, yh, slice(64, 128), x_cols, x_to[3]),
            ],
            "x5": [
                pass_on(x_before, 1 - yh, slice(0, 64), x_cols, x_to[1]),
                pass_on(x_after, 1 - yh, slice(64, 128), x_cols, x_to[3]),
            ],
            "y3": [
                pass_on(every, y_before // 2, rows_at(lax.rem(y_before, 2) * 64, 32), y_cols, y_to[1]),
                pass_on(every, y_after // 2, rows_at(lax.rem(y_after, 2) * 64 + 32, 32), y_cols, y_to[3]),
            ],
            "z5": [
                pass_on(every, every, rows_at(z_before * 32, 16), z_cols, z_to[1]),
                pass_on(every, every, rows_at(z_after * 32 + 16, 16), z_cols, z_to[3]),
            ],
        }
        for name, cols in (("sx", x_cols), ("sy", y_cols), ("sz", z_cols)):
            self.copies[name] = [pass_on(every, every, every, cols, {"core": 1 - core})]
        self.places = [
            pltpu.make_async_copy(given(rows, cols), dest(core, x, yh, rows, cols), local_sem.at[3 * g + n])
            for n, (rows, cols) in enumerate(((every, x_cols), (half, y_cols), (zq, z_cols)))
        ]

    needs = {
        "x3": ("x1",), "z3": ("z1",), "y2": ("y1",), "z4": ("z2", "z3"), "x4": ("x2",), "x5": ("x3",), "y3": ("y2",),
        "z5": ("z4",), "sx": ("x4", "x5"), "sy": ("y3",), "sz": ("z5",),
    }

    def step(self, name):
        if name == "got":
            for copy in (*self.copies["sx"], *self.copies["sy"], *self.copies["sz"]):
                copy.wait_recv()
            return
        if name == "end":
            for copies in self.copies.values():
                for copy in copies:
                    copy.wait_send()
            return
        for need in self.needs.get(name, ()):
            for copy in self.copies[need]:
                copy.wait_recv()
        if name == "z1":
            for copy in self.places:
                copy.start()
        if name == "z3":
            for copy in self.places:
                copy.wait()
        for copy in self.copies[name]:
            copy.start()


def greet_all():
    barrier = pltpu.get_barrier_semaphore()
    place = lax.axis_index(CTX)
    others = [ctx_device(lax.rem(place + d, N_CTX)) for d in range(1, N_CTX)]
    others += [peer(axis, step)[0] for axis in ("x", "y") for step in (1, 2, 3)]
    for other in others:
        pl.semaphore_signal(barrier, inc=1, device_id=other, device_id_type=MESH_ID)
    pl.semaphore_wait(barrier, len(others))


def front_kernel(
    w_attn, w_ffn, vectors, dest_ref, lengths, x_ref, cot_ref,
    out_attn, out_held, out_full, out_lse,
    out_ref, one_ref, x_t, o_t, h_t, f_t, a_low_ref, du_ref, g_ref, vec_ref, ready_ref,
    wa, w_one, w_two, w_out, vecs, small, ready, held, mixed, out_t, keys, values_t, seg_col, scores,
    mixed_rows, normal_one, slope, total, stage, shard, vec_shard, seg_ref,
    ag_send, ag_recv, vec_send, vec_recv, q_send, q_recv, o_send, o_recv, local_sem, out_sem, in_sem,
):
    core = lax.axis_index("core")
    place = lax.axis_index(CTX)
    x, yh, yl = lax.axis_index("x"), lax.axis_index("yh"), lax.axis_index("yl")

    weights = (wa, w_one, w_two, w_out)

    def dest(g):
        def view(c, xs, yhs, rows, cols):
            return weights[g].at[c, xs, yhs, rows, cols]

        return view

    gathers = [
        Gather(g, shard, dest(g), (ag_send, ag_recv), g * N_COPY, local_sem) for g in range(4)
    ]
    vec_sems = (vec_send, vec_recv)
    vec_cross = send(vec_shard, vecs.at[x, yh], vec_sems, 0, {"yh": 1 - yh, "yl": 1 - yl})
    vec_x = [send(vec_shard, vecs.at[x, yh], vec_sems, s, peer("x", s)[0]) for s in (1, 2, 3)]
    vec_x2 = [
        send(vecs.at[x, 1 - yh], vecs.at[x, 1 - yh], vec_sems, 3 + s, peer("x", s)[0]) for s in (1, 2, 3)
    ]
    fetches = []
    for g in range(4):
        start = (0, 0, FF, 3 * D)[g] + core * GROUP_COLS[g]
        source = w_ffn if g in (1, 2) else w_attn
        fetches.append(
            pltpu.make_async_copy(
                source.at[:, pl.ds(pl.multiple_of(start, 512), GROUP_COLS[g])],
                stage.at[:, GROUP_AT[g] : GROUP_AT[g] + GROUP_COLS[g]], in_sem.at[g],
            )
        )
        fetches[g].start()
    vec_shard[...] = jnp.concatenate([vectors[...], jnp.zeros((4, TOK), f32)], axis=0).astype(bf16)
    for m in range(MB):
        end = jnp.zeros((1, 1), jnp.int32)
        seg = jnp.zeros((1, TOK), jnp.int32)
        for j in range(8):
            end = end + lengths[m : m + 1, j : j + 1]
            seg = seg + jnp.where(dest_ref[m : m + 1, :] >= end, 1, 0)
        seg_ref[m] = jnp.broadcast_to(seg.astype(f32), (16, TOK)).astype(bf16)
    greet_all()
    for g in range(4):
        fetches[g].wait()
    shard[...] = stage[...].astype(bf16)
    for copy in (vec_cross, *vec_x):
        copy.start()
    done = set()

    def stages(todo):
        for g, n in todo:
            if (g, n) not in done:
                done.add((g, n))
                gathers[g].step(n)

    stages(BEFORE[:4])
    vecs[x, yh] = vec_shard[...]
    for s in range(N_CTX):
        ready[s, :, 3 * HEAD :, :] = seg_ref[...]
    vec_cross.wait_recv()
    for copy in vec_x2:
        copy.start()
    stages(BEFORE)
    vec_cross.wait_send()
    for copy in (*vec_x, *vec_x2):
        copy.wait()
    for f in range(N_FSDP):
        small[:, f * TOK : (f + 1) * TOK] = vecs[f // 2, f % 2].astype(f32)

    for part in range(6):
        c, col = part // 3, (part % 3) * 512
        kind, first = part // 2, (part % 2) * 8
        value = jnp.zeros((ROWS, 512), f32)
        weight = wa[c, :, :, :, col : col + 512].reshape(D, 512)
        value = dot(x_ref[...], weight)
        if kind != 1:
            row = 0 if kind == 0 else 1
            value = value + small[row : row + 1, first * HEAD : first * HEAD + 512]
        value = value.T.astype(bf16)
        for h in range(8):
            for m in range(MB):
                ready[first + h, m, kind * HEAD : (kind + 1) * HEAD, :] = value[
                    h * HEAD : (h + 1) * HEAD, m * TOK : (m + 1) * TOK
                ]
    swaps = [[], []]
    for m in range(MB):
        for d in range(1, N_CTX):
            t = lax.rem(place + d, N_CTX)
            swaps[m].append(send(ready.at[t, m], held.at[place, m], (q_send, q_recv), m * N_CTX + d, ctx_device(t)))
            swaps[m][-1].start()
    held[place] = ready[place]
    returns = [[], []]
    for m in range(MB):
        for d in range(1, N_CTX):
            t = lax.rem(place + d, N_CTX)
            returns[m].append(
                send(out_t.at[t, m], mixed.at[place, m], (o_send, o_recv), m * N_CTX + d, ctx_device(t))
            )
    stages(PUSHED)
    outs = [(wa.at[c], out_attn.at[:, :, :, c * 1536 : (c + 1) * 1536]) for c in range(2)]
    outs = [pltpu.make_async_copy(src, dst, out_sem.at[n]) for n, (src, dst) in enumerate(outs)]
    for copy in outs:
        copy.start()
    for m in range(MB):
        for copy in swaps[m]:
            copy.wait_recv()
        load_side(held, m, keys, None, None, values_t, seg_col)

        def query_block(j, _, m=m):
            for at, todo in STEPS.items():
                if at // NBLK == m:

                    @pl.when(j == at % NBLK)
                    def _(todo=todo):
                        stages(todo)

            query_forward(held, m, j, out_t, out_full, out_lse, keys, values_t, seg_col, scores)
            return 0

        lax.fori_loop(0, NBLK, query_block, 0)
        for copy in returns[m]:
            copy.start()
        mixed[place, m] = out_t[place, m]
    outs.append(pltpu.make_async_copy(held, out_held, out_sem.at[4]))
    outs[-1].start()

    def before(n):
        stages(LAST[n])

    for m in range(MB):
        for copy in returns[m]:
            copy.wait_recv()
    dense_part(
        mixed, x_ref, cot_ref, seg_ref, small, w_out, w_one, w_two, before,
        out_ref, one_ref, x_t, o_t, h_t, f_t, a_low_ref, du_ref, g_ref, vec_ref, ready_ref,
        mixed_rows, normal_one, slope, total,
    )
    for m in range(MB):
        for copy in (*swaps[m], *returns[m]):
            copy.wait_send()
    stages([(g, "end") for g in (0, *GROUPS)])
    for copy in outs:
        copy.wait()


def front(w_attn, w_ffn, vectors, dest, lengths, x, cot):
    vmem = pl.BlockSpec(memory_space=pltpu.VMEM)
    hbm = pl.BlockSpec(memory_space=pl.ANY)
    sem = lambda n: pltpu.SemaphoreType.DMA((n,))
    turned = jax.ShapeDtypeStruct((D, ROWS), bf16)
    return pl.pallas_call(
        front_kernel,
        in_specs=[hbm, hbm, vmem, vmem, vmem, vmem, vmem],
        out_specs=[hbm, hbm] + [vmem] * 13,
        out_shape=[
            jax.ShapeDtypeStruct((4, 2, TOK, 3 * D), bf16),
            jax.ShapeDtypeStruct((N_CTX, MB, SENT, TOK), bf16),
            jax.ShapeDtypeStruct((N_CTX, MB, HEAD, TOK), f32),
            jax.ShapeDtypeStruct((N_CTX, MB, 1, TOK), f32),
            jax.ShapeDtypeStruct((ROWS, D), bf16),
            jax.ShapeDtypeStruct((ROWS, D), f32),
            turned, turned, turned, turned,
            jax.ShapeDtypeStruct((ROWS, D), bf16),
            jax.ShapeDtypeStruct((ROWS, FF), bf16),
            jax.ShapeDtypeStruct((ROWS, FF), bf16),
            jax.ShapeDtypeStruct((N_FSDP, 16, TOK), f32),
            jax.ShapeDtypeStruct((HEADS, MB, HEAD, TOK), bf16),
        ],
        scratch_shapes=[
            *(pltpu.VMEM((2, 4, 2, TOK, GROUP_COLS[g]), bf16) for g in range(4)),
            pltpu.VMEM((4, 2, 16, TOK), bf16),
            pltpu.VMEM((16, D), f32),
            pltpu.VMEM((N_CTX, MB, SENT, TOK), bf16),
            pltpu.VMEM((N_CTX, MB, SENT, TOK), bf16),
            pltpu.VMEM((N_CTX, MB, HEAD, TOK), bf16),
            pltpu.VMEM((N_CTX, MB, HEAD, TOK), bf16),
            pltpu.VMEM((PACK, HEAD), bf16),
            pltpu.VMEM((HEAD, PACK), bf16),
            pltpu.VMEM((PACK, TOK), f32),
            pltpu.VMEM((PACK, BLK), f32),
            pltpu.VMEM((ROWS, D), bf16),
            pltpu.VMEM((ROWS, D), f32),
            pltpu.VMEM((ROWS, FF), f32),
            pltpu.VMEM((ROWS, D), f32),
            pltpu.VMEM((TOK, 6144), f32),
            pltpu.VMEM((TOK, 6144), bf16),
            pltpu.VMEM((16, TOK), bf16),
            pltpu.VMEM((MB, 16, TOK), bf16),
            sem(4 * N_COPY), sem(4 * N_COPY), sem(7), sem(7), sem(32), sem(32), sem(32), sem(32),
            sem(12), sem(6), sem(4),
        ],
        compiler_params=pltpu.CompilerParams(
            collective_id=2, has_side_effects=True, vmem_limit_bytes=60 * 2**20
        ),
        cost_estimate=pl.CostEstimate(
            flops=4 * MB * PACK * PACK * HEAD + 2 * ROWS * D * (5 * D + 4 * FF), bytes_accessed=32 * 2**20,
            transcendentals=MB * PACK * PACK,
        ),
        name="front",
    )(w_attn, w_ffn, vectors, dest, lengths, x, cot)


def back_kernel(
    left_x, left_o, left_h, left_f, right_o, right_u, right_g, vec, grad_ready, held_in, full, lse, w_qkv,
    out_attn, out_ffn, out_vec, out_sq, out_x,
    peer_left, own_right, peer_right, own_vec, peer_vec,
    *rest_refs,
):
    stores, rest_refs = rest_refs[:24], rest_refs[24:]
    (
    gathered, sq_z, sq_y, sq_x, sq_c,
    held, grad_held, out_t, landed, right_q, keys, values, keys_t, seg_col, acc_kv, square_acc, w_part,
    swap_send, swap_recv, ring_send, ring_recv, gather_send, gather_recv, sq_send, sq_recv,
    o_send, o_recv, q_send, q_recv, local_sem, out_sem,
    ) = rest_refs
    core = lax.axis_index("core")
    other = 1 - core
    place = lax.axis_index(CTX)
    row_place = lax.axis_index("yl") * 4 + lax.axis_index("z")
    lefts = (left_x, left_o, left_h, left_f)
    rights = (None, right_o, right_u, right_g)
    to_core = {"core": other}

    fetch = pltpu.make_async_copy(held_in, held, local_sem.at[0])
    fetch.start()
    fetches = [fetch]
    for i in range(1, 4):
        cols = pl.ds(pl.multiple_of(core * WIDTHS[i], 512), WIDTHS[i])
        fetches.append(
            pltpu.make_async_copy(
                rights[i].at[:, cols], own_right.at[:, OFFSETS[i] : OFFSETS[i] + WIDTHS[i]], local_sem.at[i]
            )
        )
        fetches[-1].start()
    greet_all()

    pushes, returns = [[], []], [[], []]
    for m in range(MB):
        for d in range(1, N_CTX):
            t = lax.rem(place + d, N_CTX)
            to = ctx_device(t)
            pushes[m].append(
                send(grad_ready.at[t, m], grad_held.at[place, m], (o_send, o_recv), m * N_CTX + d, to)
            )
            returns[m].append(send(out_t.at[t, m], landed.at[place, m], (q_send, q_recv), m * N_CTX + d, to))
    swaps = []
    for i in (2, 3, 1, 0):
        swaps.append(send(lefts[i], peer_left.at[i], (swap_send, swap_recv), 2 * i, to_core))
        if i:
            from_cols = pl.ds(pl.multiple_of(other * WIDTHS[i], 512), WIDTHS[i])
            swaps.append(
                send(
                    rights[i].at[:, from_cols], peer_right.at[:, OFFSETS[i] : OFFSETS[i] + WIDTHS[i]],
                    (swap_send, swap_recv), 2 * i + 1, to_core,
                )
            )
    for m in range(MB):
        for copy in pushes[m]:
            copy.start()
    for copy in swaps:
        copy.start()
    grad_held[place] = grad_ready[place]
    for copy in fetches:
        copy.wait()

    late = [(p, N_EARLY[p] * COLS, COLS) for p in range(3)] + [(0, VEC_AT, 128)]
    early = [(p, b * COLS, COLS) for p, b in EARLY]

    def number(p, at, width):
        return 12 if width != COLS else PART_AT[p] // COLS + at // COLS

    def store(kind, p, at, width):
        return stores[4 * kind + 3].at[0] if width != COLS else stores[4 * kind + p].at[at // COLS]

    def copies(p, phase, at, width):
        order = ORDERS[p]
        axis = order[phase]
        out = []
        for step in (1, 2, 3):
            to, index = peer(axis, step)
            chunk = pick(store(phase, p, at, width), axis, index, dims_after(order, phase))
            land = store(3 + phase, p, at, width).at[step - 1]
            out.append(
                send(
                    chunk, land, (ring_send, ring_recv), 39 + 39 * phase + number(p, at, width) * 3 + step - 1, to
                )
            )
        return out

    def first_copies(p, at, width):
        order = ORDERS[p]
        axis = order[0]
        n = lead(order, 1)[0]
        halves = (slice(0, n // 2), slice(n // 2, n))
        (up, up_at), (_, far_at), (down, down_at) = (peer(axis, step) for step in (1, 2, 3))
        out = []
        for k, (index, half, slot, to) in enumerate(
            (
                (far_at, 0, 2, up), (far_at, 1, 2, down), (up_at, 1, 0, up), (down_at, 0, 1, down),
                (up_at, 0, 0, up), (down_at, 1, 1, down),
            )
        ):
            chunk = pick(store(0, p, at, width), axis, index, dims_after(order, 0)).at[halves[half]]
            land = store(3, p, at, width).at[slot, halves[half]]
            out.append(send(chunk, land, (ring_send, ring_recv), number(p, at, width) * 6 + k, to))
        return out

    def begin(p, at, width):
        for copy in first_copies(p, at, width)[:4]:
            copy.start()

    def relay(p, at, width):
        order = ORDERS[p]
        axis = order[0]
        n = lead(order, 1)[0]
        all_copies = first_copies(p, at, width)
        land = store(3, p, at, width)
        for half, step in ((0, 1), (1, 3)):
            all_copies[half].wait_recv()
            own = pick(store(0, p, at, width), axis, peer(axis, step)[1], dims_after(order, 0))

            def add(i, _, own=own):
                own[i] = (own[i].astype(f32) + land[2, i].astype(f32)).astype(bf16)
                return 0

            lax.fori_loop(half * (n // 2), (half + 1) * (n // 2), add, 0)
            all_copies[4 + half].start()

    def multiply(p, b):
        i, col = PRODUCT[(p, b)]
        if i == 0:
            mine = right_q.at[:, pl.ds(pl.multiple_of(core * WIDTHS[0] + col, 512), COLS)]
        else:
            mine = own_right.at[:, OFFSETS[i] + col : OFFSETS[i] + col + COLS]
        theirs = peer_right.at[:, OFFSETS[i] + col : OFFSETS[i] + col + COLS]

        def rows_block(x, _):
            rows = pl.ds(pl.multiple_of(x * 256, 256), 256)
            value = dot(lefts[i][rows, :], mine[...]) + dot(peer_left[i, rows, :], theirs[...])
            stores[p][b, x] = value.astype(bf16).reshape(2, 2, 4, 16, COLS)
            return 0

        lax.fori_loop(0, 4, rows_block, 0)

    def reduce(phase, p, at, width):
        order = ORDERS[p]
        axis = order[phase]
        land = store(3 + phase, p, at, width)
        if phase == 0:
            all_copies = first_copies(p, at, width)
            for copy in all_copies[:2]:
                copy.wait_send()
            for copy in all_copies[2:]:
                copy.wait()
        else:
            for copy in copies(p, phase, at, width):
                copy.wait()
        own = pick(store(phase, p, at, width), axis, coordinate(axis), dims_after(order, phase))
        if phase < 2:
            dst = store(phase + 1, p, at, width)

            def add(n, _):
                value = own[n].astype(f32)
                for step in range(3 if phase else 2):
                    value = value + land[step, n].astype(f32)
                dst[n] = value.astype(bf16)
                return 0

            lax.fori_loop(0, lead(order, phase + 1)[0], add, 0)
            for copy in copies(p, phase + 1, at, width):
                copy.start()
            return
        value = own[...].astype(f32)
        for step in range(3):
            value = value + land[step].astype(f32)
        to = PART_AT[p] + at if width == COLS else 6144
        gathered[core, row_place, :, to : to + width] = value.astype(bf16)
        square = value * value
        if width != COLS:
            square = square * jnp.where(core == 0, 1.0, 0.0)
        squares = square_acc[...]
        for c in range(0, width, 128):
            squares = squares + square[:8, c : c + 128] + square[8:, c : c + 128]
        square_acc[...] = squares

    def run_task(phase, p, b):
        if phase == "relay":
            relay(p, b * COLS, COLS)
        else:
            reduce(phase, p, b * COLS, COLS)

    square_acc[...] = jnp.zeros_like(square_acc)
    for copy in swaps:
        copy.wait()
    for p, at, width in early:
        multiply(p, at // COLS)
        begin(p, at, width)

    for m in range(MB):
        load_side(held, m, keys, values, keys_t, None, seg_col)
        acc_kv[...] = jnp.zeros_like(acc_kv)
        for copy in pushes[m]:
            copy.wait_recv()

        def query_block(j, _, m=m):
            for at, tasks in TASKS.items():
                if at // NBLK == m:

                    @pl.when(j == at % NBLK)
                    def _(tasks=tasks):
                        for phase, p, b in tasks:
                            run_task(phase, p, b)

            query_t = pair(held, m, j, slice(0, HEAD))
            seg_row = pair(held, m, j, slice(3 * HEAD, 3 * HEAD + 1)).astype(f32)
            grad_t = pair(grad_held, m, j, slice(0, HEAD))
            row_lse = pair(lse, m, j, slice(0, 1))
            delta = jnp.sum(grad_t.astype(f32) * pair(full, m, j, slice(0, HEAD)), axis=0, keepdims=True)
            acc_q = jnp.zeros((HEAD, BLK), f32)
            none = jnp.zeros((BLK, HEAD), bf16)
            sides = jnp.concatenate(
                [jnp.concatenate([query_t.T, none], axis=1), jnp.concatenate([none, grad_t.T], axis=1)], axis=0
            )
            block = lambda k: slice(k * BLK, (k + 1) * BLK)
            ahead = (dot(keys[block(0), :], query_t), dot(values[block(0), :], grad_t))
            behind = None
            for k in range(NBLK + 1):
                if k < NBLK:
                    at = block(k)
                    s, dp = ahead
                    if k + 1 < NBLK:
                        ahead = (dot(keys[block(k + 1), :], query_t), dot(values[block(k + 1), :], grad_t))
                if behind is not None:
                    to, ds, pb = behind
                    acc_q = acc_q + dot(keys_t[:, to], ds)
                    acc_kv[to, :] += dot(jnp.concatenate([ds, pb], axis=1), sides)
                if k < NBLK:
                    col = seg_col[at, :]
                    same = jnp.concatenate([col, col], axis=1) == seg_row
                    p = jnp.exp2(jnp.where(same, s * SCALE2 - row_lse, NEG_LARGE))
                    behind = (at, (p * (dp - delta)).astype(bf16), p.astype(bf16))
            acc_q = (acc_q * SCALE).astype(bf16)
            out_t[2 * j, m, :HEAD, :] = acc_q[:, :TOK]
            out_t[2 * j + 1, m, :HEAD, :] = acc_q[:, TOK:]
            return 0

        lax.fori_loop(0, NBLK, query_block, 0)
        for s in range(N_CTX):
            at = slice(s * TOK, (s + 1) * TOK)
            both = acc_kv[at, :].T
            out_t[s, m, HEAD : 2 * HEAD, :] = (both[:HEAD] * SCALE).astype(bf16)
            out_t[s, m, 2 * HEAD :, :] = both[HEAD:].astype(bf16)
        for copy in returns[m]:
            copy.start()
        landed[place, m] = out_t[place, m]

    fetch_w = [
        pltpu.make_async_copy(w_qkv.at[:, n * COLS : (n + 1) * COLS], w_part.at[n % 2], local_sem.at[4 + n])
        for n in range(6)
    ]
    done = [task for tasks in TASKS.values() for task in tasks]
    for phase in ("relay", 0, 1):
        for p, b in EARLY:
            if (phase, p, b) not in done:
                run_task(phase, p, b)
    gives = []
    for m in range(MB):
        for copy in pushes[m]:
            copy.wait_send()
        for copy in returns[m]:
            copy.wait()
        if m == 0:
            fetch_w[0].start()
            fetch_w[1].start()
        for i in range(HEADS // 2):
            for kind in range(3):
                rows = slice(kind * HEAD, (kind + 1) * HEAD)
                both = jnp.concatenate([landed[2 * i, m, rows, :], landed[2 * i + 1, m, rows, :]], axis=0)
                right_q[m * TOK : (m + 1) * TOK, kind * D + i * 128 : kind * D + (i + 1) * 128] = both.T
        rows = slice(m * TOK, (m + 1) * TOK)
        gives.append(
            send(
                right_q.at[rows, pl.ds(pl.multiple_of(other * WIDTHS[0], 512), WIDTHS[0])],
                peer_right.at[rows, 0 : WIDTHS[0]], (swap_send, swap_recv), (1, 9)[m], to_core,
            )
        )
        gives[m].start()
    sum_q = jnp.sum(right_q[:, :D].astype(f32), axis=0, keepdims=True)
    sum_v = jnp.sum(right_q[:, 2 * D :].astype(f32), axis=0, keepdims=True)
    row = lax.broadcasted_iota(jnp.int32, (16, TOK), 0)
    own_vec[...] = jnp.zeros_like(own_vec)
    for f in range(N_FSDP):
        cols = slice(f * TOK, (f + 1) * TOK)
        value = jnp.where(row == 0, sum_q[:, cols], jnp.where(row == 1, sum_v[:, cols], vec[f]))
        own_vec[f // 2, f % 2, 0, 0] = value.astype(bf16)
    give_vec = send(own_vec, peer_vec, (swap_send, swap_recv), 8, to_core)
    give_vec.start()
    for copy in gives:
        copy.wait()
    for p, at, width in late:
        if width == COLS:
            multiply(p, at // COLS)
        else:
            give_vec.wait()
            stores[3][0] = (own_vec[...].astype(f32) + peer_vec[...].astype(f32)).astype(bf16)
        begin(p, at, width)
    for n in range(6):
        fetch_w[n].wait()
        part = dot_nt(right_q[:, n * COLS : (n + 1) * COLS], w_part[n % 2])
        if n == 0:
            out_x[...] = part
        else:
            out_x[...] += part
        if n < 4:
            fetch_w[n + 2].start()
    for piece in late:
        relay(*piece)
    for piece in early:
        reduce(2, *piece)
    for phase in range(3):
        for piece in late:
            reduce(phase, *piece)
    squares = square_acc[...]
    yl, z = lax.axis_index("yl"), lax.axis_index("z")
    z_first, y_first = slice(0, HALF_Z), slice(HALF_Z, 6272)
    to_y = {"yl": 1 - yl}
    gather_sems = (gather_send, gather_recv)
    sq_sems = (sq_send, sq_recv)

    def spread(buffer, axis, base):
        at = coordinate(axis)
        out = []
        for step in (1, 2, 3):
            out.append(send(buffer.at[at], buffer.at[at], sq_sems, base + step - 1, peer(axis, step)[0]))
        return out

    def total(buffer):
        return (buffer[0] + buffer[1]) + (buffer[2] + buffer[3])

    sq_z[z] = squares
    squares_z = spread(sq_z, "z", 0)
    first_z = [
        send(gathered.at[core, row_place, :, z_first], gathered.at[core, row_place, :, z_first], gather_sems, step - 1, peer("z", step)[0])
        for step in (1, 2, 3)
    ]
    first_y = send(gathered.at[core, row_place, :, y_first], gathered.at[core, row_place, :, y_first], gather_sems, 3, to_y)
    for copy in (*squares_z, *first_z, first_y):
        copy.start()
    for copy in squares_z:
        copy.wait()
    y_at = coordinate("y")
    sq_y[y_at] = total(sq_z)
    squares_y = spread(sq_y, "y", 3)
    for copy in squares_y:
        copy.start()
    for copy in (*first_z, first_y):
        copy.wait()
    quarter = pl.ds(yl * 4, 4)
    second_y = send(
        gathered.at[core, quarter, :, z_first], gathered.at[core, quarter, :, z_first], gather_sems, 4, to_y
    )
    second_y.start()
    second_z = []
    for step in (1, 2, 3):
        for half in range(2):
            view = gathered.at[core, half * 4 + z, :, y_first]
            second_z.append(send(view, view, gather_sems, 5 + (step - 1) * 2 + half, peer("z", step)[0]))
    for copy in second_z:
        copy.start()
    for copy in squares_y:
        copy.wait()
    x_at = coordinate("x")
    sq_x[x_at] = total(sq_y)
    squares_x = spread(sq_x, "x", 6)
    for copy in squares_x:
        copy.start()
    for copy in squares_x:
        copy.wait()
    sq_c[core] = total(sq_x)
    square_c = send(sq_c.at[core], sq_c.at[core], sq_sems, 9, to_core)
    square_c.start()
    square_c.wait()
    out_sq[...] = sq_c[0] + sq_c[1]
    second_y.wait()
    for copy in second_z:
        copy.wait()
    last = send(gathered.at[core], gathered.at[core], gather_sems, 11, to_core)
    last.start()
    last.wait()
    locals_ = []
    for c in range(2):
        for p in range(3):
            for b in range(N_EARLY[p] + 1):
                i, col = PRODUCT[(p, b)]
                target, base = ((out_attn, 0), (out_attn, 3072), (out_ffn, 0), (out_ffn, FF))[i]
                base = base + c * WIDTHS[i] + col
                at = PART_AT[p] + b * COLS
                locals_.append(
                    pltpu.make_async_copy(
                        gathered.at[c, :, :, at : at + COLS], target.at[:, :, base : base + COLS],
                        out_sem.at[len(locals_)],
                    )
                )
    locals_.append(pltpu.make_async_copy(gathered.at[0, :, :, 6144:], out_vec, out_sem.at[len(locals_)]))
    for copy in locals_:
        copy.start()
    for copy in locals_:
        copy.wait()


def back(lefts, rights, vec, grad_ready, held, full, lse, w_qkv):
    vmem = pl.BlockSpec(memory_space=pltpu.VMEM)
    hbm = pl.BlockSpec(memory_space=pl.ANY)
    scratch = [
        pltpu.VMEM((4, D, ROWS), bf16),
        pltpu.VMEM((ROWS, 6144), bf16),
        pltpu.VMEM((ROWS, 6144), bf16),
        pltpu.VMEM((4, 2, 2, 4, 16, 128), bf16),
        pltpu.VMEM((4, 2, 2, 4, 16, 128), bf16),
    ]
    for kind in range(6):
        n = kind if kind < 3 else kind - 2
        for p, count, width in (*((p, N_EARLY[p] + 1, COLS) for p in range(3)), (0, 1, 128)):
            landing = (3,) if kind >= 3 else ()
            scratch.append(pltpu.VMEM((count, *landing, *lead(ORDERS[p], n), 16, width), bf16))
    scratch += [
        pltpu.VMEM((2, 8, 16, 6272), bf16),
        pltpu.VMEM((4, 8, 128), f32),
        pltpu.VMEM((4, 8, 128), f32),
        pltpu.VMEM((4, 8, 128), f32),
        pltpu.VMEM((2, 8, 128), f32),
        pltpu.VMEM((N_CTX, MB, SENT, TOK), bf16),
        pltpu.VMEM((N_CTX, MB, HEAD, TOK), bf16),
        pltpu.VMEM((N_CTX, MB, 3 * HEAD, TOK), bf16),
        pltpu.VMEM((N_CTX, MB, 3 * HEAD, TOK), bf16),
        pltpu.VMEM((ROWS, 3 * D), bf16),
        pltpu.VMEM((PACK, HEAD), bf16),
        pltpu.VMEM((PACK, HEAD), bf16),
        pltpu.VMEM((HEAD, PACK), bf16),
        pltpu.VMEM((PACK, TOK), f32),
        pltpu.VMEM((PACK, 2 * HEAD), f32),
        pltpu.VMEM((8, 128), f32),
        pltpu.VMEM((2, D, COLS), bf16),
    ]
    for count in (10, 10, 156, 156, 12, 12, 10, 10, 32, 32, 32, 32, 10, 25):
        scratch.append(pltpu.SemaphoreType.DMA((count,)))
    out = pl.pallas_call(
        back_kernel,
        in_specs=[vmem] * 4 + [hbm] * 3 + [vmem, vmem, hbm, vmem, vmem, hbm],
        out_specs=[hbm, hbm, hbm, vmem, vmem],
        out_shape=[
            jax.ShapeDtypeStruct((8, 16, 4 * D), bf16),
            jax.ShapeDtypeStruct((8, 16, 2 * FF), bf16),
            jax.ShapeDtypeStruct((8, 16, 128), bf16),
            jax.ShapeDtypeStruct((8, 128), f32),
            jax.ShapeDtypeStruct((ROWS, D), f32),
        ],
        scratch_shapes=scratch,
        compiler_params=pltpu.CompilerParams(
            collective_id=1, has_side_effects=True, vmem_limit_bytes=60 * 2**20
        ),
        cost_estimate=pl.CostEstimate(
            flops=2 * 512 * D * 6144 + 10 * MB * PACK * PACK * HEAD, bytes_accessed=16 * 2**20,
            transcendentals=MB * PACK * PACK,
        ),
        name="back",
    )(*lefts, *rights, vec, grad_ready, held, full, lse, w_qkv)
    return out[0].reshape(TOK, 4 * D), out[1].reshape(TOK, 2 * FF), out[2], out[3], out[4]


def layer_stats(values, gain_row, shift_row):
    center = values - jnp.mean(values, axis=-1, keepdims=True)
    inverse = lax.rsqrt(jnp.mean(center * center, axis=-1, keepdims=True) + NORM_EPS)
    normal = center * inverse
    return (normal * gain_row + shift_row, normal, inverse)


def layer_back(grad_value, normal, inverse, gain_row):
    scaled = grad_value * gain_row
    return inverse * (
        scaled
        - jnp.mean(scaled, axis=-1, keepdims=True)
        - normal * jnp.mean(scaled * normal, axis=-1, keepdims=True)
    )


N_CHUNK = 8
CHUNK = FF // N_CHUNK
ERF_TOP = (
    -2.72614225801306e-10, 2.77068142495902e-08, -2.10102402082508e-06, -5.69250639462346e-05,
    -7.34990630326855e-04, -2.95459980854025e-03, -1.60960333262415e-02,
)
ERF_LOW = (
    -1.45660718464996e-05, -2.13374055278905e-04, -1.68282697438203e-03, -7.37332916720468e-03,
    -1.42647390514189e-02,
)


def erf(value):
    value = jnp.clip(value, -4.0, 4.0)
    square = value * value
    top, low = jnp.full_like(square, ERF_TOP[0]), jnp.full_like(square, ERF_LOW[0])
    for c in ERF_TOP[1:]:
        top = top * square + c
    for c in ERF_LOW[1:]:
        low = low * square + c
    return value * top / low


def w_block(ref, n):
    per = ref.shape[-1] // CHUNK
    at = (n % per) * CHUNK
    return ref[n // per, :, :, :, at : at + CHUNK].reshape(D, CHUNK)


def dense_part(
    mixed_ref, x_ref, cot_ref, seg_ref, small_ref, w_out, w_one, w_two, before,
    out_ref, one_ref, x_t, o_t, h_t, f_t, a_low_ref, du_ref, g_ref, vec_ref, ready_ref,
    mixed, normal_one_ref, slope, total,
):
    def row(i):
        return small_ref[i : i + 1, :]

    def put(i, value):
        for f in range(N_FSDP):
            vec_ref[f, i : i + 1, :] = value[:, f * TOK : (f + 1) * TOK]

    def sums(value):
        return jnp.sum(value, axis=0, keepdims=True)

    vec_ref[...] = jnp.zeros_like(vec_ref)
    for m in range(MB):
        tok = slice(m * TOK, (m + 1) * TOK)
        for i in range(HEADS // 2):
            both = jnp.concatenate([mixed_ref[2 * i, m], mixed_ref[2 * i + 1, m]], axis=0)
            o_t[i * 128 : (i + 1) * 128, tok] = both
            mixed[tok, i * 128 : (i + 1) * 128] = both.T
    before(0)
    branch = jnp.concatenate([dot(mixed[...], w_block(w_out, n)) for n in range(2)], axis=1)
    normed_one, normal_one, inverse_one = layer_stats(x_ref[...].astype(f32) + branch + row(2), row(4), row(5))
    normal_one_ref[...] = normal_one
    normed_low = normed_one.astype(bf16)
    h_t[...] = normed_low.T
    total[...] = normed_one + row(3)
    before(1)
    ahead = dot(normed_low, w_block(w_one, 0))
    for n in range(N_CHUNK):
        cols = slice(n * CHUNK, (n + 1) * CHUNK)
        bias = small_ref[8 + n // 2 : 9 + n // 2, (n % 2) * CHUNK : (n % 2 + 1) * CHUNK]
        u = ahead + bias
        if n + 1 < N_CHUNK:
            ahead = dot(normed_low, w_block(w_one, n + 1))
        share = 0.5 + 0.5 * erf(u * math.sqrt(0.5))
        g_ref[:, cols] = (u * share).astype(bf16)
        slope[:, cols] = share + u * (jnp.exp(-0.5 * u * u) * (1.0 / math.sqrt(2.0 * math.pi)))
    before(2)
    for n in range(N_CHUNK):
        total[...] += dot_nt(g_ref[:, n * CHUNK : (n + 1) * CHUNK], w_block(w_two, n))
    output, normal_two, inverse_two = layer_stats(total[...], row(6), row(7))
    keep = []
    for m in range(MB):
        inside = jnp.where(seg_ref[m, 0:1, :].astype(f32) < 8.0, 1.0, 0.0)
        keep.append(jnp.broadcast_to(inside, (TOK, TOK)).T[:, 0:1])
    keep = jnp.concatenate(keep, axis=0)
    out_ref[...] = (output * keep).astype(bf16)
    grad_out = cot_ref[...].astype(f32) * keep
    put(6, sums(grad_out * normal_two))
    put(7, sums(grad_out))
    grad_two = layer_back(grad_out, normal_two, inverse_two, row(6))
    f_low = grad_two.astype(bf16)
    f_t[...] = f_low.T
    put(3, sums(f_low.astype(f32)))
    total[...] = grad_two
    ahead = dot(f_low, w_block(w_two, 0))
    for n in range(N_CHUNK):
        cols = slice(n * CHUNK, (n + 1) * CHUNK)
        product = ahead
        if n + 1 < N_CHUNK:
            ahead = dot(f_low, w_block(w_two, n + 1))
        if n:
            total[...] += dot_nt(du, w_block(w_one, n - 1))
        du = (product * slope[:, cols]).astype(bf16)
        du_ref[:, cols] = du
        part = sums(du.astype(f32))
        for i in range(CHUNK // TOK):
            f = (n % 2) * (CHUNK // TOK) + i
            vec_ref[f, 8 + n // 2 : 9 + n // 2, :] = part[:, i * TOK : (i + 1) * TOK]
    grad_normed = total[...] + dot_nt(du, w_block(w_one, N_CHUNK - 1))
    normal_one = normal_one_ref[...]
    put(4, sums(grad_normed * normal_one))
    put(5, sums(grad_normed))
    grad_one = layer_back(grad_normed, normal_one, inverse_one, row(4))
    one_ref[...] = grad_one
    a_low = grad_one.astype(bf16)
    a_low_ref[...] = a_low
    put(2, sums(a_low.astype(f32)))
    for n in range(2):
        part = a_low[:, n * CHUNK : (n + 1) * CHUNK]
        part = dot_nt(part, w_block(w_out, n))
        grad_mixed = part if n == 0 else grad_mixed + part
    grad_mixed = grad_mixed.T.astype(bf16)
    for h in range(HEADS):
        for m in range(MB):
            ready_ref[h, m] = grad_mixed[h * HEAD : (h + 1) * HEAD, m * TOK : (m + 1) * TOK]
    x_t[...] = x_ref[...].T


def adamw(weight, grad_value, first, second, rate, decay):
    first_new = BETA_FIRST * first + (1.0 - BETA_FIRST) * grad_value
    second_new = BETA_SECOND * second + (1.0 - BETA_SECOND) * grad_value * grad_value
    first_hat = first_new * (1.0 / (1.0 - BETA_FIRST**STEP))
    second_hat = second_new * (1.0 / (1.0 - BETA_SECOND**STEP))
    weight_new = weight - rate * (first_hat / (jnp.sqrt(second_hat) + ADAM_EPS) + decay * weight)
    return (weight_new, first_new, second_new)


def finish_kernel(
    squares, grad_vec, grad_attn, grad_ffn, aw, am, av, fw, fm, fv, vw, vm, vv, one, grad_x, y,
    norm, aw_new, am_new, av_new, fw_new, fm_new, fv_new, vw_new, vm_new, vv_new, a_copy, f_copy, bias, dx, y_out,
):
    total = jnp.sum(jnp.sum(squares[...], axis=0, keepdims=True), axis=1, keepdims=True)
    root = jnp.sqrt(total)
    norm[...] = root
    factor = jnp.minimum(1.0, CLIP_NORM / (root + 1e-06))
    rate = D ** (-0.5)
    for grad, ins, outs, low, scale in (
        (grad_attn, (aw, am, av), (aw_new, am_new, av_new), a_copy, ATTN_RATE_SCALE * rate),
        (grad_ffn, (fw, fm, fv), (fw_new, fm_new, fv_new), f_copy, rate),
    ):
        for at in range(0, grad.shape[1], 1024):
            cols = slice(at, at + 1024)
            weight, first, second = adamw(
                ins[0][:, cols], grad[:, cols].astype(f32) * factor, ins[1][:, cols], ins[2][:, cols], scale,
                WEIGHT_DECAY,
            )
            outs[0][:, cols] = weight
            outs[1][:, cols] = first
            outs[2][:, cols] = second
            low[:, cols] = weight.astype(bf16)
    clipped = grad_vec[0].astype(f32) * factor
    vw_new[...], vm_new[...], vv_new[...] = adamw(
        vw[...], clipped[:12], vm[...], vv[...], RATE_VECTOR, 0.0
    )
    bias[...] = clipped[2:3]
    dx[...] = (one[...] + grad_x[...]).astype(bf16)
    y_out[...] = y[...]


def finish(squares, grad_vec, grad_attn, grad_ffn, attn, ffn, vec, one, grad_x, y):
    steps = 8
    rows = TOK // steps
    whole = lambda a: pl.BlockSpec(a.shape, lambda i: (0,) * len(a.shape))
    part = lambda a: pl.BlockSpec((a.shape[0] // steps, a.shape[1]), lambda i: (i, 0))
    shape = lambda a, dt=f32: jax.ShapeDtypeStruct(a.shape, dt)
    ins = [squares, grad_vec, grad_attn, grad_ffn, *attn, *ffn, *vec, one, grad_x, y]
    specs = [whole(squares), pl.BlockSpec((1, 16, TOK), lambda i: (0, 0, 0)), part(grad_attn), part(grad_ffn)]
    specs += [part(a) for a in (*attn, *ffn)] + [whole(a) for a in vec] + [part(a) for a in (one, grad_x, y)]
    outs = [jax.ShapeDtypeStruct((1, 1), f32), *(shape(a) for a in (*attn, *ffn, *vec))]
    outs += [shape(attn[0], bf16), shape(ffn[0], bf16), jax.ShapeDtypeStruct((1, TOK), f32), shape(one, bf16), shape(y, bf16)]
    out_specs = [whole(outs[0]), *(part(a) for a in outs[1:7]), *(whole(a) for a in outs[7:10])]
    out_specs += [part(outs[10]), part(outs[11]), whole(outs[12]), part(outs[13]), part(outs[14])]
    return pl.pallas_call(
        finish_kernel,
        grid=(steps,),
        in_specs=specs,
        out_specs=out_specs,
        out_shape=outs,
        compiler_params=pltpu.CompilerParams(vmem_limit_bytes=60 * 2**20),
        cost_estimate=pl.CostEstimate(flops=40 * 12 * D * TOK, bytes_accessed=44 * 2**20, transcendentals=24 * D * TOK),
        name="finish",
    )(*ins)


def shards(
    tokens, cotangent, dest, lengths, attn_weight, attn_first, attn_second,
    ffn_weight, ffn_first, ffn_second, vectors, vec_first, vec_second,
):
    x = tokens.reshape(ROWS, D)
    cot = cotangent.reshape(ROWS, D)
    (
        w_qkv, held, mixed_full, lse, output, grad_one, x_t, o_t, h_t, f_t, a_low, du, g, vec_rows, grad_ready,
    ) = front(attn_weight, ffn_weight, vectors, dest[:, 0], lengths[:, 0], x, cot)
    grad_attn, grad_ffn, grad_vec, squares, grad_x = back(
        (x_t, o_t, h_t, f_t),
        (a_low, du, g),
        vec_rows,
        grad_ready,
        held,
        mixed_full,
        lse,
        w_qkv.reshape(D, 3 * D),
    )
    (
        norm, aw, am, av, fw, fm, fv, vw, vm, vv, a_copy, f_copy, bias, input_grad, output,
    ) = finish(
        squares, grad_vec, grad_attn, grad_ffn,
        (attn_weight, attn_first, attn_second), (ffn_weight, ffn_first, ffn_second),
        (vectors, vec_first, vec_second), grad_one, grad_x, output,
    )
    return (
        output.reshape(tokens.shape), input_grad.reshape(tokens.shape), norm.reshape(()),
        aw, am, av, fw, fm, fv, vw, vm, vv, a_copy, f_copy, bias.reshape(TOK),
    )


def solution(mesh):
    fine = Mesh(mesh.devices.reshape(2, 4, 2, 4, 2), ("yl", "z", "core", "x", "yh"))
    act = P(None, FSDP, CTX, None)
    row = P(FSDP, None)
    col = P(None, FSDP)
    return jax.shard_map(
        shards,
        mesh=fine,
        in_specs=(act, act, P(None, FSDP, CTX), P(None, FSDP, None), row, row, row, row, row, row, col, col, col),
        out_specs=(act, act, P(), row, row, row, row, row, row, col, col, col, row, row, P(FSDP)),
        check_vma=False,
    )
```
